32 devices in a mesh: dp: 8 (over y, x, core), mp: 4 (over z).
Axes of the slice: x: 2, y: 2, z: 4, core: 2. Of those that a mesh axis runs over, the one named last changes fastest.
Arguments:
- tokens: int32 [32, 512], P('dp'), may hold values from 0 to 15359
- text_box: int32 [32, 512, 4], P(('dp', 'mp')), may hold values from 0 to 1000, as said below
- segments: int32 [32, 512], P(('dp', 'mp')), may hold values from 0 to 3, never falling along the last dimension, each value on 1 to 256 neighbouring positions
- alive_text: int32 [32, 512], P(('dp', 'mp')), may hold values from 0 to 1, as said below
- features: bfloat16 [1568, 256], P(('dp', 'mp')), may hold values from -6 to 6
- mask_pos: int32 [2560], P(('dp', 'mp')), may hold values from 0 to 511
- mask_label: int32 [2560], P('dp'), may hold values from 0 to 15359
- mask_valid: int32 [2560], P('dp'), may hold values from 0 to 1
- projections: float32 [4, 768, 768], P(None, 'dp')
- projections_first: float32 [4, 768, 768], P(None, 'dp'), may hold values from -7.1525574e-07 to 7.1525574e-07
- projections_second: float32 [4, 768, 768], P(None, 'dp'), may hold values from 1.249904e-15 to 4.999616e-15
- box_tables: float32 [4, 1024, 128], P(None, 'dp'), may hold values from -0.3125 to 0.3125
- box_tables_first: float32 [4, 1024, 128], P(None, 'dp'), may hold values from -7.1525574e-07 to 7.1525574e-07
- box_tables_second: float32 [4, 1024, 128], P(None, 'dp'), may hold values from 1.249904e-15 to 4.999616e-15
- position_table: float32 [512, 768], P('dp'), may hold values from -0.3125 to 0.3125
- position_table_first: float32 [512, 768], P('dp'), may hold values from -7.1525574e-07 to 7.1525574e-07
- position_table_second: float32 [512, 768], P('dp'), may hold values from 1.249904e-15 to 4.999616e-15
- visual_proj: float32 [256, 768], P('dp'), may hold values from -0.375 to 0.375
- visual_proj_first: float32 [256, 768], P('dp'), may hold values from -7.1525574e-07 to 7.1525574e-07
- visual_proj_second: float32 [256, 768], P('dp'), may hold values from 1.249904e-15 to 4.999616e-15
- small_params: float32 [17, 768], P(None, 'dp')
- small_params_first: float32 [17, 768], P(None, 'dp'), may hold values from -3.8146973e-06 to 3.8146973e-06
- small_params_second: float32 [17, 768], P(None, 'dp'), may hold values from 3.12476e-14 to 1.249904e-13
- word_table: float32 [15360, 768], P(('mp', 'dp'))
- word_table_first: float32 [15360, 768], P(('mp', 'dp')), may hold values from -7.1525574e-07 to 7.1525574e-07
- word_table_second: float32 [15360, 768], P(('mp', 'dp')), may hold values from 1.249904e-15 to 4.999616e-15
- feedforward: float32 [2, 768, 3072], P(None, 'dp', 'mp'), may hold values from -0.21875 to 0.21875
- feedforward_first: float32 [2, 768, 3072], P(None, 'dp', 'mp'), may hold values from -7.1525574e-07 to 7.1525574e-07
- feedforward_second: float32 [2, 768, 3072], P(None, 'dp', 'mp'), may hold values from 1.249904e-15 to 4.999616e-15
Outputs:
- new_projections: float32 [4, 768, 768], P(None, 'dp')
- new_projections_first: float32 [4, 768, 768], P(None, 'dp')
- new_projections_second: float32 [4, 768, 768], P(None, 'dp')
- new_box_tables: float32 [4, 1024, 128], P(None, 'dp')
- new_box_tables_first: float32 [4, 1024, 128], P(None, 'dp')
- new_box_tables_second: float32 [4, 1024, 128], P(None, 'dp')
- new_position_table: float32 [512, 768], P('dp')
- new_position_table_first: float32 [512, 768], P('dp')
- new_position_table_second: float32 [512, 768], P('dp')
- new_visual_proj: float32 [256, 768], P('dp')
- new_visual_proj_first: float32 [256, 768], P('dp')
- new_visual_proj_second: float32 [256, 768], P('dp')
- new_small_params: float32 [17, 768], P(None, 'dp')
- new_small_params_first: float32 [17, 768], P(None, 'dp')
- new_small_params_second: float32 [17, 768], P(None, 'dp')
- new_word_table: float32 [15360, 768], P(('mp', 'dp'))
- new_word_table_first: float32 [15360, 768], P(('mp', 'dp'))
- new_word_table_second: float32 [15360, 768], P(('mp', 'dp'))
- new_feedforward: float32 [2, 768, 3072], P(None, 'dp', 'mp')
- new_feedforward_first: float32 [2, 768, 3072], P(None, 'dp', 'mp')
- new_feedforward_second: float32 [2, 768, 3072], P(None, 'dp', 'mp')
- loss_sum: float32 [], replicated
- loss_count: float32 [], replicated
- grad_norm: float32 [], replicated
The draws below stay inside these ranges and needn't reach their ends.
Inputs may be any that keep to these rules, and one draw needn't show every extreme that they name: `text_box`: left < right and top < bottom in every box, each side at most 100 apart. `alive_text`: each row is 1 on a leading run of 256 or more positions and 0 after it.
All inputs are finite; a program needn't handle non-finite values.
Results may differ from the reference program's by a relative error of at most 0.02.
The reference program's roundings to bfloat16 on the way count: a program that leaves them out, or rounds other values in their place, can miss the bound.
Values may be sent and summed in bfloat16 or wider, within the bound.
A program may use at most 256 MiB of HBM per device.

```python
import math
from functools import partial
import jax
import jax.numpy as jnp
import numpy as np
from jax import lax

D = 768
H = 12
HD = 64
FF = 3072
CSZ = 128
NBOX = 1024
NPOS = 512
VCH = 256
NB = 64
GRID = 7
TEXT = 512
SEQ_DEV = 1
STEP = 10
VIS = 49
LEN = 561
VROWS = 17
VOCAB = 15360
SEQS = 32
M_DEV = 80
SLOTS = 2560
N_DP = 8
N_MP = 4


def shared_words(key):
    key = jax.random.fold_in(key, 40)
    keys = jax.random.split(key, 2)
    words = jax.random.randint(keys[0], (SEQS, TEXT), 0, VOCAB)
    words = words.at[0, 0].set(VOCAB - 1).at[0, 1].set(0)
    places = jax.random.randint(keys[1], (SLOTS,), 0, SEQ_DEV * TEXT)
    places = places.at[0].set(0).at[1].set(1).at[2].set(SEQ_DEV * TEXT - 1)
    return (words.astype(jnp.int32), places.astype(jnp.int32))


def draw_tokens(key, part):
    words, places = shared_words(key)
    return words


def draw_mask_pos(key, part):
    words, places = shared_words(key)
    return places


def draw_mask_label(key, part):
    words, places = shared_words(key)
    slot_index = jnp.arange(SLOTS, dtype=jnp.int32)
    seq_index = slot_index // M_DEV * SEQ_DEV + places // TEXT
    return words[seq_index, places % TEXT].astype(jnp.int32)


def draw_text_box(key, part):
    key = jax.random.fold_in(key, 11)
    keys = jax.random.split(key, 4)
    left_edge = jax.random.randint(keys[0], (SEQS, TEXT), 0, 901)
    top_edge = jax.random.randint(keys[1], (SEQS, TEXT), 0, 901)
    wide_span = jax.random.randint(keys[2], (SEQS, TEXT), 1, 101)
    tall_span = jax.random.randint(keys[3], (SEQS, TEXT), 1, 101)
    left_edge = left_edge.at[0, 0].set(900)
    wide_span = wide_span.at[0, 0].set(100)
    top_edge = top_edge.at[0, 0].set(900)
    tall_span = tall_span.at[0, 0].set(100)
    left_edge = left_edge.at[0, 1].set(0)
    top_edge = top_edge.at[0, 1].set(0)
    return jnp.stack([left_edge, top_edge, left_edge + wide_span, top_edge + tall_span], -1).astype(jnp.int32)


def draw_alive_text(key, part):
    key = jax.random.fold_in(key, 12)
    lengths = jax.random.randint(key, (SEQS, 1), TEXT // 2, TEXT + 1)
    lengths = lengths.at[0, 0].set(TEXT // 2)
    return (jnp.arange(TEXT)[None, :] < lengths).astype(jnp.int32)


def draw_mask_valid(key, part):
    key = jax.random.fold_in(key, 13)
    slot_index = jnp.arange(SLOTS)
    device = slot_index // M_DEV
    data_rank = device // N_MP
    model_rank = device % N_MP
    level = 150 + 350 * data_rank // max(N_DP - 1, 1) + 350 * model_rank // max(N_MP - 1, 1)
    flags = (jax.random.randint(key, (SLOTS,), 0, 1000) < level).astype(jnp.int32)
    return flags.at[0].set(1).at[1].set(0)


def draw_projections(key, part):
    key = jax.random.fold_in(key, 14)
    base_draw = jax.random.normal(key, (4, D, D), jnp.float32)
    scale = jnp.array([1.0, 1.0, 3.0, 3.0], jnp.float32)[:, None, None] * D ** (-0.5)
    return base_draw * scale


def draw_small_params(key, part):
    key = jax.random.fold_in(key, 15)
    keys = jax.random.split(key, 2)
    column = jnp.arange(D, dtype=jnp.float32)[None, :] / (D - 1)
    noise = jax.random.normal(keys[0], (VROWS, D), jnp.float32)
    gains = 0.6 * (1.0 + 2.0 * column)
    gains = gains * jax.random.uniform(keys[1], (VROWS, D), jnp.float32, 0.8, 1.2)
    row_index = jnp.arange(VROWS)[:, None]
    is_gain = (row_index == 0) | (row_index == 5) | (row_index == 8)
    spread = jnp.where(row_index >= VROWS - 3, 1.0, 0.3)
    return jnp.where(is_gain, gains, noise * spread)


def draw_word_table(key, part):
    key = jax.random.fold_in(key, 16)
    place = jnp.arange(VOCAB, dtype=jnp.float32)[:, None] / (VOCAB - 1)
    base_draw = jax.random.normal(key, (VOCAB, D), jnp.float32)
    rising = 1.0 + 2.0 * place
    return base_draw * rising * D ** (-0.5)


def block_scale(key, dims, shards, least, top_value):
    def one(position, blocks):
        heights = jax.random.uniform(jax.random.fold_in(jax.random.fold_in(key, 6), position), (blocks,), jnp.float32, least / len(shards), top_value / len(shards))
        return jnp.repeat(jnp.exp(heights), dims[position] // blocks).reshape((-1,) + (1,) * (len(dims) - position - 1))

    factor_of = one(*shards[0])
    for cut in shards[1:]:
        factor_of = factor_of * one(*cut)
    return factor_of


def profile(count, total, reach, lean):
    loads = [(1 << 20) // math.isqrt(grade ** lean) + 1 for grade in range(2, count + 1)]
    rest, counts = total - reach - (count - 1), [1] * (count - 1)
    while rest > 0:
        movable = [i for i in range(count - 1) if counts[i] < reach]
        whole, budget = sum([loads[i] for i in movable]), rest
        for i in movable:
            more = min(reach - counts[i], max(1, budget * loads[i] // whole), rest)
            counts[i] = counts[i] + more
            rest = rest - more
    return np.array([reach] + counts)


def uneven(key, count, total, bound, lean):
    if count == 2:
        one = jax.random.randint(key, (), max(1, total - bound), min(bound, total - 1) + 1)
        return jnp.stack([one, total - one])
    tallies = jnp.asarray(profile(count, total, bound, lean), jnp.int32)
    pairs = (count - 1) // 2
    donor, receiver = tallies[1:1 + 2 * pairs:2], tallies[2:2 + 2 * pairs:2]
    margin = jnp.minimum(donor - 1, bound - receiver)
    passed = jax.random.randint(jax.random.fold_in(key, 1), (pairs,), 0, 1 << 20) % (margin + 1)
    tallies = tallies.at[1:1 + 2 * pairs:2].set(donor - passed).at[2:2 + 2 * pairs:2].set(receiver + passed)
    return tallies[jax.random.permutation(jax.random.fold_in(key, 2), count)]


def gaussian(key, dims, width, most, shards=(), held_as=jnp.bfloat16):
    entries = width * jax.random.normal(key, dims, jnp.float32)
    if shards:
        entries = entries * block_scale(key, dims, shards, -0.22, 0.18)
    return jnp.clip(entries, -most, most).astype(held_as)


def setup_inputs(seed: int = 0) -> dict:
    key_list = jax.random.split(jax.random.key(seed), 30)
    tokens = draw_tokens(jax.random.fold_in(key_list[29], 71), 0)
    text_box = draw_text_box(jax.random.fold_in(key_list[29], 71), 0)
    segments = jax.vmap(lambda own: jnp.searchsorted(jnp.cumsum(uneven(own, 4, TEXT, TEXT // 2, 1)), jnp.arange(TEXT), side="right"))(jax.random.split(key_list[2], SEQS)).reshape((SEQS, TEXT)).astype(jnp.int32)
    alive_text = draw_alive_text(jax.random.fold_in(key_list[29], 71), 0)
    features = gaussian(key_list[4], (SEQS * VIS, VCH), 1.0, 6.0, ((0, 32),))
    mask_pos = draw_mask_pos(jax.random.fold_in(key_list[29], 71), 0)
    mask_label = draw_mask_label(jax.random.fold_in(key_list[29], 71), 0)
    mask_valid = draw_mask_valid(jax.random.fold_in(key_list[29], 71), 0)
    projections = draw_projections(jax.random.fold_in(key_list[29], 71), 0)
    projections_first = gaussian(key_list[9], (4, D, D), (0.11 * (0.005 * (VOCAB * D + 4 * D * D + 2 * D * FF + VCH * D + 4 * NBOX * CSZ + NPOS * D + VROWS * D) ** -0.5)), 7.152557373046875e-07, ((1, 8),), jnp.float32)
    projections_second = jnp.clip(jnp.exp(math.log(4.999616206333244e-15) - 1.3862944 * jax.random.uniform(key_list[10], (4, D, D), jnp.float32) ** block_scale(key_list[10], (4, D, D), ((1, 8),), -0.2, 0.2)), 1.249904051583311e-15, 4.999616206333244e-15)
    box_tables = gaussian(key_list[11], (4, NBOX, CSZ), 0.05, 0.3125, ((1, 8),), jnp.float32)
    box_tables_first = gaussian(key_list[12], (4, NBOX, CSZ), (0.11 * (0.005 * (VOCAB * D + 4 * D * D + 2 * D * FF + VCH * D + 4 * NBOX * CSZ + NPOS * D + VROWS * D) ** -0.5)), 7.152557373046875e-07, ((1, 8),), jnp.float32)
    box_tables_second = jnp.clip(jnp.exp(math.log(4.999616206333244e-15) - 1.3862944 * jax.random.uniform(key_list[13], (4, NBOX, CSZ), jnp.float32) ** block_scale(key_list[13], (4, NBOX, CSZ), ((1, 8),), -0.2, 0.2)), 1.249904051583311e-15, 4.999616206333244e-15)
    position_table = gaussian(key_list[14], (NPOS, D), 0.05, 0.3125, ((0, 8),), jnp.float32)
    position_table_first = gaussian(key_list[15], (NPOS, D), (0.11 * (0.005 * (VOCAB * D + 4 * D * D + 2 * D * FF + VCH * D + 4 * NBOX * CSZ + NPOS * D + VROWS * D) ** -0.5)), 7.152557373046875e-07, ((0, 8),), jnp.float32)
    position_table_second = jnp.clip(jnp.exp(math.log(4.999616206333244e-15) - 1.3862944 * jax.random.uniform(key_list[16], (NPOS, D), jnp.float32) ** block_scale(key_list[16], (NPOS, D), ((0, 8),), -0.2, 0.2)), 1.249904051583311e-15, 4.999616206333244e-15)
    visual_proj = gaussian(key_list[17], (VCH, D), VCH ** -0.5, 0.375, ((0, 8),), jnp.float32)
    visual_proj_first = gaussian(key_list[18], (VCH, D), (0.11 * (0.005 * (VOCAB * D + 4 * D * D + 2 * D * FF + VCH * D + 4 * NBOX * CSZ + NPOS * D + VROWS * D) ** -0.5)), 7.152557373046875e-07, ((0, 8),), jnp.float32)
    visual_proj_second = jnp.clip(jnp.exp(math.log(4.999616206333244e-15) - 1.3862944 * jax.random.uniform(key_list[19], (VCH, D), jnp.float32) ** block_scale(key_list[19], (VCH, D), ((0, 8),), -0.2, 0.2)), 1.249904051583311e-15, 4.999616206333244e-15)
    small_params = draw_small_params(jax.random.fold_in(key_list[29], 71), 0)
    small_params_first = gaussian(key_list[21], (VROWS, D), (0.55 * (0.005 * (VOCAB * D + 4 * D * D + 2 * D * FF + VCH * D + 4 * NBOX * CSZ + NPOS * D + VROWS * D) ** -0.5)), 3.814697265625e-06, ((1, 8),), jnp.float32)
    small_params_second = jnp.clip(jnp.exp(math.log(1.2499040431129815e-13) - 1.3862944 * jax.random.uniform(key_list[22], (VROWS, D), jnp.float32) ** block_scale(key_list[22], (VROWS, D), ((1, 8),), -0.2, 0.2)), 3.124760107782454e-14, 1.2499040431129815e-13)
    word_table = draw_word_table(jax.random.fold_in(key_list[29], 71), 0)
    word_table_first = gaussian(key_list[24], (VOCAB, D), (0.11 * (0.005 * (VOCAB * D + 4 * D * D + 2 * D * FF + VCH * D + 4 * NBOX * CSZ + NPOS * D + VROWS * D) ** -0.5)), 7.152557373046875e-07, ((0, 32),), jnp.float32)
    word_table_second = jnp.clip(jnp.exp(math.log(4.999616206333244e-15) - 1.3862944 * jax.random.uniform(key_list[25], (VOCAB, D), jnp.float32) ** block_scale(key_list[25], (VOCAB, D), ((0, 32),), -0.2, 0.2)), 1.249904051583311e-15, 4.999616206333244e-15)
    feedforward = gaussian(key_list[26], (2, D, FF), D ** -0.5, 0.21875, ((1, 8), (2, 4)), jnp.float32)
    feedforward_first = gaussian(key_list[27], (2, D, FF), (0.11 * (0.005 * (VOCAB * D + 4 * D * D + 2 * D * FF + VCH * D + 4 * NBOX * CSZ + NPOS * D + VROWS * D) ** -0.5)), 7.152557373046875e-07, ((1, 8), (2, 4)), jnp.float32)
    feedforward_second = jnp.clip(jnp.exp(math.log(4.999616206333244e-15) - 1.3862944 * jax.random.uniform(key_list[28], (2, D, FF), jnp.float32) ** block_scale(key_list[28], (2, D, FF), ((1, 8), (2, 4)), -0.2, 0.2)), 1.249904051583311e-15, 4.999616206333244e-15)
    return dict(tokens=tokens, text_box=text_box, segments=segments, alive_text=alive_text, features=features, mask_pos=mask_pos, mask_label=mask_label, mask_valid=mask_valid, projections=projections, projections_first=projections_first, projections_second=projections_second, box_tables=box_tables, box_tables_first=box_tables_first, box_tables_second=box_tables_second, position_table=position_table, position_table_first=position_table_first, position_table_second=position_table_second, visual_proj=visual_proj, visual_proj_first=visual_proj_first, visual_proj_second=visual_proj_second, small_params=small_params, small_params_first=small_params_first, small_params_second=small_params_second, word_table=word_table, word_table_first=word_table_first, word_table_second=word_table_second, feedforward=feedforward, feedforward_first=feedforward_first, feedforward_second=feedforward_second)


@jax.custom_vjp
def low(v):
    return lax.optimization_barrier(v.astype(jnp.bfloat16)).astype(jnp.float32)

@jax.custom_vjp
def low_back(v):
    return v

def low_keep(v):
    return (low(v), None)

def low_pass(kept, grad):
    return (grad,)

def back_keep(v):
    return (v, None)

def back_low(kept, grad):
    return (low(grad),)
low.defvjp(low_keep, low_pass)
low_back.defvjp(back_keep, back_low)
EXACT_PRECISION = lax.Precision.HIGHEST
MASKED = -1e+30
CLIP = 0.005
BETA_ONE = 0.9
BETA_TWO = 0.999
EPSILON = 1e-08
DECAY = 0.01
RATES = (0.02, 0.03, 0.03, 0.04, 0.3, 0.05, 0.02)

def layer_norm(value, gain, shift):
    average = lax.optimization_barrier(jnp.mean(value, -1, keepdims=True))
    centred = value - average
    variance = lax.optimization_barrier(jnp.mean(centred * centred, -1, keepdims=True))
    return centred * lax.rsqrt(variance + 1e-05) * gain + shift

def grid_boxes():
    cells = jnp.arange(GRID * GRID, dtype=jnp.int32)
    row_place = cells // GRID
    column_place = cells % GRID
    return jnp.stack([column_place * 1000 // GRID, row_place * 1000 // GRID, (column_place + 1) * 1000 // GRID, (row_place + 1) * 1000 // GRID], -1)

def spatial(boxes, tables):
    left_edge, top_edge = (boxes[..., 0], boxes[..., 1])
    right_edge, bottom_edge = (boxes[..., 2], boxes[..., 3])
    return jnp.concatenate([tables[0][left_edge], tables[1][top_edge], tables[0][right_edge], tables[1][bottom_edge], tables[2][bottom_edge - top_edge], tables[3][right_edge - left_edge]], -1)

def embed(word, vis_term, position_tab, box_tab, text_box):
    text = word + position_tab[:TEXT] + spatial(text_box, box_tab)
    visual = vis_term + position_tab[:GRID * GRID] + spatial(grid_boxes(), box_tab)[None]
    return jnp.concatenate([text, visual], 1)

def layout(text_box, segments, alive_text):
    full_box = jnp.concatenate([text_box, grid_boxes()], 0)
    positions = jnp.concatenate([jnp.arange(TEXT, dtype=jnp.int32), jnp.arange(GRID * GRID, dtype=jnp.int32)])
    segment_all = jnp.concatenate([segments, jnp.full((GRID * GRID,), -1, jnp.int32)])
    alive = jnp.concatenate([alive_text, jnp.ones((GRID * GRID,), jnp.int32)])
    shared = (segment_all[:, None] == segment_all[None, :]) | (segment_all[:, None] < 0) | (segment_all[None, :] < 0)
    allowed = shared & (alive[None, :] > 0)
    half = NB // 2

    def bucket(places, step):
        return jnp.clip((places[None, :] - places[:, None]) // step, -half, half - 1) + half
    buckets = jnp.stack([bucket(positions, 8), bucket(full_box[:, 0], 16) + NB, bucket(full_box[:, 3], 16) + 2 * NB])
    return (allowed, buckets)

def bias_of(rel_flat, buckets):
    summed = rel_flat[buckets[0]] + rel_flat[buckets[1]] + rel_flat[buckets[2]]
    return jnp.transpose(summed, (2, 0, 1))

def attend(rel_flat, queries, keys, values, text_box, segments, alive_text):
    allowed, buckets = layout(text_box, segments, alive_text)
    scaled = jnp.einsum('qhc,khc->hqk', queries, keys, precision=EXACT_PRECISION) * 0.125 + bias_of(rel_flat, buckets)
    scores = jnp.where(allowed[None], low_back(scaled), MASKED)
    shares = jax.nn.softmax(scores, -1)
    return jnp.einsum('hqk,khc->qhc', low(shares), values, precision=EXACT_PRECISION)

def layer_block(weights, block):
    projections, box_tables, position_table, visual_proj, compact_parameters, table, feedforward = weights
    tokens, text_box, segments, alive_text, feature_block = block
    seq_count = tokens.shape[0]
    word = low_back(table[tokens])
    vis_term = low_back(jnp.einsum('svc,cd->svd', feature_block, visual_proj, precision=EXACT_PRECISION))
    embedded = embed(word, vis_term, position_table, box_tables, text_box)
    normed_zero = layer_norm(embedded, compact_parameters[0], compact_parameters[1])
    bias_rows = jnp.stack([compact_parameters[2], jnp.zeros_like(compact_parameters[2]), compact_parameters[3]])
    projected = jnp.einsum('tgf,zfn->ztgn', low(normed_zero), projections[:3], precision=EXACT_PRECISION) + bias_rows[:, None, None, :]
    projected = low(low_back(projected)).reshape(3, seq_count, LEN, H, HD)
    rel_flat = compact_parameters[10 + FF // D:13 + FF // D].reshape(3 * NB, H)
    mixture = jax.vmap(partial(attend, rel_flat))(projected[0], projected[1], projected[2], text_box, segments, alive_text)
    mixture = low(low_back(mixture.reshape(seq_count, LEN, D)))
    summed_one = normed_zero + low_back(jnp.einsum('cgf,fk->cgk', mixture, projections[3], precision=EXACT_PRECISION) + compact_parameters[4])
    normed_one = layer_norm(summed_one, compact_parameters[5], compact_parameters[6])
    ffn_bias = compact_parameters[10:10 + FF // D].reshape(FF)
    pre_active = low_back(jnp.einsum('knj,jp->knp', low(normed_one), feedforward[0], precision=EXACT_PRECISION) + ffn_bias)
    active = low(jax.nn.gelu(pre_active, approximate=False))
    down_out = low_back(jnp.einsum('vtg,hg->vth', active, feedforward[1], precision=EXACT_PRECISION) + compact_parameters[7])
    return layer_norm(normed_one + down_out, compact_parameters[8], compact_parameters[9])

def adam_step(weight, grad, first, second, rate):
    first = BETA_ONE * first + (1.0 - BETA_ONE) * grad
    second = BETA_TWO * second + (1.0 - BETA_TWO) * grad * grad
    fixed_first = first / (1.0 - BETA_ONE ** STEP)
    fixed_second = second / (1.0 - BETA_TWO ** STEP)
    weight = weight - rate * (fixed_first / (jnp.sqrt(fixed_second) + EPSILON) + DECAY * weight)
    return (weight, first, second)

def reference(tokens, text_box, segments, alive_text, features, mask_pos, mask_label, mask_valid, projections, projections_first, projections_second, box_tables, box_tables_first, box_tables_second, position_table, position_table_first, position_table_second, visual_proj, visual_proj_first, visual_proj_second, small_params, small_params_first, small_params_second, word_table, word_table_first, word_table_second, feedforward, feedforward_first, feedforward_second):
    masters = (projections, box_tables, position_table, visual_proj, small_params, word_table, feedforward)
    firsts = (projections_first, box_tables_first, position_table_first, visual_proj_first, small_params_first, word_table_first, feedforward_first)
    seconds = (projections_second, box_tables_second, position_table_second, visual_proj_second, small_params_second, word_table_second, feedforward_second)
    per_block = math.gcd(SEQS, max(1, 4096 // LEN))
    block_count = SEQS // per_block
    stacked = (tokens.reshape(block_count, per_block, TEXT), text_box.reshape(block_count, per_block, TEXT, 4), segments.reshape(block_count, per_block, TEXT), alive_text.reshape(block_count, per_block, TEXT), features.astype(jnp.float32).reshape(block_count, per_block, GRID * GRID, VCH))
    slot_index = jnp.arange(SLOTS, dtype=jnp.int32)
    seq_index = slot_index // M_DEV * SEQ_DEV + mask_pos // TEXT
    picked_rows = seq_index * LEN + mask_pos % TEXT
    valid = mask_valid.astype(jnp.float32)

    def total_loss(weights):
        weights = tuple((low(part) for part in weights))
        normed_two = lax.map(jax.checkpoint(partial(layer_block, weights)), stacked)
        picked = low(normed_two.reshape(SEQS * LEN, D)[picked_rows])

        def head_block(carry, block):
            rows_in, labels, valid_in = block
            logits = low_back(jnp.dot(rows_in, weights[5].T, precision=EXACT_PRECISION))
            log_total = jax.nn.logsumexp(logits, -1)
            target = jnp.take_along_axis(logits, labels[:, None], 1)[:, 0]
            return (carry + jnp.sum(valid_in * (log_total - target)), None)
        loss, _ = lax.scan(jax.checkpoint(head_block), jnp.zeros((), jnp.float32), (picked.reshape(N_DP, N_MP * M_DEV, D), mask_label.reshape(N_DP, N_MP * M_DEV), valid.reshape(N_DP, N_MP * M_DEV)))
        return loss
    loss_sum, pullback = jax.vjp(total_loss, masters)
    gradients = pullback(jnp.ones((), jnp.float32))[0]
    loss_count = jnp.sum(valid)
    squares = jnp.zeros((), jnp.float32)
    for part in gradients:
        squares = squares + jnp.sum(part * part)
    grad_norm = jnp.sqrt(squares) / loss_count
    factor = jnp.minimum(1.0, CLIP / grad_norm)
    outputs = []
    for index in range(7):
        outputs.extend(adam_step(masters[index], gradients[index] / loss_count * factor, firsts[index], seconds[index], RATES[index]))
    return (outputs[0], outputs[1], outputs[2], outputs[3], outputs[4], outputs[5], outputs[6], outputs[7], outputs[8], outputs[9], outputs[10], outputs[11], outputs[12], outputs[13], outputs[14], outputs[15], outputs[16], outputs[17], outputs[18], outputs[19], outputs[20], loss_sum, loss_count, grad_norm)
```

```python
from functools import partial

import jax
import jax.numpy as jnp
from jax import lax
from jax.sharding import PartitionSpec as P

D = 768
H = 12
HD = 64
FF = 3072
NB = 64
GRID = 7
TEXT = 512
STEP = 10


MASKED = -1e30
CLIP = 0.005
BETA_ONE = 0.9
BETA_TWO = 0.999
EPSILON = 1e-08
DECAY = 0.01
RATES = (0.02, 0.03, 0.03, 0.04, 0.3, 0.05, 0.02)


def layer_norm(value, gain, shift):
    average = jnp.mean(value, -1, keepdims=True)
    centred = value - average
    variance = jnp.mean(centred * centred, -1, keepdims=True)
    return centred * lax.rsqrt(variance + 1e-05) * gain + shift


def grid_boxes():
    cells = jnp.arange(GRID * GRID, dtype=jnp.int32)
    row_place = cells // GRID
    column_place = cells % GRID
    return jnp.stack(
        [
            column_place * 1000 // GRID,
            row_place * 1000 // GRID,
            (column_place + 1) * 1000 // GRID,
            (row_place + 1) * 1000 // GRID,
        ],
        -1,
    )


def spatial(boxes, tables):
    left_edge, top_edge = (boxes[..., 0], boxes[..., 1])
    right_edge, bottom_edge = (boxes[..., 2], boxes[..., 3])
    return jnp.concatenate(
        [
            tables[0][left_edge],
            tables[1][top_edge],
            tables[0][right_edge],
            tables[1][bottom_edge],
            tables[2][bottom_edge - top_edge],
            tables[3][right_edge - left_edge],
        ],
        -1,
    )


def coarse(values, step):
    return (values // step, values % step)


def spread(rel_low, lag):
    places = jnp.arange(NB, dtype=jnp.int32)
    half = NB // 2
    index = jnp.clip(places[None, :] - places[:, None] - lag, -half, half - 1) + half
    hot = (index[..., None] == places).astype(jnp.bfloat16)
    table = jnp.einsum(
        "cab,kbh->khca", hot, rel_low.reshape(3, NB, H), preferred_element_type=jnp.float32
    )
    return table.astype(jnp.bfloat16)


def gathered_rel(grad_tables, lag):
    places = jnp.arange(NB, dtype=jnp.int32)
    half = NB // 2
    index = jnp.clip(places[None, :] - places[:, None] - lag, -half, half - 1) + half
    hot = (index[..., None] == places).astype(jnp.float32)
    return jnp.einsum(
        "cab,khca->kbh", hot, grad_tables, precision=lax.Precision.HIGHEST
    ).reshape(3 * NB, H)


def pair_layout(text_box, segments, alive_text, slots):
    full_box = jnp.concatenate([text_box, grid_boxes()], 0)
    positions = jnp.concatenate(
        [jnp.arange(TEXT, dtype=jnp.int32), jnp.arange(GRID * GRID, dtype=jnp.int32)]
    )
    segment_all = jnp.concatenate([segments, jnp.full((GRID * GRID,), -1, jnp.int32)])
    alive = jnp.concatenate([alive_text, jnp.ones((GRID * GRID,), jnp.int32)])
    own_segment = segment_all[slots]
    allowed = (
        (own_segment[:, None] == segment_all[None, :]) | (segment_all[None, :] < 0)
    ) & (alive[None, :] > 0)
    labels = jnp.arange(NB, dtype=jnp.int32)
    hots_key, hots_slot, below = [], [], []
    for values, step in ((positions, 8), (full_box[:, 0], 16), (full_box[:, 3], 16)):
        whole, rest = coarse(values, step)
        hots_key.append((whole[None, :] == labels[:, None]).astype(jnp.bfloat16))
        hots_slot.append((whole[slots][:, None] == labels[None, :]).astype(jnp.bfloat16))
        below.append(rest[None, :] < rest[slots][:, None])
    return allowed, jnp.stack(hots_key), jnp.stack(hots_slot), jnp.stack(below)


def pair_bias(rel_low, hots_key, hots_slot, below):
    sides = []
    for lag in range(2):
        rows = jnp.einsum(
            "kic,khca->khia", hots_slot, spread(rel_low, lag), preferred_element_type=jnp.float32
        ).astype(jnp.bfloat16)
        sides.append(
            jnp.einsum("khia,kaj->khij", rows, hots_key, preferred_element_type=jnp.float32)
        )
    return jnp.sum(jnp.where(below[:, None], sides[1], sides[0]), 0)


def pair_bias_back(grad_scores, hots_key, hots_slot, below):
    total = 0.0
    for lag in range(2):
        chosen = below if lag else ~below
        masked = jnp.where(chosen[:, None], grad_scores[None], jnp.zeros((), grad_scores.dtype))
        rows = jnp.einsum("khij,kaj->khia", masked, hots_key, preferred_element_type=jnp.float32)
        tables = jnp.einsum(
            "khia,kic->khca", rows, hots_slot.astype(jnp.float32), precision=lax.Precision.HIGHEST
        )
        total = total + gathered_rel(tables, lag)
    return total


def gelu_back(pre_piece, grad_active):
    gelu_pullback = jax.vjp(partial(jax.nn.gelu, approximate=False), pre_piece)[1]
    return gelu_pullback(grad_active)[0].astype(jnp.bfloat16)


def adam_step(weight, grad, first, second, rate):
    first = BETA_ONE * first + (1.0 - BETA_ONE) * grad
    second = BETA_TWO * second + (1.0 - BETA_TWO) * grad * grad
    fixed_first = first / (1.0 - BETA_ONE**STEP)
    fixed_second = second / (1.0 - BETA_TWO**STEP)
    weight = weight - rate * (fixed_first / (jnp.sqrt(fixed_second) + EPSILON) + DECAY * weight)
    return (weight, first, second)


def on_device(
    tokens,
    text_box,
    segments,
    alive_text,
    features,
    mask_pos,
    mask_label,
    mask_valid,
    projections,
    projections_first,
    projections_second,
    box_tables,
    box_tables_first,
    box_tables_second,
    position_table,
    position_table_first,
    position_table_second,
    visual_proj,
    visual_proj_first,
    visual_proj_second,
    small_params,
    small_params_first,
    small_params_second,
    word_table,
    word_table_first,
    word_table_second,
    feedforward,
    feedforward_first,
    feedforward_second,
):
    work_proj, work_boxes, work_places, work_visual, work_small, work_table, work_ffn = (
        lax.all_gather(projections.astype(jnp.bfloat16), "dp", axis=1, tiled=True),
        lax.all_gather(box_tables.astype(jnp.bfloat16), "dp", axis=1, tiled=True),
        lax.all_gather(position_table.astype(jnp.bfloat16), "dp", axis=0, tiled=True),
        lax.all_gather(visual_proj.astype(jnp.bfloat16), "dp", axis=0, tiled=True),
        lax.all_gather(small_params.astype(jnp.bfloat16), "dp", axis=1, tiled=True),
        lax.all_gather(word_table.astype(jnp.bfloat16), "dp", axis=0, tiled=True),
        lax.all_gather(feedforward.astype(jnp.bfloat16), "dp", axis=1, tiled=True),
    )
    small_float = work_small.astype(jnp.float32)
    model_index = lax.axis_index("mp")
    vocab_shard = work_table.shape[0]
    hidden_shard = work_ffn.shape[2]
    width = D
    seq_count = text_box.shape[0]
    length = TEXT + GRID * GRID
    row_count = seq_count * length
    rel_low = work_small[10 + FF // D : 13 + FF // D].reshape(3 * NB, H)
    local_ids = tokens - model_index * vocab_shard
    inside = (local_ids >= 0) & (local_ids < vocab_shard)
    safe_index = jnp.clip(local_ids, 0, vocab_shard - 1)
    partial_word = jnp.where(
        inside[..., None], jnp.take(work_table, safe_index, axis=0), jnp.zeros((), jnp.bfloat16)
    )
    word = lax.psum_scatter(partial_word, "mp", scatter_dimension=0, tiled=True).astype(jnp.float32)
    vis_term = jnp.dot(features, work_visual, preferred_element_type=jnp.float32).reshape(
        seq_count, GRID * GRID, width
    )

    def embed_local(word_in, vis_in, places_in, boxes_in):
        text = word_in + places_in + spatial(text_box, boxes_in)
        visual = vis_in + places_in[: GRID * GRID] + spatial(grid_boxes(), boxes_in)[None]
        return jnp.concatenate([text, visual], 1)

    embedded, embed_pullback = jax.vjp(
        embed_local, word, vis_term, work_places.astype(jnp.float32), work_boxes.astype(jnp.float32)
    )
    normed_zero, norm_zero_pullback = jax.vjp(layer_norm, embedded, small_float[0], small_float[1])
    slots = mask_pos
    slot_count = slots.shape[0]
    normed_flat = normed_zero.reshape(row_count, width)
    normed_low = normed_flat.astype(jnp.bfloat16)
    slot_zero = jnp.take(normed_flat, slots, axis=0)
    slot_low = slot_zero.astype(jnp.bfloat16)
    f32 = jnp.float32

    def dot(left, right, dims):
        return lax.dot_general(left, right, (dims, ((), ())), preferred_element_type=f32)

    queries = (dot(slot_low, work_proj[0], ((1,), (0,))) + small_float[2]).astype(jnp.bfloat16)
    keys = dot(normed_low, work_proj[1], ((1,), (0,))).astype(jnp.bfloat16)
    values = (dot(normed_low, work_proj[2], ((1,), (0,))) + small_float[3]).astype(jnp.bfloat16)
    queries = queries.reshape(slot_count, H, HD)
    keys = keys.reshape(length, H, HD)
    values = values.reshape(length, H, HD)
    allowed, hots_key, hots_slot, below = pair_layout(
        text_box[0], segments[0], alive_text[0], slots
    )
    scores = jnp.einsum("qhc,khc->hqk", queries, keys, preferred_element_type=f32) * 0.125
    scores = scores + pair_bias(rel_low, hots_key, hots_slot, below)
    scores = jnp.where(allowed[None], scores, MASKED)
    highest = jnp.max(scores, -1, keepdims=True)
    powers = jnp.exp(scores - highest)
    shares = powers / jnp.sum(powers, -1, keepdims=True)
    shares_low = shares.astype(jnp.bfloat16)
    mixture = jnp.einsum("hqk,khc->qhc", shares_low, values, preferred_element_type=f32)
    mixed_flat = mixture.astype(jnp.bfloat16).reshape(slot_count, width)
    attn_out = dot(mixed_flat, work_proj[3], ((1,), (0,))) + small_float[4]
    summed_one = slot_zero + attn_out
    normed_one, norm_one_pullback = jax.vjp(layer_norm, summed_one, small_float[5], small_float[6])
    normed_one_low = normed_one.astype(jnp.bfloat16)
    ffn_bias_full = small_float[10 : 10 + FF // D].reshape(-1)
    ffn_bias = lax.dynamic_slice_in_dim(ffn_bias_full, model_index * hidden_shard, hidden_shard)
    group_one = lax.all_gather(normed_one_low, "mp", axis=0, tiled=True)
    pre_active = dot(group_one, work_ffn[0], ((1,), (0,))) + ffn_bias
    active_low = jax.nn.gelu(pre_active, approximate=False).astype(jnp.bfloat16)
    ffn_out = (
        lax.psum_scatter(
            dot(active_low, work_ffn[1], ((1,), (1,))), "mp", scatter_dimension=0, tiled=True
        )
        + small_float[7]
    )
    summed_two = normed_one + ffn_out
    normed_two, norm_two_pullback = jax.vjp(layer_norm, summed_two, small_float[8], small_float[9])
    picked = normed_two.astype(jnp.bfloat16)
    group_picked = lax.all_gather(picked, "mp", axis=0, tiled=True)
    logits = dot(group_picked, work_table, ((1,), (1,)))
    local_high = jnp.max(logits, -1)
    local_sum = jnp.sum(jnp.exp(logits - local_high[:, None]), -1)
    label_local = mask_label - model_index * vocab_shard
    label_hit = jnp.arange(vocab_shard)[None, :] == label_local[:, None]
    target_part = jnp.sum(jnp.where(label_hit, logits, 0.0), -1)
    stats = lax.all_gather(jnp.stack([local_high, local_sum, target_part]), "mp")
    high_all = jnp.max(stats[:, 0], 0)
    sum_all = jnp.sum(stats[:, 1] * jnp.exp(stats[:, 0] - high_all), 0)
    target_all = jnp.sum(stats[:, 2], 0)
    log_rows = high_all + jnp.log(sum_all)
    valid_float = mask_valid.astype(f32)
    own_loss = lax.dynamic_slice_in_dim(
        valid_float * (log_rows - target_all), model_index * slot_count, slot_count
    )
    own_valid = lax.dynamic_slice_in_dim(valid_float, model_index * slot_count, slot_count)
    grad_logits = (
        (jnp.exp(logits - log_rows[:, None]) - label_hit.astype(f32)) * valid_float[:, None]
    ).astype(jnp.bfloat16)
    grad_table = dot(grad_logits, group_picked, ((0,), (0,)))
    grad_picked = lax.psum_scatter(
        dot(grad_logits, work_table, ((1,), (0,))), "mp", scatter_dimension=0, tiled=True
    )
    grad_summed_two, grad_gain_two, grad_shift_two = norm_two_pullback(grad_picked)
    grad_ffn_low = grad_summed_two.astype(jnp.bfloat16)
    group_grad = lax.all_gather(grad_ffn_low, "mp", axis=0, tiled=True)
    grad_down = dot(group_grad, active_low, ((0,), (0,)))
    grad_active = dot(group_grad, work_ffn[1], ((1,), (0,)))
    grad_pre = gelu_back(pre_active, grad_active)
    grad_up = dot(group_one, grad_pre, ((0,), (0,)))
    grad_ffn_bias = jnp.sum(grad_pre.astype(f32), 0)
    grad_one = grad_summed_two + lax.psum_scatter(
        dot(grad_pre, work_ffn[0], ((1,), (1,))), "mp", scatter_dimension=0, tiled=True
    )
    grad_ffn = jnp.stack([grad_up, grad_down])
    bias_full = lax.dynamic_update_slice_in_dim(
        jnp.zeros((FF,), f32), grad_ffn_bias, model_index * hidden_shard, 0
    ).reshape(FF // D, width)
    grad_summed_one, grad_gain_one, grad_shift_one = norm_one_pullback(grad_one)
    grad_attn_low = grad_summed_one.astype(jnp.bfloat16)
    grad_out_weight = dot(mixed_flat, grad_attn_low, ((0,), (0,)))
    grad_mixed = dot(grad_attn_low, work_proj[3], ((1,), (1,)))
    grad_mixed = grad_mixed.astype(jnp.bfloat16).reshape(slot_count, H, HD)
    grad_values = jnp.einsum("hqk,qhc->khc", shares_low, grad_mixed, preferred_element_type=f32)
    grad_shares = jnp.einsum("qhc,khc->hqk", grad_mixed, values, preferred_element_type=f32)
    grad_scores = shares * (grad_shares - jnp.sum(shares * grad_shares, -1, keepdims=True))
    scores_low = grad_scores.astype(jnp.bfloat16)
    grad_queries = jnp.einsum("hqk,khc->qhc", scores_low, keys, preferred_element_type=f32) * 0.125
    grad_keys = jnp.einsum("hqk,qhc->khc", scores_low, queries, preferred_element_type=f32) * 0.125
    grad_rel = pair_bias_back(scores_low, hots_key, hots_slot, below)
    grad_queries = grad_queries.astype(jnp.bfloat16).reshape(slot_count, width)
    grad_keys = grad_keys.astype(jnp.bfloat16).reshape(length, width)
    grad_values = grad_values.astype(jnp.bfloat16).reshape(length, width)
    grad_in_weight = jnp.stack(
        [
            dot(slot_low, grad_queries, ((0,), (0,))),
            dot(normed_low, grad_keys, ((0,), (0,))),
            dot(normed_low, grad_values, ((0,), (0,))),
        ]
    )
    grad_slot = grad_summed_one + dot(grad_queries, work_proj[0], ((1,), (1,)))
    grad_zero = (
        dot(grad_keys, work_proj[1], ((1,), (1,))) + dot(grad_values, work_proj[2], ((1,), (1,)))
    )
    grad_zero = grad_zero.at[slots].add(grad_slot)
    grad_embedded, grad_gain_zero, grad_shift_zero = norm_zero_pullback(
        grad_zero.reshape(seq_count, length, width)
    )
    grad_word, grad_vis, grad_places, grad_boxes = embed_pullback(grad_embedded)
    group_word = lax.all_gather(grad_word.astype(jnp.bfloat16), "mp", axis=0, tiled=True)
    grad_table = grad_table + jnp.zeros((vocab_shard, width), f32).at[safe_index].add(
        jnp.where(inside[..., None], group_word.astype(f32), 0.0)
    )
    grad_visual = dot(features, grad_vis.astype(jnp.bfloat16).reshape(-1, width), ((0,), (0,)))
    grad_small = jnp.concatenate(
        [
            jnp.stack(
                [
                    grad_gain_zero,
                    grad_shift_zero,
                    jnp.sum(grad_queries.astype(f32), 0),
                    jnp.sum(grad_values.astype(f32), 0),
                    jnp.sum(grad_attn_low.astype(jnp.float32), 0),
                    grad_gain_one,
                    grad_shift_one,
                    jnp.sum(grad_ffn_low.astype(jnp.float32), 0),
                    grad_gain_two,
                    grad_shift_two,
                ]
            ),
            bias_full,
            grad_rel.reshape(3, width),
        ],
        0,
    )
    grad_attn = jnp.concatenate([grad_in_weight, grad_out_weight[None]], 0)
    def scattered(part, axis):
        low_part = part.astype(jnp.bfloat16)
        return lax.psum_scatter(low_part, "dp", scatter_dimension=axis, tiled=True).astype(f32)

    shared_parts = (
        scattered(grad_attn, 1),
        scattered(grad_boxes, 1),
        scattered(grad_places, 0),
        scattered(grad_visual, 0),
        lax.psum_scatter(grad_small, "dp", scatter_dimension=1, tiled=True),
    )
    reduced_proj, reduced_boxes, reduced_places, reduced_visual, reduced_small = lax.psum(
        shared_parts, "mp"
    )
    reduced_table, reduced_ffn = (scattered(grad_table, 0), scattered(grad_ffn, 1))
    reduced = (
        reduced_proj,
        reduced_boxes,
        reduced_places,
        reduced_visual,
        reduced_small,
        reduced_table,
        reduced_ffn,
    )
    shared_squares = jnp.zeros((), jnp.float32)
    for part in reduced[:5]:
        shared_squares = shared_squares + jnp.sum(part * part)
    split_squares = jnp.sum(reduced_table * reduced_table) + jnp.sum(reduced_ffn * reduced_ffn)
    squares = split_squares + jnp.where(model_index == 0, shared_squares, 0.0)
    total_squares, loss_sum, loss_count = lax.psum(
        (squares, jnp.sum(own_loss), jnp.sum(own_valid)), ("dp", "mp")
    )
    grad_norm = jnp.sqrt(total_squares) / loss_count
    factor = jnp.minimum(1.0, CLIP / grad_norm)
    masters = (
        projections,
        box_tables,
        position_table,
        visual_proj,
        small_params,
        word_table,
        feedforward,
    )
    firsts = (
        projections_first,
        box_tables_first,
        position_table_first,
        visual_proj_first,
        small_params_first,
        word_table_first,
        feedforward_first,
    )
    seconds = (
        projections_second,
        box_tables_second,
        position_table_second,
        visual_proj_second,
        small_params_second,
        word_table_second,
        feedforward_second,
    )
    outputs = []
    for index in range(7):
        outputs.extend(
            adam_step(
                masters[index],
                reduced[index] / loss_count * factor,
                firsts[index],
                seconds[index],
                RATES[index],
            )
        )
    return tuple(outputs) + (loss_sum, loss_count, grad_norm)


def solution(mesh):
    in_specs = (
        P("dp", None),
        P(("dp", "mp"), None, None),
        P(("dp", "mp"), None),
        P(("dp", "mp"), None),
        P(("dp", "mp"), None),
        P(("dp", "mp")),
        P("dp"),
        P("dp"),
        P(None, "dp", None),
        P(None, "dp", None),
        P(None, "dp", None),
        P(None, "dp", None),
        P(None, "dp", None),
        P(None, "dp", None),
        P("dp", None),
        P("dp", None),
        P("dp", None),
        P("dp", None),
        P("dp", None),
        P("dp", None),
        P(None, "dp"),
        P(None, "dp"),
        P(None, "dp"),
        P(("mp", "dp"), None),
        P(("mp", "dp"), None),
        P(("mp", "dp"), None),
        P(None, "dp", "mp"),
        P(None, "dp", "mp"),
        P(None, "dp", "mp"),
    )
    out_specs = (
        P(None, "dp", None),
        P(None, "dp", None),
        P(None, "dp", None),
        P(None, "dp", None),
        P(None, "dp", None),
        P(None, "dp", None),
        P("dp", None),
        P("dp", None),
        P("dp", None),
        P("dp", None),
        P("dp", None),
        P("dp", None),
        P(None, "dp"),
        P(None, "dp"),
        P(None, "dp"),
        P(("mp", "dp"), None),
        P(("mp", "dp"), None),
        P(("mp", "dp"), None),
        P(None, "dp", "mp"),
        P(None, "dp", "mp"),
        P(None, "dp", "mp"),
        P(),
        P(),
        P(),
    )
    return jax.shard_map(
        on_device, mesh=mesh, in_specs=in_specs, out_specs=out_specs, check_vma=False
    )
```

```python
from functools import partial

import jax
import jax.numpy as jnp
from jax import lax
from jax.experimental import pallas as pl
from jax.experimental.pallas import tpu as pltpu
from jax.sharding import PartitionSpec as P

D = 768
H = 12
HD = 64
FF = 3072
NB = 64
GRID = 7
TEXT = 512
STEP = 10
VCH = 256
NBOX = 1024
VROWS = 17


MASKED = -1e30
CLIP = 0.005
BETA_ONE = 0.9
BETA_TWO = 0.999
EPSILON = 1e-08
DECAY = 0.01
RATES = (0.02, 0.03, 0.03, 0.04, 0.3, 0.05, 0.02)


def layer_norm(value, gain, shift):
    average = jnp.mean(value, -1, keepdims=True)
    centred = value - average
    variance = jnp.mean(centred * centred, -1, keepdims=True)
    return centred * lax.rsqrt(variance + 1e-05) * gain + shift


def grid_boxes():
    cells = jnp.arange(GRID * GRID, dtype=jnp.int32)
    row_place = cells // GRID
    column_place = cells % GRID
    return jnp.stack(
        [
            column_place * 1000 // GRID,
            row_place * 1000 // GRID,
            (column_place + 1) * 1000 // GRID,
            (row_place + 1) * 1000 // GRID,
        ],
        -1,
    )


def spatial(boxes, tables):
    left_edge, top_edge = (boxes[..., 0], boxes[..., 1])
    right_edge, bottom_edge = (boxes[..., 2], boxes[..., 3])
    return jnp.concatenate(
        [
            tables[0][left_edge],
            tables[1][top_edge],
            tables[0][right_edge],
            tables[1][bottom_edge],
            tables[2][bottom_edge - top_edge],
            tables[3][right_edge - left_edge],
        ],
        -1,
    )


def coarse(values, step):
    return (values // step, values % step)


def spread(rel_low, lag):
    places = jnp.arange(NB, dtype=jnp.int32)
    half = NB // 2
    index = jnp.clip(places[None, :] - places[:, None] - lag, -half, half - 1) + half
    hot = (index[..., None] == places).astype(jnp.bfloat16)
    table = jnp.einsum(
        "cab,kbh->khca", hot, rel_low.reshape(3, NB, H), preferred_element_type=jnp.float32
    )
    return table.astype(jnp.bfloat16)


def gathered_rel(grad_tables, lag):
    places = jnp.arange(NB, dtype=jnp.int32)
    half = NB // 2
    index = jnp.clip(places[None, :] - places[:, None] - lag, -half, half - 1) + half
    hot = (index[..., None] == places).astype(jnp.float32)
    return jnp.einsum(
        "cab,khca->kbh", hot, grad_tables, precision=lax.Precision.HIGHEST
    ).reshape(3 * NB, H)


def pair_layout(text_box, segments, alive_text, slots):
    full_box = jnp.concatenate([text_box, grid_boxes()], 0)
    positions = jnp.concatenate(
        [jnp.arange(TEXT, dtype=jnp.int32), jnp.arange(GRID * GRID, dtype=jnp.int32)]
    )
    segment_all = jnp.concatenate([segments, jnp.full((GRID * GRID,), -1, jnp.int32)])
    alive = jnp.concatenate([alive_text, jnp.ones((GRID * GRID,), jnp.int32)])
    own_segment = segment_all[slots]
    allowed = (
        (own_segment[:, None] == segment_all[None, :]) | (segment_all[None, :] < 0)
    ) & (alive[None, :] > 0)
    labels = jnp.arange(NB, dtype=jnp.int32)
    hots_key, hots_slot, below = [], [], []
    for values, step in ((positions, 8), (full_box[:, 0], 16), (full_box[:, 3], 16)):
        whole, rest = coarse(values, step)
        hots_key.append((whole[None, :] == labels[:, None]).astype(jnp.bfloat16))
        hots_slot.append((whole[slots][:, None] == labels[None, :]).astype(jnp.bfloat16))
        below.append(rest[None, :] < rest[slots][:, None])
    return allowed, jnp.stack(hots_key), jnp.stack(hots_slot), jnp.stack(below)


def pair_bias(rel_low, hots_key, hots_slot, below):
    sides = []
    for lag in range(2):
        rows = jnp.einsum(
            "kic,khca->khia", hots_slot, spread(rel_low, lag), preferred_element_type=jnp.float32
        ).astype(jnp.bfloat16)
        sides.append(
            jnp.einsum("khia,kaj->khij", rows, hots_key, preferred_element_type=jnp.float32)
        )
    return jnp.sum(jnp.where(below[:, None], sides[1], sides[0]), 0)


def pair_bias_back(grad_scores, hots_key, hots_slot, below):
    total = 0.0
    for lag in range(2):
        chosen = below if lag else ~below
        masked = jnp.where(chosen[:, None], grad_scores[None], jnp.zeros((), grad_scores.dtype))
        rows = jnp.einsum("khij,kaj->khia", masked, hots_key, preferred_element_type=jnp.float32)
        tables = jnp.einsum(
            "khia,kic->khca", rows, hots_slot.astype(jnp.float32), precision=lax.Precision.HIGHEST
        )
        total = total + gathered_rel(tables, lag)
    return total


def gelu_back(pre_piece, grad_active):
    gelu_pullback = jax.vjp(partial(jax.nn.gelu, approximate=False), pre_piece)[1]
    return gelu_pullback(grad_active)[0].astype(jnp.bfloat16)


def adam_step(weight, grad, first, second, rate):
    first = BETA_ONE * first + (1.0 - BETA_ONE) * grad
    second = BETA_TWO * second + (1.0 - BETA_TWO) * grad * grad
    fixed_first = first / (1.0 - BETA_ONE**STEP)
    fixed_second = second / (1.0 - BETA_TWO**STEP)
    weight = weight - rate * (fixed_first / (jnp.sqrt(fixed_second) + EPSILON) + DECAY * weight)
    return (weight, first, second)


MESH = pl.DeviceIdType.MESH
LOW = jnp.bfloat16
WIDE = jnp.float32
LANES = 128
HALF = D // 2


def pad_up(count, unit):
    return (count + unit - 1) // unit * unit


def bits_of(count):
    return count.bit_length() - 1


def flip(index, bit, ring):
    if ring and bit == 1:
        return 3 - index
    return index + (1 - 2 * ((index // 2**bit) % 2)) * 2**bit


class Plan:
    def __init__(self, dp, mp):
        self.dp, self.mp = dp, mp
        self.proj = pad_up(D // dp, 16)
        self.places = pad_up(TEXT // dp, 16)
        self.visual = pad_up(VCH // dp, 16)
        self.box = NBOX // dp
        self.box_parts = 4 * (self.box // 32)
        self.places_at = 4 * self.proj
        self.visual_at = self.places_at + self.places
        self.box_at = self.visual_at + self.visual
        self.box_rows = 32 * ((self.box_parts + 6) // 6)
        self.shared = pad_up(self.box_at + self.box_rows, 32)

    def box_slot(self, part):
        return self.box_at + 32 * (part // 6), LANES * (part % 6)


def lanes_of(stream):
    return pl.ds(stream * HALF, HALF)


def ffn_slot(part, table_rows, ffn_rows, wide):
    return table_rows + part * wide // D * ffn_rows, part * wide % D


def row_tile(rows):
    return next(t for t in (48, 32, 16) if rows % t == 0)


def reduce_kernel(plan, table_rows, ffn_rows, refs):
    (
        table_in, proj_in, ffn_in, places_in, visual_in, boxes_in, small_in, tile_in,
        shared_out, split_out, tile_out,
        shared_acc, split_acc, shared_got, split_got, ring_got, ring_own, tile_mp, tile_dp,
        load_sem, send_sem, recv_sem, ring_send, ring_recv, tile_send, tile_recv,
    ) = refs
    dp, mp = plan.dp, plan.mp
    me, here = lax.axis_index("dp"), lax.axis_index("mp")
    depth, ring_depth = bits_of(dp), bits_of(mp)
    ring = mp == 4
    loads = []

    def load(source, target):
        loads.append(pltpu.make_async_copy(source, target, load_sem.at[len(loads)]))

    for part in range(4):
        load(proj_in.at[part], shared_acc.at[:, pl.ds(part * plan.proj, plan.proj)])
    load(places_in, shared_acc.at[:, pl.ds(plan.places_at, plan.places)])
    load(visual_in, shared_acc.at[:, pl.ds(plan.visual_at, plan.visual)])
    pieces_box = plan.box // 32
    for part in range(plan.box_parts):
        row, lane = plan.box_slot(part)
        load(
            boxes_in.at[part // pieces_box, :, pl.ds(32 * (part % pieces_box), 32)],
            shared_acc.at[:, pl.ds(row, 32), pl.ds(lane, LANES)],
        )
    row, lane = plan.box_slot(plan.box_parts)
    load(small_in, shared_acc.at[:, pl.ds(row, 32), pl.ds(lane, LANES)])
    load(table_in, split_acc.at[:, pl.ds(0, table_rows)])
    for part in range(2):
        wide = ffn_in.shape[3]
        row, lane = ffn_slot(part, table_rows, ffn_rows, wide)
        load(ffn_in.at[part], split_acc.at[:, pl.ds(row, ffn_rows), pl.ds(lane, wide)])
    for copy in loads:
        copy.start()

    barrier = pltpu.get_barrier_semaphore()
    for other in range(1, dp):
        pl.semaphore_signal(
            barrier, 1, device_id={"dp": lax.rem(me + other, dp)}, device_id_type=MESH
        )
    for other in range(1, mp):
        pl.semaphore_signal(
            barrier, 1, device_id={"mp": lax.rem(here + other, mp)}, device_id_type=MESH
        )
    pl.semaphore_wait(barrier, dp + mp - 2)
    for copy in loads:
        copy.wait()

    for part in range(plan.box_parts + 1, 6 * (plan.shared - plan.box_at) // 32):
        row, lane = plan.box_slot(part)
        shared_acc[:, pl.ds(row, 32), pl.ds(lane, LANES)] = jnp.zeros((dp, 32, LANES), LOW)

    orders = ([0] + list(range(depth - 1, 0, -1)), list(range(depth)))
    pieces = []
    for acc, got, rows in (
        (shared_acc, shared_got, plan.shared),
        (split_acc, split_got, split_acc.shape[1]),
    ):
        for part in range(2):
            pieces.append((acc, got, part * (rows // 2), rows // 2))

    def chunk(order, step, free, away):
        index = 0
        for place, bit in enumerate(order):
            mine = (me // 2**bit) % 2
            if place < step or (place == step and not away):
                index = index + mine * 2**bit
            elif place == step:
                index = index + (1 - mine) * 2**bit
            else:
                index = index + ((free >> (place - step - 1)) & 1) * 2**bit
        return index

    def slot_base(step):
        return sum(2 ** (depth - 1 - s) for s in range(step))

    def region(piece, stream, step):
        acc, got, first, rows = pieces[piece]
        count = 2 ** (depth - 1 - step)
        return got.at[pl.ds(slot_base(step), count), pl.ds(first, rows), lanes_of(stream)]

    def send(piece, stream, step):
        acc, got, first, rows = pieces[piece]
        order = orders[stream]
        for free in range(2 ** (depth - 1 - step)):
            pltpu.make_async_remote_copy(
                src_ref=acc.at[chunk(order, step, free, True), pl.ds(first, rows), lanes_of(stream)],
                dst_ref=got.at[slot_base(step) + free, pl.ds(first, rows), lanes_of(stream)],
                send_sem=send_sem.at[piece, stream, step],
                recv_sem=recv_sem.at[piece, stream, step],
                device_id={"dp": flip(me, order[step], False)},
                device_id_type=MESH,
            ).start()

    def wait_bytes(piece, stream, step, sem):
        where = region(piece, stream, step)
        pltpu.make_async_copy(where, where, sem.at[piece, stream, step]).wait()

    def finish(piece, stream, step):
        acc, got, first, rows = pieces[piece]
        order = orders[stream]
        wait_bytes(piece, stream, step, recv_sem)
        tile = row_tile(rows)
        last = step == depth - 1
        out, low_out = (shared_out, True) if acc is shared_acc else (split_out, False)
        for free in range(2 ** (depth - 1 - step)):
            kept = chunk(order, step, free, False)

            def body(index, carry):
                at = pl.multiple_of(first + index * tile, 16)
                where = pl.ds(at, tile)
                total = acc[kept, where, lanes_of(stream)].astype(WIDE) + got[
                    slot_base(step) + free, where, lanes_of(stream)
                ].astype(WIDE)
                if last and not low_out:
                    out[where, lanes_of(stream)] = total
                elif last:
                    ring_own[0, where, lanes_of(stream)] = total.astype(LOW)
                else:
                    acc[kept, where, lanes_of(stream)] = total.astype(LOW)
                return carry

            lax.fori_loop(0, rows // tile, body, 0)

    ring_orders = (list(range(ring_depth)), list(range(ring_depth - 1, -1, -1)))

    def ring_copy(stream, step):
        return pltpu.make_async_remote_copy(
            src_ref=ring_own.at[step, :, lanes_of(stream)],
            dst_ref=ring_got.at[step, :, lanes_of(stream)],
            send_sem=ring_send.at[stream, step],
            recv_sem=ring_recv.at[stream, step],
            device_id={"mp": flip(here, ring_orders[stream][step], ring)},
            device_id_type=MESH,
        )

    def ring_finish(stream, step):
        ring_copy(stream, step).wait_recv()
        rows = plan.shared
        tile = row_tile(rows)

        def body(index, carry):
            where = pl.ds(pl.multiple_of(index * tile, 16), tile)
            total = ring_own[step, where, lanes_of(stream)].astype(WIDE) + ring_got[
                step, where, lanes_of(stream)
            ].astype(WIDE)
            if step == ring_depth - 1:
                shared_out[where, lanes_of(stream)] = total
            else:
                ring_own[step + 1, where, lanes_of(stream)] = total.astype(LOW)
            return carry

        lax.fori_loop(0, rows // tile, body, 0)

    everything = [(piece, stream) for piece in range(len(pieces)) for stream in range(2)]
    for piece, stream in everything:
        send(piece, stream, 0)
    for step in range(depth):
        for piece, stream in everything:
            finish(piece, stream, step)
            if step < depth - 1:
                send(piece, stream, step + 1)
            elif piece == 1:
                ring_copy(stream, 0).start()
    for step in range(ring_depth):
        for stream in range(2):
            ring_finish(stream, step)
            if step < ring_depth - 1:
                ring_copy(stream, step + 1).start()

    def squares(ref, rows):
        tile = row_tile(rows)

        def body(index, total):
            values = ref[pl.ds(pl.multiple_of(index * tile, 16), tile), :]
            return total + jnp.sum((values * values).reshape(tile // 8, 8, D), 0)

        total = lax.fori_loop(0, rows // tile, body, jnp.zeros((8, D), WIDE))
        folded = total[:, 0:LANES]
        for part in range(1, D // LANES):
            folded = folded + total[:, part * LANES : (part + 1) * LANES]
        return folded

    folded = squares(shared_out, plan.shared) * (1.0 / mp) + squares(split_out, split_out.shape[0])
    tile_mp[here, 0] = folded
    tile_mp[here, 1] = tile_in[...]

    def exchange(buffer, axis, index, count, base):
        copies = []
        for other in range(1, count):
            copies.append(
                pltpu.make_async_remote_copy(
                    src_ref=buffer.at[index],
                    dst_ref=buffer.at[index],
                    send_sem=tile_send.at[base + other],
                    recv_sem=tile_recv.at[base + other],
                    device_id={axis: lax.rem(index + other, count)},
                    device_id_type=MESH,
                )
            )
        for copy in copies:
            copy.start()
        for other in range(1, count):
            source = lax.rem(index + count - other, count)
            pltpu.make_async_copy(
                buffer.at[source], buffer.at[source], tile_recv.at[base + other]
            ).wait()
        return copies

    pending = exchange(tile_mp, "mp", here, mp, 0)
    total = tile_mp[0]
    for index in range(1, mp):
        total = total + tile_mp[index]
    tile_dp[me] = total
    pending = pending + exchange(tile_dp, "dp", me, dp, mp)
    total = tile_dp[0]
    for index in range(1, dp):
        total = total + tile_dp[index]
    tile_out[...] = total
    for copy in pending:
        copy.wait_send()
    for piece, stream in everything:
        for step in range(depth):
            wait_bytes(piece, stream, step, send_sem)
    for stream in range(2):
        for step in range(ring_depth):
            ring_copy(stream, step).wait_send()


def reduce_gradients(plan, table, proj, ffn, places, visual, boxes, small, tile):
    dp, mp = plan.dp, plan.mp
    table_rows, ffn_rows = table.shape[1], ffn.shape[2]
    split = table_rows + 2 * ffn_rows * ffn.shape[3] // D
    depth, ring_depth = bits_of(dp), bits_of(mp)
    loads = 4 + 2 + plan.box_parts + 1 + 1 + 2
    anywhere = pl.BlockSpec(memory_space=pl.ANY)
    vmem = pl.BlockSpec(memory_space=pltpu.VMEM)
    dma = pltpu.SemaphoreType.DMA

    def body(*refs):
        reduce_kernel(plan, table_rows, ffn_rows, refs)

    return pl.pallas_call(
        body,
        out_shape=(
            jax.ShapeDtypeStruct((plan.shared, D), WIDE),
            jax.ShapeDtypeStruct((split, D), WIDE),
            jax.ShapeDtypeStruct((2, 8, LANES), WIDE),
        ),
        in_specs=[anywhere] * 7 + [vmem],
        out_specs=(vmem, vmem, vmem),
        scratch_shapes=[
            pltpu.VMEM((dp, plan.shared, D), LOW),
            pltpu.VMEM((dp, split, D), LOW),
            pltpu.VMEM((dp - 1, plan.shared, D), LOW),
            pltpu.VMEM((dp - 1, split, D), LOW),
            pltpu.VMEM((ring_depth, plan.shared, D), LOW),
            pltpu.VMEM((ring_depth, plan.shared, D), LOW),
            pltpu.VMEM((mp, 2, 8, LANES), WIDE),
            pltpu.VMEM((dp, 2, 8, LANES), WIDE),
            dma((loads,)),
            dma((4, 2, depth)),
            dma((4, 2, depth)),
            dma((2, ring_depth)),
            dma((2, ring_depth)),
            dma((mp + dp,)),
            dma((mp + dp,)),
        ],
        compiler_params=pltpu.CompilerParams(
            collective_id=5, has_side_effects=True, vmem_limit_bytes=56 * 2**20
        ),
        name="reduce_gradients",
    )(table, proj, ffn, places, visual, boxes, small, tile)


def adam_kernel(plan, table_rows, ffn_rows, sizes, refs):
    shared_ref, split_ref, tile_ref = refs[:3]
    states, outs = refs[3:24], refs[24:45]
    totals = tile_ref[...]
    norm = jnp.sqrt(jnp.sum(totals[0], keepdims=True)) / totals[1, 1:2, 0:1]
    scale = jnp.minimum(1.0, CLIP / norm) / totals[1, 1:2, 0:1]

    def update(index, where, rows, grad_of):
        rate = RATES[index]
        weight, first, second = (ref[where] for ref in states[3 * index : 3 * index + 3])
        grad = grad_of * scale
        results = adam_step(weight, grad, first, second, rate)
        for ref, value in zip(outs[3 * index : 3 * index + 3], results):
            ref[where] = value

    def blocks(index, lead, source, at, rows, lane=0, wide=D):
        tile = next(t for t in (32, 24, 16, 8) if rows % t == 0)

        def body(step, carry):
            here = pl.multiple_of(step * tile, 8)
            where = (pl.ds(here, tile), slice(None))
            grad = source[pl.ds(pl.multiple_of(at + here, 8), tile), pl.ds(lane, wide)]
            update(index, where if lead is None else (lead,) + where, tile, grad)
            return carry

        lax.fori_loop(0, rows // tile, body, 0)

    for part in range(4):
        blocks(0, part, shared_ref, part * plan.proj, sizes[0])
    pieces_box = plan.box // 32
    for part in range(plan.box_parts):
        row, lane = plan.box_slot(part)
        grad = shared_ref[pl.ds(row, 32), pl.ds(lane, LANES)]
        update(1, (part // pieces_box, pl.ds(32 * (part % pieces_box), 32)), 32, grad)
    blocks(2, None, shared_ref, plan.places_at, sizes[2])
    blocks(3, None, shared_ref, plan.visual_at, sizes[3])
    row, lane = plan.box_slot(plan.box_parts)
    grad = shared_ref[pl.ds(row, 32), pl.ds(lane, LANES)]
    update(4, (slice(None), slice(None)), VROWS, grad[:VROWS, : sizes[4]])
    blocks(5, None, split_ref, 0, sizes[5])
    for part in range(2):
        wide = states[18].shape[2]
        row, lane = ffn_slot(part, table_rows, ffn_rows, wide)
        blocks(6, part, split_ref, row, sizes[6], lane, wide)


def adam_update(plan, table_rows, ffn_rows, shared, split, tile, states):
    sizes = (
        states[0].shape[1], 0, states[6].shape[0], states[9].shape[0], states[12].shape[1],
        states[15].shape[0], states[18].shape[1],
    )
    vmem = pl.BlockSpec(memory_space=pltpu.VMEM)

    def body(*refs):
        adam_kernel(plan, table_rows, ffn_rows, sizes, refs)

    return pl.pallas_call(
        body,
        out_shape=tuple(jax.ShapeDtypeStruct(part.shape, WIDE) for part in states),
        in_specs=[vmem] * 24,
        out_specs=(vmem,) * 21,
        compiler_params=pltpu.CompilerParams(vmem_limit_bytes=48 * 2**20),
        name="adam_update",
    )(shared, split, tile, *states)


def on_device(
    tokens,
    text_box,
    segments,
    alive_text,
    features,
    mask_pos,
    mask_label,
    mask_valid,
    projections,
    projections_first,
    projections_second,
    box_tables,
    box_tables_first,
    box_tables_second,
    position_table,
    position_table_first,
    position_table_second,
    visual_proj,
    visual_proj_first,
    visual_proj_second,
    small_params,
    small_params_first,
    small_params_second,
    word_table,
    word_table_first,
    word_table_second,
    feedforward,
    feedforward_first,
    feedforward_second,
):
    work_proj, work_boxes, work_places, work_visual, work_small, work_table, work_ffn = (
        lax.all_gather(projections.astype(jnp.bfloat16), "dp", axis=1, tiled=True),
        lax.all_gather(box_tables.astype(jnp.bfloat16), "dp", axis=1, tiled=True),
        lax.all_gather(position_table.astype(jnp.bfloat16), "dp", axis=0, tiled=True),
        lax.all_gather(visual_proj.astype(jnp.bfloat16), "dp", axis=0, tiled=True),
        lax.all_gather(small_params.astype(jnp.bfloat16), "dp", axis=1, tiled=True),
        lax.all_gather(word_table.astype(jnp.bfloat16), "dp", axis=0, tiled=True),
        lax.all_gather(feedforward.astype(jnp.bfloat16), "dp", axis=1, tiled=True),
    )
    small_float = work_small.astype(jnp.float32)
    model_index = lax.axis_index("mp")
    vocab_shard = work_table.shape[0]
    hidden_shard = work_ffn.shape[2]
    width = D
    seq_count = text_box.shape[0]
    length = TEXT + GRID * GRID
    row_count = seq_count * length
    rel_low = work_small[10 + FF // D : 13 + FF // D].reshape(3 * NB, H)
    local_ids = tokens - model_index * vocab_shard
    inside = (local_ids >= 0) & (local_ids < vocab_shard)
    safe_index = jnp.clip(local_ids, 0, vocab_shard - 1)
    partial_word = jnp.where(
        inside[..., None], jnp.take(work_table, safe_index, axis=0), jnp.zeros((), jnp.bfloat16)
    )
    word = lax.psum_scatter(partial_word, "mp", scatter_dimension=0, tiled=True).astype(jnp.float32)
    vis_term = jnp.dot(features, work_visual, preferred_element_type=jnp.float32).reshape(
        seq_count, GRID * GRID, width
    )

    def embed_local(word_in, vis_in, places_in, boxes_in):
        text = word_in + places_in + spatial(text_box, boxes_in)
        visual = vis_in + places_in[: GRID * GRID] + spatial(grid_boxes(), boxes_in)[None]
        return jnp.concatenate([text, visual], 1)

    embedded, embed_pullback = jax.vjp(
        embed_local, word, vis_term, work_places.astype(jnp.float32), work_boxes.astype(jnp.float32)
    )
    normed_zero, norm_zero_pullback = jax.vjp(layer_norm, embedded, small_float[0], small_float[1])
    slots = mask_pos
    slot_count = slots.shape[0]
    normed_flat = normed_zero.reshape(row_count, width)
    normed_low = normed_flat.astype(jnp.bfloat16)
    slot_zero = jnp.take(normed_flat, slots, axis=0)
    slot_low = slot_zero.astype(jnp.bfloat16)
    f32 = jnp.float32

    def dot(left, right, dims):
        return lax.dot_general(left, right, (dims, ((), ())), preferred_element_type=f32)

    queries = (dot(slot_low, work_proj[0], ((1,), (0,))) + small_float[2]).astype(jnp.bfloat16)
    keys = dot(normed_low, work_proj[1], ((1,), (0,))).astype(jnp.bfloat16)
    values = (dot(normed_low, work_proj[2], ((1,), (0,))) + small_float[3]).astype(jnp.bfloat16)
    queries = queries.reshape(slot_count, H, HD)
    keys = keys.reshape(length, H, HD)
    values = values.reshape(length, H, HD)
    allowed, hots_key, hots_slot, below = pair_layout(
        text_box[0], segments[0], alive_text[0], slots
    )
    scores = jnp.einsum("qhc,khc->hqk", queries, keys, preferred_element_type=f32) * 0.125
    scores = scores + pair_bias(rel_low, hots_key, hots_slot, below)
    scores = jnp.where(allowed[None], scores, MASKED)
    highest = jnp.max(scores, -1, keepdims=True)
    powers = jnp.exp(scores - highest)
    shares = powers / jnp.sum(powers, -1, keepdims=True)
    shares_low = shares.astype(jnp.bfloat16)
    mixture = jnp.einsum("hqk,khc->qhc", shares_low, values, preferred_element_type=f32)
    mixed_flat = mixture.astype(jnp.bfloat16).reshape(slot_count, width)
    attn_out = dot(mixed_flat, work_proj[3], ((1,), (0,))) + small_float[4]
    summed_one = slot_zero + attn_out
    normed_one, norm_one_pullback = jax.vjp(layer_norm, summed_one, small_float[5], small_float[6])
    normed_one_low = normed_one.astype(jnp.bfloat16)
    ffn_bias_full = small_float[10 : 10 + FF // D].reshape(-1)
    ffn_bias = lax.dynamic_slice_in_dim(ffn_bias_full, model_index * hidden_shard, hidden_shard)
    group_one = lax.all_gather(normed_one_low, "mp", axis=0, tiled=True)
    pre_active = dot(group_one, work_ffn[0], ((1,), (0,))) + ffn_bias
    active_low = jax.nn.gelu(pre_active, approximate=False).astype(jnp.bfloat16)
    ffn_out = (
        lax.psum_scatter(
            dot(active_low, work_ffn[1], ((1,), (1,))), "mp", scatter_dimension=0, tiled=True
        )
        + small_float[7]
    )
    summed_two = normed_one + ffn_out
    normed_two, norm_two_pullback = jax.vjp(layer_norm, summed_two, small_float[8], small_float[9])
    picked = normed_two.astype(jnp.bfloat16)
    group_picked = lax.all_gather(picked, "mp", axis=0, tiled=True)
    logits = dot(group_picked, work_table, ((1,), (1,)))
    local_high = jnp.max(logits, -1)
    local_sum = jnp.sum(jnp.exp(logits - local_high[:, None]), -1)
    label_local = mask_label - model_index * vocab_shard
    label_hit = jnp.arange(vocab_shard)[None, :] == label_local[:, None]
    target_part = jnp.sum(jnp.where(label_hit, logits, 0.0), -1)
    stats = lax.all_gather(jnp.stack([local_high, local_sum, target_part]), "mp")
    high_all = jnp.max(stats[:, 0], 0)
    sum_all = jnp.sum(stats[:, 1] * jnp.exp(stats[:, 0] - high_all), 0)
    target_all = jnp.sum(stats[:, 2], 0)
    log_rows = high_all + jnp.log(sum_all)
    valid_float = mask_valid.astype(f32)
    own_loss = lax.dynamic_slice_in_dim(
        valid_float * (log_rows - target_all), model_index * slot_count, slot_count
    )
    own_valid = lax.dynamic_slice_in_dim(valid_float, model_index * slot_count, slot_count)
    grad_logits = (
        (jnp.exp(logits - log_rows[:, None]) - label_hit.astype(f32)) * valid_float[:, None]
    ).astype(jnp.bfloat16)
    grad_table = dot(grad_logits, group_picked, ((0,), (0,)))
    grad_picked = lax.psum_scatter(
        dot(grad_logits, work_table, ((1,), (0,))), "mp", scatter_dimension=0, tiled=True
    )
    grad_summed_two, grad_gain_two, grad_shift_two = norm_two_pullback(grad_picked)
    grad_ffn_low = grad_summed_two.astype(jnp.bfloat16)
    group_grad = lax.all_gather(grad_ffn_low, "mp", axis=0, tiled=True)
    grad_down = dot(group_grad, active_low, ((0,), (0,)))
    grad_active = dot(group_grad, work_ffn[1], ((1,), (0,)))
    grad_pre = gelu_back(pre_active, grad_active)
    grad_up = dot(group_one, grad_pre, ((0,), (0,)))
    grad_ffn_bias = jnp.sum(grad_pre.astype(f32), 0)
    grad_one = grad_summed_two + lax.psum_scatter(
        dot(grad_pre, work_ffn[0], ((1,), (1,))), "mp", scatter_dimension=0, tiled=True
    )
    grad_ffn = jnp.stack([grad_up, grad_down])
    bias_full = lax.dynamic_update_slice_in_dim(
        jnp.zeros((FF,), f32), grad_ffn_bias, model_index * hidden_shard, 0
    ).reshape(FF // D, width)
    grad_summed_one, grad_gain_one, grad_shift_one = norm_one_pullback(grad_one)
    grad_attn_low = grad_summed_one.astype(jnp.bfloat16)
    grad_out_weight = dot(mixed_flat, grad_attn_low, ((0,), (0,)))
    grad_mixed = dot(grad_attn_low, work_proj[3], ((1,), (1,)))
    grad_mixed = grad_mixed.astype(jnp.bfloat16).reshape(slot_count, H, HD)
    grad_values = jnp.einsum("hqk,qhc->khc", shares_low, grad_mixed, preferred_element_type=f32)
    grad_shares = jnp.einsum("qhc,khc->hqk", grad_mixed, values, preferred_element_type=f32)
    grad_scores = shares * (grad_shares - jnp.sum(shares * grad_shares, -1, keepdims=True))
    scores_low = grad_scores.astype(jnp.bfloat16)
    grad_queries = jnp.einsum("hqk,khc->qhc", scores_low, keys, preferred_element_type=f32) * 0.125
    grad_keys = jnp.einsum("hqk,qhc->khc", scores_low, queries, preferred_element_type=f32) * 0.125
    grad_rel = pair_bias_back(scores_low, hots_key, hots_slot, below)
    grad_queries = grad_queries.astype(jnp.bfloat16).reshape(slot_count, width)
    grad_keys = grad_keys.astype(jnp.bfloat16).reshape(length, width)
    grad_values = grad_values.astype(jnp.bfloat16).reshape(length, width)
    grad_in_weight = jnp.stack(
        [
            dot(slot_low, grad_queries, ((0,), (0,))),
            dot(normed_low, grad_keys, ((0,), (0,))),
            dot(normed_low, grad_values, ((0,), (0,))),
        ]
    )
    grad_slot = grad_summed_one + dot(grad_queries, work_proj[0], ((1,), (1,)))
    grad_zero = (
        dot(grad_keys, work_proj[1], ((1,), (1,))) + dot(grad_values, work_proj[2], ((1,), (1,)))
    )
    grad_zero = grad_zero.at[slots].add(grad_slot)
    grad_embedded, grad_gain_zero, grad_shift_zero = norm_zero_pullback(
        grad_zero.reshape(seq_count, length, width)
    )
    grad_word, grad_vis, grad_places, grad_boxes = embed_pullback(grad_embedded)
    group_word = lax.all_gather(grad_word.astype(jnp.bfloat16), "mp", axis=0, tiled=True)
    grad_table = grad_table + jnp.zeros((vocab_shard, width), f32).at[safe_index].add(
        jnp.where(inside[..., None], group_word.astype(f32), 0.0)
    )
    grad_visual = dot(features, grad_vis.astype(jnp.bfloat16).reshape(-1, width), ((0,), (0,)))
    grad_small = jnp.concatenate(
        [
            jnp.stack(
                [
                    grad_gain_zero,
                    grad_shift_zero,
                    jnp.sum(grad_queries.astype(f32), 0),
                    jnp.sum(grad_values.astype(f32), 0),
                    jnp.sum(grad_attn_low.astype(jnp.float32), 0),
                    grad_gain_one,
                    grad_shift_one,
                    jnp.sum(grad_ffn_low.astype(jnp.float32), 0),
                    grad_gain_two,
                    grad_shift_two,
                ]
            ),
            bias_full,
            grad_rel.reshape(3, width),
        ],
        0,
    )
    grad_attn = jnp.concatenate([grad_in_weight, grad_out_weight[None]], 0)
    dp, mp = lax.axis_size("dp"), lax.axis_size("mp")
    plan = Plan(dp, mp)

    def split_rows(part):
        rows = part.shape[-2] // dp
        part = part.astype(LOW).reshape(part.shape[:-2] + (dp, rows, part.shape[-1]))
        extra = [(0, 0)] * (part.ndim - 2) + [(0, pad_up(rows, 16) - rows), (0, 0)]
        return jnp.pad(part, extra) if extra[-2][1] else part

    cut = small_params.shape[1]
    small_split = jnp.transpose(grad_small.reshape(VROWS, dp, cut), (1, 0, 2)).astype(LOW)
    small_split = jnp.pad(small_split, ((0, 0), (0, 32 - VROWS), (0, LANES - cut)))
    own_sums = jnp.stack([jnp.sum(own_loss), jnp.sum(own_valid)])
    own_tile = jnp.pad(own_sums[:, None], ((0, 6), (0, LANES - 1)))
    table_split, ffn_split = split_rows(grad_table), split_rows(grad_ffn)
    shared_sum, split_sum, totals = reduce_gradients(
        plan,
        table_split,
        split_rows(grad_attn),
        ffn_split,
        split_rows(grad_places),
        split_rows(grad_visual),
        grad_boxes.astype(LOW).reshape(4, dp, NBOX // dp, LANES),
        small_split,
        own_tile,
    )
    loss_sum, loss_count = (totals[1, 0, 0], totals[1, 1, 0])
    grad_norm = jnp.sqrt(jnp.sum(totals[0])) / loss_count
    states = (
        projections, projections_first, projections_second,
        box_tables, box_tables_first, box_tables_second,
        position_table, position_table_first, position_table_second,
        visual_proj, visual_proj_first, visual_proj_second,
        small_params, small_params_first, small_params_second,
        word_table, word_table_first, word_table_second,
        feedforward, feedforward_first, feedforward_second,
    )
    outputs = adam_update(
        plan, table_split.shape[1], ffn_split.shape[2], shared_sum, split_sum, totals, states
    )
    return tuple(outputs) + (loss_sum, loss_count, grad_norm)


def solution(mesh):
    in_specs = (
        P("dp", None),
        P(("dp", "mp"), None, None),
        P(("dp", "mp"), None),
        P(("dp", "mp"), None),
        P(("dp", "mp"), None),
        P(("dp", "mp")),
        P("dp"),
        P("dp"),
        P(None, "dp", None),
        P(None, "dp", None),
        P(None, "dp", None),
        P(None, "dp", None),
        P(None, "dp", None),
        P(None, "dp", None),
        P("dp", None),
        P("dp", None),
        P("dp", None),
        P("dp", None),
        P("dp", None),
        P("dp", None),
        P(None, "dp"),
        P(None, "dp"),
        P(None, "dp"),
        P(("mp", "dp"), None),
        P(("mp", "dp"), None),
        P(("mp", "dp"), None),
        P(None, "dp", "mp"),
        P(None, "dp", "mp"),
        P(None, "dp", "mp"),
    )
    out_specs = (
        P(None, "dp", None),
        P(None, "dp", None),
        P(None, "dp", None),
        P(None, "dp", None),
        P(None, "dp", None),
        P(None, "dp", None),
        P("dp", None),
        P("dp", None),
        P("dp", None),
        P("dp", None),
        P("dp", None),
        P("dp", None),
        P(None, "dp"),
        P(None, "dp"),
        P(None, "dp"),
        P(("mp", "dp"), None),
        P(("mp", "dp"), None),
        P(("mp", "dp"), None),
        P(None, "dp", "mp"),
        P(None, "dp", "mp"),
        P(None, "dp", "mp"),
        P(),
        P(),
        P(),
    )
    return jax.shard_map(
        on_device, mesh=mesh, in_specs=in_specs, out_specs=out_specs, check_vma=False
    )
```

```python
import jax
import jax.numpy as jnp
from jax import lax
from jax.experimental import pallas as pl
from jax.experimental.pallas import tpu as pltpu
from jax.sharding import PartitionSpec as P

D = 768
H = 12
HD = 64
FF = 3072
NB = 64
GRID = 7
TEXT = 512
STEP = 10
VCH = 256
NBOX = 1024
VROWS = 17


MASKED = -1e30
CLIP = 0.005
BETA_ONE = 0.9
BETA_TWO = 0.999
EPSILON = 1e-08
DECAY = 0.01
RATES = (0.02, 0.03, 0.03, 0.04, 0.3, 0.05, 0.02)


def grid_boxes():
    cells = jnp.arange(GRID * GRID, dtype=jnp.int32)
    row_place = cells // GRID
    column_place = cells % GRID
    return jnp.stack(
        [
            column_place * 1000 // GRID,
            row_place * 1000 // GRID,
            (column_place + 1) * 1000 // GRID,
            (row_place + 1) * 1000 // GRID,
        ],
        -1,
    )


def adam_step(weight, grad, first, second, rate):
    first = BETA_ONE * first + (1.0 - BETA_ONE) * grad
    second = BETA_TWO * second + (1.0 - BETA_TWO) * grad * grad
    fixed_first = first / (1.0 - BETA_ONE**STEP)
    fixed_second = second / (1.0 - BETA_TWO**STEP)
    weight = weight - rate * (fixed_first / (jnp.sqrt(fixed_second) + EPSILON) + DECAY * weight)
    return (weight, first, second)


MESH = pl.DeviceIdType.MESH
LOW = jnp.bfloat16
WIDE = jnp.float32
LANES = 128
HALF = D // 2


def pad_up(count, unit):
    return (count + unit - 1) // unit * unit


def bits_of(count):
    return count.bit_length() - 1


def flip(index, bit, ring):
    if ring and bit == 1:
        return 3 - index
    return index + (1 - 2 * ((index // 2**bit) % 2)) * 2**bit


class Plan:
    def __init__(self, dp, mp):
        self.dp, self.mp = dp, mp
        self.proj = pad_up(D // dp, 16)
        self.places = pad_up(TEXT // dp, 16)
        self.visual = pad_up(VCH // dp, 16)
        self.box = NBOX // dp
        self.box_parts = 4 * (self.box // 32)
        self.places_at = 4 * self.proj
        self.visual_at = self.places_at + self.places
        self.box_at = self.visual_at + self.visual
        self.box_rows = 32 * ((self.box_parts + 6) // 6)
        self.shared = pad_up(self.box_at + self.box_rows, 32 * mp)

    def box_slot(self, part):
        return self.box_at + 32 * (part // 6), LANES * (part % 6)


def group_of(axis, index):
    return {axis: index}


def lanes_of(stream):
    return pl.ds(stream * HALF, HALF)


def ffn_slot(part, table_rows, ffn_rows, wide):
    return table_rows + part * wide // D * ffn_rows, part * wide % D


def row_tile(rows):
    return next(t for t in (48, 32, 16) if rows % t == 0)


def reduce_kernel(plan, table_rows, ffn_rows, refs):
    (
        table_in, proj_in, out_in, ffn_in, places_in, visual_in, boxes_in, small_in, tile_in,
        shared_out, split_out, tile_out,
        shared_acc, split_acc, shared_got, split_got, ring_got, ring_own, tile_mp, tile_dp,
        load_sem, send_sem, recv_sem, ring_send, ring_recv, tile_send, tile_recv,
    ) = refs
    dp, mp = plan.dp, plan.mp
    me, here = lax.axis_index("dp"), lax.axis_index("mp")
    depth, ring_depth = bits_of(dp), bits_of(mp)
    ring = mp == 4
    loads = []

    def load(source, target):
        loads.append(pltpu.make_async_copy(source, target, load_sem.at[len(loads)]))

    for part in range(4):
        source = proj_in.at[part] if part < 3 else out_in
        load(source, shared_acc.at[:, pl.ds(part * plan.proj, plan.proj)])
    load(places_in, shared_acc.at[:, pl.ds(plan.places_at, plan.places)])
    load(visual_in, shared_acc.at[:, pl.ds(plan.visual_at, plan.visual)])
    pieces_box = plan.box // 32
    for part in range(plan.box_parts):
        row, lane = plan.box_slot(part)
        load(
            boxes_in.at[part // pieces_box, :, pl.ds(32 * (part % pieces_box), 32)],
            shared_acc.at[:, pl.ds(row, 32), pl.ds(lane, LANES)],
        )
    row, lane = plan.box_slot(plan.box_parts)
    load(small_in, shared_acc.at[:, pl.ds(row, 32), pl.ds(lane, LANES)])
    load(table_in, split_acc.at[:, pl.ds(0, table_rows)])
    for part in range(2):
        wide = ffn_in.shape[3]
        row, lane = ffn_slot(part, table_rows, ffn_rows, wide)
        load(ffn_in.at[part], split_acc.at[:, pl.ds(row, ffn_rows), pl.ds(lane, wide)])
    for copy in loads:
        copy.start()

    barrier = pltpu.get_barrier_semaphore()
    for other in range(1, dp):
        pl.semaphore_signal(
            barrier, 1, device_id={"dp": lax.rem(me + other, dp)}, device_id_type=MESH
        )
    for other in range(1, mp):
        pl.semaphore_signal(
            barrier, 1, device_id={"mp": lax.rem(here + other, mp)}, device_id_type=MESH
        )
    pl.semaphore_wait(barrier, dp + mp - 2)
    for copy in loads:
        copy.wait()

    for part in range(plan.box_parts + 1, 6 * (plan.shared - plan.box_at) // 32):
        row, lane = plan.box_slot(part)
        shared_acc[:, pl.ds(row, 32), pl.ds(lane, LANES)] = jnp.zeros((dp, 32, LANES), LOW)

    orders = ([0] + list(range(depth - 1, 0, -1)), list(range(depth)))
    pieces = []
    for acc, got, rows in (
        (shared_acc, shared_got, plan.shared),
        (split_acc, split_got, split_acc.shape[1]),
    ):
        for part in range(2):
            pieces.append((acc, got, part * (rows // 2), rows // 2))

    def chunk(order, step, free, away):
        index = 0
        for place, bit in enumerate(order):
            mine = (me // 2**bit) % 2
            if place < step or (place == step and not away):
                index = index + mine * 2**bit
            elif place == step:
                index = index + (1 - mine) * 2**bit
            else:
                index = index + ((free >> (place - step - 1)) & 1) * 2**bit
        return index

    def slot_base(step):
        return sum(2 ** (depth - 1 - s) for s in range(step))

    def region(piece, stream, step):
        acc, got, first, rows = pieces[piece]
        count = 2 ** (depth - 1 - step)
        return got.at[pl.ds(slot_base(step), count), pl.ds(first, rows), lanes_of(stream)]

    def send(piece, stream, step):
        acc, got, first, rows = pieces[piece]
        order = orders[stream]
        for free in range(2 ** (depth - 1 - step)):
            pltpu.make_async_remote_copy(
                src_ref=acc.at[chunk(order, step, free, True), pl.ds(first, rows), lanes_of(stream)],
                dst_ref=got.at[slot_base(step) + free, pl.ds(first, rows), lanes_of(stream)],
                send_sem=send_sem.at[piece, stream, step],
                recv_sem=recv_sem.at[piece, stream, step],
                device_id={"dp": flip(me, order[step], False)},
                device_id_type=MESH,
            ).start()

    def wait_bytes(piece, stream, step, sem):
        where = region(piece, stream, step)
        pltpu.make_async_copy(where, where, sem.at[piece, stream, step]).wait()

    def finish(piece, stream, step):
        acc, got, first, rows = pieces[piece]
        order = orders[stream]
        wait_bytes(piece, stream, step, recv_sem)
        tile = row_tile(rows)
        last = step == depth - 1
        out, low_out = (shared_out, True) if acc is shared_acc else (split_out, False)
        for free in range(2 ** (depth - 1 - step)):
            kept = chunk(order, step, free, False)

            def body(index, carry):
                at = pl.multiple_of(first + index * tile, 16)
                where = pl.ds(at, tile)
                total = acc[kept, where, lanes_of(stream)].astype(WIDE) + got[
                    slot_base(step) + free, where, lanes_of(stream)
                ].astype(WIDE)
                if last and not low_out:
                    out[where, lanes_of(stream)] = total
                elif last:
                    ring_own[0, where, lanes_of(stream)] = total.astype(LOW)
                else:
                    acc[kept, where, lanes_of(stream)] = total.astype(LOW)
                return carry

            lax.fori_loop(0, rows // tile, body, 0)

    ring_orders = (list(range(ring_depth)), list(range(ring_depth - 1, -1, -1)))

    def ring_copy(stream, step):
        return pltpu.make_async_remote_copy(
            src_ref=ring_own.at[step, :, lanes_of(stream)],
            dst_ref=ring_got.at[step, :, lanes_of(stream)],
            send_sem=ring_send.at[stream, step],
            recv_sem=ring_recv.at[stream, step],
            device_id={"mp": flip(here, ring_orders[stream][step], ring)},
            device_id_type=MESH,
        )

    def ring_finish(stream, step):
        ring_copy(stream, step).wait_recv()
        rows = plan.shared
        tile = row_tile(rows)

        def body(index, carry):
            where = pl.ds(pl.multiple_of(index * tile, 16), tile)
            total = ring_own[step, where, lanes_of(stream)].astype(WIDE) + ring_got[
                step, where, lanes_of(stream)
            ].astype(WIDE)
            if step == ring_depth - 1:
                shared_out[where, lanes_of(stream)] = total
            else:
                ring_own[step + 1, where, lanes_of(stream)] = total.astype(LOW)
            return carry

        lax.fori_loop(0, rows // tile, body, 0)

    everything = [(piece, stream) for piece in range(len(pieces)) for stream in range(2)]
    for piece, stream in everything:
        send(piece, stream, 0)
    for step in range(depth):
        for piece, stream in everything:
            finish(piece, stream, step)
            if step < depth - 1:
                send(piece, stream, step + 1)
            elif piece == 1:
                ring_copy(stream, 0).start()
    for step in range(ring_depth):
        for stream in range(2):
            ring_finish(stream, step)
            if step < ring_depth - 1:
                ring_copy(stream, step + 1).start()

    def squares(ref, rows):
        tile = row_tile(rows)

        def body(index, total):
            values = ref[pl.ds(pl.multiple_of(index * tile, 16), tile), :]
            return total + jnp.sum((values * values).reshape(tile // 8, 8, D), 0)

        total = lax.fori_loop(0, rows // tile, body, jnp.zeros((8, D), WIDE))
        folded = total[:, 0:LANES]
        for part in range(1, D // LANES):
            folded = folded + total[:, part * LANES : (part + 1) * LANES]
        return folded

    folded = squares(shared_out, plan.shared) * (1.0 / mp) + squares(split_out, split_out.shape[0])
    own = lax.broadcasted_iota(jnp.int32, (8, LANES), 0)
    tile_mp[here, 0] = folded
    tile_mp[here, 1] = tile_in[...]

    def exchange(buffer, axis, index, count, base):
        copies = []
        for other in range(1, count):
            copies.append(
                pltpu.make_async_remote_copy(
                    src_ref=buffer.at[index],
                    dst_ref=buffer.at[index],
                    send_sem=tile_send.at[base + other],
                    recv_sem=tile_recv.at[base + other],
                    device_id={axis: lax.rem(index + other, count)},
                    device_id_type=MESH,
                )
            )
        for copy in copies:
            copy.start()
        for other in range(1, count):
            source = lax.rem(index + count - other, count)
            pltpu.make_async_copy(
                buffer.at[source], buffer.at[source], tile_recv.at[base + other]
            ).wait()
        return copies

    pending = exchange(tile_mp, "mp", here, mp, 0)
    total = tile_mp[0]
    for index in range(1, mp):
        total = total + tile_mp[index]
    tile_dp[me] = total
    pending = pending + exchange(tile_dp, "dp", me, dp, mp)
    total = tile_dp[0]
    for index in range(1, dp):
        total = total + tile_dp[index]
    tile_out[...] = total
    for copy in pending:
        copy.wait_send()
    for piece, stream in everything:
        for step in range(depth):
            wait_bytes(piece, stream, step, send_sem)
    for stream in range(2):
        for step in range(ring_depth):
            ring_copy(stream, step).wait_send()


def reduce_gradients(plan, table, proj, out, ffn, places, visual, boxes, small, tile):
    dp, mp = plan.dp, plan.mp
    table_rows, ffn_rows = table.shape[1], ffn.shape[2]
    split = table_rows + 2 * ffn_rows * ffn.shape[3] // D
    depth, ring_depth = bits_of(dp), bits_of(mp)
    loads = 4 + 2 + plan.box_parts + 1 + 1 + 2
    anywhere = pl.BlockSpec(memory_space=pl.ANY)
    vmem = pl.BlockSpec(memory_space=pltpu.VMEM)
    dma = pltpu.SemaphoreType.DMA

    def body(*refs):
        reduce_kernel(plan, table_rows, ffn_rows, refs)

    return pl.pallas_call(
        body,
        out_shape=(
            jax.ShapeDtypeStruct((plan.shared, D), WIDE),
            jax.ShapeDtypeStruct((split, D), WIDE),
            jax.ShapeDtypeStruct((2, 8, LANES), WIDE),
        ),
        in_specs=[anywhere] * 8 + [vmem],
        out_specs=(vmem, vmem, vmem),
        scratch_shapes=[
            pltpu.VMEM((dp, plan.shared, D), LOW),
            pltpu.VMEM((dp, split, D), LOW),
            pltpu.VMEM((dp - 1, plan.shared, D), LOW),
            pltpu.VMEM((dp - 1, split, D), LOW),
            pltpu.VMEM((ring_depth, plan.shared, D), LOW),
            pltpu.VMEM((ring_depth, plan.shared, D), LOW),
            pltpu.VMEM((mp, 2, 8, LANES), WIDE),
            pltpu.VMEM((dp, 2, 8, LANES), WIDE),
            dma((loads,)),
            dma((4, 2, depth)),
            dma((4, 2, depth)),
            dma((2, ring_depth)),
            dma((2, ring_depth)),
            dma((mp + dp,)),
            dma((mp + dp,)),
        ],
        compiler_params=pltpu.CompilerParams(
            collective_id=5, has_side_effects=True, vmem_limit_bytes=56 * 2**20
        ),
        name="reduce_gradients",
    )(table, proj, out, ffn, places, visual, boxes, small, tile)


def adam_kernel(plan, table_rows, ffn_rows, sizes, refs):
    shared_ref, split_ref, tile_ref = refs[:3]
    states, outs = refs[3:24], refs[24:45]
    totals = tile_ref[...]
    norm = jnp.sqrt(jnp.sum(totals[0], keepdims=True)) / totals[1, 1:2, 0:1]
    scale = jnp.minimum(1.0, CLIP / norm) / totals[1, 1:2, 0:1]

    def update(index, where, rows, grad_of):
        rate = RATES[index]
        weight, first, second = (ref[where] for ref in states[3 * index : 3 * index + 3])
        grad = grad_of * scale
        results = adam_step(weight, grad, first, second, rate)
        for ref, value in zip(outs[3 * index : 3 * index + 3], results):
            ref[where] = value

    def blocks(index, lead, source, at, rows, lane=0, wide=D):
        tile = next(t for t in (32, 24, 16, 8) if rows % t == 0)

        def body(step, carry):
            here = pl.multiple_of(step * tile, 8)
            where = (pl.ds(here, tile), slice(None))
            grad = source[pl.ds(pl.multiple_of(at + here, 8), tile), pl.ds(lane, wide)]
            update(index, where if lead is None else (lead,) + where, tile, grad)
            return carry

        lax.fori_loop(0, rows // tile, body, 0)

    for part in range(4):
        blocks(0, part, shared_ref, part * plan.proj, sizes[0])
    pieces_box = plan.box // 32
    for part in range(plan.box_parts):
        row, lane = plan.box_slot(part)
        grad = shared_ref[pl.ds(row, 32), pl.ds(lane, LANES)]
        update(1, (part // pieces_box, pl.ds(32 * (part % pieces_box), 32)), 32, grad)
    blocks(2, None, shared_ref, plan.places_at, sizes[2])
    blocks(3, None, shared_ref, plan.visual_at, sizes[3])
    row, lane = plan.box_slot(plan.box_parts)
    grad = shared_ref[pl.ds(row, 32), pl.ds(lane, LANES)]
    update(4, (slice(None), slice(None)), VROWS, grad[:VROWS, : sizes[4]])
    blocks(5, None, split_ref, 0, sizes[5])
    for part in range(2):
        wide = states[18].shape[2]
        row, lane = ffn_slot(part, table_rows, ffn_rows, wide)
        blocks(6, part, split_ref, row, sizes[6], lane, wide)


def adam_update(plan, table_rows, ffn_rows, shared, split, tile, states):
    sizes = (
        states[0].shape[1], 0, states[6].shape[0], states[9].shape[0], states[12].shape[1],
        states[15].shape[0], states[18].shape[1],
    )
    vmem = pl.BlockSpec(memory_space=pltpu.VMEM)

    def body(*refs):
        adam_kernel(plan, table_rows, ffn_rows, sizes, refs)

    return pl.pallas_call(
        body,
        out_shape=tuple(jax.ShapeDtypeStruct(part.shape, WIDE) for part in states),
        in_specs=[vmem] * 24,
        out_specs=(vmem,) * 21,
        compiler_params=pltpu.CompilerParams(vmem_limit_bytes=48 * 2**20),
        name="adam_update",
    )(shared, split, tile, *states)


def combos(index, bits, ring):
    found = [index]
    for bit in bits:
        found = found + [flip(one, bit, ring) for one in found]
    return found


class Ring:
    def __init__(self, mp, sems):
        self.mp, self.here, self.ring = mp, lax.axis_index("mp"), mp == 4
        self.send, self.recv = sems
        depth = bits_of(mp)
        self.depth = depth
        self.orders = (list(range(depth)), list(range(depth - 1, -1, -1)))
        self.started = []

    def barrier(self):
        barrier = pltpu.get_barrier_semaphore()
        for other in range(1, self.mp):
            pl.semaphore_signal(
                barrier, 1, device_id={"mp": lax.rem(self.here + other, self.mp)},
                device_id_type=MESH,
            )
        pl.semaphore_wait(barrier, self.mp - 1)

    def copy(self, source, target, number, stream, index, peer):
        made = pltpu.make_async_remote_copy(
            src_ref=source, dst_ref=target,
            send_sem=self.send.at[number, stream, index],
            recv_sem=self.recv.at[number, stream, index],
            device_id={"mp": peer}, device_id_type=MESH,
        )
        return made

    def gather_start(self, buffer, number, stream, step):
        order = self.orders[stream]
        peer = flip(self.here, order[step], self.ring)
        for place, slot in enumerate(combos(self.here, order[:step], self.ring)):
            part = buffer.at[slot, :, lanes_of(stream)]
            made = self.copy(part, part, number, stream, 2**step - 1 + place, peer)
            made.start()
            self.started.append(made)

    def gather_wait(self, buffer, number, stream, step):
        order = self.orders[stream]
        peer = flip(self.here, order[step], self.ring)
        for place, slot in enumerate(combos(peer, order[:step], self.ring)):
            part = buffer.at[slot, :, lanes_of(stream)]
            self.copy(part, part, number, stream, 2**step - 1 + place, peer).wait_recv()

    def gather(self, buffer, number):
        for stream in range(2):
            self.gather_start(buffer, number, stream, 0)
        for step in range(self.depth):
            for stream in range(2):
                self.gather_wait(buffer, number, stream, step)
                if step < self.depth - 1:
                    self.gather_start(buffer, number, stream, step + 1)

    def base(self, step):
        return sum(2 ** (self.depth - 1 - s) for s in range(step))

    def reduce_start(self, buffer, got, number, stream, step):
        order = self.orders[stream]
        peer = flip(self.here, order[step], self.ring)
        for place, slot in enumerate(combos(peer, order[step + 1 :], self.ring)):
            index = self.base(step) + place
            made = self.copy(
                buffer.at[slot, :, lanes_of(stream)],
                got.at[index, :, lanes_of(stream)],
                number, stream, index, peer,
            )
            made.start()
            self.started.append(made)

    def reduce_wait(self, buffer, got, number, stream, step):
        order = self.orders[stream]
        peer = flip(self.here, order[step], self.ring)
        for place, slot in enumerate(combos(self.here, order[step + 1 :], self.ring)):
            index = self.base(step) + place
            part = got.at[index, :, lanes_of(stream)]
            self.copy(part, part, number, stream, index, peer).wait_recv()
            where = (slot, slice(None), lanes_of(stream))
            total = buffer[where].astype(WIDE) + got[index, :, lanes_of(stream)].astype(WIDE)
            buffer[where] = total.astype(buffer.dtype)

    def reduce_begin(self, buffer, got, number):
        for stream in range(2):
            self.reduce_start(buffer, got, number, stream, 0)

    def reduce_rest(self, buffer, got, number, between=()):
        between = list(between)
        for step in range(self.depth):
            if between:
                between.pop(0)()
            for stream in range(2):
                self.reduce_wait(buffer, got, number, stream, step)
                if step < self.depth - 1:
                    self.reduce_start(buffer, got, number, stream, step + 1)
        for rest in between:
            rest()

    def finish(self):
        for made in self.started:
            made.wait_send()


def mm(left, right, dims):
    return lax.dot_general(left, right, (dims, ((), ())), preferred_element_type=WIDE)


NN, NT, TN = ((1,), (0,)), ((1,), (1,)), ((0,), (0,))


def norm_rows(value):
    centred = value - jnp.mean(value, -1, keepdims=True)
    scale = lax.rsqrt(jnp.mean(centred * centred, -1, keepdims=True) + 1e-05)
    return centred * scale, scale


def norm_back(grad, plain, scale, gain):
    inner = grad * gain
    return scale * (
        inner
        - jnp.mean(inner, -1, keepdims=True)
        - plain * jnp.mean(inner * plain, -1, keepdims=True)
    )


def column_sum(value):
    return jnp.sum(value, 0, keepdims=True)


def head_kernel(mp, refs):
    (
        mixed_ref, zero_ref, out_weight, small_ref, bias_ref, ffn_ref, table_ref, label_ref,
        valid_ref,
        grad_zero_ref, grad_mixed_ref, grad_out_ref, grad_ffn_ref, grad_table_ref, rows_ref,
        bias_out, sums_ref,
        ffn, table, one, picked, down, sums_two, grad_picked, grad_one, got_two, got_picked,
        got_one, logits, low_logits, stats, load_sem, send_sem, recv_sem, stat_send, stat_recv,
    ) = refs
    ring = Ring(mp, (send_sem, recv_sem))
    here = ring.here
    slots = mixed_ref.shape[0]
    group = slots * mp
    load_ffn = pltpu.make_async_copy(ffn_ref, ffn, load_sem.at[0])
    load_table = pltpu.make_async_copy(table_ref, table, load_sem.at[1])
    load_ffn.start()
    load_table.start()
    ring.barrier()
    row = lambda index: small_ref[index : index + 1, :]

    out = mm(mixed_ref[...], out_weight[...], NN) + row(4)
    plain_one, scale_one = norm_rows(zero_ref[...] + out)
    normed_one = plain_one * row(5) + row(6)
    one[here] = normed_one.astype(LOW)
    ring.gather(one, 0)
    load_ffn.wait()
    hidden = ffn.shape[2]
    group_one = one[...].reshape(group, D)
    before = mm(group_one, ffn[0], NN) + bias_ref[...]
    erf_part = 0.5 * (1.0 + lax.erf(before * (0.5**0.5)))
    active = (before * erf_part).astype(LOW)
    slope = erf_part + before * jnp.exp(-0.5 * before * before) * 0.3989422804014327
    sums_two[...] = mm(active, ffn[1], NT).astype(sums_two.dtype).reshape(mp, slots, D)
    ring.reduce_begin(sums_two, got_two, 1)
    load_table.wait()
    ring.reduce_rest(sums_two, got_two, 1)
    plain_two, scale_two = norm_rows(normed_one + (sums_two[here].astype(WIDE) + row(7)))
    picked[here] = (plain_two * row(8) + row(9)).astype(LOW)
    ring.gather(picked, 2)

    group_picked = picked[...].reshape(group, D)
    vocab = table.shape[0]
    tile = next(t for t in (480, 512, 256, 128) if vocab % t == 0)
    tiles = vocab // tile
    label = label_ref[...] - here * vocab
    valid = valid_ref[...].astype(WIDE)

    def forward(index, carry):
        highest, total, target = carry
        where = pl.ds(pl.multiple_of(index * tile, 16), tile)
        values = mm(table[where, :], group_picked, NT)
        logits[where, :] = values
        higher = jnp.maximum(highest, jnp.max(values, 0, keepdims=True))
        total = total * jnp.exp(highest - higher) + column_sum(jnp.exp(values - higher))
        word = lax.broadcasted_iota(jnp.int32, (tile, group), 0) + index * tile
        target = target + column_sum(jnp.where(word == label, values, 0.0))
        return higher, total, target

    blank = jnp.zeros((1, group), WIDE)
    highest, total, target = lax.fori_loop(0, tiles, forward, (blank - 1e30, blank, blank))
    stats[here, 0:1, 0:group] = highest
    stats[here, 1:2, 0:group] = total
    stats[here, 2:3, 0:group] = target
    stat_copies = []
    for other in range(1, mp):
        made = pltpu.make_async_remote_copy(
            src_ref=stats.at[here], dst_ref=stats.at[here],
            send_sem=stat_send.at[other], recv_sem=stat_recv.at[other],
            device_id={"mp": lax.rem(here + other, mp)}, device_id_type=MESH,
        )
        made.start()
        stat_copies.append(made)
    for other in range(1, mp):
        source = lax.rem(here + mp - other, mp)
        pltpu.make_async_copy(stats.at[source], stats.at[source], stat_recv.at[other]).wait()
    highest = stats[0, 0:1, 0:group]
    for index in range(1, mp):
        highest = jnp.maximum(highest, stats[index, 0:1, 0:group])
    total, target = blank, blank
    for index in range(mp):
        total = total + stats[index, 1:2, 0:group] * jnp.exp(stats[index, 0:1, 0:group] - highest)
        target = target + stats[index, 2:3, 0:group]
    log_rows = highest + jnp.log(total)
    place = lax.broadcasted_iota(jnp.int32, (1, group), 1)
    own = (place >= here * slots) & (place < (here + 1) * slots)
    loss = jnp.sum(jnp.where(own, valid * (log_rows - target), 0.0), -1, keepdims=True)
    count = jnp.sum(jnp.where(own, valid, 0.0), -1, keepdims=True)
    first_lane = lax.broadcasted_iota(jnp.int32, (8, LANES), 1) == 0
    first_row = lax.broadcasted_iota(jnp.int32, (8, LANES), 0)
    sums_ref[...] = jnp.where(
        first_lane & (first_row == 0), loss, jnp.where(first_lane & (first_row == 1), count, 0.0)
    )

    def backward(index, grad):
        where = pl.ds(pl.multiple_of(index * tile, 16), tile)
        word = lax.broadcasted_iota(jnp.int32, (tile, group), 0) + index * tile
        hit = jnp.where(word == label, 1.0, 0.0)
        values = ((jnp.exp(logits[where, :] - log_rows) - hit) * valid).astype(LOW)
        low_logits[where, :] = values
        return grad + mm(values, table[where, :], TN)

    grad = lax.fori_loop(0, tiles, backward, jnp.zeros((group, D), WIDE))
    grad_picked[...] = grad.astype(grad_picked.dtype).reshape(mp, slots, D)

    def table_part(first, last):
        def run():
            def body(index, carry):
                where = pl.ds(pl.multiple_of(index * tile, 16), tile)
                grad_table_ref[where, :] = mm(low_logits[where, :], group_picked, NN).astype(LOW)
                return carry

            lax.fori_loop(first, last, body, 0)

        return run

    ring.reduce_begin(grad_picked, got_picked, 3)
    middle = tiles // 2
    ring.reduce_rest(
        grad_picked, got_picked, 3, [table_part(0, middle), table_part(middle, tiles)]
    )
    grad_two = grad_picked[here].astype(WIDE)
    rows_ref[8:9, :] = column_sum(grad_two * plain_two)
    rows_ref[9:10, :] = column_sum(grad_two)
    grad_sum_two = norm_back(grad_two, plain_two, scale_two, row(8))
    low_two = grad_sum_two.astype(LOW)
    rows_ref[7:8, :] = column_sum(low_two.astype(WIDE))
    down[here] = low_two
    ring.gather(down, 4)
    group_down = down[...].reshape(group, D)
    grad_active = mm(group_down, ffn[1], NN)
    grad_before = (grad_active * slope).astype(LOW)
    grad_one[...] = mm(grad_before, ffn[0], NT).astype(grad_one.dtype).reshape(mp, slots, D)

    def up_part():
        grad_ffn_ref[0] = mm(group_one, grad_before, TN).astype(LOW)
        bias_out[...] = column_sum(grad_before.astype(WIDE))

    def down_part():
        grad_ffn_ref[1] = mm(group_down, active, TN).astype(LOW)

    ring.reduce_begin(grad_one, got_one, 5)
    ring.reduce_rest(grad_one, got_one, 5, [up_part, down_part])
    grad = grad_sum_two + grad_one[here].astype(WIDE)
    rows_ref[5:6, :] = column_sum(grad * plain_one)
    rows_ref[6:7, :] = column_sum(grad)
    grad = norm_back(grad, plain_one, scale_one, row(5))
    low = grad.astype(LOW)
    rows_ref[4:5, :] = column_sum(low.astype(WIDE))
    grad_zero_ref[...] = grad
    grad_mixed_ref[...] = mm(low, out_weight[...], NT).astype(LOW)
    grad_out_ref[...] = mm(mixed_ref[...], low, TN).astype(LOW)
    for index in list(range(4)) + list(range(10, 16)):
        rows_ref[index : index + 1, :] = jnp.zeros((1, D), WIDE)
    ring.finish()
    for made in stat_copies:
        made.wait_send()


def head_step(mp, mixed, zero, out_weight, small, bias, ffn, table, label, valid):
    slots, hidden, vocab = mixed.shape[0], ffn.shape[2], table.shape[0]
    group = slots * mp
    wide_group = pad_up(group, LANES)
    vmem = pl.BlockSpec(memory_space=pltpu.VMEM)
    anywhere = pl.BlockSpec(memory_space=pl.ANY)
    dma = pltpu.SemaphoreType.DMA
    exchanged = [pltpu.VMEM((mp, slots, D), LOW)] * 6
    got = [pltpu.VMEM((mp - 1, slots, D), LOW)] * 3

    def body(*refs):
        head_kernel(mp, refs)

    return pl.pallas_call(
        body,
        out_shape=(
            jax.ShapeDtypeStruct((slots, D), WIDE),
            jax.ShapeDtypeStruct((slots, D), LOW),
            jax.ShapeDtypeStruct((D, D), LOW),
            jax.ShapeDtypeStruct((2, D, hidden), LOW),
            jax.ShapeDtypeStruct((vocab, D), LOW),
            jax.ShapeDtypeStruct((16, D), WIDE),
            jax.ShapeDtypeStruct((1, hidden), WIDE),
            jax.ShapeDtypeStruct((8, LANES), WIDE),
        ),
        in_specs=[vmem] * 5 + [anywhere] * 2 + [vmem] * 2,
        out_specs=(vmem,) * 8,
        scratch_shapes=[
            pltpu.VMEM((2, D, hidden), LOW),
            pltpu.VMEM((vocab, D), LOW),
            *exchanged,
            *got,
            pltpu.VMEM((vocab, group), WIDE),
            pltpu.VMEM((vocab, group), LOW),
            pltpu.VMEM((mp, 8, wide_group), WIDE),
            dma((2,)),
            dma((6, 2, mp - 1)),
            dma((6, 2, mp - 1)),
            dma((mp,)),
            dma((mp,)),
        ],
        compiler_params=pltpu.CompilerParams(
            collective_id=3, has_side_effects=True, vmem_limit_bytes=56 * 2**20
        ),
        name="head_step",
    )(mixed, zero, out_weight, small, bias, ffn, table, label, valid)


ROWS = 576
KINDS = ((6, 3), (0, 4), (3, 4))


def token_info(text_box, segments, alive_text):
    boxes = jnp.concatenate([text_box, grid_boxes()], 0)
    visual = GRID * GRID
    places = jnp.concatenate([jnp.arange(TEXT), jnp.arange(visual)]).astype(jnp.int32)
    owner = jnp.concatenate([segments, jnp.full((visual,), -1, jnp.int32)])
    alive = jnp.concatenate([alive_text, jnp.ones((visual,), jnp.int32)])
    columns = [
        boxes[:, 0], boxes[:, 1], boxes[:, 2], boxes[:, 3], boxes[:, 3] - boxes[:, 1],
        boxes[:, 2] - boxes[:, 0], places, owner, alive,
    ]
    rows = jnp.stack(columns + [jnp.zeros_like(places)] * 7)
    return jnp.pad(rows, ((0, 0), (0, ROWS - TEXT - visual)))


def edge_rows(rel_low):
    table = jnp.transpose(rel_low.reshape(3, NB, H), (0, 2, 1)).astype(WIDE)
    rows = jnp.pad(table, ((0, 0), (0, 0), (NB // 2, NB // 2)), mode="edge")
    return jnp.pad(rows.reshape(3 * H, 2 * NB), ((0, 4), (0, 0)))


def edge_rows_back(grad):
    grad = grad[: 3 * H].reshape(3, H, 2 * NB)
    half = NB // 2
    low = jnp.sum(grad[..., : half + 1], -1, keepdims=True)
    high = jnp.sum(grad[..., 3 * half - 1 :], -1, keepdims=True)
    table = jnp.concatenate([low, grad[..., half + 1 : 3 * half - 1], high], -1)
    return jnp.transpose(table, (0, 2, 1)).reshape(3 * NB * H)


def key_hot(rows_ref, kind):
    column, shift = KINDS[kind]
    coarse_row = jnp.right_shift(rows_ref[column : column + 1, :], shift)
    place = lax.broadcasted_iota(jnp.int32, (2 * NB, ROWS), 0)
    first = jnp.where(place == coarse_row, 1.0, 0.0).astype(LOW)
    second = jnp.where(place == coarse_row + NB, 1.0, 0.0).astype(LOW)
    return first, second


def below_of(rows_ref, slot_ref, kind):
    column, shift = KINDS[kind]
    mask = 2**shift - 1
    rest_key = jnp.bitwise_and(rows_ref[column : column + 1, :], mask)
    rest_slot = jnp.bitwise_and(slot_ref[:, column : column + 1], mask)
    return rest_key < rest_slot


def take_slots(slots, pos_ref, pairs):
    def body(index, carry):
        at = pos_ref[index]
        for source, target in pairs:
            target[pl.ds(index, 1), :] = source[pl.ds(at, 1), :]
        return carry

    lax.fori_loop(0, slots, body, 0)


def half_mask(rows):
    slots = rows // 2
    row = lax.broadcasted_iota(jnp.int32, (rows, LANES), 0)
    lane = lax.broadcasted_iota(jnp.int32, (rows, LANES), 1)
    return (row < slots) == (lane < HD)


def pair_rows(value):
    both = jnp.concatenate([value, value], 0)
    return jnp.where(half_mask(both.shape[0]), both, jnp.zeros((), both.dtype))


def pair_lanes(value):
    slots = value.shape[0] // 2
    lane = lax.broadcasted_iota(jnp.int32, (slots, LANES), 1)
    return jnp.where(lane < HD, value[:slots], value[slots:])


def front_kernel(
    pos_ref, word_ref, features_ref, places_ref, boxes_ref, visual_ref, small_ref, edges_ref,
    columns_ref, rows_ref, weights_ref,
    mixed_ref, zero_ref, zero_low_ref, low_ref, plain_ref, scale_ref, query_ref, key_ref,
    value_ref, shares_ref,
    normed_ref, slot_ref, bias_ref, spread_ref, stacked_ref,
):
    slots = mixed_ref.shape[0]
    row = lambda index: small_ref[index : index + 1, :]
    tile = 96
    lookups = (0, 1, 0, 1, 2, 3)

    normed_ref[0:TEXT, :] = word_ref[...].astype(WIDE) + places_ref[...].astype(WIDE)
    normed_ref[TEXT:ROWS, :] = mm(features_ref[...], visual_ref[...], NN) + places_ref[
        0 : ROWS - TEXT, :
    ].astype(WIDE)

    def embed(index, carry):
        where = pl.ds(pl.multiple_of(index * tile, 16), tile)
        place = lax.broadcasted_iota(jnp.int32, (tile, NBOX), 1)
        found = []
        for column, table in enumerate(lookups):
            hot = jnp.where(place == columns_ref[where, column : column + 1], 1.0, 0.0).astype(LOW)
            found.append(mm(hot, boxes_ref[table], NN))
        embedded = normed_ref[where, :] + jnp.concatenate(found, -1)
        plain, scale = norm_rows(embedded)
        normed = plain * row(0) + row(1)
        plain_ref[where, :] = plain
        scale_ref[where, :] = scale
        normed_ref[where, :] = normed
        low_ref[where, :] = normed.astype(LOW)
        return carry

    lax.fori_loop(0, ROWS // tile, embed, 0)
    take_slots(slots, pos_ref, ((normed_ref, zero_ref), (columns_ref, slot_ref)))
    low = low_ref[...]
    zero_low = zero_ref[...].astype(LOW)
    zero_low_ref[...] = zero_low
    query_ref[...] = (mm(zero_low, weights_ref[0], NN) + row(2)).astype(LOW)
    key_ref[...] = mm(low, weights_ref[1], NN).astype(LOW)
    value_ref[...] = (mm(low, weights_ref[2], NN) + row(3)).astype(LOW)

    lane = lax.broadcasted_iota(jnp.int32, (NB, LANES), 1)
    for kind in range(3):
        column, shift = KINDS[kind]
        for head in range(H):
            edge = jnp.broadcast_to(edges_ref[kind * H + head : kind * H + head + 1, :], (NB, LANES))
            near = pltpu.roll(edge, NB, 1, stride=1, stride_axis=0)
            far = pltpu.roll(edge, 1, 1, stride=1, stride_axis=0)
            spread_ref[:, head * LANES : (head + 1) * LANES] = jnp.where(
                lane < NB, near, far
            ).astype(LOW)
        coarse_slot = jnp.right_shift(slot_ref[:, column : column + 1], shift)
        place = lax.broadcasted_iota(jnp.int32, (slots, NB), 1)
        hot = jnp.where(place == coarse_slot, 1.0, 0.0).astype(LOW)
        wide = mm(hot, spread_ref[...], NN).astype(LOW)
        for head in range(H):
            stacked_ref[head * slots : (head + 1) * slots, :] = wide[
                :, head * LANES : (head + 1) * LANES
            ]
        first, second = key_hot(rows_ref, kind)
        below = below_of(rows_ref, slot_ref, kind)

        def add(head, carry):
            where = pl.ds(pl.multiple_of(head * 2 * slots, 16), 2 * slots)
            rows = stacked_ref[where, :]
            both = jnp.concatenate([below, below], 0)
            found = jnp.where(both, mm(rows, second, NN), mm(rows, first, NN))
            bias_ref[where, :] = found if kind == 0 else bias_ref[where, :] + found
            return carry

        lax.fori_loop(0, H // 2, add, 0)

    owner = rows_ref[7:8, :]
    allowed = ((slot_ref[:, 7:8] == owner) | (owner < 0)) & (rows_ref[8:9, :] > 0)
    allowed = jnp.concatenate([allowed, allowed], 0)
    for pair in range(H // 2):
        lanes = slice(pair * LANES, (pair + 1) * LANES)
        rows = slice(pair * 2 * slots, (pair + 1) * 2 * slots)
        scores = mm(pair_rows(query_ref[:, lanes]), key_ref[:, lanes], NT) * 0.125
        scores = jnp.where(allowed, scores + bias_ref[rows, :], MASKED)
        powers = jnp.exp(scores - jnp.max(scores, -1, keepdims=True))
        shares = powers / jnp.sum(powers, -1, keepdims=True)
        shares_ref[rows, :] = shares
        mixed_ref[:, lanes] = pair_lanes(mm(shares.astype(LOW), value_ref[:, lanes], NN)).astype(LOW)


def front_step(pos, word, features, places, boxes, visual, small, edges, columns, rows, weights):
    slots = pos.shape[0]
    vmem = pl.BlockSpec(memory_space=pltpu.VMEM)
    shape = jax.ShapeDtypeStruct
    return pl.pallas_call(
        front_kernel,
        out_shape=(
            shape((slots, D), LOW), shape((slots, D), WIDE), shape((slots, D), LOW),
            shape((ROWS, D), LOW), shape((ROWS, D), WIDE), shape((ROWS, 1), WIDE),
            shape((slots, D), LOW), shape((ROWS, D), LOW), shape((ROWS, D), LOW),
            shape((H * slots, ROWS), WIDE),
        ),
        in_specs=[pl.BlockSpec(memory_space=pltpu.SMEM)] + [vmem] * 10,
        out_specs=(vmem,) * 10,
        scratch_shapes=[
            pltpu.VMEM((ROWS, D), WIDE),
            pltpu.VMEM((slots, 16), jnp.int32),
            pltpu.VMEM((H * slots, ROWS), WIDE),
            pltpu.VMEM((NB, H * LANES), LOW),
            pltpu.VMEM((H * slots, LANES), LOW),
        ],
        compiler_params=pltpu.CompilerParams(vmem_limit_bytes=56 * 2**20),
        name="front_step",
    )(pos, word, features, places, boxes, visual, small, edges, columns, rows, weights)


def back_kernel(
    pos_ref, grad_zero_ref, grad_mixed_ref, shares_ref, query_ref, key_ref, value_ref,
    zero_low_ref, low_ref, plain_ref, scale_ref, features_ref, small_ref, columns_ref, rows_ref,
    weights_ref,
    word_out, places_out, boxes_out, visual_out, weights_out, edges_out, sums_out,
    slot_ref, score_ref, grad_query, grad_key, grad_value, grad_rows, turned_ref, grad_slot,
):
    slots = grad_zero_ref.shape[0]
    take_slots(slots, pos_ref, ((columns_ref, slot_ref),))
    for pair in range(H // 2):
        lanes = slice(pair * LANES, (pair + 1) * LANES)
        rows = slice(pair * 2 * slots, (pair + 1) * 2 * slots)
        grad_mixed = pair_rows(grad_mixed_ref[:, lanes])
        shares = shares_ref[rows, :]
        grad_value[:, lanes] = mm(shares.astype(LOW), grad_mixed, TN).astype(LOW)
        grad_shares = mm(grad_mixed, value_ref[:, lanes], NT)
        scores = shares * (grad_shares - jnp.sum(shares * grad_shares, -1, keepdims=True))
        scores = scores.astype(LOW)
        score_ref[rows, :] = scores
        grad_query[:, lanes] = pair_lanes(mm(scores, key_ref[:, lanes], NN) * 0.125).astype(LOW)
        grad_key[:, lanes] = (mm(scores, pair_rows(query_ref[:, lanes]), TN) * 0.125).astype(LOW)

    lane = lax.broadcasted_iota(jnp.int32, (NB, LANES), 1)
    for kind in range(3):
        column, shift = KINDS[kind]
        first, second = key_hot(rows_ref, kind)
        below = below_of(rows_ref, slot_ref, kind)
        coarse_slot = jnp.right_shift(slot_ref[:, column : column + 1], shift)
        place = lax.broadcasted_iota(jnp.int32, (slots, NB), 1)
        hot = jnp.where(place == NB - 1 - coarse_slot, 1.0, 0.0).astype(LOW)

        def collect(pair, carry):
            where = pl.ds(pl.multiple_of(pair * 2 * slots, 16), 2 * slots)
            both = jnp.concatenate([below, below], 0)
            scores = score_ref[where, :]
            none = jnp.zeros((), LOW)
            found = mm(jnp.where(both, none, scores), first, NT) + mm(
                jnp.where(both, scores, none), second, NT
            )
            turned_ref[where, :] = found.astype(LOW)
            return carry

        lax.fori_loop(0, H // 2, collect, 0)
        for head in range(H):
            part = mm(hot, turned_ref[head * slots : (head + 1) * slots, :], TN)
            near = pltpu.roll(jnp.where(lane < NB, part, 0.0), 1, 1, stride=1, stride_axis=0)
            far = pltpu.roll(jnp.where(lane < NB, 0.0, part), NB, 1, stride=1, stride_axis=0)
            edges_out[kind * H + head : kind * H + head + 1, :] = column_sum(near + far)
    edges_out[3 * H :, :] = jnp.zeros((4, LANES), WIDE)

    low = low_ref[...]
    weights_out[0] = mm(zero_low_ref[...], grad_query[...], TN).astype(LOW)
    weights_out[1] = mm(low, grad_key[...], TN).astype(LOW)
    weights_out[2] = mm(low, grad_value[...], TN).astype(LOW)
    sums_out[2:3, :] = column_sum(grad_query[...].astype(WIDE))
    sums_out[3:4, :] = column_sum(grad_value[...].astype(WIDE))
    sums_out[4:8, :] = jnp.zeros((4, D), WIDE)
    grad_rows[...] = mm(grad_key[...], weights_ref[1], NT) + mm(grad_value[...], weights_ref[2], NT)
    grad_slot[...] = grad_zero_ref[...] + mm(grad_query[...], weights_ref[0], NT)

    def put(index, carry):
        at = pl.ds(pos_ref[index], 1)
        grad_rows[at, :] = grad_rows[at, :] + grad_slot[pl.ds(index, 1), :]
        return carry

    lax.fori_loop(0, slots, put, 0)
    gain = small_ref[0:1, :]
    tile = 96

    def normed_back(index, carry):
        where = pl.ds(pl.multiple_of(index * tile, 16), tile)
        grad, plain = grad_rows[where, :], plain_ref[where, :]
        grad_rows[where, :] = norm_back(grad, plain, scale_ref[where, :], gain)
        return carry[0] + column_sum(grad * plain), carry[1] + column_sum(grad)

    blank = jnp.zeros((1, D), WIDE)
    gains, shifts = lax.fori_loop(0, ROWS // tile, normed_back, (blank, blank))
    sums_out[0:1, :] = gains
    sums_out[1:2, :] = shifts
    grad_low = grad_rows[...].astype(LOW)
    word_out[...] = grad_low[0:TEXT, :]
    extra = ROWS - TEXT
    places_out[...] = grad_rows[0:TEXT, :].astype(LOW)
    places_out[0:extra, :] = (grad_rows[0:extra, :] + grad_rows[TEXT:ROWS, :]).astype(LOW)
    visual_out[...] = mm(features_ref[...], grad_low[TEXT:ROWS, :], TN).astype(LOW)
    block = 256

    def table(index, carry):
        where = pl.ds(pl.multiple_of(index * block, 16), block)
        place = lax.broadcasted_iota(jnp.int32, (block, ROWS), 0) + index * block
        found = []
        for column in range(6):
            hot = jnp.where(place == rows_ref[column : column + 1, :], 1.0, 0.0).astype(LOW)
            found.append(mm(hot, grad_low[:, column * LANES : (column + 1) * LANES], NN))
        boxes_out[0, where, :] = (found[0] + found[2]).astype(LOW)
        boxes_out[1, where, :] = (found[1] + found[3]).astype(LOW)
        boxes_out[2, where, :] = found[4].astype(LOW)
        boxes_out[3, where, :] = found[5].astype(LOW)
        return carry

    lax.fori_loop(0, NBOX // block, table, 0)


def back_step(
    pos, grad_zero, grad_mixed, shares, query, key, value, zero_low, low, plain, scale, features,
    small, columns, rows, weights,
):
    slots = pos.shape[0]
    vmem = pl.BlockSpec(memory_space=pltpu.VMEM)
    shape = jax.ShapeDtypeStruct
    return pl.pallas_call(
        back_kernel,
        out_shape=(
            shape((TEXT, D), LOW), shape((TEXT, D), LOW), shape((4, NBOX, LANES), LOW),
            shape((VCH, D), LOW), shape((3, D, D), LOW), shape((3 * H + 4, LANES), WIDE),
            shape((8, D), WIDE),
        ),
        in_specs=[pl.BlockSpec(memory_space=pltpu.SMEM)] + [vmem] * 15,
        out_specs=(vmem,) * 7,
        scratch_shapes=[
            pltpu.VMEM((slots, 16), jnp.int32),
            pltpu.VMEM((H * slots, ROWS), LOW),
            pltpu.VMEM((slots, D), LOW),
            pltpu.VMEM((ROWS, D), LOW),
            pltpu.VMEM((ROWS, D), LOW),
            pltpu.VMEM((ROWS, D), WIDE),
            pltpu.VMEM((H * slots, LANES), LOW),
            pltpu.VMEM((slots, D), WIDE),
        ],
        compiler_params=pltpu.CompilerParams(vmem_limit_bytes=56 * 2**20),
        name="back_step",
    )(
        pos, grad_zero, grad_mixed, shares, query, key, value, zero_low, low, plain, scale,
        features, small, columns, rows, weights,
    )


def on_device(
    tokens, text_box, segments, alive_text, features, mask_pos, mask_label, mask_valid, *states
):
    (projections, box_tables, position_table, visual_proj, small_params, word_table, feedforward) = (
        states[::3]
    )
    dp, mp = lax.axis_size("dp"), lax.axis_size("mp")
    plan = Plan(dp, mp)

    def gathered(part, axis):
        return lax.all_gather(part.astype(LOW), "dp", axis=axis, tiled=True)

    work_table = gathered(word_table, 0)
    work_small = gathered(small_params, 1)
    work_boxes = gathered(box_tables, 1)
    work_places = gathered(position_table, 0)
    work_visual = gathered(visual_proj, 0)
    work_proj = gathered(projections, 1)
    work_ffn = gathered(feedforward, 1)
    model_index = lax.axis_index("mp")
    vocab_shard, hidden_shard = work_table.shape[0], work_ffn.shape[2]
    small_float = work_small.astype(WIDE)

    local_ids = tokens - model_index * vocab_shard
    inside = (local_ids >= 0) & (local_ids < vocab_shard)
    safe_index = jnp.clip(local_ids, 0, vocab_shard - 1)
    partial_word = jnp.where(
        inside[..., None], jnp.take(work_table, safe_index, axis=0), jnp.zeros((), LOW)
    )
    word = lax.psum_scatter(partial_word, "mp", scatter_dimension=0, tiled=True)[0]

    info = token_info(text_box[0], segments[0], alive_text[0])
    columns = info.T
    visual_rows = jnp.pad(features, ((0, ROWS - TEXT - features.shape[0]), (0, 0)))
    edges = edge_rows(work_small[10 + FF // D : 13 + FF // D].reshape(3 * NB, H))
    (
        mixed, slot_zero, slot_low, normed_low, plain, scale, queries, keys, values, shares,
    ) = front_step(
        mask_pos, word, visual_rows, work_places, work_boxes, work_visual, small_float, edges,
        columns, info, work_proj[:3],
    )
    ffn_bias_full = small_float[10 : 10 + FF // D].reshape(1, -1)
    ffn_bias = lax.dynamic_slice_in_dim(ffn_bias_full, model_index * hidden_shard, hidden_shard, 1)
    (
        grad_slot, grad_mixed, grad_out_weight, grad_ffn, grad_table, head_rows, grad_ffn_bias,
        own_tile,
    ) = head_step(
        mp, mixed, slot_zero, work_proj[3], small_float, ffn_bias, work_ffn, work_table,
        mask_label[None, :], mask_valid[None, :],
    )
    grad_word, grad_places, grad_boxes, grad_visual, grad_in_weight, grad_edges, front_rows = (
        back_step(
            mask_pos, grad_slot, grad_mixed, shares, queries, keys, values, slot_low, normed_low,
            plain, scale, visual_rows, small_float, columns, info, work_proj[:3],
        )
    )
    bias_full = lax.dynamic_update_slice_in_dim(
        jnp.zeros((FF,), WIDE), grad_ffn_bias[0], model_index * hidden_shard, 0
    ).reshape(FF // D, D)
    grad_small = jnp.concatenate(
        [front_rows[:4], head_rows[4:10], bias_full, edge_rows_back(grad_edges).reshape(3, D)], 0
    )
    group_word = lax.all_gather(grad_word[None], "mp", axis=0, tiled=True)
    grad_table = grad_table.astype(WIDE) + jnp.zeros((vocab_shard, D), WIDE).at[safe_index].add(
        jnp.where(inside[..., None], group_word.astype(WIDE), 0.0)
    )

    def split_rows(part):
        rows = part.shape[-2] // dp
        part = part.astype(LOW).reshape(part.shape[:-2] + (dp, rows, part.shape[-1]))
        extra = [(0, 0)] * (part.ndim - 2) + [(0, pad_up(rows, 16) - rows), (0, 0)]
        return jnp.pad(part, extra) if extra[-2][1] else part

    cut = small_params.shape[1]
    small_split = jnp.transpose(grad_small.reshape(VROWS, dp, cut), (1, 0, 2)).astype(LOW)
    small_split = jnp.pad(small_split, ((0, 0), (0, 32 - VROWS), (0, LANES - cut)))
    table_split, ffn_split = split_rows(grad_table), split_rows(grad_ffn)
    shared_sum, split_sum, totals = reduce_gradients(
        plan,
        table_split,
        split_rows(grad_in_weight),
        split_rows(grad_out_weight),
        ffn_split,
        split_rows(grad_places),
        split_rows(grad_visual),
        grad_boxes.reshape(4, dp, NBOX // dp, LANES),
        small_split,
        own_tile,
    )
    loss_sum, loss_count = (totals[1, 0, 0], totals[1, 1, 0])
    grad_norm = jnp.sqrt(jnp.sum(totals[0])) / loss_count
    outputs = adam_update(
        plan, table_split.shape[1], ffn_split.shape[2], shared_sum, split_sum, totals, states
    )
    return tuple(outputs) + (loss_sum, loss_count, grad_norm)


def solution(mesh):
    in_specs = (
        P("dp", None),
        P(("dp", "mp"), None, None),
        P(("dp", "mp"), None),
        P(("dp", "mp"), None),
        P(("dp", "mp"), None),
        P(("dp", "mp")),
        P("dp"),
        P("dp"),
        P(None, "dp", None),
        P(None, "dp", None),
        P(None, "dp", None),
        P(None, "dp", None),
        P(None, "dp", None),
        P(None, "dp", None),
        P("dp", None),
        P("dp", None),
        P("dp", None),
        P("dp", None),
        P("dp", None),
        P("dp", None),
        P(None, "dp"),
        P(None, "dp"),
        P(None, "dp"),
        P(("mp", "dp"), None),
        P(("mp", "dp"), None),
        P(("mp", "dp"), None),
        P(None, "dp", "mp"),
        P(None, "dp", "mp"),
        P(None, "dp", "mp"),
    )
    out_specs = (
        P(None, "dp", None),
        P(None, "dp", None),
        P(None, "dp", None),
        P(None, "dp", None),
        P(None, "dp", None),
        P(None, "dp", None),
        P("dp", None),
        P("dp", None),
        P("dp", None),
        P("dp", None),
        P("dp", None),
        P("dp", None),
        P(None, "dp"),
        P(None, "dp"),
        P(None, "dp"),
        P(("mp", "dp"), None),
        P(("mp", "dp"), None),
        P(("mp", "dp"), None),
        P(None, "dp", "mp"),
        P(None, "dp", "mp"),
        P(None, "dp", "mp"),
        P(),
        P(),
        P(),
    )
    return jax.shard_map(
        on_device, mesh=mesh, in_specs=in_specs, out_specs=out_specs, check_vma=False
    )
```

```python
import jax
import jax.numpy as jnp
from jax import lax
from jax.experimental import pallas as pl
from jax.experimental.pallas import tpu as pltpu
from jax.sharding import PartitionSpec as P

D = 768
H = 12
HD = 64
FF = 3072
NB = 64
GRID = 7
TEXT = 512
STEP = 10
VCH = 256
NBOX = 1024
VROWS = 17


MASKED = -1e30
CLIP = 0.005
BETA_ONE = 0.9
BETA_TWO = 0.999
EPSILON = 1e-08
DECAY = 0.01
RATES = (0.02, 0.03, 0.03, 0.04, 0.3, 0.05, 0.02)


def grid_boxes():
    cells = jnp.arange(GRID * GRID, dtype=jnp.int32)
    row_place = cells // GRID
    column_place = cells % GRID
    return jnp.stack(
        [
            column_place * 1000 // GRID,
            row_place * 1000 // GRID,
            (column_place + 1) * 1000 // GRID,
            (row_place + 1) * 1000 // GRID,
        ],
        -1,
    )


def adam_step(weight, grad, first, second, rate):
    first = BETA_ONE * first + (1.0 - BETA_ONE) * grad
    second = BETA_TWO * second + (1.0 - BETA_TWO) * grad * grad
    fixed_first = first / (1.0 - BETA_ONE**STEP)
    fixed_second = second / (1.0 - BETA_TWO**STEP)
    weight = weight - rate * (fixed_first / (jnp.sqrt(fixed_second) + EPSILON) + DECAY * weight)
    return (weight, first, second)


MESH = pl.DeviceIdType.MESH
LOW = jnp.bfloat16
WIDE = jnp.float32
LANES = 128
HALF = D // 2


def pad_up(count, unit):
    return (count + unit - 1) // unit * unit


def bits_of(count):
    return count.bit_length() - 1


def flip(index, bit):
    return index + (1 - 2 * ((index // 2**bit) % 2)) * 2**bit


class Plan:
    def __init__(self, dp, mp):
        self.dp, self.mp = dp, mp
        self.proj = pad_up(D // dp, 16)
        self.places = pad_up(TEXT // dp, 16)
        self.visual = pad_up(VCH // dp, 16)
        self.box = NBOX // dp
        self.box_parts = 4 * (self.box // 32)
        self.places_at = 4 * self.proj
        self.visual_at = self.places_at + self.places
        self.box_at = self.visual_at + self.visual
        self.box_rows = 32 * ((self.box_parts + 6) // 6)
        self.shared = pad_up(self.box_at + self.box_rows, 32 * mp)

    def box_slot(self, part):
        return self.box_at + 32 * (part // 6), LANES * (part % 6)


def group_of(axis, index):
    return {axis: index}


def lanes_of(stream):
    return pl.ds(stream * HALF, HALF)


def ffn_slot(part, table_rows, ffn_rows, wide):
    return table_rows + part * wide // D * ffn_rows, part * wide % D


def row_tile(rows):
    return next(t for t in (48, 32, 16) if rows % t == 0)


def reduce_kernel(plan, table_rows, ffn_rows, vocab_rows, refs):
    (
        table_in, proj_in, out_in, ffn_in, places_in, visual_in, boxes_in, small_in, tile_in,
        word_in, tokens_ref,
        shared_out, split_out, tile_out,
        shared_acc, split_acc, shared_got, split_got, ring_got, ring_own, words, tile_mp, tile_dp,
        load_sem, send_sem, recv_sem, ring_send, ring_recv, word_send, word_recv, tile_send,
        tile_recv,
    ) = refs
    dp, mp = plan.dp, plan.mp
    me, here = lax.axis_index("dp"), lax.axis_index("mp")
    depth, ring_depth = bits_of(dp), bits_of(mp)
    loads = []

    def load(source, target):
        loads.append(pltpu.make_async_copy(source, target, load_sem.at[len(loads)]))
        loads[-1].start()

    load(word_in, words.at[here])
    for part in range(4):
        source = proj_in.at[part] if part < 3 else out_in
        load(source, shared_acc.at[:, pl.ds(part * plan.proj, plan.proj)])
    load(places_in, shared_acc.at[:, pl.ds(plan.places_at, plan.places)])
    load(visual_in, shared_acc.at[:, pl.ds(plan.visual_at, plan.visual)])
    pieces_box = plan.box // 32
    for part in range(plan.box_parts):
        row, lane = plan.box_slot(part)
        load(
            boxes_in.at[part // pieces_box, :, pl.ds(32 * (part % pieces_box), 32)],
            shared_acc.at[:, pl.ds(row, 32), pl.ds(lane, LANES)],
        )
    row, lane = plan.box_slot(plan.box_parts)
    load(small_in, shared_acc.at[:, pl.ds(row, 32), pl.ds(lane, LANES)])
    first_loads = len(loads)
    for part in range(2):
        wide = ffn_in.shape[3]
        row, lane = ffn_slot(part, table_rows, ffn_rows, wide)
        load(ffn_in.at[part], split_acc.at[:, pl.ds(row, ffn_rows), pl.ds(lane, wide)])
    load(table_in, split_acc.at[:, pl.ds(0, table_rows)])

    barrier = pltpu.get_barrier_semaphore()
    for other in range(1, dp):
        pl.semaphore_signal(
            barrier, 1, device_id={"dp": lax.rem(me + other, dp)}, device_id_type=MESH
        )
    for other in range(1, mp):
        pl.semaphore_signal(
            barrier, 1, device_id={"mp": lax.rem(here + other, mp)}, device_id_type=MESH
        )
    pl.semaphore_wait(barrier, dp + mp - 2)
    for part in range(plan.box_parts + 1, 6 * (plan.shared - plan.box_at) // 32):
        row, lane = plan.box_slot(part)
        shared_acc[:, pl.ds(row, 32), pl.ds(lane, LANES)] = jnp.zeros((dp, 32, LANES), LOW)

    ring = Ring(mp, (word_send, word_recv))
    loads[0].wait()
    for stream in range(2):
        ring.gather_start(words, 0, stream, 0)

    def word_step(step):
        for stream in range(2):
            ring.gather_wait(words, 0, stream, step)
            if step < ring.depth - 1:
                ring.gather_start(words, 0, stream, step + 1)

    orders = ([0] + list(range(depth - 1, 0, -1)), list(range(depth)))
    half, rest = plan.shared // 2, split_acc.shape[1] - table_rows
    pieces = (
        (shared_acc, shared_got, 0, half),
        (shared_acc, shared_got, half, half),
        (split_acc, split_got, table_rows, rest),
        (split_acc, split_got, 0, table_rows // 2),
        (split_acc, split_got, table_rows // 2, table_rows // 2),
    )

    def chunk(order, step, free, away):
        index = 0
        for place, bit in enumerate(order):
            mine = (me // 2**bit) % 2
            if place < step or (place == step and not away):
                index = index + mine * 2**bit
            elif place == step:
                index = index + (1 - mine) * 2**bit
            else:
                index = index + ((free >> (place - step - 1)) & 1) * 2**bit
        return index

    def slot_base(step):
        return sum(2 ** (depth - 1 - s) for s in range(step))

    def send_one(piece, stream, step, free):
        acc, got, first, rows = pieces[piece]
        order = orders[stream]
        pltpu.make_async_remote_copy(
            src_ref=acc.at[chunk(order, step, free, True), pl.ds(first, rows), lanes_of(stream)],
            dst_ref=got.at[slot_base(step) + free, pl.ds(first, rows), lanes_of(stream)],
            send_sem=send_sem.at[piece, stream, step],
            recv_sem=recv_sem.at[piece, stream, step],
            device_id={"dp": flip(me, order[step])},
            device_id_type=MESH,
        ).start()

    def send(piece, step):
        for stream in range(2):
            for free in range(2 ** (depth - 1 - step)):
                send_one(piece, stream, step, free)

    def wait_bytes(piece, stream, step, sem):
        acc, got, first, rows = pieces[piece]
        count = 2 ** (depth - 1 - step)
        where = got.at[pl.ds(slot_base(step), count), pl.ds(first, rows), lanes_of(stream)]
        pltpu.make_async_copy(where, where, sem.at[piece, stream, step]).wait()

    def add(piece, stream, step):
        acc, got, first, rows = pieces[piece]
        order = orders[stream]
        wait_bytes(piece, stream, step, recv_sem)
        tile = row_tile(rows)
        last = step == depth - 1
        for free in range(2 ** (depth - 1 - step)):
            kept = chunk(order, step, free, False)

            def body(index, carry):
                at = pl.multiple_of(first + index * tile, 16)
                where = pl.ds(at, tile)
                total = acc[kept, where, lanes_of(stream)].astype(WIDE) + got[
                    slot_base(step) + free, where, lanes_of(stream)
                ].astype(WIDE)
                if last and acc is split_acc:
                    split_out[where, lanes_of(stream)] = total
                elif last:
                    ring_own[0, where, lanes_of(stream)] = total.astype(LOW)
                else:
                    acc[kept, where, lanes_of(stream)] = total.astype(LOW)
                return carry

            lax.fori_loop(0, rows // tile, body, 0)

    def advance(piece, step):
        for stream in range(2):
            add(piece, stream, step)
            if step < depth - 1:
                for free in range(2 ** (depth - 2 - step)):
                    send_one(piece, stream, step + 1, free)

    ring_orders = (list(range(ring_depth)), list(range(ring_depth - 1, -1, -1)))

    def ring_copy(stream, step):
        return pltpu.make_async_remote_copy(
            src_ref=ring_own.at[step, :, lanes_of(stream)],
            dst_ref=ring_got.at[step, :, lanes_of(stream)],
            send_sem=ring_send.at[stream, step],
            recv_sem=ring_recv.at[stream, step],
            device_id={"mp": flip(here, ring_orders[stream][step])},
            device_id_type=MESH,
        )

    def ring_step(step):
        for stream in range(2):
            ring_copy(stream, step).wait_recv()
            rows = plan.shared
            tile = row_tile(rows)

            def body(index, carry):
                where = pl.ds(pl.multiple_of(index * tile, 16), tile)
                total = ring_own[step, where, lanes_of(stream)].astype(WIDE) + ring_got[
                    step, where, lanes_of(stream)
                ].astype(WIDE)
                if step == ring_depth - 1:
                    shared_out[where, lanes_of(stream)] = total
                else:
                    ring_own[step + 1, where, lanes_of(stream)] = total.astype(LOW)
                return carry

            lax.fori_loop(0, rows // tile, body, 0)
            if step < ring_depth - 1:
                ring_copy(stream, step + 1).start()

    ids = tokens_ref[...] - here * (vocab_rows * dp)

    def scatter(index):
        local = ids - index * vocab_rows
        local = jnp.where(local < vocab_rows, local, -1)
        place = lax.broadcasted_iota(jnp.int32, (table_rows, ids.shape[1]), 0)
        hot = jnp.where(place == local, 1.0, 0.0).astype(LOW)
        where = (index, pl.ds(0, table_rows))
        total = split_acc[where].astype(WIDE) + mm(hot, words[...].reshape(mp * TEXT, D), NN)
        split_acc[where] = total.astype(LOW)

    for copy in loads[1:first_loads]:
        copy.wait()
    send(0, 0)
    send(1, 0)
    for copy in loads[first_loads:]:
        copy.wait()
    send(2, 0)
    for step in range(depth):
        for piece in range(3):
            advance(piece, step)
            if step == depth - 1 and piece == 1:
                for stream in range(2):
                    ring_copy(stream, 0).start()
        if step < ring.depth - 1:
            word_step(step)
    for step in range(min(depth, ring.depth - 1), ring.depth):
        word_step(step)
    count = 2 ** (depth - 1)
    other_core, own_core = 1 - me % 2, me % 2

    def scatter_other(index, carry):
        scatter(other_core + 2 * index)
        return carry

    def scatter_own(index, carry):
        scatter(own_core + 2 * index)
        return carry

    lax.fori_loop(0, count, scatter_other, 0)
    send(3, 0)
    send(4, 0)
    lax.fori_loop(0, count, scatter_own, 0)
    for step in range(max(depth, ring_depth)):
        for piece in (3, 4):
            if step < depth:
                advance(piece, step)
        if step < ring_depth:
            ring_step(step)

    def squares(ref, rows):
        tile = row_tile(rows)

        def body(index, total):
            values = ref[pl.ds(pl.multiple_of(index * tile, 16), tile), :]
            return total + jnp.sum((values * values).reshape(tile // 8, 8, D), 0)

        total = lax.fori_loop(0, rows // tile, body, jnp.zeros((8, D), WIDE))
        folded = total[:, 0:LANES]
        for part in range(1, D // LANES):
            folded = folded + total[:, part * LANES : (part + 1) * LANES]
        return folded

    folded = squares(shared_out, plan.shared) * (1.0 / mp) + squares(split_out, split_out.shape[0])
    tile_mp[here, 0] = folded
    tile_mp[here, 1] = tile_in[...]

    def exchange(buffer, axis, index, count, base):
        copies = []
        for other in range(1, count):
            copies.append(
                pltpu.make_async_remote_copy(
                    src_ref=buffer.at[index],
                    dst_ref=buffer.at[index],
                    send_sem=tile_send.at[base + other],
                    recv_sem=tile_recv.at[base + other],
                    device_id={axis: lax.rem(index + other, count)},
                    device_id_type=MESH,
                )
            )
        for copy in copies:
            copy.start()
        for other in range(1, count):
            source = lax.rem(index + count - other, count)
            pltpu.make_async_copy(
                buffer.at[source], buffer.at[source], tile_recv.at[base + other]
            ).wait()
        return copies

    pending = exchange(tile_mp, "mp", here, mp, 0)
    total = tile_mp[0]
    for index in range(1, mp):
        total = total + tile_mp[index]
    tile_dp[me] = total
    pending = pending + exchange(tile_dp, "dp", me, dp, mp)
    total = tile_dp[0]
    for index in range(1, dp):
        total = total + tile_dp[index]
    tile_out[...] = total
    for copy in pending:
        copy.wait_send()
    ring.finish()
    for piece in range(len(pieces)):
        for stream in range(2):
            for step in range(depth):
                wait_bytes(piece, stream, step, send_sem)
    for stream in range(2):
        for step in range(ring_depth):
            ring_copy(stream, step).wait_send()


def reduce_gradients(
    plan, vocab_rows, table, proj, out, ffn, places, visual, boxes, small, tile, word, tokens
):
    dp, mp = plan.dp, plan.mp
    table_rows, ffn_rows = table.shape[1], ffn.shape[2]
    split = table_rows + 2 * ffn_rows * ffn.shape[3] // D
    depth, ring_depth = bits_of(dp), bits_of(mp)
    anywhere = pl.BlockSpec(memory_space=pl.ANY)
    vmem = pl.BlockSpec(memory_space=pltpu.VMEM)
    dma = pltpu.SemaphoreType.DMA

    def body(*refs):
        reduce_kernel(plan, table_rows, ffn_rows, vocab_rows, refs)

    return pl.pallas_call(
        body,
        out_shape=(
            jax.ShapeDtypeStruct((plan.shared, D), WIDE),
            jax.ShapeDtypeStruct((split, D), WIDE),
            jax.ShapeDtypeStruct((2, 8, LANES), WIDE),
        ),
        in_specs=[anywhere] * 8 + [vmem, anywhere, vmem],
        out_specs=(vmem, vmem, vmem),
        scratch_shapes=[
            pltpu.VMEM((dp, plan.shared, D), LOW),
            pltpu.VMEM((dp, split, D), LOW),
            pltpu.VMEM((dp - 1, plan.shared, D), LOW),
            pltpu.VMEM((dp - 1, split, D), LOW),
            pltpu.VMEM((ring_depth, plan.shared, D), LOW),
            pltpu.VMEM((ring_depth, plan.shared, D), LOW),
            pltpu.VMEM((mp, TEXT, D), LOW),
            pltpu.VMEM((mp, 2, 8, LANES), WIDE),
            pltpu.VMEM((dp, 2, 8, LANES), WIDE),
            dma((plan.box_parts + 12,)),
            dma((5, 2, depth)),
            dma((5, 2, depth)),
            dma((2, ring_depth)),
            dma((2, ring_depth)),
            dma((1, 2, mp - 1)),
            dma((1, 2, mp - 1)),
            dma((mp + dp,)),
            dma((mp + dp,)),
        ],
        compiler_params=pltpu.CompilerParams(
            collective_id=5, has_side_effects=True, vmem_limit_bytes=58 * 2**20
        ),
        name="reduce_gradients",
    )(table, proj, out, ffn, places, visual, boxes, small, tile, word, tokens)


def adam_kernel(plan, table_rows, ffn_rows, sizes, refs):
    shared_ref, split_ref, tile_ref = refs[:3]
    states, outs = refs[3:24], refs[24:45]
    totals = tile_ref[...]
    norm = jnp.sqrt(jnp.sum(totals[0], keepdims=True)) / totals[1, 1:2, 0:1]
    scale = jnp.minimum(1.0, CLIP / norm) / totals[1, 1:2, 0:1]

    def update(index, where, rows, grad_of):
        rate = RATES[index]
        weight, first, second = (ref[where] for ref in states[3 * index : 3 * index + 3])
        grad = grad_of * scale
        results = adam_step(weight, grad, first, second, rate)
        for ref, value in zip(outs[3 * index : 3 * index + 3], results):
            ref[where] = value

    def blocks(index, lead, source, at, rows, lane=0, wide=D):
        tile = next(t for t in (32, 24, 16, 8) if rows % t == 0)

        def body(step, carry):
            here = pl.multiple_of(step * tile, 8)
            where = (pl.ds(here, tile), slice(None))
            grad = source[pl.ds(pl.multiple_of(at + here, 8), tile), pl.ds(lane, wide)]
            update(index, where if lead is None else (lead,) + where, tile, grad)
            return carry

        lax.fori_loop(0, rows // tile, body, 0)

    for part in range(4):
        blocks(0, part, shared_ref, part * plan.proj, sizes[0])
    pieces_box = plan.box // 32
    for part in range(plan.box_parts):
        row, lane = plan.box_slot(part)
        grad = shared_ref[pl.ds(row, 32), pl.ds(lane, LANES)]
        update(1, (part // pieces_box, pl.ds(32 * (part % pieces_box), 32)), 32, grad)
    blocks(2, None, shared_ref, plan.places_at, sizes[2])
    blocks(3, None, shared_ref, plan.visual_at, sizes[3])
    row, lane = plan.box_slot(plan.box_parts)
    grad = shared_ref[pl.ds(row, 32), pl.ds(lane, LANES)]
    update(4, (slice(None), slice(None)), VROWS, grad[:VROWS, : sizes[4]])
    blocks(5, None, split_ref, 0, sizes[5])
    for part in range(2):
        wide = states[18].shape[2]
        row, lane = ffn_slot(part, table_rows, ffn_rows, wide)
        blocks(6, part, split_ref, row, sizes[6], lane, wide)


def adam_update(plan, table_rows, ffn_rows, shared, split, tile, states):
    sizes = (
        states[0].shape[1], 0, states[6].shape[0], states[9].shape[0], states[12].shape[1],
        states[15].shape[0], states[18].shape[1],
    )
    vmem = pl.BlockSpec(memory_space=pltpu.VMEM)

    def body(*refs):
        adam_kernel(plan, table_rows, ffn_rows, sizes, refs)

    return pl.pallas_call(
        body,
        out_shape=tuple(jax.ShapeDtypeStruct(part.shape, WIDE) for part in states),
        in_specs=[vmem] * 24,
        out_specs=(vmem,) * 21,
        compiler_params=pltpu.CompilerParams(vmem_limit_bytes=48 * 2**20),
        name="adam_update",
    )(shared, split, tile, *states)


def combos(index, bits):
    found = [index]
    for bit in bits:
        found = found + [flip(one, bit) for one in found]
    return found


class Ring:
    def __init__(self, mp, sems):
        self.mp, self.here = mp, lax.axis_index("mp")
        self.send, self.recv = sems
        depth = bits_of(mp)
        self.depth = depth
        self.orders = (list(range(depth)), list(range(depth - 1, -1, -1)))
        self.started = []

    def barrier(self):
        barrier = pltpu.get_barrier_semaphore()
        for other in range(1, self.mp):
            pl.semaphore_signal(
                barrier, 1, device_id={"mp": lax.rem(self.here + other, self.mp)},
                device_id_type=MESH,
            )
        pl.semaphore_wait(barrier, self.mp - 1)

    def copy(self, source, target, number, stream, index, peer):
        made = pltpu.make_async_remote_copy(
            src_ref=source, dst_ref=target,
            send_sem=self.send.at[number, stream, index],
            recv_sem=self.recv.at[number, stream, index],
            device_id={"mp": peer}, device_id_type=MESH,
        )
        return made

    def gather_start(self, buffer, number, stream, step):
        order = self.orders[stream]
        peer = flip(self.here, order[step])
        for place, slot in enumerate(combos(self.here, order[:step])):
            part = buffer.at[slot, :, lanes_of(stream)]
            made = self.copy(part, part, number, stream, 2**step - 1 + place, peer)
            made.start()
            self.started.append(made)

    def gather_wait(self, buffer, number, stream, step):
        order = self.orders[stream]
        peer = flip(self.here, order[step])
        for place, slot in enumerate(combos(peer, order[:step])):
            part = buffer.at[slot, :, lanes_of(stream)]
            self.copy(part, part, number, stream, 2**step - 1 + place, peer).wait_recv()

    def gather(self, buffer, number):
        for stream in range(2):
            self.gather_start(buffer, number, stream, 0)
        for step in range(self.depth):
            for stream in range(2):
                self.gather_wait(buffer, number, stream, step)
                if step < self.depth - 1:
                    self.gather_start(buffer, number, stream, step + 1)

    def base(self, step):
        return sum(2 ** (self.depth - 1 - s) for s in range(step))

    def reduce_one(self, buffer, got, number, stream, step, place):
        order = self.orders[stream]
        peer = flip(self.here, order[step])
        slot = combos(peer, order[step + 1 :])[place]
        index = self.base(step) + place
        made = self.copy(
            buffer.at[slot, :, lanes_of(stream)],
            got.at[index, :, lanes_of(stream)],
            number, stream, index, peer,
        )
        made.start()
        self.started.append(made)

    def reduce_start(self, buffer, got, number, stream, step):
        for place in range(2 ** (self.depth - 1 - step)):
            self.reduce_one(buffer, got, number, stream, step, place)

    def reduce_wait(self, buffer, got, number, stream, step):
        order = self.orders[stream]
        peer = flip(self.here, order[step])
        for place, slot in enumerate(combos(self.here, order[step + 1 :])):
            index = self.base(step) + place
            part = got.at[index, :, lanes_of(stream)]
            self.copy(part, part, number, stream, index, peer).wait_recv()
            where = (slot, slice(None), lanes_of(stream))
            total = buffer[where].astype(WIDE) + got[index, :, lanes_of(stream)].astype(WIDE)
            buffer[where] = total.astype(buffer.dtype)

    def reduce_begin(self, buffer, got, number):
        for stream in range(2):
            self.reduce_start(buffer, got, number, stream, 0)

    def reduce_rest(self, buffer, got, number, between=()):
        between = list(between)
        for step in range(self.depth):
            if between:
                between.pop(0)()
            for stream in range(2):
                self.reduce_wait(buffer, got, number, stream, step)
                if step < self.depth - 1:
                    self.reduce_start(buffer, got, number, stream, step + 1)
        for rest in between:
            rest()

    def finish(self):
        for made in self.started:
            made.wait_send()


def mm(left, right, dims):
    return lax.dot_general(left, right, (dims, ((), ())), preferred_element_type=WIDE)


NN, NT, TN = ((1,), (0,)), ((1,), (1,)), ((0,), (0,))


def norm_rows(value):
    centred = value - jnp.mean(value, -1, keepdims=True)
    scale = lax.rsqrt(jnp.mean(centred * centred, -1, keepdims=True) + 1e-05)
    return centred * scale, scale


def norm_back(grad, plain, scale, gain):
    inner = grad * gain
    return scale * (
        inner
        - jnp.mean(inner, -1, keepdims=True)
        - plain * jnp.mean(inner * plain, -1, keepdims=True)
    )


def column_sum(value):
    return jnp.sum(value, 0, keepdims=True)


def head_kernel(mp, refs):
    (
        mixed_ref, zero_ref, out_weight, small_ref, bias_ref, ffn_ref, table_ref, label_ref,
        valid_ref,
        grad_zero_ref, grad_mixed_ref, grad_out_ref, grad_ffn_ref, grad_table_ref, rows_ref,
        bias_out, sums_ref,
        ffn, table, one, picked, down, sums_two, grad_picked, grad_one, got_two, got_picked,
        got_one, logits, low_logits, stats, load_sem, send_sem, recv_sem, stat_send, stat_recv,
    ) = refs
    ring = Ring(mp, (send_sem, recv_sem))
    here = ring.here
    slots = mixed_ref.shape[0]
    group = slots * mp
    load_ffn = pltpu.make_async_copy(ffn_ref, ffn, load_sem.at[0])
    load_table = pltpu.make_async_copy(table_ref, table, load_sem.at[1])
    load_ffn.start()
    load_table.start()
    ring.barrier()
    row = lambda index: small_ref[index : index + 1, :]

    out = mm(mixed_ref[...], out_weight[...], NN) + row(4)
    plain_one, scale_one = norm_rows(zero_ref[...] + out)
    normed_one = plain_one * row(5) + row(6)
    one[here] = normed_one.astype(LOW)
    ring.gather(one, 0)
    load_ffn.wait()
    hidden = ffn.shape[2]
    group_one = one[...].reshape(group, D)
    before = mm(group_one, ffn[0], NN) + bias_ref[...]
    erf_part = 0.5 * (1.0 + lax.erf(before * (0.5**0.5)))
    active = (before * erf_part).astype(LOW)
    slope = erf_part + before * jnp.exp(-0.5 * before * before) * 0.3989422804014327
    sums_two[...] = mm(active, ffn[1], NT).astype(sums_two.dtype).reshape(mp, slots, D)
    ring.reduce_begin(sums_two, got_two, 1)
    load_table.wait()
    ring.reduce_rest(sums_two, got_two, 1)
    plain_two, scale_two = norm_rows(normed_one + (sums_two[here].astype(WIDE) + row(7)))
    picked[here] = (plain_two * row(8) + row(9)).astype(LOW)
    ring.gather(picked, 2)

    group_picked = picked[...].reshape(group, D)
    vocab = table.shape[0]
    tile = next(t for t in (480, 512, 256, 128) if vocab % t == 0)
    tiles = vocab // tile
    label = label_ref[...] - here * vocab
    valid = valid_ref[...].astype(WIDE)

    def forward(index, carry):
        highest, total, target = carry
        where = pl.ds(pl.multiple_of(index * tile, 16), tile)
        values = mm(table[where, :], group_picked, NT)
        logits[where, :] = values
        higher = jnp.maximum(highest, jnp.max(values, 0, keepdims=True))
        total = total * jnp.exp(highest - higher) + column_sum(jnp.exp(values - higher))
        word = lax.broadcasted_iota(jnp.int32, (tile, group), 0) + index * tile
        target = target + column_sum(jnp.where(word == label, values, 0.0))
        return higher, total, target

    blank = jnp.zeros((1, group), WIDE)
    highest, total, target = lax.fori_loop(0, tiles, forward, (blank - 1e30, blank, blank))
    stats[here, 0:1, 0:group] = highest
    stats[here, 1:2, 0:group] = total
    stats[here, 2:3, 0:group] = target
    stat_copies = []
    for other in range(1, mp):
        made = pltpu.make_async_remote_copy(
            src_ref=stats.at[here], dst_ref=stats.at[here],
            send_sem=stat_send.at[other], recv_sem=stat_recv.at[other],
            device_id={"mp": lax.rem(here + other, mp)}, device_id_type=MESH,
        )
        made.start()
        stat_copies.append(made)
    for other in range(1, mp):
        source = lax.rem(here + mp - other, mp)
        pltpu.make_async_copy(stats.at[source], stats.at[source], stat_recv.at[other]).wait()
    highest = stats[0, 0:1, 0:group]
    for index in range(1, mp):
        highest = jnp.maximum(highest, stats[index, 0:1, 0:group])
    total, target = blank, blank
    for index in range(mp):
        total = total + stats[index, 1:2, 0:group] * jnp.exp(stats[index, 0:1, 0:group] - highest)
        target = target + stats[index, 2:3, 0:group]
    log_rows = highest + jnp.log(total)
    place = lax.broadcasted_iota(jnp.int32, (1, group), 1)
    own = (place >= here * slots) & (place < (here + 1) * slots)
    loss = jnp.sum(jnp.where(own, valid * (log_rows - target), 0.0), -1, keepdims=True)
    count = jnp.sum(jnp.where(own, valid, 0.0), -1, keepdims=True)
    first_lane = lax.broadcasted_iota(jnp.int32, (8, LANES), 1) == 0
    first_row = lax.broadcasted_iota(jnp.int32, (8, LANES), 0)
    sums_ref[...] = jnp.where(
        first_lane & (first_row == 0), loss, jnp.where(first_lane & (first_row == 1), count, 0.0)
    )

    def backward(index, grad):
        where = pl.ds(pl.multiple_of(index * tile, 16), tile)
        word = lax.broadcasted_iota(jnp.int32, (tile, group), 0) + index * tile
        hit = jnp.where(word == label, 1.0, 0.0)
        values = ((jnp.exp(logits[where, :] - log_rows) - hit) * valid).astype(LOW)
        low_logits[where, :] = values
        return grad + mm(values, table[where, :], TN)

    grad = lax.fori_loop(0, tiles, backward, jnp.zeros((group, D), WIDE))
    grad_picked[...] = grad.astype(grad_picked.dtype).reshape(mp, slots, D)

    def table_part(first, last):
        def run():
            def body(index, carry):
                where = pl.ds(pl.multiple_of(index * tile, 16), tile)
                grad_table_ref[where, :] = mm(low_logits[where, :], group_picked, NN).astype(LOW)
                return carry

            lax.fori_loop(first, last, body, 0)

        return run

    ring.reduce_begin(grad_picked, got_picked, 3)
    middle = tiles // 2
    ring.reduce_rest(
        grad_picked, got_picked, 3, [table_part(0, middle), table_part(middle, tiles)]
    )
    grad_two = grad_picked[here].astype(WIDE)
    rows_ref[8:9, :] = column_sum(grad_two * plain_two)
    rows_ref[9:10, :] = column_sum(grad_two)
    grad_sum_two = norm_back(grad_two, plain_two, scale_two, row(8))
    low_two = grad_sum_two.astype(LOW)
    rows_ref[7:8, :] = column_sum(low_two.astype(WIDE))
    down[here] = low_two
    ring.gather(down, 4)
    group_down = down[...].reshape(group, D)
    grad_active = mm(group_down, ffn[1], NN)
    grad_before = (grad_active * slope).astype(LOW)
    grad_one[...] = mm(grad_before, ffn[0], NT).astype(grad_one.dtype).reshape(mp, slots, D)

    def up_part():
        grad_ffn_ref[0] = mm(group_one, grad_before, TN).astype(LOW)
        bias_out[...] = column_sum(grad_before.astype(WIDE))

    def down_part():
        grad_ffn_ref[1] = mm(group_down, active, TN).astype(LOW)

    ring.reduce_begin(grad_one, got_one, 5)
    ring.reduce_rest(grad_one, got_one, 5, [up_part, down_part])
    grad = grad_sum_two + grad_one[here].astype(WIDE)
    rows_ref[5:6, :] = column_sum(grad * plain_one)
    rows_ref[6:7, :] = column_sum(grad)
    grad = norm_back(grad, plain_one, scale_one, row(5))
    low = grad.astype(LOW)
    rows_ref[4:5, :] = column_sum(low.astype(WIDE))
    grad_zero_ref[...] = grad
    grad_mixed_ref[...] = mm(low, out_weight[...], NT).astype(LOW)
    grad_out_ref[...] = mm(mixed_ref[...], low, TN).astype(LOW)
    for index in list(range(4)) + list(range(10, 16)):
        rows_ref[index : index + 1, :] = jnp.zeros((1, D), WIDE)
    ring.finish()
    for made in stat_copies:
        made.wait_send()


def head_step(mp, mixed, zero, out_weight, small, bias, ffn, table, label, valid):
    slots, hidden, vocab = mixed.shape[0], ffn.shape[2], table.shape[0]
    group = slots * mp
    wide_group = pad_up(group, LANES)
    vmem = pl.BlockSpec(memory_space=pltpu.VMEM)
    anywhere = pl.BlockSpec(memory_space=pl.ANY)
    dma = pltpu.SemaphoreType.DMA
    exchanged = [pltpu.VMEM((mp, slots, D), LOW)] * 6
    got = [pltpu.VMEM((mp - 1, slots, D), LOW)] * 3

    def body(*refs):
        head_kernel(mp, refs)

    return pl.pallas_call(
        body,
        out_shape=(
            jax.ShapeDtypeStruct((slots, D), WIDE),
            jax.ShapeDtypeStruct((slots, D), LOW),
            jax.ShapeDtypeStruct((D, D), LOW),
            jax.ShapeDtypeStruct((2, D, hidden), LOW),
            jax.ShapeDtypeStruct((vocab, D), LOW),
            jax.ShapeDtypeStruct((16, D), WIDE),
            jax.ShapeDtypeStruct((1, hidden), WIDE),
            jax.ShapeDtypeStruct((8, LANES), WIDE),
        ),
        in_specs=[vmem] * 5 + [anywhere] * 2 + [vmem] * 2,
        out_specs=(vmem,) * 8,
        scratch_shapes=[
            pltpu.VMEM((2, D, hidden), LOW),
            pltpu.VMEM((vocab, D), LOW),
            *exchanged,
            *got,
            pltpu.VMEM((vocab, group), WIDE),
            pltpu.VMEM((vocab, group), LOW),
            pltpu.VMEM((mp, 8, wide_group), WIDE),
            dma((2,)),
            dma((6, 2, mp - 1)),
            dma((6, 2, mp - 1)),
            dma((mp,)),
            dma((mp,)),
        ],
        compiler_params=pltpu.CompilerParams(
            collective_id=3, has_side_effects=True, vmem_limit_bytes=56 * 2**20
        ),
        name="head_step",
    )(mixed, zero, out_weight, small, bias, ffn, table, label, valid)


def gather_kernel(plan, table_rows, refs):
    (
        word_in, proj_in, boxes_in, places_in, visual_in, small_in, ffn_in, tokens_ref,
        table_out, proj_out, boxes_out, places_out, visual_out, small_out, ffn_out, word_out,
        table_buf, shared_buf, ffn_buf, sums, got, acc,
        out_sem, send_sem, recv_sem, ring_send, ring_recv,
    ) = refs
    dp, mp = plan.dp, plan.mp
    me = lax.axis_index("dp")
    ring = Ring(mp, (ring_send, ring_recv))
    here = ring.here
    depth = bits_of(dp)
    rows = word_in.shape[0]
    table_buf[me, 0:rows, :] = word_in[...].astype(LOW)
    barrier = pltpu.get_barrier_semaphore()
    for other in range(1, dp):
        pl.semaphore_signal(
            barrier, 1, device_id={"dp": lax.rem(me + other, dp)}, device_id_type=MESH
        )
    for other in range(1, mp):
        pl.semaphore_signal(
            barrier, 1, device_id={"mp": lax.rem(here + other, mp)}, device_id_type=MESH
        )
    pl.semaphore_wait(barrier, dp + mp - 2)

    half = table_rows // 2
    pieces = (
        (table_buf, 0, half),
        (table_buf, half, half),
        (shared_buf, plan.places_at, plan.shared - plan.places_at),
        (shared_buf, 0, plan.places_at),
        (ffn_buf, 0, ffn_buf.shape[1]),
    )
    orders = (list(range(1, depth)) + [0], list(range(depth - 1, -1, -1)))
    started = []

    def part_of(piece, stream, slot):
        buffer, first, count = pieces[piece]
        return buffer.at[slot, pl.ds(first, count), lanes_of(stream)]

    def copy(piece, stream, step, place, slot):
        part = part_of(piece, stream, slot)
        index = 2**step - 1 + place
        return pltpu.make_async_remote_copy(
            src_ref=part, dst_ref=part,
            send_sem=send_sem.at[piece, stream, index],
            recv_sem=recv_sem.at[piece, stream, index],
            device_id={"dp": flip(me, orders[stream][step])},
            device_id_type=MESH,
        )

    def start(piece, step):
        for stream in range(2):
            for place, slot in enumerate(combos(me, orders[stream][:step])):
                made = copy(piece, stream, step, place, slot)
                made.start()
                started.append(made)

    def wait(piece, step):
        for stream in range(2):
            peer = flip(me, orders[stream][step])
            for place, slot in enumerate(combos(peer, orders[stream][:step])):
                copy(piece, stream, step, place, slot).wait_recv()

    outs = []

    def put(source, target):
        made = pltpu.make_async_copy(source, target, out_sem.at[len(outs)])
        made.start()
        outs.append(made)

    start(0, 0)
    start(1, 0)

    def cast(target, first, source):
        count = source.shape[0]
        target[me, first : first + count, : source.shape[1]] = source.astype(LOW)

    for part in range(4):
        cast(shared_buf, part * plan.proj, proj_in[part])
    cast(shared_buf, plan.places_at, places_in[...])
    cast(shared_buf, plan.visual_at, visual_in[...])
    pieces_box = plan.box // 32
    for part in range(plan.box_parts):
        row, lane = plan.box_slot(part)
        first = 32 * (part % pieces_box)
        shared_buf[me, row : row + 32, lane : lane + LANES] = boxes_in[
            part // pieces_box, first : first + 32, :
        ].astype(LOW)
    row, lane = plan.box_slot(plan.box_parts)
    shared_buf[me, row : row + 32, lane : lane + LANES] = small_in[...].astype(LOW)
    for part in range(plan.box_parts + 1, 6 * (plan.shared - plan.box_at) // 32):
        spare_row, spare_lane = plan.box_slot(part)
        shared_buf[me, spare_row : spare_row + 32, spare_lane : spare_lane + LANES] = jnp.zeros(
            (32, LANES), LOW
        )
    ffn_rows = ffn_out.shape[2]
    wide = ffn_in.shape[2]
    for part in range(2):
        at, shift = ffn_slot(part, 0, ffn_rows, wide)
        ffn_buf[me, at : at + ffn_in.shape[1], shift : shift + wide] = ffn_in[part].astype(LOW)

    for step in range(depth):
        for piece in range(2):
            wait(piece, step)
            if step < depth - 1:
                start(piece, step + 1)
        if step == depth - 2:
            start(2, 0)
    put(table_buf, table_out)

    vocab = rows * dp

    def lookup(slot):
        ids = tokens_ref[slot] - here * vocab

        def body(index, carry):
            local = ids - index * rows
            local = jnp.where(local < rows, local, -1)
            place = lax.broadcasted_iota(jnp.int32, (TEXT, table_rows), 1)
            hot = jnp.where(place == local, 1.0, 0.0).astype(LOW)
            found = mm(hot, table_buf[index], NN)

            @pl.when(index == 0)
            def _():
                acc[...] = found

            @pl.when(index > 0)
            def _():
                acc[...] = acc[...] + found

            return carry

        lax.fori_loop(0, dp, body, 0)
        sums[slot] = acc[...].astype(LOW)

    events = []
    for piece, ahead in ((2, 3), (3, 4), (4, None)):
        for step in range(depth):
            events.append((piece, step, ahead if step == depth - 2 else None))

    def advance():
        if not events:
            return
        piece, step, ahead = events.pop(0)
        wait(piece, step)
        if step < depth - 1:
            start(piece, step + 1)
        if ahead is not None:
            start(ahead, 0)

    masks = sorted(range(mp), key=lambda mask: -bin(mask).count("1"))
    for mask in masks:
        slot = here
        for bit in range(ring.depth):
            if mask >> bit & 1:
                slot = flip(slot, bit)
        lookup(slot)
        for stream in range(2):
            order = ring.orders[stream]
            if mask >> order[0] & 1:
                place = sum((mask >> bit & 1) << t for t, bit in enumerate(order[1:]))
                ring.reduce_one(sums, got, 0, stream, 0, place)
        if mask != masks[-1]:
            advance()
    while len(events) > 2:
        advance()
    for step in range(ring.depth):
        for stream in range(2):
            ring.reduce_wait(sums, got, 0, stream, step)
            if step < ring.depth - 1:
                ring.reduce_start(sums, got, 0, stream, step + 1)
        advance()
    word_out[...] = sums[here]
    while events:
        advance()
    for part in range(4):
        put(shared_buf.at[:, pl.ds(part * plan.proj, plan.proj)], proj_out.at[part])
    put(shared_buf.at[:, pl.ds(plan.places_at, plan.places)], places_out)
    put(shared_buf.at[:, pl.ds(plan.visual_at, plan.visual)], visual_out)
    for part in range(plan.box_parts):
        at, shift = plan.box_slot(part)
        put(
            shared_buf.at[:, pl.ds(at, 32), pl.ds(shift, LANES)],
            boxes_out.at[part // pieces_box, :, pl.ds(32 * (part % pieces_box), 32)],
        )
    put(shared_buf.at[:, pl.ds(row, 32), pl.ds(lane, LANES)], small_out)
    for part in range(2):
        at, shift = ffn_slot(part, 0, ffn_rows, wide)
        put(ffn_buf.at[:, pl.ds(at, ffn_rows), pl.ds(shift, wide)], ffn_out.at[part])
    for made in started:
        made.wait_send()
    ring.finish()
    for made in outs:
        made.wait()


def gather_weights(plan, word, proj, boxes, places, visual, small, ffn, tokens):
    dp, mp = plan.dp, plan.mp
    table_rows, ffn_rows, wide = pad_up(word.shape[0], 32), pad_up(ffn.shape[1], 16), ffn.shape[2]
    ffn_all = 2 * ffn_rows * wide // D
    depth = bits_of(dp)
    anywhere = pl.BlockSpec(memory_space=pl.ANY)
    vmem = pl.BlockSpec(memory_space=pltpu.VMEM)
    dma = pltpu.SemaphoreType.DMA
    shape = jax.ShapeDtypeStruct

    def body(*refs):
        gather_kernel(plan, table_rows, refs)

    return pl.pallas_call(
        body,
        out_shape=(
            shape((dp, table_rows, D), LOW), shape((4, dp, plan.proj, D), LOW),
            shape((4, dp, plan.box, LANES), LOW), shape((dp, plan.places, D), LOW),
            shape((dp, plan.visual, D), LOW), shape((dp, 32, LANES), LOW),
            shape((2, dp, ffn_rows, wide), LOW), shape((TEXT, D), LOW),
        ),
        in_specs=[vmem] * 8,
        out_specs=(anywhere,) * 7 + (vmem,),
        scratch_shapes=[
            pltpu.VMEM((dp, table_rows, D), LOW),
            pltpu.VMEM((dp, plan.shared, D), LOW),
            pltpu.VMEM((dp, ffn_all, D), LOW),
            pltpu.VMEM((mp, TEXT, D), LOW),
            pltpu.VMEM((mp - 1, TEXT, D), LOW),
            pltpu.VMEM((TEXT, D), WIDE),
            dma((plan.box_parts + 10,)),
            dma((5, 2, dp - 1)),
            dma((5, 2, dp - 1)),
            dma((1, 2, mp - 1)),
            dma((1, 2, mp - 1)),
        ],
        compiler_params=pltpu.CompilerParams(
            collective_id=1, has_side_effects=True, vmem_limit_bytes=56 * 2**20
        ),
        name="gather_weights",
    )(word, proj, boxes, places, visual, small, ffn, tokens)


ROWS = 576
KINDS = ((6, 3), (0, 4), (3, 4))


def token_info(text_box, segments, alive_text):
    boxes = jnp.concatenate([text_box, grid_boxes()], 0)
    visual = GRID * GRID
    places = jnp.concatenate([jnp.arange(TEXT), jnp.arange(visual)]).astype(jnp.int32)
    owner = jnp.concatenate([segments, jnp.full((visual,), -1, jnp.int32)])
    alive = jnp.concatenate([alive_text, jnp.ones((visual,), jnp.int32)])
    columns = [
        boxes[:, 0], boxes[:, 1], boxes[:, 2], boxes[:, 3], boxes[:, 3] - boxes[:, 1],
        boxes[:, 2] - boxes[:, 0], places, owner, alive,
    ]
    rows = jnp.stack(columns + [jnp.zeros_like(places)] * 7)
    return jnp.pad(rows, ((0, 0), (0, ROWS - TEXT - visual)))


def edge_rows(rel_low):
    table = jnp.transpose(rel_low.reshape(3, NB, H), (0, 2, 1)).astype(WIDE)
    rows = jnp.pad(table, ((0, 0), (0, 0), (NB // 2, NB // 2)), mode="edge")
    return jnp.pad(rows.reshape(3 * H, 2 * NB), ((0, 4), (0, 0)))


def edge_rows_back(grad):
    grad = grad[: 3 * H].reshape(3, H, 2 * NB)
    half = NB // 2
    low = jnp.sum(grad[..., : half + 1], -1, keepdims=True)
    high = jnp.sum(grad[..., 3 * half - 1 :], -1, keepdims=True)
    table = jnp.concatenate([low, grad[..., half + 1 : 3 * half - 1], high], -1)
    return jnp.transpose(table, (0, 2, 1)).reshape(3 * NB * H)


def key_hot(rows_ref, kind):
    column, shift = KINDS[kind]
    coarse_row = jnp.right_shift(rows_ref[column : column + 1, :], shift)
    place = lax.broadcasted_iota(jnp.int32, (2 * NB, ROWS), 0)
    first = jnp.where(place == coarse_row, 1.0, 0.0).astype(LOW)
    second = jnp.where(place == coarse_row + NB, 1.0, 0.0).astype(LOW)
    return first, second


def below_of(rows_ref, slot_ref, kind):
    column, shift = KINDS[kind]
    mask = 2**shift - 1
    rest_key = jnp.bitwise_and(rows_ref[column : column + 1, :], mask)
    rest_slot = jnp.bitwise_and(slot_ref[:, column : column + 1], mask)
    return rest_key < rest_slot


def take_slots(slots, pos_ref, pairs):
    def body(index, carry):
        at = pos_ref[index]
        for source, target in pairs:
            target[pl.ds(index, 1), :] = source[pl.ds(at, 1), :]
        return carry

    lax.fori_loop(0, slots, body, 0)


def half_mask(rows):
    slots = rows // 2
    row = lax.broadcasted_iota(jnp.int32, (rows, LANES), 0)
    lane = lax.broadcasted_iota(jnp.int32, (rows, LANES), 1)
    return (row < slots) == (lane < HD)


def pair_rows(value):
    both = jnp.concatenate([value, value], 0)
    return jnp.where(half_mask(both.shape[0]), both, jnp.zeros((), both.dtype))


def pair_lanes(value):
    slots = value.shape[0] // 2
    lane = lax.broadcasted_iota(jnp.int32, (slots, LANES), 1)
    return jnp.where(lane < HD, value[:slots], value[slots:])


def front_kernel(
    pos_ref, word_ref, features_ref, places_ref, boxes_ref, visual_ref, small_ref, edges_ref,
    columns_ref, rows_ref, weights_ref,
    mixed_ref, zero_ref, zero_low_ref, low_ref, plain_ref, scale_ref, query_ref, key_ref,
    value_ref, shares_ref,
    normed_ref, slot_ref, bias_ref, spread_ref, stacked_ref,
):
    slots = mixed_ref.shape[0]
    row = lambda index: small_ref[index : index + 1, :]
    tile = 96
    lookups = (0, 1, 0, 1, 2, 3)

    normed_ref[0:TEXT, :] = word_ref[...].astype(WIDE) + places_ref[...].astype(WIDE)
    normed_ref[TEXT:ROWS, :] = mm(features_ref[...], visual_ref[...], NN) + places_ref[
        0 : ROWS - TEXT, :
    ].astype(WIDE)

    def embed(index, carry):
        where = pl.ds(pl.multiple_of(index * tile, 16), tile)
        place = lax.broadcasted_iota(jnp.int32, (tile, NBOX), 1)
        found = []
        for column, table in enumerate(lookups):
            hot = jnp.where(place == columns_ref[where, column : column + 1], 1.0, 0.0).astype(LOW)
            found.append(mm(hot, boxes_ref[table], NN))
        embedded = normed_ref[where, :] + jnp.concatenate(found, -1)
        plain, scale = norm_rows(embedded)
        normed = plain * row(0) + row(1)
        plain_ref[where, :] = plain
        scale_ref[where, :] = scale
        normed_ref[where, :] = normed
        low_ref[where, :] = normed.astype(LOW)
        return carry

    lax.fori_loop(0, ROWS // tile, embed, 0)
    take_slots(slots, pos_ref, ((normed_ref, zero_ref), (columns_ref, slot_ref)))
    low = low_ref[...]
    zero_low = zero_ref[...].astype(LOW)
    zero_low_ref[...] = zero_low
    query_ref[...] = (mm(zero_low, weights_ref[0], NN) + row(2)).astype(LOW)
    key_ref[...] = mm(low, weights_ref[1], NN).astype(LOW)
    value_ref[...] = (mm(low, weights_ref[2], NN) + row(3)).astype(LOW)

    lane = lax.broadcasted_iota(jnp.int32, (NB, LANES), 1)
    for kind in range(3):
        column, shift = KINDS[kind]
        for head in range(H):
            edge = jnp.broadcast_to(edges_ref[kind * H + head : kind * H + head + 1, :], (NB, LANES))
            near = pltpu.roll(edge, NB, 1, stride=1, stride_axis=0)
            far = pltpu.roll(edge, 1, 1, stride=1, stride_axis=0)
            spread_ref[:, head * LANES : (head + 1) * LANES] = jnp.where(
                lane < NB, near, far
            ).astype(LOW)
        coarse_slot = jnp.right_shift(slot_ref[:, column : column + 1], shift)
        place = lax.broadcasted_iota(jnp.int32, (slots, NB), 1)
        hot = jnp.where(place == coarse_slot, 1.0, 0.0).astype(LOW)
        wide = mm(hot, spread_ref[...], NN).astype(LOW)
        for head in range(H):
            stacked_ref[head * slots : (head + 1) * slots, :] = wide[
                :, head * LANES : (head + 1) * LANES
            ]
        first, second = key_hot(rows_ref, kind)
        below = below_of(rows_ref, slot_ref, kind)

        def add(head, carry):
            where = pl.ds(pl.multiple_of(head * 2 * slots, 16), 2 * slots)
            rows = stacked_ref[where, :]
            both = jnp.concatenate([below, below], 0)
            found = jnp.where(both, mm(rows, second, NN), mm(rows, first, NN))
            bias_ref[where, :] = found if kind == 0 else bias_ref[where, :] + found
            return carry

        lax.fori_loop(0, H // 2, add, 0)

    owner = rows_ref[7:8, :]
    allowed = ((slot_ref[:, 7:8] == owner) | (owner < 0)) & (rows_ref[8:9, :] > 0)
    allowed = jnp.concatenate([allowed, allowed], 0)
    for pair in range(H // 2):
        lanes = slice(pair * LANES, (pair + 1) * LANES)
        rows = slice(pair * 2 * slots, (pair + 1) * 2 * slots)
        scores = mm(pair_rows(query_ref[:, lanes]), key_ref[:, lanes], NT) * 0.125
        scores = jnp.where(allowed, scores + bias_ref[rows, :], MASKED)
        powers = jnp.exp(scores - jnp.max(scores, -1, keepdims=True))
        shares = powers / jnp.sum(powers, -1, keepdims=True)
        shares_ref[rows, :] = shares
        mixed_ref[:, lanes] = pair_lanes(mm(shares.astype(LOW), value_ref[:, lanes], NN)).astype(LOW)


def front_step(pos, word, features, places, boxes, visual, small, edges, columns, rows, weights):
    slots = pos.shape[0]
    vmem = pl.BlockSpec(memory_space=pltpu.VMEM)
    shape = jax.ShapeDtypeStruct
    return pl.pallas_call(
        front_kernel,
        out_shape=(
            shape((slots, D), LOW), shape((slots, D), WIDE), shape((slots, D), LOW),
            shape((ROWS, D), LOW), shape((ROWS, D), WIDE), shape((ROWS, 1), WIDE),
            shape((slots, D), LOW), shape((ROWS, D), LOW), shape((ROWS, D), LOW),
            shape((H * slots, ROWS), WIDE),
        ),
        in_specs=[pl.BlockSpec(memory_space=pltpu.SMEM)] + [vmem] * 10,
        out_specs=(vmem,) * 10,
        scratch_shapes=[
            pltpu.VMEM((ROWS, D), WIDE),
            pltpu.VMEM((slots, 16), jnp.int32),
            pltpu.VMEM((H * slots, ROWS), WIDE),
            pltpu.VMEM((NB, H * LANES), LOW),
            pltpu.VMEM((H * slots, LANES), LOW),
        ],
        compiler_params=pltpu.CompilerParams(vmem_limit_bytes=56 * 2**20),
        name="front_step",
    )(pos, word, features, places, boxes, visual, small, edges, columns, rows, weights)


def back_kernel(
    pos_ref, grad_zero_ref, grad_mixed_ref, shares_ref, query_ref, key_ref, value_ref,
    zero_low_ref, low_ref, plain_ref, scale_ref, features_ref, small_ref, columns_ref, rows_ref,
    weights_ref,
    word_out, places_out, boxes_out, visual_out, weights_out, edges_out, sums_out,
    slot_ref, score_ref, grad_query, grad_key, grad_value, grad_rows, turned_ref, grad_slot,
):
    slots = grad_zero_ref.shape[0]
    take_slots(slots, pos_ref, ((columns_ref, slot_ref),))
    for pair in range(H // 2):
        lanes = slice(pair * LANES, (pair + 1) * LANES)
        rows = slice(pair * 2 * slots, (pair + 1) * 2 * slots)
        grad_mixed = pair_rows(grad_mixed_ref[:, lanes])
        shares = shares_ref[rows, :]
        grad_value[:, lanes] = mm(shares.astype(LOW), grad_mixed, TN).astype(LOW)
        grad_shares = mm(grad_mixed, value_ref[:, lanes], NT)
        scores = shares * (grad_shares - jnp.sum(shares * grad_shares, -1, keepdims=True))
        scores = scores.astype(LOW)
        score_ref[rows, :] = scores
        grad_query[:, lanes] = pair_lanes(mm(scores, key_ref[:, lanes], NN) * 0.125).astype(LOW)
        grad_key[:, lanes] = (mm(scores, pair_rows(query_ref[:, lanes]), TN) * 0.125).astype(LOW)

    lane = lax.broadcasted_iota(jnp.int32, (NB, LANES), 1)
    for kind in range(3):
        column, shift = KINDS[kind]
        first, second = key_hot(rows_ref, kind)
        below = below_of(rows_ref, slot_ref, kind)
        coarse_slot = jnp.right_shift(slot_ref[:, column : column + 1], shift)
        place = lax.broadcasted_iota(jnp.int32, (slots, NB), 1)
        hot = jnp.where(place == NB - 1 - coarse_slot, 1.0, 0.0).astype(LOW)

        def collect(pair, carry):
            where = pl.ds(pl.multiple_of(pair * 2 * slots, 16), 2 * slots)
            both = jnp.concatenate([below, below], 0)
            scores = score_ref[where, :]
            none = jnp.zeros((), LOW)
            found = mm(jnp.where(both, none, scores), first, NT) + mm(
                jnp.where(both, scores, none), second, NT
            )
            turned_ref[where, :] = found.astype(LOW)
            return carry

        lax.fori_loop(0, H // 2, collect, 0)
        for head in range(H):
            part = mm(hot, turned_ref[head * slots : (head + 1) * slots, :], TN)
            near = pltpu.roll(jnp.where(lane < NB, part, 0.0), 1, 1, stride=1, stride_axis=0)
            far = pltpu.roll(jnp.where(lane < NB, 0.0, part), NB, 1, stride=1, stride_axis=0)
            edges_out[kind * H + head : kind * H + head + 1, :] = column_sum(near + far)
    edges_out[3 * H :, :] = jnp.zeros((4, LANES), WIDE)

    low = low_ref[...]
    weights_out[0] = mm(zero_low_ref[...], grad_query[...], TN).astype(LOW)
    weights_out[1] = mm(low, grad_key[...], TN).astype(LOW)
    weights_out[2] = mm(low, grad_value[...], TN).astype(LOW)
    sums_out[2:3, :] = column_sum(grad_query[...].astype(WIDE))
    sums_out[3:4, :] = column_sum(grad_value[...].astype(WIDE))
    sums_out[4:8, :] = jnp.zeros((4, D), WIDE)
    grad_rows[...] = mm(grad_key[...], weights_ref[1], NT) + mm(grad_value[...], weights_ref[2], NT)
    grad_slot[...] = grad_zero_ref[...] + mm(grad_query[...], weights_ref[0], NT)

    def put(index, carry):
        at = pl.ds(pos_ref[index], 1)
        grad_rows[at, :] = grad_rows[at, :] + grad_slot[pl.ds(index, 1), :]
        return carry

    lax.fori_loop(0, slots, put, 0)
    gain = small_ref[0:1, :]
    tile = 96

    def normed_back(index, carry):
        where = pl.ds(pl.multiple_of(index * tile, 16), tile)
        grad, plain = grad_rows[where, :], plain_ref[where, :]
        grad_rows[where, :] = norm_back(grad, plain, scale_ref[where, :], gain)
        return carry[0] + column_sum(grad * plain), carry[1] + column_sum(grad)

    blank = jnp.zeros((1, D), WIDE)
    gains, shifts = lax.fori_loop(0, ROWS // tile, normed_back, (blank, blank))
    sums_out[0:1, :] = gains
    sums_out[1:2, :] = shifts
    grad_low = grad_rows[...].astype(LOW)
    word_out[...] = grad_low[0:TEXT, :]
    extra = ROWS - TEXT
    places_out[...] = grad_rows[0:TEXT, :].astype(LOW)
    places_out[0:extra, :] = (grad_rows[0:extra, :] + grad_rows[TEXT:ROWS, :]).astype(LOW)
    visual_out[...] = mm(features_ref[...], grad_low[TEXT:ROWS, :], TN).astype(LOW)
    block = 256

    def table(index, carry):
        where = pl.ds(pl.multiple_of(index * block, 16), block)
        place = lax.broadcasted_iota(jnp.int32, (block, ROWS), 0) + index * block
        found = []
        for column in range(6):
            hot = jnp.where(place == rows_ref[column : column + 1, :], 1.0, 0.0).astype(LOW)
            found.append(mm(hot, grad_low[:, column * LANES : (column + 1) * LANES], NN))
        boxes_out[0, where, :] = (found[0] + found[2]).astype(LOW)
        boxes_out[1, where, :] = (found[1] + found[3]).astype(LOW)
        boxes_out[2, where, :] = found[4].astype(LOW)
        boxes_out[3, where, :] = found[5].astype(LOW)
        return carry

    lax.fori_loop(0, NBOX // block, table, 0)


def back_step(
    pos, grad_zero, grad_mixed, shares, query, key, value, zero_low, low, plain, scale, features,
    small, columns, rows, weights,
):
    slots = pos.shape[0]
    vmem = pl.BlockSpec(memory_space=pltpu.VMEM)
    shape = jax.ShapeDtypeStruct
    return pl.pallas_call(
        back_kernel,
        out_shape=(
            shape((TEXT, D), LOW), shape((TEXT, D), LOW), shape((4, NBOX, LANES), LOW),
            shape((VCH, D), LOW), shape((3, D, D), LOW), shape((3 * H + 4, LANES), WIDE),
            shape((8, D), WIDE),
        ),
        in_specs=[pl.BlockSpec(memory_space=pltpu.SMEM)] + [vmem] * 15,
        out_specs=(vmem,) * 7,
        scratch_shapes=[
            pltpu.VMEM((slots, 16), jnp.int32),
            pltpu.VMEM((H * slots, ROWS), LOW),
            pltpu.VMEM((slots, D), LOW),
            pltpu.VMEM((ROWS, D), LOW),
            pltpu.VMEM((ROWS, D), LOW),
            pltpu.VMEM((ROWS, D), WIDE),
            pltpu.VMEM((H * slots, LANES), LOW),
            pltpu.VMEM((slots, D), WIDE),
        ],
        compiler_params=pltpu.CompilerParams(vmem_limit_bytes=56 * 2**20),
        name="back_step",
    )(
        pos, grad_zero, grad_mixed, shares, query, key, value, zero_low, low, plain, scale,
        features, small, columns, rows, weights,
    )


def on_device(
    tokens, text_box, segments, alive_text, features, mask_pos, mask_label, mask_valid, *states
):
    (projections, box_tables, position_table, visual_proj, small_params, word_table, feedforward) = (
        states[::3]
    )
    dp, mp = lax.axis_size("dp"), lax.axis_size("mp")
    plan = Plan(dp, mp)

    cut = small_params.shape[1]
    (
        table_parts, proj_parts, box_parts, place_parts, visual_parts, small_parts, ffn_parts, word,
    ) = gather_weights(
        plan, word_table, projections, box_tables, position_table, visual_proj,
        jnp.pad(small_params, ((0, 32 - VROWS), (0, LANES - cut))), feedforward, tokens[..., None],
    )

    def joined(parts, rows):
        parts = parts[..., :rows, :]
        return parts.reshape(parts.shape[:-3] + (dp * rows, parts.shape[-1]))

    work_table = joined(table_parts, word_table.shape[0])
    work_proj = joined(proj_parts, D // dp)
    work_boxes = joined(box_parts, NBOX // dp)
    work_places = joined(place_parts, TEXT // dp)
    work_visual = joined(visual_parts, VCH // dp)
    work_ffn = joined(ffn_parts, D // dp)
    work_small = jnp.transpose(small_parts[:, :VROWS, :cut], (1, 0, 2)).reshape(VROWS, D)
    model_index = lax.axis_index("mp")
    vocab_shard, hidden_shard = work_table.shape[0], work_ffn.shape[2]
    small_float = work_small.astype(WIDE)
    info = token_info(text_box[0], segments[0], alive_text[0])
    columns = info.T
    visual_rows = jnp.pad(features, ((0, ROWS - TEXT - features.shape[0]), (0, 0)))
    edges = edge_rows(work_small[10 + FF // D : 13 + FF // D].reshape(3 * NB, H))
    (
        mixed, slot_zero, slot_low, normed_low, plain, scale, queries, keys, values, shares,
    ) = front_step(
        mask_pos, word, visual_rows, work_places, work_boxes, work_visual, small_float, edges,
        columns, info, work_proj[:3],
    )
    ffn_bias_full = small_float[10 : 10 + FF // D].reshape(1, -1)
    ffn_bias = lax.dynamic_slice_in_dim(ffn_bias_full, model_index * hidden_shard, hidden_shard, 1)
    (
        grad_slot, grad_mixed, grad_out_weight, grad_ffn, grad_table, head_rows, grad_ffn_bias,
        own_tile,
    ) = head_step(
        mp, mixed, slot_zero, work_proj[3], small_float, ffn_bias, work_ffn, work_table,
        mask_label[None, :], mask_valid[None, :],
    )
    grad_word, grad_places, grad_boxes, grad_visual, grad_in_weight, grad_edges, front_rows = (
        back_step(
            mask_pos, grad_slot, grad_mixed, shares, queries, keys, values, slot_low, normed_low,
            plain, scale, visual_rows, small_float, columns, info, work_proj[:3],
        )
    )
    bias_full = lax.dynamic_update_slice_in_dim(
        jnp.zeros((FF,), WIDE), grad_ffn_bias[0], model_index * hidden_shard, 0
    ).reshape(FF // D, D)
    grad_small = jnp.concatenate(
        [front_rows[:4], head_rows[4:10], bias_full, edge_rows_back(grad_edges).reshape(3, D)], 0
    )
    def split_rows(part):
        rows = part.shape[-2] // dp
        part = part.astype(LOW).reshape(part.shape[:-2] + (dp, rows, part.shape[-1]))
        extra = [(0, 0)] * (part.ndim - 2) + [(0, pad_up(rows, 16) - rows), (0, 0)]
        return jnp.pad(part, extra) if extra[-2][1] else part

    small_split = jnp.transpose(grad_small.reshape(VROWS, dp, cut), (1, 0, 2)).astype(LOW)
    small_split = jnp.pad(small_split, ((0, 0), (0, 32 - VROWS), (0, LANES - cut)))
    table_split, ffn_split = split_rows(grad_table), split_rows(grad_ffn)
    shared_sum, split_sum, totals = reduce_gradients(
        plan,
        word_table.shape[0],
        table_split,
        split_rows(grad_in_weight),
        split_rows(grad_out_weight),
        ffn_split,
        split_rows(grad_places),
        split_rows(grad_visual),
        grad_boxes.reshape(4, dp, NBOX // dp, LANES),
        small_split,
        own_tile,
        grad_word,
        tokens.reshape(1, -1),
    )
    loss_sum, loss_count = (totals[1, 0, 0], totals[1, 1, 0])
    grad_norm = jnp.sqrt(jnp.sum(totals[0])) / loss_count
    outputs = adam_update(
        plan, table_split.shape[1], ffn_split.shape[2], shared_sum, split_sum, totals, states
    )
    return tuple(outputs) + (loss_sum, loss_count, grad_norm)


def solution(mesh):
    in_specs = (
        P("dp", None),
        P(("dp", "mp"), None, None),
        P(("dp", "mp"), None),
        P(("dp", "mp"), None),
        P(("dp", "mp"), None),
        P(("dp", "mp")),
        P("dp"),
        P("dp"),
        P(None, "dp", None),
        P(None, "dp", None),
        P(None, "dp", None),
        P(None, "dp", None),
        P(None, "dp", None),
        P(None, "dp", None),
        P("dp", None),
        P("dp", None),
        P("dp", None),
        P("dp", None),
        P("dp", None),
        P("dp", None),
        P(None, "dp"),
        P(None, "dp"),
        P(None, "dp"),
        P(("mp", "dp"), None),
        P(("mp", "dp"), None),
        P(("mp", "dp"), None),
        P(None, "dp", "mp"),
        P(None, "dp", "mp"),
        P(None, "dp", "mp"),
    )
    out_specs = (
        P(None, "dp", None),
        P(None, "dp", None),
        P(None, "dp", None),
        P(None, "dp", None),
        P(None, "dp", None),
        P(None, "dp", None),
        P("dp", None),
        P("dp", None),
        P("dp", None),
        P("dp", None),
        P("dp", None),
        P("dp", None),
        P(None, "dp"),
        P(None, "dp"),
        P(None, "dp"),
        P(("mp", "dp"), None),
        P(("mp", "dp"), None),
        P(("mp", "dp"), None),
        P(None, "dp", "mp"),
        P(None, "dp", "mp"),
        P(None, "dp", "mp"),
        P(),
        P(),
        P(),
    )
    return jax.shard_map(
        on_device, mesh=mesh, in_specs=in_specs, out_specs=out_specs, check_vma=False
    )
```

```python
import jax
import jax.numpy as jnp
from jax import lax
from jax.experimental import pallas as pl
from jax.experimental.pallas import tpu as pltpu
from jax.sharding import PartitionSpec as P

D = 768
H = 12
HD = 64
FF = 3072
NB = 64
GRID = 7
TEXT = 512
STEP = 10
VCH = 256
NBOX = 1024
VROWS = 17


MASKED = -1e30
CLIP = 0.005
BETA_ONE = 0.9
BETA_TWO = 0.999
EPSILON = 1e-08
DECAY = 0.01
RATES = (0.02, 0.03, 0.03, 0.04, 0.3, 0.05, 0.02)


def grid_boxes():
    cells = jnp.arange(GRID * GRID, dtype=jnp.int32)
    row_place = cells // GRID
    column_place = cells % GRID
    return jnp.stack(
        [
            column_place * 1000 // GRID,
            row_place * 1000 // GRID,
            (column_place + 1) * 1000 // GRID,
            (row_place + 1) * 1000 // GRID,
        ],
        -1,
    )


def adam_step(weight, grad, first, second, rate):
    first = BETA_ONE * first + (1.0 - BETA_ONE) * grad
    second = BETA_TWO * second + (1.0 - BETA_TWO) * grad * grad
    fixed_first = first / (1.0 - BETA_ONE**STEP)
    fixed_second = second / (1.0 - BETA_TWO**STEP)
    weight = weight - rate * (fixed_first / (jnp.sqrt(fixed_second) + EPSILON) + DECAY * weight)
    return (weight, first, second)


MESH = pl.DeviceIdType.MESH
LOW = jnp.bfloat16
WIDE = jnp.float32
LANES = 128
HALF = D // 2


def pad_up(count, unit):
    return (count + unit - 1) // unit * unit


def bits_of(count):
    return count.bit_length() - 1


def flip(index, bit):
    return index + (1 - 2 * ((index // 2**bit) % 2)) * 2**bit


class Plan:
    def __init__(self, dp, mp):
        self.dp, self.mp = dp, mp
        self.proj = pad_up(D // dp, 16)
        self.places = pad_up(TEXT // dp, 16)
        self.visual = pad_up(VCH // dp, 16)
        self.box = NBOX // dp
        self.box_parts = 4 * (self.box // 32)
        self.places_at = 4 * self.proj
        self.visual_at = self.places_at + self.places
        self.box_at = self.visual_at + self.visual
        self.box_rows = 32 * ((self.box_parts + 6) // 6)
        self.shared = pad_up(self.box_at + self.box_rows, 32 * mp)

    def box_slot(self, part):
        return self.box_at + 32 * (part // 6), LANES * (part % 6)


def group_of(axis, index):
    return {axis: index}


def lanes_of(stream):
    return pl.ds(stream * HALF, HALF)


def ffn_slot(part, table_rows, ffn_rows, wide):
    return table_rows + part * wide // D * ffn_rows, part * wide % D


def row_tile(rows):
    return next(t for t in (48, 32, 16) if rows % t == 0)


def reduce_kernel(plan, table_rows, ffn_rows, refs):
    (
        table_in, proj_in, out_in, ffn_in, places_in, visual_in, boxes_in, word_in, front_in,
        head_in, bias_in, tile_in, place_in, ids_in,
        shared_out, split_out, tile_out,
        shared_acc, split_acc, shared_got, split_got, ring_got, ring_own, own_words, packed, words, small_all,
        tile_mp, tile_dp,
        load_sem, send_sem, recv_sem, ring_send, ring_recv, word_send, word_recv, tile_send,
        tile_recv,
    ) = refs
    dp, mp = plan.dp, plan.mp
    me, here = lax.axis_index("dp"), lax.axis_index("mp")
    depth, ring_depth = bits_of(dp), bits_of(mp)
    loads = []

    def load(source, target):
        loads.append(pltpu.make_async_copy(source, target, load_sem.at[len(loads)]))
        loads[-1].start()

    load(word_in, own_words)
    for part in range(4):
        source = proj_in.at[part] if part < 3 else out_in
        load(source, shared_acc.at[:, pl.ds(part * plan.proj, plan.proj)])
    load(places_in, shared_acc.at[:, pl.ds(plan.places_at, plan.places)])
    load(visual_in, shared_acc.at[:, pl.ds(plan.visual_at, plan.visual)])
    pieces_box = plan.box // 32
    for part in range(plan.box_parts):
        row, lane = plan.box_slot(part)
        load(
            boxes_in.at[part // pieces_box, :, pl.ds(32 * (part % pieces_box), 32)],
            shared_acc.at[:, pl.ds(row, 32), pl.ds(lane, LANES)],
        )
    first_loads = len(loads)
    for part in range(2):
        wide = ffn_in.shape[3]
        row, lane = ffn_slot(part, table_rows, ffn_rows, wide)
        load(ffn_in.at[part], split_acc.at[:, pl.ds(row, ffn_rows), pl.ds(lane, wide)])
    load(table_in, split_acc.at[:, pl.ds(0, table_rows)])

    barrier = pltpu.get_barrier_semaphore()
    for other in range(1, dp):
        pl.semaphore_signal(
            barrier, 1, device_id={"dp": lax.rem(me + other, dp)}, device_id_type=MESH
        )
    for other in range(1, mp):
        pl.semaphore_signal(
            barrier, 1, device_id={"mp": lax.rem(here + other, mp)}, device_id_type=MESH
        )
    pl.semaphore_wait(barrier, dp + mp - 2)
    hidden = bias_in.shape[1]
    start = here * hidden
    small_all[0:4, :] = front_in[0:4, :]
    small_all[4:10, :] = head_in[4:10, :]
    small_all[10:14, :] = jnp.zeros((4, D), WIDE)
    small_all[
        pl.ds(10 + start // D, 1), pl.ds(pl.multiple_of(lax.rem(start, D), LANES), hidden)
    ] = bias_in[...]
    small_all[14:17, :] = front_in[4:7, :]
    cut = D // dp
    row, lane = plan.box_slot(plan.box_parts)
    shared_acc[:, pl.ds(row, 32), pl.ds(lane, LANES)] = jnp.zeros((dp, 32, LANES), LOW)
    for part in range(dp):
        shared_acc[part, row : row + VROWS, lane : lane + cut] = small_all[
            0:VROWS, part * cut : (part + 1) * cut
        ].astype(LOW)
    for part in range(plan.box_parts + 1, 6 * (plan.shared - plan.box_at) // 32):
        row, lane = plan.box_slot(part)
        shared_acc[:, pl.ds(row, 32), pl.ds(lane, LANES)] = jnp.zeros((dp, 32, LANES), LOW)

    loads[0].wait()
    room = words.shape[1]
    entry = lax.broadcasted_iota(jnp.int32, (mp * room, TEXT), 0)
    hot = jnp.where(entry == place_in[...], 1.0, 0.0).astype(LOW)
    packed[...] = mm(hot, own_words[...], NN).astype(LOW).reshape(mp, room, D)
    word_copies = []
    for other in range(1, mp):
        target = lax.rem(here + other, mp)
        word_copies.append(
            pltpu.make_async_remote_copy(
                src_ref=packed.at[target], dst_ref=words.at[here],
                send_sem=word_send.at[other - 1], recv_sem=word_recv.at[other - 1],
                device_id={"mp": target}, device_id_type=MESH,
            )
        )
        word_copies[-1].start()
    words[here] = packed[here]

    orders = ([0] + list(range(depth - 1, 0, -1)), list(range(depth)))
    half, rest = plan.shared // 2, split_acc.shape[1] - table_rows
    pieces = (
        (shared_acc, shared_got, 0, half),
        (shared_acc, shared_got, half, half),
        (split_acc, split_got, table_rows, rest),
        (split_acc, split_got, 0, table_rows // 2),
        (split_acc, split_got, table_rows // 2, table_rows // 2),
    )

    def chunk(order, step, free, away):
        index = 0
        for place, bit in enumerate(order):
            mine = (me // 2**bit) % 2
            if place < step or (place == step and not away):
                index = index + mine * 2**bit
            elif place == step:
                index = index + (1 - mine) * 2**bit
            else:
                index = index + ((free >> (place - step - 1)) & 1) * 2**bit
        return index

    def slot_base(step):
        return sum(2 ** (depth - 1 - s) for s in range(step))

    def send_one(piece, stream, step, free):
        acc, got, first, rows = pieces[piece]
        order = orders[stream]
        pltpu.make_async_remote_copy(
            src_ref=acc.at[chunk(order, step, free, True), pl.ds(first, rows), lanes_of(stream)],
            dst_ref=got.at[slot_base(step) + free, pl.ds(first, rows), lanes_of(stream)],
            send_sem=send_sem.at[piece, stream, step],
            recv_sem=recv_sem.at[piece, stream, step],
            device_id={"dp": flip(me, order[step])},
            device_id_type=MESH,
        ).start()

    def send(piece, step):
        for stream in range(2):
            for free in range(2 ** (depth - 1 - step)):
                send_one(piece, stream, step, free)

    def wait_bytes(piece, stream, step, sem):
        acc, got, first, rows = pieces[piece]
        count = 2 ** (depth - 1 - step)
        where = got.at[pl.ds(slot_base(step), count), pl.ds(first, rows), lanes_of(stream)]
        pltpu.make_async_copy(where, where, sem.at[piece, stream, step]).wait()

    def add(piece, stream, step):
        acc, got, first, rows = pieces[piece]
        order = orders[stream]
        wait_bytes(piece, stream, step, recv_sem)
        tile = row_tile(rows)
        last = step == depth - 1
        for free in range(2 ** (depth - 1 - step)):
            kept = chunk(order, step, free, False)

            def body(index, carry):
                at = pl.multiple_of(first + index * tile, 16)
                where = pl.ds(at, tile)
                total = acc[kept, where, lanes_of(stream)].astype(WIDE) + got[
                    slot_base(step) + free, where, lanes_of(stream)
                ].astype(WIDE)
                if last and acc is split_acc:
                    split_out[where, lanes_of(stream)] = total
                elif last:
                    ring_own[0, where, lanes_of(stream)] = total.astype(LOW)
                else:
                    acc[kept, where, lanes_of(stream)] = total.astype(LOW)
                return carry

            lax.fori_loop(0, rows // tile, body, 0)

    def advance(piece, step):
        for stream in range(2):
            add(piece, stream, step)
            if step < depth - 1:
                for free in range(2 ** (depth - 2 - step)):
                    send_one(piece, stream, step + 1, free)

    ring_orders = (list(range(ring_depth)), list(range(ring_depth - 1, -1, -1)))

    def ring_copy(piece, stream, step):
        where = pl.ds(piece * half, half)
        return pltpu.make_async_remote_copy(
            src_ref=ring_own.at[step, where, lanes_of(stream)],
            dst_ref=ring_got.at[step, where, lanes_of(stream)],
            send_sem=ring_send.at[piece, stream, step],
            recv_sem=ring_recv.at[piece, stream, step],
            device_id={"mp": flip(here, ring_orders[stream][step])},
            device_id_type=MESH,
        )

    def ring_step(piece, step):
        for stream in range(2):
            ring_copy(piece, stream, step).wait_recv()
            tile = row_tile(half)

            def body(index, carry):
                where = pl.ds(pl.multiple_of(piece * half + index * tile, 16), tile)
                total = ring_own[step, where, lanes_of(stream)].astype(WIDE) + ring_got[
                    step, where, lanes_of(stream)
                ].astype(WIDE)
                if step == ring_depth - 1:
                    shared_out[where, lanes_of(stream)] = total
                else:
                    ring_own[step + 1, where, lanes_of(stream)] = total.astype(LOW)
                return carry

            lax.fori_loop(0, half // tile, body, 0)
            if step < ring_depth - 1:
                ring_copy(piece, stream, step + 1).start()

    def scatter(index):
        local = ids_in[...] - index * table_rows
        entry = lax.broadcasted_iota(jnp.int32, (table_rows, mp * room), 0)
        hot = jnp.where(entry == local, 1.0, 0.0).astype(LOW)
        where = (index, pl.ds(0, table_rows))
        total = split_acc[where].astype(WIDE) + mm(hot, words[...].reshape(mp * room, D), NN)
        split_acc[where] = total.astype(LOW)

    count = 2 ** (depth - 1)
    other_core, own_core = 1 - me % 2, me % 2

    def scatter_other(index, carry):
        scatter(other_core + 2 * index)
        return carry

    def scatter_own(index, carry):
        scatter(own_core + 2 * index)
        return carry

    for copy in loads[1:first_loads]:
        copy.wait()
    send(0, 0)
    send(1, 0)
    for copy in loads[first_loads:]:
        copy.wait()
    advance(0, 0)
    advance(1, 0)
    send(2, 0)
    for other in range(1, mp):
        source = lax.rem(here + mp - other, mp)
        pltpu.make_async_copy(words.at[source], words.at[source], word_recv.at[other - 1]).wait()
    lax.fori_loop(0, count, scatter_other, 0)
    send(3, 0)
    send(4, 0)
    for step in range(1, depth):
        for piece in (0, 1):
            advance(piece, step)
            if step == depth - 1:
                for stream in range(2):
                    ring_copy(piece, stream, 0).start()
        if step == 1:
            lax.fori_loop(0, count, scatter_own, 0)
        if step == depth - 1:
            for later in (2, 3, 4):
                advance(later, 0)
    for step in range(max(depth - 1, ring_depth)):
        if step < depth - 1:
            for piece in (2, 3, 4):
                advance(piece, step + 1)
        if step < ring_depth:
            for piece in (0, 1):
                ring_step(piece, step)

    def squares(ref, rows):
        tile = row_tile(rows)

        def body(index, total):
            values = ref[pl.ds(pl.multiple_of(index * tile, 16), tile), :]
            return total + jnp.sum((values * values).reshape(tile // 8, 8, D), 0)

        total = lax.fori_loop(0, rows // tile, body, jnp.zeros((8, D), WIDE))
        folded = total[:, 0:LANES]
        for part in range(1, D // LANES):
            folded = folded + total[:, part * LANES : (part + 1) * LANES]
        return folded

    folded = squares(shared_out, plan.shared) * (1.0 / mp) + squares(split_out, split_out.shape[0])
    tile_mp[here, 0] = folded
    tile_mp[here, 1] = tile_in[...]

    def exchange(buffer, axis, index, count, base):
        copies = []
        for other in range(1, count):
            copies.append(
                pltpu.make_async_remote_copy(
                    src_ref=buffer.at[index],
                    dst_ref=buffer.at[index],
                    send_sem=tile_send.at[base + other],
                    recv_sem=tile_recv.at[base + other],
                    device_id={axis: lax.rem(index + other, count)},
                    device_id_type=MESH,
                )
            )
        for copy in copies:
            copy.start()
        for other in range(1, count):
            source = lax.rem(index + count - other, count)
            pltpu.make_async_copy(
                buffer.at[source], buffer.at[source], tile_recv.at[base + other]
            ).wait()
        return copies

    pending = exchange(tile_mp, "mp", here, mp, 0)
    total = tile_mp[0]
    for index in range(1, mp):
        total = total + tile_mp[index]
    tile_dp[me] = total
    pending = pending + exchange(tile_dp, "dp", me, dp, mp)
    total = tile_dp[0]
    for index in range(1, dp):
        total = total + tile_dp[index]
    tile_out[...] = total
    for copy in pending:
        copy.wait_send()
    for copy in word_copies:
        copy.wait_send()
    for piece in range(len(pieces)):
        for stream in range(2):
            for step in range(depth):
                wait_bytes(piece, stream, step, send_sem)
    for piece in range(2):
        for stream in range(2):
            for step in range(ring_depth):
                ring_copy(piece, stream, step).wait_send()


def reduce_gradients(
    plan, table, proj, out, ffn, places, visual, boxes, word, front, head, bias, tile,
    place, ids,
):
    dp, mp = plan.dp, plan.mp
    table_rows, ffn_rows = table.shape[1], ffn.shape[2]
    split = table_rows + 2 * ffn_rows * ffn.shape[3] // D
    depth, ring_depth = bits_of(dp), bits_of(mp)
    anywhere = pl.BlockSpec(memory_space=pl.ANY)
    vmem = pl.BlockSpec(memory_space=pltpu.VMEM)
    dma = pltpu.SemaphoreType.DMA

    def body(*refs):
        reduce_kernel(plan, table_rows, ffn_rows, refs)

    return pl.pallas_call(
        body,
        out_shape=(
            jax.ShapeDtypeStruct((plan.shared, D), WIDE),
            jax.ShapeDtypeStruct((split, D), WIDE),
            jax.ShapeDtypeStruct((2, 8, LANES), WIDE),
        ),
        in_specs=[anywhere] * 8 + [vmem] * 6,
        out_specs=(vmem, vmem, vmem),
        scratch_shapes=[
            pltpu.VMEM((dp, plan.shared, D), LOW),
            pltpu.VMEM((dp, split, D), LOW),
            pltpu.VMEM((dp - 1, plan.shared, D), LOW),
            pltpu.VMEM((dp - 1, split, D), LOW),
            pltpu.VMEM((ring_depth, plan.shared, D), LOW),
            pltpu.VMEM((ring_depth, plan.shared, D), LOW),
            pltpu.VMEM((TEXT, D), LOW),
            pltpu.VMEM((mp, word_room(mp), D), LOW),
            pltpu.VMEM((mp, word_room(mp), D), LOW),
            pltpu.VMEM((24, D), WIDE),
            pltpu.VMEM((mp, 2, 8, LANES), WIDE),
            pltpu.VMEM((dp, 2, 8, LANES), WIDE),
            dma((plan.box_parts + 12,)),
            dma((5, 2, depth)),
            dma((5, 2, depth)),
            dma((2, 2, ring_depth)),
            dma((2, 2, ring_depth)),
            dma((mp - 1,)),
            dma((mp - 1,)),
            dma((mp + dp,)),
            dma((mp + dp,)),
        ],
        compiler_params=pltpu.CompilerParams(
            collective_id=5, has_side_effects=True, vmem_limit_bytes=58 * 2**20
        ),
        name="reduce_gradients",
    )(table, proj, out, ffn, places, visual, boxes, word, front, head, bias, tile, place, ids)


def adam_kernel(plan, table_rows, ffn_rows, refs):
    shared_ref, split_ref, tile_ref = refs[:3]
    states, outs, scalars = refs[3:24], refs[24:45], refs[45:48]
    held, load_sem, store_sem = refs[48:69], refs[69], refs[70]
    order = (5, 6, 0, 1, 2, 3, 4)
    loads, stores = {}, []
    for index in order:
        for part in range(3 * index, 3 * index + 3):
            loads[part] = pltpu.make_async_copy(states[part], held[part], load_sem.at[part])
            loads[part].start()
    totals = tile_ref[...]
    count = totals[1, 1:2, 0:1]
    norm = jnp.sqrt(jnp.sum(totals[0], keepdims=True)) / count
    scale = jnp.minimum(1.0, CLIP / norm) / count
    scalars[0][...] = totals[1, 0:1, 0:1]
    scalars[1][...] = count
    scalars[2][...] = norm

    def update(index, where, grad):
        mine = held[3 * index : 3 * index + 3]
        weight, first, second = (ref[where] for ref in mine)
        for ref, value in zip(mine, adam_step(weight, grad * scale, first, second, RATES[index])):
            ref[where] = value

    def blocks(index, lead, source, at, lane=0, wide=D):
        rows = held[3 * index].shape[-2]
        tile = next(t for t in (32, 24, 16, 8) if rows % t == 0)

        def body(step, carry):
            here = pl.multiple_of(step * tile, 8)
            where = (pl.ds(here, tile), slice(None))
            grad = source[pl.ds(pl.multiple_of(at + here, 8), tile), pl.ds(lane, wide)]
            update(index, where if lead is None else (lead,) + where, grad)
            return carry

        lax.fori_loop(0, rows // tile, body, 0)

    pieces_box = plan.box // 32
    for index in order:
        for part in range(3 * index, 3 * index + 3):
            loads[part].wait()
        if index == 0:
            for part in range(4):
                blocks(0, part, shared_ref, part * plan.proj)
        elif index == 1:
            for part in range(plan.box_parts):
                row, lane = plan.box_slot(part)
                grad = shared_ref[pl.ds(row, 32), pl.ds(lane, LANES)]
                update(1, (part // pieces_box, pl.ds(32 * (part % pieces_box), 32)), grad)
        elif index == 2:
            blocks(2, None, shared_ref, plan.places_at)
        elif index == 3:
            blocks(3, None, shared_ref, plan.visual_at)
        elif index == 4:
            row, lane = plan.box_slot(plan.box_parts)
            grad = shared_ref[pl.ds(row, 32), pl.ds(lane, LANES)]
            update(4, (slice(None), slice(None)), grad[:VROWS, : held[12].shape[1]])
        elif index == 5:
            blocks(5, None, split_ref, 0)
        else:
            for part in range(2):
                wide = held[18].shape[2]
                row, lane = ffn_slot(part, table_rows, ffn_rows, wide)
                blocks(6, part, split_ref, row, lane, wide)
        for part in range(3 * index, 3 * index + 3):
            stores.append(pltpu.make_async_copy(held[part], outs[part], store_sem.at[part]))
            stores[-1].start()
    for store in stores:
        store.wait()


def adam_update(plan, table_rows, ffn_rows, shared, split, tile, states):
    vmem = pl.BlockSpec(memory_space=pltpu.VMEM)
    anywhere = pl.BlockSpec(memory_space=pl.ANY)
    scalar = jax.ShapeDtypeStruct((1, 1), WIDE)

    def body(*refs):
        adam_kernel(plan, table_rows, ffn_rows, refs)

    return pl.pallas_call(
        body,
        out_shape=tuple(jax.ShapeDtypeStruct(part.shape, WIDE) for part in states) + (scalar,) * 3,
        in_specs=[vmem] * 3 + [anywhere] * 21,
        out_specs=(anywhere,) * 21 + (vmem,) * 3,
        scratch_shapes=[pltpu.VMEM(part.shape, WIDE) for part in states]
        + [pltpu.SemaphoreType.DMA((21,)), pltpu.SemaphoreType.DMA((21,))],
        compiler_params=pltpu.CompilerParams(vmem_limit_bytes=58 * 2**20),
        name="adam_update",
    )(shared, split, tile, *states)


def combos(index, bits):
    found = [index]
    for bit in bits:
        found = found + [flip(one, bit) for one in found]
    return found


class Ring:
    def __init__(self, mp, sems):
        self.mp, self.here = mp, lax.axis_index("mp")
        self.send, self.recv = sems
        depth = bits_of(mp)
        self.depth = depth
        self.orders = (list(range(depth)), list(range(depth - 1, -1, -1)))
        self.started = []

    def barrier(self):
        barrier = pltpu.get_barrier_semaphore()
        for other in range(1, self.mp):
            pl.semaphore_signal(
                barrier, 1, device_id={"mp": lax.rem(self.here + other, self.mp)},
                device_id_type=MESH,
            )
        pl.semaphore_wait(barrier, self.mp - 1)

    def copy(self, source, target, number, stream, index, peer):
        made = pltpu.make_async_remote_copy(
            src_ref=source, dst_ref=target,
            send_sem=self.send.at[number, stream, index],
            recv_sem=self.recv.at[number, stream, index],
            device_id={"mp": peer}, device_id_type=MESH,
        )
        return made

    def gather_start(self, buffer, number, stream, step):
        order = self.orders[stream]
        peer = flip(self.here, order[step])
        for place, slot in enumerate(combos(self.here, order[:step])):
            part = buffer.at[slot, :, lanes_of(stream)]
            made = self.copy(part, part, number, stream, 2**step - 1 + place, peer)
            made.start()
            self.started.append(made)

    def gather_wait(self, buffer, number, stream, step):
        order = self.orders[stream]
        peer = flip(self.here, order[step])
        for place, slot in enumerate(combos(peer, order[:step])):
            part = buffer.at[slot, :, lanes_of(stream)]
            self.copy(part, part, number, stream, 2**step - 1 + place, peer).wait_recv()

    def gather(self, buffer, number):
        for stream in range(2):
            self.gather_start(buffer, number, stream, 0)
        for step in range(self.depth):
            for stream in range(2):
                self.gather_wait(buffer, number, stream, step)
                if step < self.depth - 1:
                    self.gather_start(buffer, number, stream, step + 1)

    def base(self, step):
        return sum(2 ** (self.depth - 1 - s) for s in range(step))

    def reduce_one(self, buffer, got, number, stream, step, place):
        order = self.orders[stream]
        peer = flip(self.here, order[step])
        slot = combos(peer, order[step + 1 :])[place]
        index = self.base(step) + place
        made = self.copy(
            buffer.at[slot, :, lanes_of(stream)],
            got.at[index, :, lanes_of(stream)],
            number, stream, index, peer,
        )
        made.start()
        self.started.append(made)

    def reduce_start(self, buffer, got, number, stream, step):
        for place in range(2 ** (self.depth - 1 - step)):
            self.reduce_one(buffer, got, number, stream, step, place)

    def reduce_wait(self, buffer, got, number, stream, step):
        order = self.orders[stream]
        peer = flip(self.here, order[step])
        for place, slot in enumerate(combos(self.here, order[step + 1 :])):
            index = self.base(step) + place
            part = got.at[index, :, lanes_of(stream)]
            self.copy(part, part, number, stream, index, peer).wait_recv()
            where = (slot, slice(None), lanes_of(stream))
            total = buffer[where].astype(WIDE) + got[index, :, lanes_of(stream)].astype(WIDE)
            buffer[where] = total.astype(buffer.dtype)

    def reduce_begin(self, buffer, got, number):
        for stream in range(2):
            self.reduce_start(buffer, got, number, stream, 0)

    def reduce_rest(self, buffer, got, number, between=()):
        between = list(between)
        for step in range(self.depth):
            if between:
                between.pop(0)()
            for stream in range(2):
                self.reduce_wait(buffer, got, number, stream, step)
                if step < self.depth - 1:
                    self.reduce_start(buffer, got, number, stream, step + 1)
        for rest in between:
            rest()

    def finish(self):
        for made in self.started:
            made.wait_send()


def mm(left, right, dims):
    return lax.dot_general(left, right, (dims, ((), ())), preferred_element_type=WIDE)


NN, NT, TN = ((1,), (0,)), ((1,), (1,)), ((0,), (0,))


def norm_rows(value):
    centred = value - jnp.mean(value, -1, keepdims=True)
    scale = lax.rsqrt(jnp.mean(centred * centred, -1, keepdims=True) + 1e-05)
    return centred * scale, scale


def norm_back(grad, plain, scale, gain):
    inner = grad * gain
    return scale * (
        inner
        - jnp.mean(inner, -1, keepdims=True)
        - plain * jnp.mean(inner * plain, -1, keepdims=True)
    )


def column_sum(value):
    return jnp.sum(value, 0, keepdims=True)


def head_kernel(mp, refs):
    (
        mixed_ref, zero_ref, weights_in, small_ref, ffn_ref, table_ref, marks_ref,
        grad_zero_ref, grad_mixed_ref, grad_out_ref, grad_ffn_ref, grad_table_ref, rows_ref,
        bias_out, sums_ref,
        ffn, table, out_weight, one, picked, down, sums_two, grad_picked, grad_one, got_two, got_picked,
        got_one, logits, low_logits, stats, load_sem, send_sem, recv_sem, stat_send, stat_recv,
    ) = refs
    ring = Ring(mp, (send_sem, recv_sem))
    here = ring.here
    slots = mixed_ref.shape[0]
    group = slots * mp
    load_ffn = pltpu.make_async_copy(ffn_ref, ffn, load_sem.at[0])
    load_table = pltpu.make_async_copy(table_ref, table, load_sem.at[1])
    load_out = pltpu.make_async_copy(weights_in.at[3], out_weight, load_sem.at[2])
    load_out.start()
    load_ffn.start()
    load_table.start()
    ring.barrier()
    row = lambda index: small_ref[index : index + 1, :]

    load_out.wait()
    out = mm(mixed_ref[...], out_weight[...], NN) + row(4)
    plain_one, scale_one = norm_rows(zero_ref[...] + out)
    normed_one = plain_one * row(5) + row(6)
    one[here] = normed_one.astype(LOW)
    ring.gather(one, 0)
    load_ffn.wait()
    hidden = ffn.shape[2]
    group_one = one[...].reshape(group, D)
    start = here * hidden
    bias = small_ref[
        pl.ds(10 + start // D, 1), pl.ds(pl.multiple_of(lax.rem(start, D), LANES), hidden)
    ]
    before = mm(group_one, ffn[0], NN) + bias
    erf_part = 0.5 * (1.0 + lax.erf(before * (0.5**0.5)))
    active = (before * erf_part).astype(LOW)
    slope = erf_part + before * jnp.exp(-0.5 * before * before) * 0.3989422804014327
    sums_two[...] = mm(active, ffn[1], NT).astype(sums_two.dtype).reshape(mp, slots, D)
    ring.reduce_begin(sums_two, got_two, 1)
    load_table.wait()
    ring.reduce_rest(sums_two, got_two, 1)
    plain_two, scale_two = norm_rows(normed_one + (sums_two[here].astype(WIDE) + row(7)))
    picked[here] = (plain_two * row(8) + row(9)).astype(LOW)
    ring.gather(picked, 2)

    group_picked = picked[...].reshape(group, D)
    vocab = table.shape[0]
    tile = next(t for t in (480, 512, 256, 128) if vocab % t == 0)
    tiles = vocab // tile
    label = marks_ref[0:1, :] - here * vocab
    valid = marks_ref[1:2, :].astype(WIDE)

    def forward(index, carry):
        highest, total, target = carry
        where = pl.ds(pl.multiple_of(index * tile, 16), tile)
        values = mm(table[where, :], group_picked, NT)
        logits[where, :] = values
        higher = jnp.maximum(highest, jnp.max(values, 0, keepdims=True))
        total = total * jnp.exp(highest - higher) + column_sum(jnp.exp(values - higher))
        word = lax.broadcasted_iota(jnp.int32, (tile, group), 0) + index * tile
        target = target + column_sum(jnp.where(word == label, values, 0.0))
        return higher, total, target

    blank = jnp.zeros((1, group), WIDE)
    highest, total, target = lax.fori_loop(0, tiles, forward, (blank - 1e30, blank, blank))
    stats[here, 0:1, 0:group] = highest
    stats[here, 1:2, 0:group] = total
    stats[here, 2:3, 0:group] = target
    stat_copies = []
    for other in range(1, mp):
        made = pltpu.make_async_remote_copy(
            src_ref=stats.at[here], dst_ref=stats.at[here],
            send_sem=stat_send.at[other], recv_sem=stat_recv.at[other],
            device_id={"mp": lax.rem(here + other, mp)}, device_id_type=MESH,
        )
        made.start()
        stat_copies.append(made)
    for other in range(1, mp):
        source = lax.rem(here + mp - other, mp)
        pltpu.make_async_copy(stats.at[source], stats.at[source], stat_recv.at[other]).wait()
    highest = stats[0, 0:1, 0:group]
    for index in range(1, mp):
        highest = jnp.maximum(highest, stats[index, 0:1, 0:group])
    total, target = blank, blank
    for index in range(mp):
        total = total + stats[index, 1:2, 0:group] * jnp.exp(stats[index, 0:1, 0:group] - highest)
        target = target + stats[index, 2:3, 0:group]
    log_rows = highest + jnp.log(total)
    place = lax.broadcasted_iota(jnp.int32, (1, group), 1)
    own = (place >= here * slots) & (place < (here + 1) * slots)
    loss = jnp.sum(jnp.where(own, valid * (log_rows - target), 0.0), -1, keepdims=True)
    count = jnp.sum(jnp.where(own, valid, 0.0), -1, keepdims=True)
    first_lane = lax.broadcasted_iota(jnp.int32, (8, LANES), 1) == 0
    first_row = lax.broadcasted_iota(jnp.int32, (8, LANES), 0)
    sums_ref[...] = jnp.where(
        first_lane & (first_row == 0), loss, jnp.where(first_lane & (first_row == 1), count, 0.0)
    )

    def backward(index, grad):
        where = pl.ds(pl.multiple_of(index * tile, 16), tile)
        word = lax.broadcasted_iota(jnp.int32, (tile, group), 0) + index * tile
        hit = jnp.where(word == label, 1.0, 0.0)
        values = ((jnp.exp(logits[where, :] - log_rows) - hit) * valid).astype(LOW)
        low_logits[where, :] = values
        return grad + mm(values, table[where, :], TN)

    grad = lax.fori_loop(0, tiles, backward, jnp.zeros((group, D), WIDE))
    grad_picked[...] = grad.astype(grad_picked.dtype).reshape(mp, slots, D)

    def table_part(first, last):
        def run():
            def body(index, carry):
                where = pl.ds(pl.multiple_of(index * tile, 16), tile)
                grad_table_ref[where, :] = mm(low_logits[where, :], group_picked, NN).astype(LOW)
                return carry

            lax.fori_loop(first, last, body, 0)

        return run

    ring.reduce_begin(grad_picked, got_picked, 3)
    middle = tiles // 2
    ring.reduce_rest(
        grad_picked, got_picked, 3, [table_part(0, middle), table_part(middle, tiles)]
    )
    grad_two = grad_picked[here].astype(WIDE)
    rows_ref[8:9, :] = column_sum(grad_two * plain_two)
    rows_ref[9:10, :] = column_sum(grad_two)
    grad_sum_two = norm_back(grad_two, plain_two, scale_two, row(8))
    low_two = grad_sum_two.astype(LOW)
    rows_ref[7:8, :] = column_sum(low_two.astype(WIDE))
    down[here] = low_two
    ring.gather(down, 4)
    group_down = down[...].reshape(group, D)
    grad_active = mm(group_down, ffn[1], NN)
    grad_before = (grad_active * slope).astype(LOW)
    grad_one[...] = mm(grad_before, ffn[0], NT).astype(grad_one.dtype).reshape(mp, slots, D)

    def up_part():
        grad_ffn_ref[0] = mm(group_one, grad_before, TN).astype(LOW)
        bias_out[...] = column_sum(grad_before.astype(WIDE))

    def down_part():
        grad_ffn_ref[1] = mm(group_down, active, TN).astype(LOW)

    ring.reduce_begin(grad_one, got_one, 5)
    ring.reduce_rest(grad_one, got_one, 5, [up_part, down_part])
    grad = grad_sum_two + grad_one[here].astype(WIDE)
    rows_ref[5:6, :] = column_sum(grad * plain_one)
    rows_ref[6:7, :] = column_sum(grad)
    grad = norm_back(grad, plain_one, scale_one, row(5))
    low = grad.astype(LOW)
    rows_ref[4:5, :] = column_sum(low.astype(WIDE))
    grad_zero_ref[...] = grad
    grad_mixed_ref[...] = mm(low, out_weight[...], NT).astype(LOW)
    grad_out_ref[...] = mm(mixed_ref[...], low, TN).astype(LOW)
    for index in list(range(4)) + list(range(10, 16)):
        rows_ref[index : index + 1, :] = jnp.zeros((1, D), WIDE)
    ring.finish()
    for made in stat_copies:
        made.wait_send()


def head_step(mp, mixed, zero, weights, small, ffn, table, marks):
    slots, hidden, vocab = mixed.shape[0], ffn.shape[2], table.shape[0]
    group = slots * mp
    wide_group = pad_up(group, LANES)
    vmem = pl.BlockSpec(memory_space=pltpu.VMEM)
    anywhere = pl.BlockSpec(memory_space=pl.ANY)
    dma = pltpu.SemaphoreType.DMA
    exchanged = [pltpu.VMEM((mp, slots, D), LOW)] * 6
    got = [pltpu.VMEM((mp - 1, slots, D), LOW)] * 3

    def body(*refs):
        head_kernel(mp, refs)

    return pl.pallas_call(
        body,
        out_shape=(
            jax.ShapeDtypeStruct((slots, D), WIDE),
            jax.ShapeDtypeStruct((slots, D), LOW),
            jax.ShapeDtypeStruct((D, D), LOW),
            jax.ShapeDtypeStruct((2, D, hidden), LOW),
            jax.ShapeDtypeStruct((vocab, D), LOW),
            jax.ShapeDtypeStruct((16, D), WIDE),
            jax.ShapeDtypeStruct((1, hidden), WIDE),
            jax.ShapeDtypeStruct((8, LANES), WIDE),
        ),
        in_specs=[vmem, vmem, anywhere, vmem, anywhere, anywhere, vmem],
        out_specs=(vmem,) * 8,
        scratch_shapes=[
            pltpu.VMEM((2, D, hidden), LOW),
            pltpu.VMEM((vocab, D), LOW),
            pltpu.VMEM((D, D), LOW),
            *exchanged,
            *got,
            pltpu.VMEM((vocab, group), WIDE),
            pltpu.VMEM((vocab, group), LOW),
            pltpu.VMEM((mp, 8, wide_group), WIDE),
            dma((3,)),
            dma((6, 2, mp - 1)),
            dma((6, 2, mp - 1)),
            dma((mp,)),
            dma((mp,)),
        ],
        compiler_params=pltpu.CompilerParams(
            collective_id=3, has_side_effects=True, vmem_limit_bytes=56 * 2**20
        ),
        name="head_step",
    )(mixed, zero, weights, small, ffn, table, marks)


def gather_kernel(plan, table_rows, refs):
    (
        word_in, proj_in, boxes_in, places_in, visual_in, small_in, ffn_in, tokens_ref,
        table_out, proj_out, boxes_out, places_out, visual_out, ffn_out, word_out, small_out,
        place_out, ids_out, most_out,
        table_buf, shared_buf, ffn_buf, packed, got, key_ref, ids_ref, most_ref,
        out_sem, send_sem, recv_sem, word_send, word_recv, most_send, most_recv,
    ) = refs
    dp, mp = plan.dp, plan.mp
    me = lax.axis_index("dp")
    here = lax.axis_index("mp")
    depth = bits_of(dp)
    rows = word_in.shape[0]
    table_buf[me, 0:rows, :] = word_in[...].astype(LOW)
    barrier = pltpu.get_barrier_semaphore()
    for other in range(1, dp):
        pl.semaphore_signal(
            barrier, 1, device_id={"dp": lax.rem(me + other, dp)}, device_id_type=MESH
        )
    for other in range(1, mp):
        pl.semaphore_signal(
            barrier, 1, device_id={"mp": lax.rem(here + other, mp)}, device_id_type=MESH
        )
    pl.semaphore_wait(barrier, dp + mp - 2)

    half = table_rows // 2
    pieces = (
        (table_buf, 0, half),
        (table_buf, half, half),
        (shared_buf, plan.places_at, plan.shared - plan.places_at),
        (shared_buf, 0, plan.places_at),
        (ffn_buf, 0, ffn_buf.shape[1]),
    )
    orders = (list(range(1, depth)) + [0], list(range(depth - 1, -1, -1)))
    started = []

    def part_of(piece, stream, slot):
        buffer, first, count = pieces[piece]
        return buffer.at[slot, pl.ds(first, count), lanes_of(stream)]

    def copy(piece, stream, step, place, slot):
        part = part_of(piece, stream, slot)
        index = 2**step - 1 + place
        return pltpu.make_async_remote_copy(
            src_ref=part, dst_ref=part,
            send_sem=send_sem.at[piece, stream, index],
            recv_sem=recv_sem.at[piece, stream, index],
            device_id={"dp": flip(me, orders[stream][step])},
            device_id_type=MESH,
        )

    def start(piece, step):
        for stream in range(2):
            for place, slot in enumerate(combos(me, orders[stream][:step])):
                made = copy(piece, stream, step, place, slot)
                made.start()
                started.append(made)

    def wait(piece, step):
        for stream in range(2):
            peer = flip(me, orders[stream][step])
            for place, slot in enumerate(combos(peer, orders[stream][:step])):
                copy(piece, stream, step, place, slot).wait_recv()

    outs = []

    def put(source, target):
        made = pltpu.make_async_copy(source, target, out_sem.at[len(outs)])
        made.start()
        outs.append(made)

    start(0, 0)
    start(1, 0)

    def cast(target, first, source):
        count = source.shape[0]
        target[me, first : first + count, : source.shape[1]] = source.astype(LOW)

    for part in range(4):
        cast(shared_buf, part * plan.proj, proj_in[part])
    cast(shared_buf, plan.places_at, places_in[...])
    cast(shared_buf, plan.visual_at, visual_in[...])
    pieces_box = plan.box // 32
    for part in range(plan.box_parts):
        row, lane = plan.box_slot(part)
        first = 32 * (part % pieces_box)
        shared_buf[me, row : row + 32, lane : lane + LANES] = boxes_in[
            part // pieces_box, first : first + 32, :
        ].astype(LOW)
    row, lane = plan.box_slot(plan.box_parts)
    cut = small_in.shape[1]
    shared_buf[me, row : row + 32, lane : lane + LANES] = jnp.zeros((32, LANES), LOW)
    shared_buf[me, row : row + VROWS, lane : lane + cut] = small_in[...].astype(LOW)
    for part in range(plan.box_parts + 1, 6 * (plan.shared - plan.box_at) // 32):
        spare_row, spare_lane = plan.box_slot(part)
        shared_buf[me, spare_row : spare_row + 32, spare_lane : spare_lane + LANES] = jnp.zeros(
            (32, LANES), LOW
        )
    ffn_rows = ffn_out.shape[2]
    wide = ffn_in.shape[2]
    for part in range(2):
        at, shift = ffn_slot(part, 0, ffn_rows, wide)
        ffn_buf[me, at : at + ffn_in.shape[1], shift : shift + wide] = ffn_in[part].astype(LOW)

    vocab, room = rows * dp, got.shape[1]
    tokens = tokens_ref[...]
    first = lax.broadcasted_iota(jnp.int32, (TEXT, TEXT), 0)
    second = lax.broadcasted_iota(jnp.int32, (TEXT, TEXT), 1)
    before = jnp.where(first < second, 1.0, 0.0).astype(LOW)

    def ranked(ids, shard):
        inside = (ids >= shard * vocab) & (ids < (shard + 1) * vocab)
        rank = mm(jnp.where(inside, 1.0, 0.0).astype(LOW), before, NN).astype(jnp.int32)
        return inside, rank

    inside, rank = ranked(tokens, here)
    key_ref[...] = jnp.where(inside & (rank < room), rank, -1)
    own = tokens_ref[pl.ds(here, 1), :]
    place = jnp.full((1, TEXT), -1, jnp.int32)
    for shard in range(mp):
        inside, rank = ranked(own, shard)
        place = jnp.where(inside & (rank < room), rank + shard * room, place)
    place_out[...] = place
    most = jnp.zeros((mp, 1), WIDE)
    for shard in range(mp):
        inside = (tokens >= shard * vocab) & (tokens < (shard + 1) * vocab)
        most = jnp.maximum(most, jnp.sum(jnp.where(inside, 1.0, 0.0), -1, keepdims=True))
    most = jnp.max(most, 0, keepdims=True)
    most_ref[me] = jnp.broadcast_to(most, (8, LANES))
    most_copies = []
    for other in range(1, dp):
        made = pltpu.make_async_remote_copy(
            src_ref=most_ref.at[me], dst_ref=most_ref.at[me],
            send_sem=most_send.at[other], recv_sem=most_recv.at[other],
            device_id={"dp": lax.rem(me + other, dp)}, device_id_type=MESH,
        )
        made.start()
        most_copies.append(made)
    ids = tokens - here * vocab
    if table_rows != rows:
        ids = jnp.where(ids >= 0, ids // rows * table_rows + ids % rows, 0)
    ids_ref[...] = ids
    entry = lax.broadcasted_iota(jnp.int32, (room, TEXT), 0)

    def listed(slot):
        chosen = entry == key_ref[pl.ds(slot, 1), :]
        return jnp.sum(jnp.where(chosen, ids_ref[pl.ds(slot, 1), :] + 1, 0), -1, keepdims=True) - 1

    turns = [lax.rem(here + other, mp) for other in range(1, mp)] + [here]
    lists = [listed(slot) for slot in turns]
    columns = jnp.concatenate([listed(slot) for slot in range(mp)], 0)
    all_room = room * mp
    corner = lax.broadcasted_iota(jnp.int32, (all_room, all_room), 0) == lax.broadcasted_iota(
        jnp.int32, (all_room, all_room), 1
    )
    ids_out[...] = column_sum(jnp.where(corner, columns, 0))

    for step in range(depth):
        for piece in range(2):
            wait(piece, step)
            if step < depth - 1:
                start(piece, step + 1)
        if step == depth - 2:
            for piece in range(2, len(pieces)):
                start(piece, 0)
    put(table_buf, table_out)

    word_copies = []
    for turn in range(0, mp, 2):
        wanted = jnp.concatenate(lists[turn : turn + 2], 0)
        column = lax.broadcasted_iota(jnp.int32, (2 * room, dp * table_rows), 1)
        hot = jnp.where(column == wanted, 1.0, 0.0).astype(LOW)
        found = mm(hot, table_buf[...].reshape(dp * table_rows, D), NN).astype(LOW)
        for part in range(2):
            slot = turns[turn + part]
            rows_of = found[part * room : (part + 1) * room]
            if turn + part == mp - 1:
                got[here] = rows_of
                continue
            packed[turn + part] = rows_of
            made = pltpu.make_async_remote_copy(
                src_ref=packed.at[turn + part], dst_ref=got.at[here],
                send_sem=word_send.at[turn + part], recv_sem=word_recv.at[turn + part],
                device_id={"mp": slot}, device_id_type=MESH,
            )
            made.start()
            word_copies.append(made)

    def advance(step):
        for piece in range(2, len(pieces)):
            wait(piece, step)
            if step < depth - 1:
                start(piece, step + 1)

    advance(0)
    for other in range(1, mp):
        source = lax.rem(here + mp - other, mp)
        pltpu.make_async_copy(got.at[source], got.at[source], word_recv.at[other - 1]).wait()
    across = jnp.sum(jnp.where(first == second, place, 0), -1, keepdims=True)
    column = lax.broadcasted_iota(jnp.int32, (TEXT, all_room), 1)
    hot = jnp.where(column == across, 1.0, 0.0).astype(LOW)
    word_out[...] = mm(hot, got[...].reshape(all_room, D), NN).astype(LOW)
    for step in range(1, depth):
        advance(step)
    for other in range(1, dp):
        source = lax.rem(me + dp - other, dp)
        pltpu.make_async_copy(
            most_ref.at[source], most_ref.at[source], most_recv.at[other]
        ).wait()
    most = most_ref[0]
    for part in range(1, dp):
        most = jnp.maximum(most, most_ref[part])
    most_out[...] = most[0:1, 0:1]
    row, lane = plan.box_slot(plan.box_parts)
    for part in range(dp):
        small_out[:, part * cut : (part + 1) * cut] = shared_buf[
            part, row : row + 24, lane : lane + cut
        ].astype(WIDE)
    for part in range(4):
        put(shared_buf.at[:, pl.ds(part * plan.proj, plan.proj)], proj_out.at[part])
    put(shared_buf.at[:, pl.ds(plan.places_at, plan.places)], places_out)
    put(shared_buf.at[:, pl.ds(plan.visual_at, plan.visual)], visual_out)
    for part in range(plan.box_parts):
        at, shift = plan.box_slot(part)
        put(
            shared_buf.at[:, pl.ds(at, 32), pl.ds(shift, LANES)],
            boxes_out.at[part // pieces_box, :, pl.ds(32 * (part % pieces_box), 32)],
        )
    for part in range(2):
        at, shift = ffn_slot(part, 0, ffn_rows, wide)
        put(ffn_buf.at[:, pl.ds(at, ffn_rows), pl.ds(shift, wide)], ffn_out.at[part])
    for made in started:
        made.wait_send()
    for made in word_copies + most_copies:
        made.wait_send()
    for made in outs:
        made.wait()


def word_room(mp):
    return pad_up(TEXT // mp * 11 // 8, 16)


def gather_weights(plan, word, proj, boxes, places, visual, small, ffn, tokens):
    dp, mp = plan.dp, plan.mp
    table_rows, ffn_rows, wide = pad_up(word.shape[0], 32), pad_up(ffn.shape[1], 16), ffn.shape[2]
    ffn_all = 2 * ffn_rows * wide // D
    room = word_room(mp)
    anywhere = pl.BlockSpec(memory_space=pl.ANY)
    vmem = pl.BlockSpec(memory_space=pltpu.VMEM)
    dma = pltpu.SemaphoreType.DMA
    shape = jax.ShapeDtypeStruct

    def body(*refs):
        gather_kernel(plan, table_rows, refs)

    return pl.pallas_call(
        body,
        out_shape=(
            shape((dp, table_rows, D), LOW), shape((4, dp, plan.proj, D), LOW),
            shape((4, dp, plan.box, LANES), LOW), shape((dp, plan.places, D), LOW),
            shape((dp, plan.visual, D), LOW), shape((2, dp, ffn_rows, wide), LOW),
            shape((TEXT, D), LOW), shape((24, D), WIDE), shape((1, TEXT), jnp.int32),
            shape((1, mp * room), jnp.int32), shape((1, 1), WIDE),
        ),
        in_specs=[vmem] * 8,
        out_specs=(anywhere,) * 6 + (vmem,) * 5,
        scratch_shapes=[
            pltpu.VMEM((dp, table_rows, D), LOW),
            pltpu.VMEM((dp, plan.shared, D), LOW),
            pltpu.VMEM((dp, ffn_all, D), LOW),
            pltpu.VMEM((mp - 1, room, D), LOW),
            pltpu.VMEM((mp, room, D), LOW),
            pltpu.VMEM((mp, TEXT), jnp.int32),
            pltpu.VMEM((mp, TEXT), jnp.int32),
            pltpu.VMEM((dp, 8, LANES), WIDE),
            dma((plan.box_parts + 10,)),
            dma((5, 2, dp - 1)),
            dma((5, 2, dp - 1)),
            dma((mp - 1,)),
            dma((mp - 1,)),
            dma((dp,)),
            dma((dp,)),
        ],
        compiler_params=pltpu.CompilerParams(
            collective_id=1, has_side_effects=True, vmem_limit_bytes=56 * 2**20
        ),
        name="gather_weights",
    )(word, proj, boxes, places, visual, small, ffn, tokens)


ROWS = 576
KINDS = ((6, 3), (0, 4), (3, 4))


def token_info(text_box, segments, alive_text):
    boxes = jnp.concatenate([text_box, grid_boxes()], 0)
    visual = GRID * GRID
    places = jnp.concatenate([jnp.arange(TEXT), jnp.arange(visual)]).astype(jnp.int32)
    owner = jnp.concatenate([segments, jnp.full((visual,), -1, jnp.int32)])
    alive = jnp.concatenate([alive_text, jnp.ones((visual,), jnp.int32)])
    columns = [
        boxes[:, 0], boxes[:, 1], boxes[:, 2], boxes[:, 3], boxes[:, 3] - boxes[:, 1],
        boxes[:, 2] - boxes[:, 0], places, owner, alive,
    ]
    rows = jnp.stack(columns + [jnp.zeros_like(places)] * 7)
    return jnp.pad(rows, ((0, 0), (0, ROWS - TEXT - visual)))


def edge_hot():
    entry = lax.broadcasted_iota(jnp.int32, (D, LANES), 0)
    place = lax.broadcasted_iota(jnp.int32, (D, LANES), 1)
    first = jnp.clip(place - NB // 2, 0, NB - 1) * H
    return jnp.where((entry >= first) & (entry < first + H), 1.0, 0.0).astype(LOW)


def head_mask():
    entry = lax.broadcasted_iota(jnp.int32, (16, D), 1)
    return lax.rem(entry, H) == lax.broadcasted_iota(jnp.int32, (16, D), 0)


def edge_rows(small_ref, kind):
    first = 10 + FF // D
    row = small_ref[first + kind : first + kind + 1, :]
    return mm(jnp.where(head_mask(), row, 0.0).astype(LOW), edge_hot(), NN)


def edge_rows_back(grad):
    high = grad.astype(LOW)
    low = (grad - high.astype(WIDE)).astype(LOW)
    hot = edge_hot()
    return column_sum(jnp.where(head_mask(), mm(high, hot, NT) + mm(low, hot, NT), 0.0))


def key_hot(rows_ref, kind):
    column, shift = KINDS[kind]
    coarse_row = jnp.right_shift(rows_ref[column : column + 1, :], shift)
    place = lax.broadcasted_iota(jnp.int32, (2 * NB, ROWS), 0)
    first = jnp.where(place == coarse_row, 1.0, 0.0).astype(LOW)
    second = jnp.where(place == coarse_row + NB, 1.0, 0.0).astype(LOW)
    return first, second


def below_of(rows_ref, slot_ref, kind):
    column, shift = KINDS[kind]
    mask = 2**shift - 1
    rest_key = jnp.bitwise_and(rows_ref[column : column + 1, :], mask)
    rest_slot = jnp.bitwise_and(slot_ref[:, column : column + 1], mask)
    return rest_key < rest_slot


def take_slots(slots, pos_ref, pairs):
    def body(index, carry):
        at = pos_ref[index]
        for source, target in pairs:
            target[pl.ds(index, 1), :] = source[pl.ds(at, 1), :]
        return carry

    lax.fori_loop(0, slots, body, 0)


def half_mask(rows):
    slots = rows // 2
    row = lax.broadcasted_iota(jnp.int32, (rows, LANES), 0)
    lane = lax.broadcasted_iota(jnp.int32, (rows, LANES), 1)
    return (row < slots) == (lane < HD)


def pair_rows(value):
    both = jnp.concatenate([value, value], 0)
    return jnp.where(half_mask(both.shape[0]), both, jnp.zeros((), both.dtype))


def pair_lanes(value):
    slots = value.shape[0] // 2
    lane = lax.broadcasted_iota(jnp.int32, (slots, LANES), 1)
    return jnp.where(lane < HD, value[:slots], value[slots:])


def front_kernel(
    pos_ref, word_ref, features_ref, places_ref, boxes_ref, visual_ref, small_ref,
    columns_ref, rows_ref, weights_in,
    mixed_ref, zero_ref, zero_low_ref, low_ref, plain_ref, scale_ref, query_ref, key_ref,
    value_ref, shares_ref,
    normed_ref, slot_ref, bias_ref, spread_ref, stacked_ref, weights_ref, load_sem,
):
    load = pltpu.make_async_copy(weights_in.at[0:3], weights_ref, load_sem)
    load.start()
    slots = mixed_ref.shape[0]
    row = lambda index: small_ref[index : index + 1, :]
    tile = 96
    lookups = (0, 1, 0, 1, 2, 3)

    normed_ref[0:TEXT, :] = word_ref[...].astype(WIDE) + places_ref[...].astype(WIDE)
    visual = features_ref.shape[0]
    normed_ref[TEXT : TEXT + visual, :] = mm(features_ref[...], visual_ref[...], NN) + places_ref[
        0:visual, :
    ].astype(WIDE)
    normed_ref[TEXT + visual : ROWS, :] = jnp.zeros((ROWS - TEXT - visual, D), WIDE)

    def embed(index, carry):
        where = pl.ds(pl.multiple_of(index * tile, 16), tile)
        place = lax.broadcasted_iota(jnp.int32, (tile, NBOX), 1)
        found = []
        for column, table in enumerate(lookups):
            hot = jnp.where(place == columns_ref[where, column : column + 1], 1.0, 0.0).astype(LOW)
            found.append(mm(hot, boxes_ref[table], NN))
        embedded = normed_ref[where, :] + jnp.concatenate(found, -1)
        plain, scale = norm_rows(embedded)
        normed = plain * row(0) + row(1)
        plain_ref[where, :] = plain
        scale_ref[where, :] = scale
        normed_ref[where, :] = normed
        low_ref[where, :] = normed.astype(LOW)
        return carry

    lax.fori_loop(0, ROWS // tile, embed, 0)
    take_slots(slots, pos_ref, ((normed_ref, zero_ref), (columns_ref, slot_ref)))
    low = low_ref[...]
    zero_low = zero_ref[...].astype(LOW)
    zero_low_ref[...] = zero_low
    load.wait()
    query_ref[...] = (mm(zero_low, weights_ref[0], NN) + row(2)).astype(LOW)
    key_ref[...] = mm(low, weights_ref[1], NN).astype(LOW)
    value_ref[...] = (mm(low, weights_ref[2], NN) + row(3)).astype(LOW)

    lane = lax.broadcasted_iota(jnp.int32, (NB, LANES), 1)
    for kind in range(3):
        column, shift = KINDS[kind]
        edges = edge_rows(small_ref, kind)
        for head in range(H):
            edge = jnp.broadcast_to(edges[head : head + 1, :], (NB, LANES))
            near = pltpu.roll(edge, NB, 1, stride=1, stride_axis=0)
            far = pltpu.roll(edge, 1, 1, stride=1, stride_axis=0)
            spread_ref[:, head * LANES : (head + 1) * LANES] = jnp.where(
                lane < NB, near, far
            ).astype(LOW)
        coarse_slot = jnp.right_shift(slot_ref[:, column : column + 1], shift)
        place = lax.broadcasted_iota(jnp.int32, (slots, NB), 1)
        hot = jnp.where(place == coarse_slot, 1.0, 0.0).astype(LOW)
        wide = mm(hot, spread_ref[...], NN).astype(LOW)
        for head in range(H):
            stacked_ref[head * slots : (head + 1) * slots, :] = wide[
                :, head * LANES : (head + 1) * LANES
            ]
        first, second = key_hot(rows_ref, kind)
        below = below_of(rows_ref, slot_ref, kind)

        def add(head, carry):
            where = pl.ds(pl.multiple_of(head * 2 * slots, 16), 2 * slots)
            rows = stacked_ref[where, :]
            both = jnp.concatenate([below, below], 0)
            found = jnp.where(both, mm(rows, second, NN), mm(rows, first, NN))
            bias_ref[where, :] = found if kind == 0 else bias_ref[where, :] + found
            return carry

        lax.fori_loop(0, H // 2, add, 0)

    owner = rows_ref[7:8, :]
    allowed = ((slot_ref[:, 7:8] == owner) | (owner < 0)) & (rows_ref[8:9, :] > 0)
    allowed = jnp.concatenate([allowed, allowed], 0)
    for pair in range(H // 2):
        lanes = slice(pair * LANES, (pair + 1) * LANES)
        rows = slice(pair * 2 * slots, (pair + 1) * 2 * slots)
        scores = mm(pair_rows(query_ref[:, lanes]), key_ref[:, lanes], NT) * 0.125
        scores = jnp.where(allowed, scores + bias_ref[rows, :], MASKED)
        powers = jnp.exp(scores - jnp.max(scores, -1, keepdims=True))
        shares = powers / jnp.sum(powers, -1, keepdims=True)
        shares_ref[rows, :] = shares
        mixed_ref[:, lanes] = pair_lanes(mm(shares.astype(LOW), value_ref[:, lanes], NN)).astype(LOW)


def front_step(pos, word, features, places, boxes, visual, small, columns, rows, weights):
    slots = pos.shape[0]
    vmem = pl.BlockSpec(memory_space=pltpu.VMEM)
    shape = jax.ShapeDtypeStruct
    return pl.pallas_call(
        front_kernel,
        out_shape=(
            shape((slots, D), LOW), shape((slots, D), WIDE), shape((slots, D), LOW),
            shape((ROWS, D), LOW), shape((ROWS, D), WIDE), shape((ROWS, 1), WIDE),
            shape((slots, D), LOW), shape((ROWS, D), LOW), shape((ROWS, D), LOW),
            shape((H * slots, ROWS), WIDE),
        ),
        in_specs=[pl.BlockSpec(memory_space=pltpu.SMEM)] + [vmem] * 8 + [pl.BlockSpec(memory_space=pl.ANY)],
        out_specs=(vmem,) * 10,
        scratch_shapes=[
            pltpu.VMEM((ROWS, D), WIDE),
            pltpu.VMEM((slots, 16), jnp.int32),
            pltpu.VMEM((H * slots, ROWS), WIDE),
            pltpu.VMEM((NB, H * LANES), LOW),
            pltpu.VMEM((H * slots, LANES), LOW),
            pltpu.VMEM((3, D, D), LOW),
            pltpu.SemaphoreType.DMA,
        ],
        compiler_params=pltpu.CompilerParams(vmem_limit_bytes=56 * 2**20),
        name="front_step",
    )(pos, word, features, places, boxes, visual, small, columns, rows, weights)


def back_kernel(
    pos_ref, grad_zero_ref, grad_mixed_ref, shares_ref, query_ref, key_ref, value_ref,
    zero_low_ref, low_ref, plain_ref, scale_ref, features_ref, small_ref, columns_ref, rows_ref,
    weights_in,
    word_out, places_out, boxes_out, visual_out, weights_out, sums_out,
    slot_ref, score_ref, grad_query, grad_key, grad_value, grad_rows, turned_ref, grad_slot, edges_out,
    weights_ref, load_sem,
):
    load = pltpu.make_async_copy(weights_in.at[0:3], weights_ref, load_sem)
    load.start()
    slots = grad_zero_ref.shape[0]
    take_slots(slots, pos_ref, ((columns_ref, slot_ref),))
    for pair in range(H // 2):
        lanes = slice(pair * LANES, (pair + 1) * LANES)
        rows = slice(pair * 2 * slots, (pair + 1) * 2 * slots)
        grad_mixed = pair_rows(grad_mixed_ref[:, lanes])
        shares = shares_ref[rows, :]
        grad_value[:, lanes] = mm(shares.astype(LOW), grad_mixed, TN).astype(LOW)
        grad_shares = mm(grad_mixed, value_ref[:, lanes], NT)
        scores = shares * (grad_shares - jnp.sum(shares * grad_shares, -1, keepdims=True))
        scores = scores.astype(LOW)
        score_ref[rows, :] = scores
        grad_query[:, lanes] = pair_lanes(mm(scores, key_ref[:, lanes], NN) * 0.125).astype(LOW)
        grad_key[:, lanes] = (mm(scores, pair_rows(query_ref[:, lanes]), TN) * 0.125).astype(LOW)

    lane = lax.broadcasted_iota(jnp.int32, (NB, LANES), 1)
    for kind in range(3):
        column, shift = KINDS[kind]
        first, second = key_hot(rows_ref, kind)
        below = below_of(rows_ref, slot_ref, kind)
        coarse_slot = jnp.right_shift(slot_ref[:, column : column + 1], shift)
        place = lax.broadcasted_iota(jnp.int32, (slots, NB), 1)
        hot = jnp.where(place == NB - 1 - coarse_slot, 1.0, 0.0).astype(LOW)

        def collect(pair, carry):
            where = pl.ds(pl.multiple_of(pair * 2 * slots, 16), 2 * slots)
            both = jnp.concatenate([below, below], 0)
            scores = score_ref[where, :]
            none = jnp.zeros((), LOW)
            found = mm(jnp.where(both, none, scores), first, NT) + mm(
                jnp.where(both, scores, none), second, NT
            )
            turned_ref[where, :] = found.astype(LOW)
            return carry

        lax.fori_loop(0, H // 2, collect, 0)
        for head in range(H):
            part = mm(hot, turned_ref[head * slots : (head + 1) * slots, :], TN)
            near = pltpu.roll(jnp.where(lane < NB, part, 0.0), 1, 1, stride=1, stride_axis=0)
            far = pltpu.roll(jnp.where(lane < NB, 0.0, part), NB, 1, stride=1, stride_axis=0)
            edges_out[head : head + 1, :] = column_sum(near + far)
        edges_out[H:16, :] = jnp.zeros((16 - H, LANES), WIDE)
        sums_out[4 + kind : 5 + kind, :] = edge_rows_back(edges_out[...])

    low = low_ref[...]
    weights_out[0] = mm(zero_low_ref[...], grad_query[...], TN).astype(LOW)
    weights_out[1] = mm(low, grad_key[...], TN).astype(LOW)
    weights_out[2] = mm(low, grad_value[...], TN).astype(LOW)
    sums_out[2:3, :] = column_sum(grad_query[...].astype(WIDE))
    sums_out[3:4, :] = column_sum(grad_value[...].astype(WIDE))
    sums_out[7:8, :] = jnp.zeros((1, D), WIDE)
    load.wait()
    grad_rows[...] = mm(grad_key[...], weights_ref[1], NT) + mm(grad_value[...], weights_ref[2], NT)
    grad_slot[...] = grad_zero_ref[...] + mm(grad_query[...], weights_ref[0], NT)

    def put(index, carry):
        at = pl.ds(pos_ref[index], 1)
        grad_rows[at, :] = grad_rows[at, :] + grad_slot[pl.ds(index, 1), :]
        return carry

    lax.fori_loop(0, slots, put, 0)
    gain = small_ref[0:1, :]
    tile = 96

    def normed_back(index, carry):
        where = pl.ds(pl.multiple_of(index * tile, 16), tile)
        grad, plain = grad_rows[where, :], plain_ref[where, :]
        grad_rows[where, :] = norm_back(grad, plain, scale_ref[where, :], gain)
        return carry[0] + column_sum(grad * plain), carry[1] + column_sum(grad)

    blank = jnp.zeros((1, D), WIDE)
    gains, shifts = lax.fori_loop(0, ROWS // tile, normed_back, (blank, blank))
    sums_out[0:1, :] = gains
    sums_out[1:2, :] = shifts
    grad_low = grad_rows[...].astype(LOW)
    word_out[...] = grad_low[0:TEXT, :]
    extra = ROWS - TEXT
    places_out[...] = grad_rows[0:TEXT, :].astype(LOW)
    places_out[0:extra, :] = (grad_rows[0:extra, :] + grad_rows[TEXT:ROWS, :]).astype(LOW)
    visual = features_ref.shape[0]
    visual_out[...] = mm(features_ref[...], grad_low[TEXT : TEXT + visual, :], TN).astype(LOW)
    block = 256

    def table(index, carry):
        where = pl.ds(pl.multiple_of(index * block, 16), block)
        place = lax.broadcasted_iota(jnp.int32, (block, ROWS), 0) + index * block
        found = []
        for column in range(6):
            hot = jnp.where(place == rows_ref[column : column + 1, :], 1.0, 0.0).astype(LOW)
            found.append(mm(hot, grad_low[:, column * LANES : (column + 1) * LANES], NN))
        boxes_out[0, where, :] = (found[0] + found[2]).astype(LOW)
        boxes_out[1, where, :] = (found[1] + found[3]).astype(LOW)
        boxes_out[2, where, :] = found[4].astype(LOW)
        boxes_out[3, where, :] = found[5].astype(LOW)
        return carry

    lax.fori_loop(0, NBOX // block, table, 0)


def back_step(
    pos, grad_zero, grad_mixed, shares, query, key, value, zero_low, low, plain, scale, features,
    small, columns, rows, weights,
):
    slots = pos.shape[0]
    vmem = pl.BlockSpec(memory_space=pltpu.VMEM)
    shape = jax.ShapeDtypeStruct
    return pl.pallas_call(
        back_kernel,
        out_shape=(
            shape((TEXT, D), LOW), shape((TEXT, D), LOW), shape((4, NBOX, LANES), LOW),
            shape((VCH, D), LOW), shape((3, D, D), LOW), shape((8, D), WIDE),
        ),
        in_specs=[pl.BlockSpec(memory_space=pltpu.SMEM)]
        + [vmem] * 14
        + [pl.BlockSpec(memory_space=pl.ANY)],
        out_specs=(vmem,) * 6,
        scratch_shapes=[
            pltpu.VMEM((slots, 16), jnp.int32),
            pltpu.VMEM((H * slots, ROWS), LOW),
            pltpu.VMEM((slots, D), LOW),
            pltpu.VMEM((ROWS, D), LOW),
            pltpu.VMEM((ROWS, D), LOW),
            pltpu.VMEM((ROWS, D), WIDE),
            pltpu.VMEM((H * slots, LANES), LOW),
            pltpu.VMEM((slots, D), WIDE),
            pltpu.VMEM((16, LANES), WIDE),
            pltpu.VMEM((3, D, D), LOW),
            pltpu.SemaphoreType.DMA,
        ],
        compiler_params=pltpu.CompilerParams(vmem_limit_bytes=56 * 2**20),
        name="back_step",
    )(
        pos, grad_zero, grad_mixed, shares, query, key, value, zero_low, low, plain, scale,
        features, small, columns, rows, weights,
    )


def on_device(
    tokens, text_box, segments, alive_text, features, mask_pos, mask_label, mask_valid, *states
):
    (projections, box_tables, position_table, visual_proj, small_params, word_table, feedforward) = (
        states[::3]
    )
    dp, mp = lax.axis_size("dp"), lax.axis_size("mp")
    plan = Plan(dp, mp)
    (
        table_parts, proj_parts, box_parts, place_parts, visual_parts, ffn_parts, word, small,
        places, ids, most,
    ) = (
        gather_weights(
            plan, word_table, projections, box_tables, position_table, visual_proj, small_params,
            feedforward, tokens,
        )
    )

    def joined(parts, rows):
        parts = parts[..., :rows, :]
        return parts.reshape(parts.shape[:-3] + (dp * rows, parts.shape[-1]))

    work_table = joined(table_parts, word_table.shape[0])
    work_proj = joined(proj_parts, D // dp)
    work_boxes = joined(box_parts, NBOX // dp)
    work_places = joined(place_parts, TEXT // dp)
    work_visual = joined(visual_parts, VCH // dp)
    work_ffn = joined(ffn_parts, D // dp)
    vocab_shard = work_table.shape[0]
    room = word_room(mp)
    crowded = most[0, 0] > room

    def local_words():
        local_ids = tokens - lax.axis_index("mp") * vocab_shard
        inside = (local_ids >= 0) & (local_ids < vocab_shard)
        return inside, jnp.clip(local_ids, 0, vocab_shard - 1)

    def exchange_words(state):
        inside, index = local_words()
        found = jnp.where(inside[..., None], jnp.take(work_table, index, axis=0), jnp.zeros((), LOW))
        return False, lax.psum_scatter(found, "mp", scatter_dimension=0, tiled=True)[0]

    word = lax.while_loop(lambda state: state[0], exchange_words, (crowded, word))[1]
    info = token_info(text_box[0], segments[0], alive_text[0])
    columns = info.T
    (
        mixed, slot_zero, slot_low, normed_low, plain, scale, queries, keys, values, shares,
    ) = front_step(
        mask_pos, word, features, work_places, work_boxes, work_visual, small, columns, info,
        work_proj,
    )
    (
        grad_slot, grad_mixed, grad_out_weight, grad_ffn, grad_table, head_rows, grad_ffn_bias,
        own_tile,
    ) = head_step(
        mp, mixed, slot_zero, work_proj, small, work_ffn, work_table,
        jnp.stack([mask_label, mask_valid]),
    )
    grad_word, grad_places, grad_boxes, grad_visual, grad_in_weight, front_rows = back_step(
        mask_pos, grad_slot, grad_mixed, shares, queries, keys, values, slot_low, normed_low,
        plain, scale, features, small, columns, info, work_proj,
    )

    def exchange_word_gradients(state):
        inside, index = local_words()
        shard = tokens // vocab_shard
        same = (shard[..., None] == jnp.arange(mp)).astype(jnp.int32)
        rank = jnp.sum((jnp.cumsum(same, 1) - same) * same, -1)
        late = rank >= room
        own = lax.dynamic_index_in_dim(late, lax.axis_index("mp"), 0, False)
        sent = jnp.where(own[:, None], grad_word, jnp.zeros((), LOW))
        group = lax.all_gather(sent, "mp", axis=0).astype(WIDE)
        group = jnp.where((inside & late)[..., None], group, 0.0)
        return False, state[1].astype(WIDE).at[index].add(group).astype(LOW)

    grad_table = lax.while_loop(
        lambda state: state[0], exchange_word_gradients, (crowded, grad_table)
    )[1]

    def split_rows(part):
        rows = part.shape[-2] // dp
        part = part.astype(LOW).reshape(part.shape[:-2] + (dp, rows, part.shape[-1]))
        extra = [(0, 0)] * (part.ndim - 2) + [(0, pad_up(rows, 16) - rows), (0, 0)]
        return jnp.pad(part, extra) if extra[-2][1] else part

    table_split, ffn_split = split_rows(grad_table), split_rows(grad_ffn)
    shared_sum, split_sum, totals = reduce_gradients(
        plan,
        table_split,
        split_rows(grad_in_weight),
        split_rows(grad_out_weight),
        ffn_split,
        split_rows(grad_places),
        split_rows(grad_visual),
        grad_boxes.reshape(4, dp, NBOX // dp, LANES),
        grad_word,
        front_rows,
        head_rows,
        grad_ffn_bias,
        own_tile,
        places,
        ids,
    )
    outputs = adam_update(
        plan, table_split.shape[1], ffn_split.shape[2], shared_sum, split_sum, totals, states
    )
    return tuple(outputs[:21]) + tuple(part.reshape(()) for part in outputs[21:])


def solution(mesh):
    in_specs = (
        P("dp", None),
        P(("dp", "mp"), None, None),
        P(("dp", "mp"), None),
        P(("dp", "mp"), None),
        P(("dp", "mp"), None),
        P(("dp", "mp")),
        P("dp"),
        P("dp"),
        P(None, "dp", None),
        P(None, "dp", None),
        P(None, "dp", None),
        P(None, "dp", None),
        P(None, "dp", None),
        P(None, "dp", None),
        P("dp", None),
        P("dp", None),
        P("dp", None),
        P("dp", None),
        P("dp", None),
        P("dp", None),
        P(None, "dp"),
        P(None, "dp"),
        P(None, "dp"),
        P(("mp", "dp"), None),
        P(("mp", "dp"), None),
        P(("mp", "dp"), None),
        P(None, "dp", "mp"),
        P(None, "dp", "mp"),
        P(None, "dp", "mp"),
    )
    out_specs = (
        P(None, "dp", None),
        P(None, "dp", None),
        P(None, "dp", None),
        P(None, "dp", None),
        P(None, "dp", None),
        P(None, "dp", None),
        P("dp", None),
        P("dp", None),
        P("dp", None),
        P("dp", None),
        P("dp", None),
        P("dp", None),
        P(None, "dp"),
        P(None, "dp"),
        P(None, "dp"),
        P(("mp", "dp"), None),
        P(("mp", "dp"), None),
        P(("mp", "dp"), None),
        P(None, "dp", "mp"),
        P(None, "dp", "mp"),
        P(None, "dp", "mp"),
        P(),
        P(),
        P(),
    )
    return jax.shard_map(
        on_device, mesh=mesh, in_specs=in_specs, out_specs=out_specs, check_vma=False
    )
```

```python
import jax
import jax.numpy as jnp
from jax import lax
from jax.experimental import pallas as pl
from jax.experimental.pallas import tpu as pltpu
from jax.sharding import PartitionSpec as P

D = 768
H = 12
HD = 64
FF = 3072
NB = 64
GRID = 7
TEXT = 512
STEP = 10
VCH = 256
NBOX = 1024
VROWS = 17


MASKED = -1e30
CLIP = 0.005
BETA_ONE = 0.9
BETA_TWO = 0.999
EPSILON = 1e-08
DECAY = 0.01
RATES = (0.02, 0.03, 0.03, 0.04, 0.3, 0.05, 0.02)


def grid_boxes():
    cells = jnp.arange(GRID * GRID, dtype=jnp.int32)
    row_place = cells // GRID
    column_place = cells % GRID
    return jnp.stack(
        [
            column_place * 1000 // GRID,
            row_place * 1000 // GRID,
            (column_place + 1) * 1000 // GRID,
            (row_place + 1) * 1000 // GRID,
        ],
        -1,
    )


def adam_step(weight, grad, first, second, rate):
    first = BETA_ONE * first + (1.0 - BETA_ONE) * grad
    second = BETA_TWO * second + (1.0 - BETA_TWO) * grad * grad
    fixed_first = first / (1.0 - BETA_ONE**STEP)
    fixed_second = second / (1.0 - BETA_TWO**STEP)
    weight = weight - rate * (fixed_first / (jnp.sqrt(fixed_second) + EPSILON) + DECAY * weight)
    return (weight, first, second)


MESH = pl.DeviceIdType.MESH
LOW = jnp.bfloat16
WIDE = jnp.float32
LANES = 128
HALF = D // 2


def pad_up(count, unit):
    return (count + unit - 1) // unit * unit


def bits_of(count):
    return count.bit_length() - 1


def flip(index, bit):
    return index + (1 - 2 * ((index // 2**bit) % 2)) * 2**bit


class Plan:
    def __init__(self, dp, mp):
        self.dp, self.mp = dp, mp
        self.proj = pad_up(D // dp, 16)
        self.places = pad_up(TEXT // dp, 16)
        self.visual = pad_up(VCH // dp, 16)
        self.box = NBOX // dp
        self.box_parts = 4 * (self.box // 32)
        self.places_at = 4 * self.proj
        self.visual_at = self.places_at + self.places
        self.box_at = self.visual_at + self.visual
        self.box_rows = 32 * ((self.box_parts + 6) // 6)
        self.shared = pad_up(self.box_at + self.box_rows, 32 * mp)

    def box_slot(self, part):
        return self.box_at + 32 * (part // 6), LANES * (part % 6)


def group_of(axis, index):
    return {axis: index}


def lanes_of(stream):
    return pl.ds(stream * HALF, HALF)


def ffn_slot(part, table_rows, ffn_rows, wide):
    return table_rows + part * wide // D * ffn_rows, part * wide % D


def row_tile(rows):
    return next(t for t in (48, 32, 16) if rows % t == 0)


def adam_kernel(plan, table_rows, ffn_rows, refs):
    shared_ref, split_ref, tile_ref = refs[:3]
    states, outs, scalars = refs[3:24], refs[24:45], refs[45:48]
    held, load_sem, store_sem = refs[48:69], refs[69], refs[70]
    order = (5, 6, 0, 1, 2, 3, 4)
    loads, stores = {}, []
    for index in order:
        for part in range(3 * index, 3 * index + 3):
            loads[part] = pltpu.make_async_copy(states[part], held[part], load_sem.at[part])
            loads[part].start()
    totals = tile_ref[...]
    count = totals[1, 1:2, 0:1]
    norm = jnp.sqrt(jnp.sum(totals[0], keepdims=True)) / count
    scale = jnp.minimum(1.0, CLIP / norm) / count
    scalars[0][...] = totals[1, 0:1, 0:1]
    scalars[1][...] = count
    scalars[2][...] = norm

    def update(index, where, grad):
        mine = held[3 * index : 3 * index + 3]
        weight, first, second = (ref[where] for ref in mine)
        for ref, value in zip(mine, adam_step(weight, grad * scale, first, second, RATES[index])):
            ref[where] = value

    def blocks(index, lead, source, at, lane=0, wide=D):
        rows = held[3 * index].shape[-2]
        tile = next(t for t in (32, 24, 16, 8) if rows % t == 0)

        def body(step, carry):
            here = pl.multiple_of(step * tile, 8)
            where = (pl.ds(here, tile), slice(None))
            grad = source[pl.ds(pl.multiple_of(at + here, 8), tile), pl.ds(lane, wide)]
            update(index, where if lead is None else (lead,) + where, grad)
            return carry

        lax.fori_loop(0, rows // tile, body, 0)

    pieces_box = plan.box // 32
    for index in order:
        for part in range(3 * index, 3 * index + 3):
            loads[part].wait()
        if index == 0:
            for part in range(4):
                blocks(0, part, shared_ref, part * plan.proj)
        elif index == 1:
            for part in range(plan.box_parts):
                row, lane = plan.box_slot(part)
                grad = shared_ref[pl.ds(row, 32), pl.ds(lane, LANES)]
                update(1, (part // pieces_box, pl.ds(32 * (part % pieces_box), 32)), grad)
        elif index == 2:
            blocks(2, None, shared_ref, plan.places_at)
        elif index == 3:
            blocks(3, None, shared_ref, plan.visual_at)
        elif index == 4:
            row, lane = plan.box_slot(plan.box_parts)
            grad = shared_ref[pl.ds(row, 32), pl.ds(lane, LANES)]
            update(4, (slice(None), slice(None)), grad[:VROWS, : held[12].shape[1]])
        elif index == 5:
            blocks(5, None, split_ref, 0)
        else:
            for part in range(2):
                wide = held[18].shape[2]
                row, lane = ffn_slot(part, table_rows, ffn_rows, wide)
                blocks(6, part, split_ref, row, lane, wide)
        for part in range(3 * index, 3 * index + 3):
            stores.append(pltpu.make_async_copy(held[part], outs[part], store_sem.at[part]))
            stores[-1].start()
    for store in stores:
        store.wait()


def adam_update(plan, table_rows, ffn_rows, shared, split, tile, states):
    vmem = pl.BlockSpec(memory_space=pltpu.VMEM)
    anywhere = pl.BlockSpec(memory_space=pl.ANY)
    scalar = jax.ShapeDtypeStruct((1, 1), WIDE)

    def body(*refs):
        adam_kernel(plan, table_rows, ffn_rows, refs)

    return pl.pallas_call(
        body,
        out_shape=tuple(jax.ShapeDtypeStruct(part.shape, WIDE) for part in states) + (scalar,) * 3,
        in_specs=[vmem] * 3 + [anywhere] * 21,
        out_specs=(anywhere,) * 21 + (vmem,) * 3,
        scratch_shapes=[pltpu.VMEM(part.shape, WIDE) for part in states]
        + [pltpu.SemaphoreType.DMA((21,)), pltpu.SemaphoreType.DMA((21,))],
        compiler_params=pltpu.CompilerParams(vmem_limit_bytes=58 * 2**20),
        name="adam_update",
    )(shared, split, tile, *states)


def combos(index, bits):
    found = [index]
    for bit in bits:
        found = found + [flip(one, bit) for one in found]
    return found


class Ring:
    def __init__(self, mp, sems):
        self.mp, self.here = mp, lax.axis_index("mp")
        self.send, self.recv = sems
        depth = bits_of(mp)
        self.depth = depth
        self.orders = (list(range(depth)), list(range(depth - 1, -1, -1)))
        self.started = []

    def barrier(self):
        barrier = pltpu.get_barrier_semaphore()
        for other in range(1, self.mp):
            pl.semaphore_signal(
                barrier, 1, device_id={"mp": lax.rem(self.here + other, self.mp)},
                device_id_type=MESH,
            )
        pl.semaphore_wait(barrier, self.mp - 1)

    def copy(self, source, target, number, stream, index, peer):
        made = pltpu.make_async_remote_copy(
            src_ref=source, dst_ref=target,
            send_sem=self.send.at[number, stream, index],
            recv_sem=self.recv.at[number, stream, index],
            device_id={"mp": peer}, device_id_type=MESH,
        )
        return made

    def gather_start(self, buffer, number, stream, step):
        order = self.orders[stream]
        peer = flip(self.here, order[step])
        for place, slot in enumerate(combos(self.here, order[:step])):
            part = buffer.at[slot, :, lanes_of(stream)]
            made = self.copy(part, part, number, stream, 2**step - 1 + place, peer)
            made.start()
            self.started.append(made)

    def gather_wait(self, buffer, number, stream, step):
        order = self.orders[stream]
        peer = flip(self.here, order[step])
        for place, slot in enumerate(combos(peer, order[:step])):
            part = buffer.at[slot, :, lanes_of(stream)]
            self.copy(part, part, number, stream, 2**step - 1 + place, peer).wait_recv()

    def gather(self, buffer, number):
        for stream in range(2):
            self.gather_start(buffer, number, stream, 0)
        for step in range(self.depth):
            for stream in range(2):
                self.gather_wait(buffer, number, stream, step)
                if step < self.depth - 1:
                    self.gather_start(buffer, number, stream, step + 1)

    def base(self, step):
        return sum(2 ** (self.depth - 1 - s) for s in range(step))

    def reduce_one(self, buffer, got, number, stream, step, place):
        order = self.orders[stream]
        peer = flip(self.here, order[step])
        slot = combos(peer, order[step + 1 :])[place]
        index = self.base(step) + place
        made = self.copy(
            buffer.at[slot, :, lanes_of(stream)],
            got.at[index, :, lanes_of(stream)],
            number, stream, index, peer,
        )
        made.start()
        self.started.append(made)

    def reduce_start(self, buffer, got, number, stream, step):
        for place in range(2 ** (self.depth - 1 - step)):
            self.reduce_one(buffer, got, number, stream, step, place)

    def reduce_wait(self, buffer, got, number, stream, step):
        order = self.orders[stream]
        peer = flip(self.here, order[step])
        for place, slot in enumerate(combos(self.here, order[step + 1 :])):
            index = self.base(step) + place
            part = got.at[index, :, lanes_of(stream)]
            self.copy(part, part, number, stream, index, peer).wait_recv()
            where = (slot, slice(None), lanes_of(stream))
            total = buffer[where].astype(WIDE) + got[index, :, lanes_of(stream)].astype(WIDE)
            buffer[where] = total.astype(buffer.dtype)

    def reduce_begin(self, buffer, got, number):
        for stream in range(2):
            self.reduce_start(buffer, got, number, stream, 0)

    def reduce_rest(self, buffer, got, number, between=()):
        between = list(between)
        for step in range(self.depth):
            if between:
                between.pop(0)()
            for stream in range(2):
                self.reduce_wait(buffer, got, number, stream, step)
                if step < self.depth - 1:
                    self.reduce_start(buffer, got, number, stream, step + 1)
        for rest in between:
            rest()

    def finish(self):
        for made in self.started:
            made.wait_send()


def mm(left, right, dims):
    return lax.dot_general(left, right, (dims, ((), ())), preferred_element_type=WIDE)


NN, NT, TN = ((1,), (0,)), ((1,), (1,)), ((0,), (0,))


def norm_rows(value):
    centred = value - jnp.mean(value, -1, keepdims=True)
    scale = lax.rsqrt(jnp.mean(centred * centred, -1, keepdims=True) + 1e-05)
    return centred * scale, scale


def norm_back(grad, plain, scale, gain):
    inner = grad * gain
    return scale * (
        inner
        - jnp.mean(inner, -1, keepdims=True)
        - plain * jnp.mean(inner * plain, -1, keepdims=True)
    )


def column_sum(value):
    return jnp.sum(value, 0, keepdims=True)


def halves_of(slots):
    first = pad_up(slots // 2, 16)
    return ((0, first), (first, slots - first))


def head_kernel(mp, vocab_tile, refs):
    (
        mixed_ref, zero_ref, weights_in, small_ref, ffn_ref, table_ref, marks_zero, marks_one,
        grad_zero_ref, grad_mixed_ref, grad_out_ref, grad_ffn_ref, grad_table_ref, rows_ref,
        bias_out, sums_ref,
        ffn, table, out_weight, *scratch,
    ) = refs
    load_sem, send_sem, recv_sem, stat_send, stat_recv = scratch[-5:]
    ring = Ring(mp, (send_sem, recv_sem))
    here = ring.here
    slots, vocab, hidden = mixed_ref.shape[0], table.shape[0], ffn.shape[2]
    load_ffn = pltpu.make_async_copy(ffn_ref, ffn, load_sem.at[0])
    load_table = pltpu.make_async_copy(table_ref, table, load_sem.at[1])
    load_out = pltpu.make_async_copy(weights_in.at[3], out_weight, load_sem.at[2])
    load_out.start()
    load_ffn.start()
    load_table.start()
    ring.barrier()
    row = lambda index: small_ref[index : index + 1, :]
    start = here * hidden
    bias = small_ref[
        pl.ds(10 + start // D, 1), pl.ds(pl.multiple_of(lax.rem(start, D), LANES), hidden)
    ]
    load_out.wait()
    load_ffn.wait()
    load_table.wait()
    kept = [{}, {}]
    waiting = []

    def gathering(buffer, number):
        for stream in range(2):
            ring.gather_start(buffer, number, stream, 0)
        for step in range(ring.depth):
            yield
            for stream in range(2):
                ring.gather_wait(buffer, number, stream, step)
                if step < ring.depth - 1:
                    ring.gather_start(buffer, number, stream, step + 1)

    def reducing(buffer, got, number):
        ring.reduce_begin(buffer, got, number)
        for step in range(ring.depth):
            yield
            for stream in range(2):
                ring.reduce_wait(buffer, got, number, stream, step)
                if step < ring.depth - 1:
                    ring.reduce_start(buffer, got, number, stream, step + 1)

    def run(part):
        first, count = halves_of(slots)[part]
        group = count * mp
        rows = slice(first, first + count)
        keep = kept[part]
        one, picked, down, sums_two, grad_picked, grad_one, *rest = scratch[12 * part : 12 * part + 12]
        got_two, got_picked, got_one, logits, low_logits, stats = rest
        marks_ref = marks_one if part else marks_zero
        base = 6 * part

        out = mm(mixed_ref[rows, :], out_weight[...], NN) + row(4)
        plain_one, scale_one = norm_rows(zero_ref[rows, :] + out)
        normed_one = plain_one * row(5) + row(6)
        one[here] = normed_one.astype(LOW)
        yield from gathering(one, base)
        group_one = one[...].reshape(group, D)
        before = mm(group_one, ffn[0], NN) + bias
        erf_part = 0.5 * (1.0 + lax.erf(before * (0.5**0.5)))
        active = (before * erf_part).astype(LOW)
        sums_two[...] = mm(active, ffn[1], NT).astype(LOW).reshape(mp, count, D)
        slope = erf_part + before * jnp.exp(-0.5 * before * before) * 0.3989422804014327
        yield from reducing(sums_two, got_two, base + 1)
        plain_two, scale_two = norm_rows(normed_one + (sums_two[here].astype(WIDE) + row(7)))
        picked[here] = (plain_two * row(8) + row(9)).astype(LOW)
        yield from gathering(picked, base + 2)
        group_picked = picked[...].reshape(group, D)
        label = marks_ref[0:1, :] - here * vocab
        valid = marks_ref[1:2, :].astype(WIDE)
        tiles = vocab // vocab_tile

        def forward(index, carry):
            highest, total, target = carry
            where = pl.ds(pl.multiple_of(index * vocab_tile, 16), vocab_tile)
            values = mm(table[where, :], group_picked, NT)
            logits[where, :] = values
            higher = jnp.maximum(highest, jnp.max(values, 0, keepdims=True))
            total = total * jnp.exp(highest - higher) + column_sum(jnp.exp(values - higher))
            word = lax.broadcasted_iota(jnp.int32, (vocab_tile, group), 0) + index * vocab_tile
            target = target + column_sum(jnp.where(word == label, values, 0.0))
            return higher, total, target

        blank = jnp.zeros((1, group), WIDE)
        highest, total, target = lax.fori_loop(0, tiles, forward, (blank - 1e30, blank, blank))
        stats[here, 0:1, 0:group] = highest
        stats[here, 1:2, 0:group] = total
        stats[here, 2:3, 0:group] = target
        for other in range(1, mp):
            made = pltpu.make_async_remote_copy(
                src_ref=stats.at[here], dst_ref=stats.at[here],
                send_sem=stat_send.at[part, other], recv_sem=stat_recv.at[part, other],
                device_id={"mp": lax.rem(here + other, mp)}, device_id_type=MESH,
            )
            made.start()
            waiting.append(made)
        yield
        for other in range(1, mp):
            source = lax.rem(here + mp - other, mp)
            pltpu.make_async_copy(
                stats.at[source], stats.at[source], stat_recv.at[part, other]
            ).wait()
        highest = stats[0, 0:1, 0:group]
        for index in range(1, mp):
            highest = jnp.maximum(highest, stats[index, 0:1, 0:group])
        total, target = blank, blank
        for index in range(mp):
            scaled = jnp.exp(stats[index, 0:1, 0:group] - highest)
            total = total + stats[index, 1:2, 0:group] * scaled
            target = target + stats[index, 2:3, 0:group]
        log_rows = highest + jnp.log(total)
        place = lax.broadcasted_iota(jnp.int32, (1, group), 1)
        own = (place >= here * count) & (place < (here + 1) * count)
        keep["loss"] = jnp.sum(
            jnp.where(own, valid * (log_rows - target), 0.0), -1, keepdims=True
        )
        keep["count"] = jnp.sum(jnp.where(own, valid, 0.0), -1, keepdims=True)

        def backward(index, grad):
            where = pl.ds(pl.multiple_of(index * vocab_tile, 16), vocab_tile)
            word = lax.broadcasted_iota(jnp.int32, (vocab_tile, group), 0) + index * vocab_tile
            hit = jnp.where(word == label, 1.0, 0.0)
            values = ((jnp.exp(logits[where, :] - log_rows) - hit) * valid).astype(LOW)
            low_logits[where, :] = values
            return grad + mm(values, table[where, :], TN)

        grad = lax.fori_loop(0, tiles, backward, jnp.zeros((group, D), WIDE))
        grad_picked[...] = grad.astype(LOW).reshape(mp, count, D)
        keep["picked"], keep["low_logits"] = group_picked, low_logits
        yield from reducing(grad_picked, got_picked, base + 3)
        grad_two = grad_picked[here].astype(WIDE)
        keep[8] = column_sum(grad_two * plain_two)
        keep[9] = column_sum(grad_two)
        grad_sum_two = norm_back(grad_two, plain_two, scale_two, row(8))
        low_two = grad_sum_two.astype(LOW)
        keep[7] = column_sum(low_two.astype(WIDE))
        down[here] = low_two
        yield from gathering(down, base + 4)
        group_down = down[...].reshape(group, D)
        grad_active = mm(group_down, ffn[1], NN)
        grad_before = (grad_active * slope).astype(LOW)
        grad_one[...] = mm(grad_before, ffn[0], NT).astype(LOW).reshape(mp, count, D)
        keep["up"] = (group_one, grad_before)
        keep["down"] = (group_down, active)
        yield from reducing(grad_one, got_one, base + 5)
        grad = grad_sum_two + grad_one[here].astype(WIDE)
        keep[5] = column_sum(grad * plain_one)
        keep[6] = column_sum(grad)
        grad = norm_back(grad, plain_one, scale_one, row(5))
        low = grad.astype(LOW)
        keep[4] = column_sum(low.astype(WIDE))
        grad_zero_ref[rows, :] = grad
        grad_mixed_ref[rows, :] = mm(low, out_weight[...], NT).astype(LOW)
        keep["out"] = low

    def both(name):
        return [jnp.concatenate([kept[0][name][side], kept[1][name][side]], 0) for side in range(2)]

    def table_part(first, last):
        def work():
            def body(index, carry):
                where = pl.ds(pl.multiple_of(index * vocab_tile, 16), vocab_tile)
                total = mm(kept[0]["low_logits"][where, :], kept[0]["picked"], NN)
                total = total + mm(kept[1]["low_logits"][where, :], kept[1]["picked"], NN)
                grad_table_ref[where, :] = total.astype(LOW)
                return carry

            lax.fori_loop(first, last, body, 0)

        return work

    def up_part():
        left, right = both("up")
        grad_ffn_ref[0] = mm(left, right, TN).astype(LOW)
        bias_out[...] = column_sum(right.astype(WIDE))

    def down_part():
        left, right = both("down")
        grad_ffn_ref[1] = mm(left, right, TN).astype(LOW)

    tiles = vocab // vocab_tile
    quarter = max(1, tiles // 4)
    fillers = [
        table_part(first, min(first + quarter, tiles)) for first in range(0, tiles, quarter)
    ]
    late = [up_part, down_part]
    runs = [run(0), run(1)]
    live = [True, True]
    while any(live):
        for part in range(2):
            if live[part]:
                live[part] = next(runs[part], "done") != "done"
        if "down" in kept[1] and late:
            late.pop(0)()
        elif "low_logits" in kept[1] and fillers:
            fillers.pop(0)()
    for work in fillers + late:
        work()
    grad_out_ref[...] = mm(
        mixed_ref[...], jnp.concatenate([kept[0]["out"], kept[1]["out"]], 0), TN
    ).astype(LOW)
    first_lane = lax.broadcasted_iota(jnp.int32, (8, LANES), 1) == 0
    first_row = lax.broadcasted_iota(jnp.int32, (8, LANES), 0)
    loss, count = (kept[0][name] + kept[1][name] for name in ("loss", "count"))
    sums_ref[...] = jnp.where(
        first_lane & (first_row == 0), loss, jnp.where(first_lane & (first_row == 1), count, 0.0)
    )
    for index in range(16):
        value = kept[0][index] + kept[1][index] if 4 <= index < 10 else jnp.zeros((1, D), WIDE)
        rows_ref[index : index + 1, :] = value
    ring.finish()
    for made in waiting:
        made.wait_send()


def head_step(mp, mixed, zero, weights, small, ffn, table, marks):
    slots, hidden, vocab = mixed.shape[0], ffn.shape[2], table.shape[0]
    vmem = pl.BlockSpec(memory_space=pltpu.VMEM)
    anywhere = pl.BlockSpec(memory_space=pl.ANY)
    dma = pltpu.SemaphoreType.DMA
    tile = next(t for t in (480, 512, 256, 128) if vocab % t == 0)
    scratch = []
    for first, count in halves_of(slots):
        group = mp * count
        scratch += [pltpu.VMEM((mp, count, D), LOW)] * 6
        scratch += [pltpu.VMEM((mp - 1, count, D), LOW)] * 3
        scratch += [
            pltpu.VMEM((vocab, group), WIDE),
            pltpu.VMEM((vocab, group), LOW),
            pltpu.VMEM((mp, 8, pad_up(group, LANES)), WIDE),
        ]

    def body(*refs):
        head_kernel(mp, tile, refs)

    def marks_of(first, count):
        return marks.reshape(2, mp, slots)[:, :, first : first + count].reshape(2, mp * count)

    return pl.pallas_call(
        body,
        out_shape=(
            jax.ShapeDtypeStruct((slots, D), WIDE),
            jax.ShapeDtypeStruct((slots, D), LOW),
            jax.ShapeDtypeStruct((D, D), LOW),
            jax.ShapeDtypeStruct((2, D, hidden), LOW),
            jax.ShapeDtypeStruct((vocab, D), LOW),
            jax.ShapeDtypeStruct((16, D), WIDE),
            jax.ShapeDtypeStruct((1, hidden), WIDE),
            jax.ShapeDtypeStruct((8, LANES), WIDE),
        ),
        in_specs=[vmem, vmem, anywhere, vmem, anywhere, anywhere, vmem, vmem],
        out_specs=(vmem,) * 8,
        scratch_shapes=[
            pltpu.VMEM((2, D, hidden), LOW),
            pltpu.VMEM((vocab, D), LOW),
            pltpu.VMEM((D, D), LOW),
            *scratch,
            dma((3,)),
            dma((12, 2, mp - 1)),
            dma((12, 2, mp - 1)),
            dma((2, mp)),
            dma((2, mp)),
        ],
        compiler_params=pltpu.CompilerParams(
            collective_id=3, has_side_effects=True, vmem_limit_bytes=58 * 2**20
        ),
        name="head_step",
    )(mixed, zero, weights, small, ffn, table, *(marks_of(*half) for half in halves_of(slots)))


def gather_kernel(plan, table_rows, refs):
    (
        word_in, proj_in, boxes_in, places_in, visual_in, small_in, ffn_in, tokens_ref,
        table_out, proj_out, boxes_out, places_out, visual_out, ffn_out, word_out, small_out,
        place_out, ids_out, most_out,
        table_buf, shared_buf, ffn_buf, packed, got, key_ref, ids_ref, most_ref,
        out_sem, send_sem, recv_sem, word_send, word_recv, most_send, most_recv,
    ) = refs
    dp, mp = plan.dp, plan.mp
    me = lax.axis_index("dp")
    here = lax.axis_index("mp")
    depth = bits_of(dp)
    rows = word_in.shape[0]
    table_buf[me, 0:rows, :] = word_in[...].astype(LOW)
    barrier = pltpu.get_barrier_semaphore()
    for other in range(1, dp):
        pl.semaphore_signal(
            barrier, 1, device_id={"dp": lax.rem(me + other, dp)}, device_id_type=MESH
        )
    for other in range(1, mp):
        pl.semaphore_signal(
            barrier, 1, device_id={"mp": lax.rem(here + other, mp)}, device_id_type=MESH
        )
    pl.semaphore_wait(barrier, dp + mp - 2)

    half = table_rows // 2
    pieces = (
        (table_buf, 0, half),
        (table_buf, half, half),
        (shared_buf, plan.places_at, plan.shared - plan.places_at),
        (shared_buf, 0, plan.places_at),
        (ffn_buf, 0, ffn_buf.shape[1]),
    )
    orders = (list(range(1, depth)) + [0], list(range(depth - 1, -1, -1)))
    started = []

    def part_of(piece, stream, slot):
        buffer, first, count = pieces[piece]
        return buffer.at[slot, pl.ds(first, count), lanes_of(stream)]

    def copy(piece, stream, step, place, slot):
        part = part_of(piece, stream, slot)
        index = 2**step - 1 + place
        return pltpu.make_async_remote_copy(
            src_ref=part, dst_ref=part,
            send_sem=send_sem.at[piece, stream, index],
            recv_sem=recv_sem.at[piece, stream, index],
            device_id={"dp": flip(me, orders[stream][step])},
            device_id_type=MESH,
        )

    def start(piece, step):
        for stream in range(2):
            for place, slot in enumerate(combos(me, orders[stream][:step])):
                made = copy(piece, stream, step, place, slot)
                made.start()
                started.append(made)

    def wait(piece, step):
        for stream in range(2):
            peer = flip(me, orders[stream][step])
            for place, slot in enumerate(combos(peer, orders[stream][:step])):
                copy(piece, stream, step, place, slot).wait_recv()

    outs = []

    def put(source, target):
        made = pltpu.make_async_copy(source, target, out_sem.at[len(outs)])
        made.start()
        outs.append(made)

    start(0, 0)
    start(1, 0)

    def cast(target, first, source):
        count = source.shape[0]
        target[me, first : first + count, : source.shape[1]] = source.astype(LOW)

    for part in range(4):
        cast(shared_buf, part * plan.proj, proj_in[part])
    cast(shared_buf, plan.places_at, places_in[...])
    cast(shared_buf, plan.visual_at, visual_in[...])
    pieces_box = plan.box // 32
    for part in range(plan.box_parts):
        row, lane = plan.box_slot(part)
        first = 32 * (part % pieces_box)
        shared_buf[me, row : row + 32, lane : lane + LANES] = boxes_in[
            part // pieces_box, first : first + 32, :
        ].astype(LOW)
    row, lane = plan.box_slot(plan.box_parts)
    cut = small_in.shape[1]
    shared_buf[me, row : row + 32, lane : lane + LANES] = jnp.zeros((32, LANES), LOW)
    shared_buf[me, row : row + VROWS, lane : lane + cut] = small_in[...].astype(LOW)
    for part in range(plan.box_parts + 1, 6 * (plan.shared - plan.box_at) // 32):
        spare_row, spare_lane = plan.box_slot(part)
        shared_buf[me, spare_row : spare_row + 32, spare_lane : spare_lane + LANES] = jnp.zeros(
            (32, LANES), LOW
        )
    ffn_rows = ffn_out.shape[2]
    wide = ffn_in.shape[2]
    for part in range(2):
        at, shift = ffn_slot(part, 0, ffn_rows, wide)
        ffn_buf[me, at : at + ffn_in.shape[1], shift : shift + wide] = ffn_in[part].astype(LOW)

    vocab, room = rows * dp, got.shape[1]
    tokens = tokens_ref[...]
    first = lax.broadcasted_iota(jnp.int32, (TEXT, TEXT), 0)
    second = lax.broadcasted_iota(jnp.int32, (TEXT, TEXT), 1)
    before = jnp.where(first < second, 1.0, 0.0).astype(LOW)

    def ranked(ids, shard):
        inside = (ids >= shard * vocab) & (ids < (shard + 1) * vocab)
        rank = mm(jnp.where(inside, 1.0, 0.0).astype(LOW), before, NN).astype(jnp.int32)
        return inside, rank

    inside, rank = ranked(tokens, here)
    key_ref[...] = jnp.where(inside & (rank < room), rank, -1)
    own = tokens_ref[pl.ds(here, 1), :]
    place = jnp.full((1, TEXT), -1, jnp.int32)
    for shard in range(mp):
        inside, rank = ranked(own, shard)
        place = jnp.where(inside & (rank < room), rank + shard * room, place)
    place_out[...] = place
    most = jnp.zeros((mp, 1), WIDE)
    for shard in range(mp):
        inside = (tokens >= shard * vocab) & (tokens < (shard + 1) * vocab)
        most = jnp.maximum(most, jnp.sum(jnp.where(inside, 1.0, 0.0), -1, keepdims=True))
    most = jnp.max(most, 0, keepdims=True)
    most_ref[me] = jnp.broadcast_to(most, (8, LANES))
    most_copies = []
    for other in range(1, dp):
        made = pltpu.make_async_remote_copy(
            src_ref=most_ref.at[me], dst_ref=most_ref.at[me],
            send_sem=most_send.at[other], recv_sem=most_recv.at[other],
            device_id={"dp": lax.rem(me + other, dp)}, device_id_type=MESH,
        )
        made.start()
        most_copies.append(made)
    ids = tokens - here * vocab
    if table_rows != rows:
        ids = jnp.where(ids >= 0, ids // rows * table_rows + ids % rows, 0)
    ids_ref[...] = ids
    entry = lax.broadcasted_iota(jnp.int32, (room, TEXT), 0)

    def listed(slot):
        chosen = entry == key_ref[pl.ds(slot, 1), :]
        return jnp.sum(jnp.where(chosen, ids_ref[pl.ds(slot, 1), :] + 1, 0), -1, keepdims=True) - 1

    turns = [lax.rem(here + other, mp) for other in range(1, mp)] + [here]
    lists = [listed(slot) for slot in turns]
    columns = jnp.concatenate([listed(slot) for slot in range(mp)], 0)
    all_room = room * mp
    corner = lax.broadcasted_iota(jnp.int32, (all_room, all_room), 0) == lax.broadcasted_iota(
        jnp.int32, (all_room, all_room), 1
    )
    ids_out[...] = column_sum(jnp.where(corner, columns, 0))

    for step in range(depth):
        for piece in range(2):
            wait(piece, step)
            if step < depth - 1:
                start(piece, step + 1)
        if step == depth - 2:
            for piece in range(2, len(pieces)):
                start(piece, 0)
    put(table_buf, table_out)

    word_copies = []
    for turn in range(0, mp, 2):
        wanted = jnp.concatenate(lists[turn : turn + 2], 0)
        column = lax.broadcasted_iota(jnp.int32, (2 * room, dp * table_rows), 1)
        hot = jnp.where(column == wanted, 1.0, 0.0).astype(LOW)
        found = mm(hot, table_buf[...].reshape(dp * table_rows, D), NN).astype(LOW)
        for part in range(2):
            slot = turns[turn + part]
            rows_of = found[part * room : (part + 1) * room]
            if turn + part == mp - 1:
                got[here] = rows_of
                continue
            packed[turn + part] = rows_of
            made = pltpu.make_async_remote_copy(
                src_ref=packed.at[turn + part], dst_ref=got.at[here],
                send_sem=word_send.at[turn + part], recv_sem=word_recv.at[turn + part],
                device_id={"mp": slot}, device_id_type=MESH,
            )
            made.start()
            word_copies.append(made)

    def advance(step):
        for piece in range(2, len(pieces)):
            wait(piece, step)
            if step < depth - 1:
                start(piece, step + 1)

    advance(0)
    for other in range(1, mp):
        source = lax.rem(here + mp - other, mp)
        pltpu.make_async_copy(got.at[source], got.at[source], word_recv.at[other - 1]).wait()
    across = jnp.sum(jnp.where(first == second, place, 0), -1, keepdims=True)
    column = lax.broadcasted_iota(jnp.int32, (TEXT, all_room), 1)
    hot = jnp.where(column == across, 1.0, 0.0).astype(LOW)
    word_out[...] = mm(hot, got[...].reshape(all_room, D), NN).astype(LOW)
    for step in range(1, depth):
        advance(step)
    for other in range(1, dp):
        source = lax.rem(me + dp - other, dp)
        pltpu.make_async_copy(
            most_ref.at[source], most_ref.at[source], most_recv.at[other]
        ).wait()
    most = most_ref[0]
    for part in range(1, dp):
        most = jnp.maximum(most, most_ref[part])
    most_out[...] = most[0:1, 0:1]
    row, lane = plan.box_slot(plan.box_parts)
    for part in range(dp):
        small_out[:, part * cut : (part + 1) * cut] = shared_buf[
            part, row : row + 24, lane : lane + cut
        ].astype(WIDE)
    for part in range(4):
        put(shared_buf.at[:, pl.ds(part * plan.proj, plan.proj)], proj_out.at[part])
    put(shared_buf.at[:, pl.ds(plan.places_at, plan.places)], places_out)
    put(shared_buf.at[:, pl.ds(plan.visual_at, plan.visual)], visual_out)
    for part in range(plan.box_parts):
        at, shift = plan.box_slot(part)
        put(
            shared_buf.at[:, pl.ds(at, 32), pl.ds(shift, LANES)],
            boxes_out.at[part // pieces_box, :, pl.ds(32 * (part % pieces_box), 32)],
        )
    for part in range(2):
        at, shift = ffn_slot(part, 0, ffn_rows, wide)
        put(ffn_buf.at[:, pl.ds(at, ffn_rows), pl.ds(shift, wide)], ffn_out.at[part])
    for made in started:
        made.wait_send()
    for made in word_copies + most_copies:
        made.wait_send()
    for made in outs:
        made.wait()


def word_room(mp):
    return pad_up(TEXT // mp * 11 // 8, 16)


def gather_weights(plan, word, proj, boxes, places, visual, small, ffn, tokens):
    dp, mp = plan.dp, plan.mp
    table_rows, ffn_rows, wide = pad_up(word.shape[0], 32), pad_up(ffn.shape[1], 16), ffn.shape[2]
    ffn_all = 2 * ffn_rows * wide // D
    room = word_room(mp)
    anywhere = pl.BlockSpec(memory_space=pl.ANY)
    vmem = pl.BlockSpec(memory_space=pltpu.VMEM)
    dma = pltpu.SemaphoreType.DMA
    shape = jax.ShapeDtypeStruct

    def body(*refs):
        gather_kernel(plan, table_rows, refs)

    return pl.pallas_call(
        body,
        out_shape=(
            shape((dp, table_rows, D), LOW), shape((4, dp, plan.proj, D), LOW),
            shape((4, dp, plan.box, LANES), LOW), shape((dp, plan.places, D), LOW),
            shape((dp, plan.visual, D), LOW), shape((2, dp, ffn_rows, wide), LOW),
            shape((TEXT, D), LOW), shape((24, D), WIDE), shape((1, TEXT), jnp.int32),
            shape((1, mp * room), jnp.int32), shape((1, 1), WIDE),
        ),
        in_specs=[vmem] * 8,
        out_specs=(anywhere,) * 6 + (vmem,) * 5,
        scratch_shapes=[
            pltpu.VMEM((dp, table_rows, D), LOW),
            pltpu.VMEM((dp, plan.shared, D), LOW),
            pltpu.VMEM((dp, ffn_all, D), LOW),
            pltpu.VMEM((mp - 1, room, D), LOW),
            pltpu.VMEM((mp, room, D), LOW),
            pltpu.VMEM((mp, TEXT), jnp.int32),
            pltpu.VMEM((mp, TEXT), jnp.int32),
            pltpu.VMEM((dp, 8, LANES), WIDE),
            dma((plan.box_parts + 10,)),
            dma((5, 2, dp - 1)),
            dma((5, 2, dp - 1)),
            dma((mp - 1,)),
            dma((mp - 1,)),
            dma((dp,)),
            dma((dp,)),
        ],
        compiler_params=pltpu.CompilerParams(
            collective_id=1, has_side_effects=True, vmem_limit_bytes=56 * 2**20
        ),
        name="gather_weights",
    )(word, proj, boxes, places, visual, small, ffn, tokens)


ROWS = 576
KINDS = ((6, 3), (0, 4), (3, 4))


def token_info(text_box, segments, alive_text, mask_pos):
    boxes = jnp.concatenate([text_box, grid_boxes()], 0)
    visual = GRID * GRID
    places = jnp.concatenate([jnp.arange(TEXT), jnp.arange(visual)]).astype(jnp.int32)
    owner = jnp.concatenate([segments, jnp.full((visual,), -1, jnp.int32)])
    alive = jnp.concatenate([alive_text, jnp.ones((visual,), jnp.int32)])
    columns = [
        boxes[:, 0], boxes[:, 1], boxes[:, 2], boxes[:, 3], boxes[:, 3] - boxes[:, 1],
        boxes[:, 2] - boxes[:, 0], places, owner, alive,
    ]
    slots = jnp.pad(mask_pos, (0, TEXT + visual - mask_pos.shape[0]))
    rows = jnp.stack(columns + [slots] + [jnp.zeros_like(places)] * 6)
    return jnp.pad(rows, ((0, 0), (0, ROWS - TEXT - visual)))


def edge_hot():
    entry = lax.broadcasted_iota(jnp.int32, (D, LANES), 0)
    place = lax.broadcasted_iota(jnp.int32, (D, LANES), 1)
    first = jnp.clip(place - NB // 2, 0, NB - 1) * H
    return jnp.where((entry >= first) & (entry < first + H), 1.0, 0.0).astype(LOW)


def head_mask():
    entry = lax.broadcasted_iota(jnp.int32, (16, D), 1)
    return lax.rem(entry, H) == lax.broadcasted_iota(jnp.int32, (16, D), 0)


def edge_rows(small_ref, kind):
    first = 10 + FF // D
    row = small_ref[first + kind : first + kind + 1, :]
    return mm(jnp.where(head_mask(), row, 0.0).astype(LOW), edge_hot(), NN)


def edge_rows_back(grad):
    high = grad.astype(LOW)
    low = (grad - high.astype(WIDE)).astype(LOW)
    hot = edge_hot()
    return column_sum(jnp.where(head_mask(), mm(high, hot, NT) + mm(low, hot, NT), 0.0))


def key_hot(rows_ref, kind):
    column, shift = KINDS[kind]
    coarse_row = jnp.right_shift(rows_ref[column : column + 1, :], shift)
    place = lax.broadcasted_iota(jnp.int32, (2 * NB, ROWS), 0)
    first = jnp.where(place == coarse_row, 1.0, 0.0).astype(LOW)
    second = jnp.where(place == coarse_row + NB, 1.0, 0.0).astype(LOW)
    return first, second


def below_of(rows_ref, slot_ref, kind):
    column, shift = KINDS[kind]
    mask = 2**shift - 1
    rest_key = jnp.bitwise_and(rows_ref[column : column + 1, :], mask)
    rest_slot = jnp.bitwise_and(slot_ref[:, column : column + 1], mask)
    return rest_key < rest_slot


def take_slots(slots, pos_ref, pairs):
    def body(index, carry):
        at = pos_ref[index]
        for source, target in pairs:
            target[pl.ds(index, 1), :] = source[pl.ds(at, 1), :]
        return carry

    lax.fori_loop(0, slots, body, 0)


def half_mask(rows):
    slots = rows // 2
    row = lax.broadcasted_iota(jnp.int32, (rows, LANES), 0)
    lane = lax.broadcasted_iota(jnp.int32, (rows, LANES), 1)
    return (row < slots) == (lane < HD)


def pair_rows(value):
    both = jnp.concatenate([value, value], 0)
    return jnp.where(half_mask(both.shape[0]), both, jnp.zeros((), both.dtype))


def pair_lanes(value):
    slots = value.shape[0] // 2
    lane = lax.broadcasted_iota(jnp.int32, (slots, LANES), 1)
    return jnp.where(lane < HD, value[:slots], value[slots:])


def front_kernel(
    pos_ref, word_ref, features_ref, places_ref, boxes_ref, visual_ref, small_ref,
    columns_ref, rows_ref, weights_in,
    mixed_ref, zero_ref, zero_low_ref, low_ref, plain_ref, scale_ref, query_ref, key_ref,
    value_ref, shares_ref,
    normed_ref, slot_ref, bias_ref, spread_ref, stacked_ref, weights_ref, load_sem,
):
    load = pltpu.make_async_copy(weights_in.at[0:3], weights_ref, load_sem)
    load.start()
    slots = mixed_ref.shape[0]
    row = lambda index: small_ref[index : index + 1, :]
    tile = 96
    lookups = (0, 1, 0, 1, 2, 3)

    normed_ref[0:TEXT, :] = word_ref[...].astype(WIDE) + places_ref[...].astype(WIDE)
    visual = features_ref.shape[0]
    normed_ref[TEXT : TEXT + visual, :] = mm(features_ref[...], visual_ref[...], NN) + places_ref[
        0:visual, :
    ].astype(WIDE)
    normed_ref[TEXT + visual : ROWS, :] = jnp.zeros((ROWS - TEXT - visual, D), WIDE)

    def embed(index, carry):
        where = pl.ds(pl.multiple_of(index * tile, 16), tile)
        place = lax.broadcasted_iota(jnp.int32, (tile, NBOX), 1)
        found = []
        for column, table in enumerate(lookups):
            hot = jnp.where(place == columns_ref[where, column : column + 1], 1.0, 0.0).astype(LOW)
            found.append(mm(hot, boxes_ref[table], NN))
        embedded = normed_ref[where, :] + jnp.concatenate(found, -1)
        plain, scale = norm_rows(embedded)
        normed = plain * row(0) + row(1)
        plain_ref[where, :] = plain
        scale_ref[where, :] = scale
        normed_ref[where, :] = normed
        low_ref[where, :] = normed.astype(LOW)
        return carry

    lax.fori_loop(0, ROWS // tile, embed, 0)
    take_slots(slots, pos_ref, ((normed_ref, zero_ref), (columns_ref, slot_ref)))
    low = low_ref[...]
    zero_low = zero_ref[...].astype(LOW)
    zero_low_ref[...] = zero_low
    load.wait()
    query_ref[...] = (mm(zero_low, weights_ref[0], NN) + row(2)).astype(LOW)
    key_ref[...] = mm(low, weights_ref[1], NN).astype(LOW)
    value_ref[...] = (mm(low, weights_ref[2], NN) + row(3)).astype(LOW)

    lane = lax.broadcasted_iota(jnp.int32, (NB, LANES), 1)
    for kind in range(3):
        column, shift = KINDS[kind]
        edges = edge_rows(small_ref, kind)
        for head in range(H):
            edge = jnp.broadcast_to(edges[head : head + 1, :], (NB, LANES))
            near = pltpu.roll(edge, NB, 1, stride=1, stride_axis=0)
            far = pltpu.roll(edge, 1, 1, stride=1, stride_axis=0)
            spread_ref[:, head * LANES : (head + 1) * LANES] = jnp.where(
                lane < NB, near, far
            ).astype(LOW)
        coarse_slot = jnp.right_shift(slot_ref[:, column : column + 1], shift)
        place = lax.broadcasted_iota(jnp.int32, (slots, NB), 1)
        hot = jnp.where(place == coarse_slot, 1.0, 0.0).astype(LOW)
        wide = mm(hot, spread_ref[...], NN).astype(LOW)
        for head in range(H):
            stacked_ref[head * slots : (head + 1) * slots, :] = wide[
                :, head * LANES : (head + 1) * LANES
            ]
        first, second = key_hot(rows_ref, kind)
        below = below_of(rows_ref, slot_ref, kind)

        def add(head, carry):
            where = pl.ds(pl.multiple_of(head * 2 * slots, 16), 2 * slots)
            rows = stacked_ref[where, :]
            both = jnp.concatenate([below, below], 0)
            found = jnp.where(both, mm(rows, second, NN), mm(rows, first, NN))
            bias_ref[where, :] = found if kind == 0 else bias_ref[where, :] + found
            return carry

        lax.fori_loop(0, H // 2, add, 0)

    owner = rows_ref[7:8, :]
    allowed = ((slot_ref[:, 7:8] == owner) | (owner < 0)) & (rows_ref[8:9, :] > 0)
    allowed = jnp.concatenate([allowed, allowed], 0)
    for pair in range(H // 2):
        lanes = slice(pair * LANES, (pair + 1) * LANES)
        rows = slice(pair * 2 * slots, (pair + 1) * 2 * slots)
        scores = mm(pair_rows(query_ref[:, lanes]), key_ref[:, lanes], NT) * 0.125
        scores = jnp.where(allowed, scores + bias_ref[rows, :], MASKED)
        powers = jnp.exp(scores - jnp.max(scores, -1, keepdims=True))
        shares = powers / jnp.sum(powers, -1, keepdims=True)
        shares_ref[rows, :] = shares
        mixed_ref[:, lanes] = pair_lanes(mm(shares.astype(LOW), value_ref[:, lanes], NN)).astype(LOW)


def front_step(pos, word, features, places, boxes, visual, small, columns, rows, weights):
    slots = pos.shape[0]
    vmem = pl.BlockSpec(memory_space=pltpu.VMEM)
    shape = jax.ShapeDtypeStruct
    return pl.pallas_call(
        front_kernel,
        out_shape=(
            shape((slots, D), LOW), shape((slots, D), WIDE), shape((slots, D), LOW),
            shape((ROWS, D), LOW), shape((ROWS, D), WIDE), shape((ROWS, 1), WIDE),
            shape((slots, D), LOW), shape((ROWS, D), LOW), shape((ROWS, D), LOW),
            shape((H * slots, ROWS), WIDE),
        ),
        in_specs=[pl.BlockSpec(memory_space=pltpu.SMEM)] + [vmem] * 8 + [pl.BlockSpec(memory_space=pl.ANY)],
        out_specs=(vmem,) * 10,
        scratch_shapes=[
            pltpu.VMEM((ROWS, D), WIDE),
            pltpu.VMEM((slots, 16), jnp.int32),
            pltpu.VMEM((H * slots, ROWS), WIDE),
            pltpu.VMEM((NB, H * LANES), LOW),
            pltpu.VMEM((H * slots, LANES), LOW),
            pltpu.VMEM((3, D, D), LOW),
            pltpu.SemaphoreType.DMA,
        ],
        compiler_params=pltpu.CompilerParams(vmem_limit_bytes=56 * 2**20),
        name="front_step",
    )(pos, word, features, places, boxes, visual, small, columns, rows, weights)


def back_kernel(plan, table_rows, ffn_rows, refs):
    (
        pos_ref, grad_zero_ref, grad_mixed_ref, shares_ref, query_ref, key_ref, value_ref,
        zero_low_ref, low_ref, plain_ref, scale_ref, features_ref, small_ref, columns_ref,
        rows_ref, weights_in, table_in, out_in, ffn_in, head_in, bias_in, tile_in, place_in, ids_in,
        shared_out, split_out, tile_out, word_out,
        slot_ref, score_ref, grad_query, grad_key, grad_value, grad_rows, grad_low, turned_ref,
        grad_slot, edges_ref, weights_ref,
        shared_acc, split_acc, shared_got, split_got, ring_got, ring_own, packed, words, small_all,
        tile_mp, tile_dp,
        load_sem, send_sem, recv_sem, ring_send, ring_recv, word_send, word_recv, tile_send,
        tile_recv,
    ) = refs
    dp, mp = plan.dp, plan.mp
    me, here = lax.axis_index("dp"), lax.axis_index("mp")
    depth, ring_depth = bits_of(dp), bits_of(mp)
    slots = grad_zero_ref.shape[0]
    loads = []
    if plan.proj * dp != D:
        shared_acc[...] = jnp.zeros(shared_acc.shape, LOW)

    def load(source, target):
        loads.append(pltpu.make_async_copy(source, target, load_sem.at[len(loads)]))
        loads[-1].start()

    load(out_in, shared_acc.at[:, pl.ds(3 * plan.proj, plan.proj)])
    for part in range(2):
        wide = ffn_in.shape[3]
        row, lane = ffn_slot(part, table_rows, ffn_rows, wide)
        load(ffn_in.at[part], split_acc.at[:, pl.ds(row, ffn_rows), pl.ds(lane, wide)])
    load(weights_in.at[0:3], weights_ref)
    load(table_in, split_acc.at[:, pl.ds(0, table_rows)])

    barrier = pltpu.get_barrier_semaphore()
    for other in range(1, dp):
        pl.semaphore_signal(
            barrier, 1, device_id={"dp": lax.rem(me + other, dp)}, device_id_type=MESH
        )
    for other in range(1, mp):
        pl.semaphore_signal(
            barrier, 1, device_id={"mp": lax.rem(here + other, mp)}, device_id_type=MESH
        )
    pl.semaphore_wait(barrier, dp + mp - 2)

    orders = ([0] + list(range(depth - 1, 0, -1)), list(range(depth)))
    out_at, rest = 3 * plan.proj, split_acc.shape[1] - table_rows
    pieces = (
        (shared_acc, shared_got, out_at, plan.proj),
        (shared_acc, shared_got, 0, out_at),
        (shared_acc, shared_got, plan.places_at, plan.shared - plan.places_at),
        (split_acc, split_got, table_rows, rest),
        (split_acc, split_got, 0, table_rows // 2),
        (split_acc, split_got, table_rows // 2, table_rows // 2),
    )

    def chunk(order, step, free, away):
        index = 0
        for place, bit in enumerate(order):
            mine = (me // 2**bit) % 2
            if place < step or (place == step and not away):
                index = index + mine * 2**bit
            elif place == step:
                index = index + (1 - mine) * 2**bit
            else:
                index = index + ((free >> (place - step - 1)) & 1) * 2**bit
        return index

    def slot_base(step):
        return sum(2 ** (depth - 1 - s) for s in range(step))

    def send_one(piece, stream, step, free):
        acc, got, first, rows = pieces[piece]
        order = orders[stream]
        pltpu.make_async_remote_copy(
            src_ref=acc.at[chunk(order, step, free, True), pl.ds(first, rows), lanes_of(stream)],
            dst_ref=got.at[slot_base(step) + free, pl.ds(first, rows), lanes_of(stream)],
            send_sem=send_sem.at[piece, stream, step],
            recv_sem=recv_sem.at[piece, stream, step],
            device_id={"dp": flip(me, order[step])},
            device_id_type=MESH,
        ).start()

    def send(piece, step):
        for stream in range(2):
            for free in range(2 ** (depth - 1 - step)):
                send_one(piece, stream, step, free)

    def wait_bytes(piece, stream, step, sem):
        acc, got, first, rows = pieces[piece]
        count = 2 ** (depth - 1 - step)
        where = got.at[pl.ds(slot_base(step), count), pl.ds(first, rows), lanes_of(stream)]
        pltpu.make_async_copy(where, where, sem.at[piece, stream, step]).wait()

    def add(piece, stream, step):
        acc, got, first, rows = pieces[piece]
        order = orders[stream]
        wait_bytes(piece, stream, step, recv_sem)
        tile = row_tile(rows)
        last = step == depth - 1
        for free in range(2 ** (depth - 1 - step)):
            kept = chunk(order, step, free, False)

            def body(index, carry):
                at = pl.multiple_of(first + index * tile, 16)
                where = pl.ds(at, tile)
                total = acc[kept, where, lanes_of(stream)].astype(WIDE) + got[
                    slot_base(step) + free, where, lanes_of(stream)
                ].astype(WIDE)
                if last and acc is split_acc:
                    split_out[where, lanes_of(stream)] = total
                elif last:
                    ring_own[0, where, lanes_of(stream)] = total.astype(LOW)
                else:
                    acc[kept, where, lanes_of(stream)] = total.astype(LOW)
                return carry

            lax.fori_loop(0, rows // tile, body, 0)

    ring_orders = (list(range(ring_depth)), list(range(ring_depth - 1, -1, -1)))

    def ring_copy(piece, stream, step):
        where = pl.ds(pieces[piece][2], pieces[piece][3])
        return pltpu.make_async_remote_copy(
            src_ref=ring_own.at[step, where, lanes_of(stream)],
            dst_ref=ring_got.at[step, where, lanes_of(stream)],
            send_sem=ring_send.at[piece, stream, step],
            recv_sem=ring_recv.at[piece, stream, step],
            device_id={"mp": flip(here, ring_orders[stream][step])},
            device_id_type=MESH,
        )

    def ring_step(piece, step):
        first, rows = pieces[piece][2:]
        for stream in range(2):
            ring_copy(piece, stream, step).wait_recv()
            tile = row_tile(rows)

            def body(index, carry):
                where = pl.ds(pl.multiple_of(first + index * tile, 16), tile)
                total = ring_own[step, where, lanes_of(stream)].astype(WIDE) + ring_got[
                    step, where, lanes_of(stream)
                ].astype(WIDE)
                if step == ring_depth - 1:
                    shared_out[where, lanes_of(stream)] = total
                else:
                    ring_own[step + 1, where, lanes_of(stream)] = total.astype(LOW)
                return carry

            lax.fori_loop(0, rows // tile, body, 0)
            if step < ring_depth - 1:
                ring_copy(piece, stream, step + 1).start()

    def advance(piece, step):
        for stream in range(2):
            add(piece, stream, step)
            if step < depth - 1:
                for free in range(2 ** (depth - 2 - step)):
                    send_one(piece, stream, step + 1, free)
            elif piece < 3:
                ring_copy(piece, stream, 0).start()

    room = words.shape[1]

    def scatter(index):
        local = ids_in[...] - index * table_rows
        entry = lax.broadcasted_iota(jnp.int32, (table_rows, mp * room), 0)
        hot = jnp.where(entry == local, 1.0, 0.0).astype(LOW)
        where = (index, pl.ds(0, table_rows))
        total = split_acc[where].astype(WIDE) + mm(hot, words[...].reshape(mp * room, D), NN)
        split_acc[where] = total.astype(LOW)

    count = 2 ** (depth - 1)
    other_core, own_core = 1 - me % 2, me % 2

    def scatter_other(index, carry):
        scatter(other_core + 2 * index)
        return carry

    def scatter_own(index, carry):
        scatter(own_core + 2 * index)
        return carry

    for copy in loads[:3]:
        copy.wait()
    send(0, 0)
    send(3, 0)

    take_slots(slots, pos_ref, ((columns_ref, slot_ref),))
    for pair in range(H // 2):
        lanes = slice(pair * LANES, (pair + 1) * LANES)
        rows = slice(pair * 2 * slots, (pair + 1) * 2 * slots)
        grad_mixed = pair_rows(grad_mixed_ref[:, lanes])
        shares = shares_ref[rows, :]
        grad_value[:, lanes] = mm(shares.astype(LOW), grad_mixed, TN).astype(LOW)
        grad_shares = mm(grad_mixed, value_ref[:, lanes], NT)
        scores = shares * (grad_shares - jnp.sum(shares * grad_shares, -1, keepdims=True))
        scores = scores.astype(LOW)
        score_ref[rows, :] = scores
        grad_query[:, lanes] = pair_lanes(mm(scores, key_ref[:, lanes], NN) * 0.125).astype(LOW)
        grad_key[:, lanes] = (mm(scores, pair_rows(query_ref[:, lanes]), TN) * 0.125).astype(LOW)
    advance(0, 0)
    advance(3, 0)

    loads[3].wait()
    grad_slot[...] = grad_zero_ref[...] + mm(grad_query[...], weights_ref[0], NT)
    entry = lax.broadcasted_iota(jnp.int32, (ROWS, slots), 0)
    put = jnp.where(entry == rows_ref[9:10, 0:slots], 1.0, 0.0).astype(LOW)
    high = grad_slot[...].astype(LOW)
    small_part = (grad_slot[...] - high.astype(WIDE)).astype(LOW)
    grad_rows[...] = (
        mm(grad_key[...], weights_ref[1], NT)
        + mm(grad_value[...], weights_ref[2], NT)
        + (mm(put, high, NN) + mm(put, small_part, NN))
    )
    gain = small_ref[0:1, :]
    tile = 96

    def normed_back(index, carry):
        where = pl.ds(pl.multiple_of(index * tile, 16), tile)
        grad, plain = grad_rows[where, :], plain_ref[where, :]
        value = norm_back(grad, plain, scale_ref[where, :], gain)
        grad_rows[where, :] = value
        grad_low[where, :] = value.astype(LOW)
        return carry[0] + column_sum(grad * plain), carry[1] + column_sum(grad)

    blank = jnp.zeros((1, D), WIDE)
    gains, shifts = lax.fori_loop(0, ROWS // tile, normed_back, (blank, blank))
    small_all[0:1, :] = gains
    small_all[1:2, :] = shifts

    keep_words = pltpu.make_async_copy(grad_low.at[0:TEXT], word_out, load_sem.at[5])
    keep_words.start()
    entry = lax.broadcasted_iota(jnp.int32, (mp * room, TEXT), 0)
    hot = jnp.where(entry == place_in[...], 1.0, 0.0).astype(LOW)
    packed[...] = mm(hot, grad_low[0:TEXT, :], NN).astype(LOW).reshape(mp, room, D)
    word_copies = []
    for other in range(1, mp):
        target = lax.rem(here + other, mp)
        word_copies.append(
            pltpu.make_async_remote_copy(
                src_ref=packed.at[target], dst_ref=words.at[here],
                send_sem=word_send.at[other - 1], recv_sem=word_recv.at[other - 1],
                device_id={"mp": target}, device_id_type=MESH,
            )
        )
        word_copies[-1].start()
    words[here] = packed[here]

    rows = D // dp
    for part, (left, right) in enumerate(
        ((zero_low_ref, grad_query), (low_ref, grad_key), (low_ref, grad_value))
    ):
        grad = mm(left[...], right[...], TN).reshape(dp, rows, D)
        first = part * plan.proj
        shared_acc[:, first : first + rows, :] = grad.astype(LOW)
    send(1, 0)
    advance(0, 1)
    advance(3, 1)

    extra, rows = ROWS - TEXT, TEXT // dp
    grad_rows[0:extra, :] = grad_rows[0:extra, :] + grad_rows[TEXT:ROWS, :]
    first = plan.places_at
    shared_acc[:, first : first + rows, :] = grad_rows[0:TEXT, :].reshape(dp, rows, D).astype(LOW)
    visual, rows, first = features_ref.shape[0], VCH // dp, plan.visual_at
    grad = mm(features_ref[...], grad_low[TEXT : TEXT + visual, :], TN)
    shared_acc[:, first : first + rows, :] = grad.reshape(dp, rows, D).astype(LOW)
    block = max(plan.box, 256)
    chunks, pieces_box = block // plan.box, plan.box // 32

    def table(index, carry):
        entry = lax.broadcasted_iota(jnp.int32, (block, ROWS), 0) + index * block
        found = []
        for column in range(6):
            hot = jnp.where(entry == rows_ref[column : column + 1, :], 1.0, 0.0).astype(LOW)
            found.append(mm(hot, grad_low[:, column * LANES : (column + 1) * LANES], NN))
        for number, grad in enumerate((found[0] + found[2], found[1] + found[3], *found[4:])):
            for part in range(block // 32):
                at, lane = plan.box_slot(number * pieces_box + part % pieces_box)
                shared_acc[index * chunks + part // pieces_box, at : at + 32, lane : lane + LANES] = (
                    grad[part * 32 : part * 32 + 32].astype(LOW)
                )
        return carry

    lax.fori_loop(0, NBOX // block, table, 0)
    advance(1, 0)

    lane = lax.broadcasted_iota(jnp.int32, (NB, LANES), 1)
    for kind in range(3):
        column, shift = KINDS[kind]
        first, second = key_hot(rows_ref, kind)
        below = below_of(rows_ref, slot_ref, kind)
        coarse_slot = jnp.right_shift(slot_ref[:, column : column + 1], shift)
        place = lax.broadcasted_iota(jnp.int32, (slots, NB), 1)
        hot = jnp.where(place == NB - 1 - coarse_slot, 1.0, 0.0).astype(LOW)

        def collect(pair, carry):
            where = pl.ds(pl.multiple_of(pair * 2 * slots, 16), 2 * slots)
            both = jnp.concatenate([below, below], 0)
            scores = score_ref[where, :]
            none = jnp.zeros((), LOW)
            found = mm(jnp.where(both, none, scores), first, NT) + mm(
                jnp.where(both, scores, none), second, NT
            )
            turned_ref[where, :] = found.astype(LOW)
            return carry

        lax.fori_loop(0, H // 2, collect, 0)
        for head in range(H):
            part = mm(hot, turned_ref[head * slots : (head + 1) * slots, :], TN)
            near = pltpu.roll(jnp.where(lane < NB, part, 0.0), 1, 1, stride=1, stride_axis=0)
            far = pltpu.roll(jnp.where(lane < NB, 0.0, part), NB, 1, stride=1, stride_axis=0)
            edges_ref[head : head + 1, :] = column_sum(near + far)
        edges_ref[H:16, :] = jnp.zeros((16 - H, LANES), WIDE)
        small_all[14 + kind : 15 + kind, :] = edge_rows_back(edges_ref[...])

    hidden = bias_in.shape[1]
    start = here * hidden
    small_all[2:3, :] = column_sum(grad_query[...].astype(WIDE))
    small_all[3:4, :] = column_sum(grad_value[...].astype(WIDE))
    small_all[4:10, :] = head_in[4:10, :]
    small_all[10:14, :] = jnp.zeros((4, D), WIDE)
    small_all[
        pl.ds(10 + start // D, 1), pl.ds(pl.multiple_of(lax.rem(start, D), LANES), hidden)
    ] = bias_in[...]
    cut = D // dp
    row, lane = plan.box_slot(plan.box_parts)
    shared_acc[:, pl.ds(row, 32), pl.ds(lane, LANES)] = jnp.zeros((dp, 32, LANES), LOW)
    for part in range(dp):
        shared_acc[part, row : row + VROWS, lane : lane + cut] = small_all[
            0:VROWS, part * cut : (part + 1) * cut
        ].astype(LOW)
    for part in range(plan.box_parts + 1, 6 * (plan.shared - plan.box_at) // 32):
        row, lane = plan.box_slot(part)
        shared_acc[:, pl.ds(row, 32), pl.ds(lane, LANES)] = jnp.zeros((dp, 32, LANES), LOW)
    send(2, 0)
    advance(0, 2)
    advance(3, 2)
    advance(2, 0)
    loads[4].wait()
    for other in range(1, mp):
        source = lax.rem(here + mp - other, mp)
        pltpu.make_async_copy(words.at[source], words.at[source], word_recv.at[other - 1]).wait()
    lax.fori_loop(0, count, scatter_other, 0)
    send(4, 0)
    send(5, 0)
    advance(1, 1)
    lax.fori_loop(0, count, scatter_own, 0)
    for step in range(2, depth - 1):
        for piece in range(4):
            if piece != 2:
                advance(piece, step)
    advance(2, 1)
    advance(1, depth - 1)
    for step in range(2, depth - 1):
        advance(2, step)
    advance(4, 0)
    advance(5, 0)
    advance(2, depth - 1)
    for step in range(max(depth - 1, ring_depth)):
        if step < ring_depth:
            ring_step(0, step)
        if step < depth - 1:
            advance(4, step + 1)
            advance(5, step + 1)
        if step < ring_depth:
            ring_step(1, step)
            ring_step(2, step)

    def squares(ref, rows):
        tile = row_tile(rows)

        def body(index, total):
            values = ref[pl.ds(pl.multiple_of(index * tile, 16), tile), :]
            return total + jnp.sum((values * values).reshape(tile // 8, 8, D), 0)

        total = lax.fori_loop(0, rows // tile, body, jnp.zeros((8, D), WIDE))
        folded = total[:, 0:LANES]
        for part in range(1, D // LANES):
            folded = folded + total[:, part * LANES : (part + 1) * LANES]
        return folded

    folded = squares(shared_out, plan.shared) * (1.0 / mp) + squares(split_out, split_out.shape[0])
    tile_mp[here, 0] = folded
    tile_mp[here, 1] = tile_in[...]

    def exchange(buffer, axis, index, count, base):
        copies = []
        for other in range(1, count):
            copies.append(
                pltpu.make_async_remote_copy(
                    src_ref=buffer.at[index],
                    dst_ref=buffer.at[index],
                    send_sem=tile_send.at[base + other],
                    recv_sem=tile_recv.at[base + other],
                    device_id={axis: lax.rem(index + other, count)},
                    device_id_type=MESH,
                )
            )
        for copy in copies:
            copy.start()
        for other in range(1, count):
            source = lax.rem(index + count - other, count)
            pltpu.make_async_copy(
                buffer.at[source], buffer.at[source], tile_recv.at[base + other]
            ).wait()
        return copies

    pending = exchange(tile_mp, "mp", here, mp, 0)
    total = tile_mp[0]
    for index in range(1, mp):
        total = total + tile_mp[index]
    tile_dp[me] = total
    pending = pending + exchange(tile_dp, "dp", me, dp, mp)
    total = tile_dp[0]
    for index in range(1, dp):
        total = total + tile_dp[index]
    tile_out[...] = total
    for copy in pending:
        copy.wait_send()
    keep_words.wait()
    for copy in word_copies:
        copy.wait_send()
    for piece in range(len(pieces)):
        for stream in range(2):
            for step in range(depth):
                wait_bytes(piece, stream, step, send_sem)
    for piece in range(3):
        for stream in range(2):
            for step in range(ring_depth):
                ring_copy(piece, stream, step).wait_send()


def back_step(
    plan, pos, grad_zero, grad_mixed, shares, query, key, value, zero_low, low, plain, scale,
    features, small, columns, rows, weights, table, out, ffn, head, bias, tile, place, ids,
):
    dp, mp = plan.dp, plan.mp
    slots = pos.shape[0]
    table_rows, ffn_rows = table.shape[1], ffn.shape[2]
    split = table_rows + 2 * ffn_rows * ffn.shape[3] // D
    depth, ring_depth = bits_of(dp), bits_of(mp)
    anywhere = pl.BlockSpec(memory_space=pl.ANY)
    vmem = pl.BlockSpec(memory_space=pltpu.VMEM)
    dma = pltpu.SemaphoreType.DMA
    low_scratch = lambda *shape: pltpu.VMEM(shape, LOW)
    wide_scratch = lambda *shape: pltpu.VMEM(shape, WIDE)

    def body(*refs):
        back_kernel(plan, table_rows, ffn_rows, refs)

    return pl.pallas_call(
        body,
        out_shape=(
            jax.ShapeDtypeStruct((plan.shared, D), WIDE),
            jax.ShapeDtypeStruct((split, D), WIDE),
            jax.ShapeDtypeStruct((2, 8, LANES), WIDE),
            jax.ShapeDtypeStruct((TEXT, D), LOW),
        ),
        in_specs=[pl.BlockSpec(memory_space=pltpu.SMEM)]
        + [vmem] * 14
        + [anywhere] * 4
        + [vmem] * 5,
        out_specs=(vmem, vmem, vmem, anywhere),
        scratch_shapes=[
            pltpu.VMEM((slots, 16), jnp.int32),
            low_scratch(H * slots, ROWS),
            low_scratch(slots, D),
            low_scratch(ROWS, D),
            low_scratch(ROWS, D),
            wide_scratch(ROWS, D),
            low_scratch(ROWS, D),
            low_scratch(H * slots, LANES),
            wide_scratch(slots, D),
            wide_scratch(16, LANES),
            low_scratch(3, D, D),
            low_scratch(dp, plan.shared, D),
            low_scratch(dp, split, D),
            low_scratch(dp - 1, plan.shared, D),
            low_scratch(dp - 1, split, D),
            low_scratch(ring_depth, plan.shared, D),
            low_scratch(ring_depth, plan.shared, D),
            low_scratch(mp, word_room(mp), D),
            low_scratch(mp, word_room(mp), D),
            wide_scratch(24, D),
            wide_scratch(mp, 2, 8, LANES),
            wide_scratch(dp, 2, 8, LANES),
            dma((6,)),
            dma((6, 2, depth)),
            dma((6, 2, depth)),
            dma((3, 2, ring_depth)),
            dma((3, 2, ring_depth)),
            dma((mp - 1,)),
            dma((mp - 1,)),
            dma((mp + dp,)),
            dma((mp + dp,)),
        ],
        compiler_params=pltpu.CompilerParams(
            collective_id=5, has_side_effects=True, vmem_limit_bytes=62 * 2**20
        ),
        name="back_step",
    )(
        pos, grad_zero, grad_mixed, shares, query, key, value, zero_low, low, plain, scale,
        features, small, columns, rows, weights, table, out, ffn, head, bias, tile, place, ids,
    )


def on_device(
    tokens, text_box, segments, alive_text, features, mask_pos, mask_label, mask_valid, *states
):
    (projections, box_tables, position_table, visual_proj, small_params, word_table, feedforward) = (
        states[::3]
    )
    dp, mp = lax.axis_size("dp"), lax.axis_size("mp")
    plan = Plan(dp, mp)
    (
        table_parts, proj_parts, box_parts, place_parts, visual_parts, ffn_parts, word, small,
        places, ids, most,
    ) = (
        gather_weights(
            plan, word_table, projections, box_tables, position_table, visual_proj, small_params,
            feedforward, tokens,
        )
    )

    def joined(parts, rows):
        parts = parts[..., :rows, :]
        return parts.reshape(parts.shape[:-3] + (dp * rows, parts.shape[-1]))

    work_table = joined(table_parts, word_table.shape[0])
    work_proj = joined(proj_parts, D // dp)
    work_boxes = joined(box_parts, NBOX // dp)
    work_places = joined(place_parts, TEXT // dp)
    work_visual = joined(visual_parts, VCH // dp)
    work_ffn = joined(ffn_parts, D // dp)
    vocab_shard = work_table.shape[0]
    room = word_room(mp)
    crowded = most[0, 0] > room

    def local_words():
        local_ids = tokens - lax.axis_index("mp") * vocab_shard
        inside = (local_ids >= 0) & (local_ids < vocab_shard)
        return inside, jnp.clip(local_ids, 0, vocab_shard - 1)

    def exchange_words(state):
        inside, index = local_words()
        found = jnp.where(inside[..., None], jnp.take(work_table, index, axis=0), jnp.zeros((), LOW))
        return False, lax.psum_scatter(found, "mp", scatter_dimension=0, tiled=True)[0]

    word = lax.while_loop(lambda state: state[0], exchange_words, (crowded, word))[1]
    info = token_info(text_box[0], segments[0], alive_text[0], mask_pos)
    columns = info.T
    (
        mixed, slot_zero, slot_low, normed_low, plain, scale, queries, keys, values, shares,
    ) = front_step(
        mask_pos, word, features, work_places, work_boxes, work_visual, small, columns, info,
        work_proj,
    )
    (
        grad_slot, grad_mixed, grad_out_weight, grad_ffn, grad_table, head_rows, grad_ffn_bias,
        own_tile,
    ) = head_step(
        mp, mixed, slot_zero, work_proj, small, work_ffn, work_table,
        jnp.stack([mask_label, mask_valid]),
    )
    def split_rows(part):
        rows = part.shape[-2] // dp
        part = part.astype(LOW).reshape(part.shape[:-2] + (dp, rows, part.shape[-1]))
        extra = [(0, 0)] * (part.ndim - 2) + [(0, pad_up(rows, 16) - rows), (0, 0)]
        return jnp.pad(part, extra) if extra[-2][1] else part

    table_split, ffn_split = split_rows(grad_table), split_rows(grad_ffn)
    shared_sum, split_sum, totals, grad_word = back_step(
        plan, mask_pos, grad_slot, grad_mixed, shares, queries, keys, values, slot_low, normed_low,
        plain, scale, features, small, columns, info, work_proj, table_split,
        split_rows(grad_out_weight), ffn_split, head_rows, grad_ffn_bias, own_tile, places, ids,
    )
    def exchange_word_gradients(state):
        inside, index = local_words()
        shard = tokens // vocab_shard
        same = (shard[..., None] == jnp.arange(mp)).astype(jnp.int32)
        rank = jnp.sum((jnp.cumsum(same, 1) - same) * same, -1)
        late = rank >= room
        own = lax.dynamic_index_in_dim(late, lax.axis_index("mp"), 0, False)
        sent = jnp.where(own[:, None], grad_word, jnp.zeros((), LOW))
        group = lax.all_gather(sent, "mp", axis=0).astype(WIDE)
        group = jnp.where((inside & late)[..., None], group, 0.0)
        extra = jnp.zeros((vocab_shard, D), WIDE).at[index].add(group)
        part = lax.psum_scatter(extra, "dp", scatter_dimension=0, tiled=True)
        split = state[1].at[: part.shape[0]].add(part)
        squares = jnp.sum(shared_sum * shared_sum) / mp + jnp.sum(split * split)
        squares = lax.psum(squares, ("dp", "mp"))
        return False, split, jnp.zeros_like(totals).at[0, 0, 0].set(squares).at[1].set(totals[1])

    _, split_sum, totals = lax.while_loop(
        lambda state: state[0], exchange_word_gradients, (crowded, split_sum, totals)
    )
    outputs = adam_update(
        plan, table_split.shape[1], ffn_split.shape[2], shared_sum, split_sum, totals, states
    )
    return tuple(outputs[:21]) + tuple(part.reshape(()) for part in outputs[21:])


def solution(mesh):
    in_specs = (
        P("dp", None),
        P(("dp", "mp"), None, None),
        P(("dp", "mp"), None),
        P(("dp", "mp"), None),
        P(("dp", "mp"), None),
        P(("dp", "mp")),
        P("dp"),
        P("dp"),
        P(None, "dp", None),
        P(None, "dp", None),
        P(None, "dp", None),
        P(None, "dp", None),
        P(None, "dp", None),
        P(None, "dp", None),
        P("dp", None),
        P("dp", None),
        P("dp", None),
        P("dp", None),
        P("dp", None),
        P("dp", None),
        P(None, "dp"),
        P(None, "dp"),
        P(None, "dp"),
        P(("mp", "dp"), None),
        P(("mp", "dp"), None),
        P(("mp", "dp"), None),
        P(None, "dp", "mp"),
        P(None, "dp", "mp"),
        P(None, "dp", "mp"),
    )
    out_specs = (
        P(None, "dp", None),
        P(None, "dp", None),
        P(None, "dp", None),
        P(None, "dp", None),
        P(None, "dp", None),
        P(None, "dp", None),
        P("dp", None),
        P("dp", None),
        P("dp", None),
        P("dp", None),
        P("dp", None),
        P("dp", None),
        P(None, "dp"),
        P(None, "dp"),
        P(None, "dp"),
        P(("mp", "dp"), None),
        P(("mp", "dp"), None),
        P(("mp", "dp"), None),
        P(None, "dp", "mp"),
        P(None, "dp", "mp"),
        P(None, "dp", "mp"),
        P(),
        P(),
        P(),
    )
    return jax.shard_map(
        on_device, mesh=mesh, in_specs=in_specs, out_specs=out_specs, check_vma=False
    )
```

```python
import jax
import jax.numpy as jnp
import numpy as np
from jax import lax
from jax.experimental import pallas as pl
from jax.experimental.pallas import tpu as pltpu
from jax.sharding import PartitionSpec as P

D = 768
H = 12
HD = 64
FF = 3072
NB = 64
GRID = 7
TEXT = 512
STEP = 10
VCH = 256
NBOX = 1024
VROWS = 17


MASKED = -1e30
CLIP = 0.005
BETA_ONE = 0.9
BETA_TWO = 0.999
EPSILON = 1e-08
DECAY = 0.01
RATES = (0.02, 0.03, 0.03, 0.04, 0.3, 0.05, 0.02)


def adam_step(weight, grad, first, second, rate):
    first = BETA_ONE * first + (1.0 - BETA_ONE) * grad
    second = BETA_TWO * second + (1.0 - BETA_TWO) * grad * grad
    fixed_first = first * (1.0 / (1.0 - BETA_ONE**STEP))
    fixed_second = second * (1.0 / (1.0 - BETA_TWO**STEP))
    weight = weight - rate * (fixed_first / (jnp.sqrt(fixed_second) + EPSILON) + DECAY * weight)
    return (weight, first, second)


MESH = pl.DeviceIdType.MESH
LOW = jnp.bfloat16
WIDE = jnp.float32
LANES = 128
HALF = D // 2


def pad_up(count, unit):
    return (count + unit - 1) // unit * unit


def bits_of(count):
    return count.bit_length() - 1


def flip(index, bit):
    return index + (1 - 2 * ((index // 2**bit) % 2)) * 2**bit


class Plan:
    def __init__(self, dp, mp):
        self.dp, self.mp = dp, mp
        self.proj = pad_up(D // dp, 16)
        self.places = pad_up(TEXT // dp, 16)
        self.visual = pad_up(VCH // dp, 16)
        self.box = NBOX // dp
        self.box_parts = 4 * (self.box // 32)
        self.places_at = 4 * self.proj
        self.visual_at = self.places_at + self.places
        self.box_at = self.visual_at + self.visual
        self.box_rows = 32 * ((self.box_parts + 6) // 6)
        self.shared = pad_up(self.box_at + self.box_rows, 32 * mp)

    def box_slot(self, part):
        return self.box_at + 32 * (part // 6), LANES * (part % 6)


def group_of(axis, index):
    return {axis: index}


def lanes_of(stream):
    return pl.ds(stream * HALF, HALF)


def ffn_slot(part, table_rows, ffn_rows, wide):
    return table_rows + part * wide // D * ffn_rows, part * wide % D


def row_tile(rows):
    return next(t for t in (48, 32, 16) if rows % t == 0)


def adam_kernel(plan, table_rows, ffn_rows, refs):
    shared_ref, split_ref, tile_ref = refs[:3]
    states, outs, scalars = refs[3:24], refs[24:45], refs[45:48]
    held, load_sem, store_sem = refs[48:69], refs[69], refs[70]
    order = (5, 6, 0, 1, 2, 3, 4)
    loads, stores = {}, []
    for index in order:
        for part in range(3 * index, 3 * index + 3):
            loads[part] = pltpu.make_async_copy(states[part], held[part], load_sem.at[part])
            loads[part].start()
    totals = tile_ref[...]
    count = totals[1, 1:2, 0:1]
    norm = jnp.sqrt(jnp.sum(totals[0], keepdims=True)) / count
    scale = jnp.minimum(1.0, CLIP / norm) / count
    scalars[0][...] = totals[1, 0:1, 0:1]
    scalars[1][...] = count
    scalars[2][...] = norm

    def update(index, where, grad):
        mine = held[3 * index : 3 * index + 3]
        weight, first, second = (ref[where] for ref in mine)
        for ref, value in zip(mine, adam_step(weight, grad * scale, first, second, RATES[index])):
            ref[where] = value

    def blocks(index, lead, source, at, lane=0, wide=D):
        rows = held[3 * index].shape[-2]
        tile = next(t for t in (32, 24, 16, 8) if rows % t == 0)

        def body(step, carry):
            here = pl.multiple_of(step * tile, 8)
            where = (pl.ds(here, tile), slice(None))
            grad = source[pl.ds(pl.multiple_of(at + here, 8), tile), pl.ds(lane, wide)]
            update(index, where if lead is None else (lead,) + where, grad)
            return carry

        lax.fori_loop(0, rows // tile, body, 0)

    pieces_box = plan.box // 32
    for index in order:
        for part in range(3 * index, 3 * index + 3):
            loads[part].wait()
        if index == 0:
            for part in range(4):
                blocks(0, part, shared_ref, part * plan.proj)
        elif index == 1:
            for part in range(plan.box_parts):
                row, lane = plan.box_slot(part)
                grad = shared_ref[pl.ds(row, 32), pl.ds(lane, LANES)]
                update(1, (part // pieces_box, pl.ds(32 * (part % pieces_box), 32)), grad)
        elif index == 2:
            blocks(2, None, shared_ref, plan.places_at)
        elif index == 3:
            blocks(3, None, shared_ref, plan.visual_at)
        elif index == 4:
            row, lane = plan.box_slot(plan.box_parts)
            grad = shared_ref[pl.ds(row, 32), pl.ds(lane, LANES)]
            update(4, (slice(None), slice(None)), grad[:VROWS, : held[12].shape[1]])
        elif index == 5:
            blocks(5, None, split_ref, 0)
        else:
            for part in range(2):
                wide = held[18].shape[2]
                row, lane = ffn_slot(part, table_rows, ffn_rows, wide)
                blocks(6, part, split_ref, row, lane, wide)
        for part in range(3 * index, 3 * index + 3):
            stores.append(pltpu.make_async_copy(held[part], outs[part], store_sem.at[part]))
            stores[-1].start()
    for store in stores:
        store.wait()


def adam_update(plan, table_rows, ffn_rows, shared, split, tile, states):
    vmem = pl.BlockSpec(memory_space=pltpu.VMEM)
    anywhere = pl.BlockSpec(memory_space=pl.ANY)
    scalar = jax.ShapeDtypeStruct((1, 1), WIDE)

    def body(*refs):
        adam_kernel(plan, table_rows, ffn_rows, refs)

    return pl.pallas_call(
        body,
        out_shape=tuple(jax.ShapeDtypeStruct(part.shape, WIDE) for part in states) + (scalar,) * 3,
        in_specs=[vmem] * 3 + [anywhere] * 21,
        out_specs=(anywhere,) * 21 + (vmem,) * 3,
        scratch_shapes=[pltpu.VMEM(part.shape, WIDE) for part in states]
        + [pltpu.SemaphoreType.DMA((21,)), pltpu.SemaphoreType.DMA((21,))],
        compiler_params=pltpu.CompilerParams(vmem_limit_bytes=58 * 2**20),
        name="adam_update",
    )(shared, split, tile, *states)


def combos(index, bits):
    found = [index]
    for bit in bits:
        found = found + [flip(one, bit) for one in found]
    return found


class Ring:
    def __init__(self, mp, sems):
        self.mp, self.here = mp, lax.axis_index("mp")
        self.send, self.recv = sems
        depth = bits_of(mp)
        self.depth = depth
        self.orders = (list(range(depth)), list(range(depth - 1, -1, -1)))
        self.started = []

    def barrier(self):
        barrier = pltpu.get_barrier_semaphore()
        for other in range(1, self.mp):
            pl.semaphore_signal(
                barrier, 1, device_id={"mp": lax.rem(self.here + other, self.mp)},
                device_id_type=MESH,
            )
        pl.semaphore_wait(barrier, self.mp - 1)

    def copy(self, source, target, number, stream, index, peer):
        made = pltpu.make_async_remote_copy(
            src_ref=source, dst_ref=target,
            send_sem=self.send.at[number, stream, index],
            recv_sem=self.recv.at[number, stream, index],
            device_id={"mp": peer}, device_id_type=MESH,
        )
        return made

    def gather_start(self, buffer, number, stream, step):
        order = self.orders[stream]
        peer = flip(self.here, order[step])
        for place, slot in enumerate(combos(self.here, order[:step])):
            part = buffer.at[slot, :, lanes_of(stream)]
            made = self.copy(part, part, number, stream, 2**step - 1 + place, peer)
            made.start()
            self.started.append(made)

    def gather_wait(self, buffer, number, stream, step):
        order = self.orders[stream]
        peer = flip(self.here, order[step])
        for place, slot in enumerate(combos(peer, order[:step])):
            part = buffer.at[slot, :, lanes_of(stream)]
            self.copy(part, part, number, stream, 2**step - 1 + place, peer).wait_recv()

    def gather(self, buffer, number):
        for stream in range(2):
            self.gather_start(buffer, number, stream, 0)
        for step in range(self.depth):
            for stream in range(2):
                self.gather_wait(buffer, number, stream, step)
                if step < self.depth - 1:
                    self.gather_start(buffer, number, stream, step + 1)

    def base(self, step):
        return sum(2 ** (self.depth - 1 - s) for s in range(step))

    def reduce_one(self, buffer, got, number, stream, step, place):
        order = self.orders[stream]
        peer = flip(self.here, order[step])
        slot = combos(peer, order[step + 1 :])[place]
        index = self.base(step) + place
        made = self.copy(
            buffer.at[slot, :, lanes_of(stream)],
            got.at[index, :, lanes_of(stream)],
            number, stream, index, peer,
        )
        made.start()
        self.started.append(made)

    def reduce_start(self, buffer, got, number, stream, step):
        for place in range(2 ** (self.depth - 1 - step)):
            self.reduce_one(buffer, got, number, stream, step, place)

    def reduce_wait(self, buffer, got, number, stream, step):
        order = self.orders[stream]
        peer = flip(self.here, order[step])
        for place, slot in enumerate(combos(self.here, order[step + 1 :])):
            index = self.base(step) + place
            part = got.at[index, :, lanes_of(stream)]
            self.copy(part, part, number, stream, index, peer).wait_recv()
            where = (slot, slice(None), lanes_of(stream))
            total = buffer[where].astype(WIDE) + got[index, :, lanes_of(stream)].astype(WIDE)
            buffer[where] = total.astype(buffer.dtype)

    def reduce_begin(self, buffer, got, number):
        for stream in range(2):
            self.reduce_start(buffer, got, number, stream, 0)

    def reduce_rest(self, buffer, got, number, between=()):
        between = list(between)
        for step in range(self.depth):
            if between:
                between.pop(0)()
            for stream in range(2):
                self.reduce_wait(buffer, got, number, stream, step)
                if step < self.depth - 1:
                    self.reduce_start(buffer, got, number, stream, step + 1)
        for rest in between:
            rest()

    def finish(self):
        for made in self.started:
            made.wait_send()


def mm(left, right, dims):
    return lax.dot_general(left, right, (dims, ((), ())), preferred_element_type=WIDE)


NN, NT, TN = ((1,), (0,)), ((1,), (1,)), ((0,), (0,))


def norm_rows(value):
    centred = value - jnp.mean(value, -1, keepdims=True)
    scale = lax.rsqrt(jnp.mean(centred * centred, -1, keepdims=True) + 1e-05)
    return centred * scale, scale


def norm_back(grad, plain, scale, gain):
    inner = grad * gain
    return scale * (
        inner
        - jnp.mean(inner, -1, keepdims=True)
        - plain * jnp.mean(inner * plain, -1, keepdims=True)
    )


def column_sum(value):
    return jnp.sum(value, 0, keepdims=True)


def halves_of(slots):
    first = pad_up(slots // 2, 16)
    return ((0, first), (first, slots - first))


def head_kernel(mp, vocab_tile, refs):
    (
        mixed_ref, zero_ref, weights_in, small_ref, ffn_ref, table_ref, marks_zero, marks_one,
        grad_zero_ref, grad_mixed_ref, grad_out_ref, grad_ffn_ref, grad_table_ref, rows_ref,
        bias_out, sums_ref,
        ffn, table, out_weight, *scratch,
    ) = refs
    load_sem, send_sem, recv_sem, stat_send, stat_recv = scratch[-5:]
    ring = Ring(mp, (send_sem, recv_sem))
    here = ring.here
    slots, vocab, hidden = mixed_ref.shape[0], table.shape[0], ffn.shape[2]
    load_ffn = pltpu.make_async_copy(ffn_ref, ffn, load_sem.at[0])
    load_table = pltpu.make_async_copy(table_ref, table, load_sem.at[1])
    load_out = pltpu.make_async_copy(weights_in.at[3], out_weight, load_sem.at[2])
    load_out.start()
    load_ffn.start()
    load_table.start()
    ring.barrier()
    row = lambda index: small_ref[index : index + 1, :]
    start = here * hidden
    bias = small_ref[
        pl.ds(10 + start // D, 1), pl.ds(pl.multiple_of(lax.rem(start, D), LANES), hidden)
    ]
    load_out.wait()
    load_ffn.wait()
    load_table.wait()
    kept = [{}, {}]
    waiting = []

    def gathering(buffer, number):
        for stream in range(2):
            ring.gather_start(buffer, number, stream, 0)
        for step in range(ring.depth):
            yield
            for stream in range(2):
                ring.gather_wait(buffer, number, stream, step)
                if step < ring.depth - 1:
                    ring.gather_start(buffer, number, stream, step + 1)

    def reducing(buffer, got, number):
        ring.reduce_begin(buffer, got, number)
        for step in range(ring.depth):
            yield
            for stream in range(2):
                ring.reduce_wait(buffer, got, number, stream, step)
                if step < ring.depth - 1:
                    ring.reduce_start(buffer, got, number, stream, step + 1)

    def run(part):
        first, count = halves_of(slots)[part]
        group = count * mp
        rows = slice(first, first + count)
        keep = kept[part]
        one, picked, down, sums_two, grad_picked, grad_one, *rest = scratch[12 * part : 12 * part + 12]
        got_two, got_picked, got_one, logits, low_logits, stats = rest
        marks_ref = marks_one if part else marks_zero
        base = 6 * part

        out = mm(mixed_ref[rows, :], out_weight[...], NN) + row(4)
        plain_one, scale_one = norm_rows(zero_ref[rows, :] + out)
        normed_one = plain_one * row(5) + row(6)
        one[here] = normed_one.astype(LOW)
        yield from gathering(one, base)
        group_one = one[...].reshape(group, D)
        before = mm(group_one, ffn[0], NN) + bias
        erf_part = 0.5 * (1.0 + lax.erf(before * (0.5**0.5)))
        active = (before * erf_part).astype(LOW)
        sums_two[...] = mm(active, ffn[1], NT).astype(LOW).reshape(mp, count, D)
        slope = erf_part + before * jnp.exp(-0.5 * before * before) * 0.3989422804014327
        yield from reducing(sums_two, got_two, base + 1)
        plain_two, scale_two = norm_rows(normed_one + (sums_two[here].astype(WIDE) + row(7)))
        picked[here] = (plain_two * row(8) + row(9)).astype(LOW)
        yield from gathering(picked, base + 2)
        group_picked = picked[...].reshape(group, D)
        label = marks_ref[0:1, :] - here * vocab
        valid = marks_ref[1:2, :].astype(WIDE)
        tiles = vocab // vocab_tile

        def forward(index, carry):
            highest, total, target = carry
            where = pl.ds(pl.multiple_of(index * vocab_tile, 16), vocab_tile)
            values = mm(table[where, :], group_picked, NT)
            logits[where, :] = values
            higher = jnp.maximum(highest, jnp.max(values, 0, keepdims=True))
            total = total * jnp.exp(highest - higher) + column_sum(jnp.exp(values - higher))
            word = lax.broadcasted_iota(jnp.int32, (vocab_tile, group), 0) + index * vocab_tile
            target = target + column_sum(jnp.where(word == label, values, 0.0))
            return higher, total, target

        blank = jnp.zeros((1, group), WIDE)
        highest, total, target = lax.fori_loop(0, tiles, forward, (blank - 1e30, blank, blank))
        stats[here, 0:1, 0:group] = highest
        stats[here, 1:2, 0:group] = total
        stats[here, 2:3, 0:group] = target
        for other in range(1, mp):
            made = pltpu.make_async_remote_copy(
                src_ref=stats.at[here], dst_ref=stats.at[here],
                send_sem=stat_send.at[part, other], recv_sem=stat_recv.at[part, other],
                device_id={"mp": lax.rem(here + other, mp)}, device_id_type=MESH,
            )
            made.start()
            waiting.append(made)
        yield
        for other in range(1, mp):
            source = lax.rem(here + mp - other, mp)
            pltpu.make_async_copy(
                stats.at[source], stats.at[source], stat_recv.at[part, other]
            ).wait()
        highest = stats[0, 0:1, 0:group]
        for index in range(1, mp):
            highest = jnp.maximum(highest, stats[index, 0:1, 0:group])
        total, target = blank, blank
        for index in range(mp):
            scaled = jnp.exp(stats[index, 0:1, 0:group] - highest)
            total = total + stats[index, 1:2, 0:group] * scaled
            target = target + stats[index, 2:3, 0:group]
        log_rows = highest + jnp.log(total)
        place = lax.broadcasted_iota(jnp.int32, (1, group), 1)
        own = (place >= here * count) & (place < (here + 1) * count)
        keep["loss"] = jnp.sum(
            jnp.where(own, valid * (log_rows - target), 0.0), -1, keepdims=True
        )
        keep["count"] = jnp.sum(jnp.where(own, valid, 0.0), -1, keepdims=True)

        def backward(index, grad):
            where = pl.ds(pl.multiple_of(index * vocab_tile, 16), vocab_tile)
            word = lax.broadcasted_iota(jnp.int32, (vocab_tile, group), 0) + index * vocab_tile
            hit = jnp.where(word == label, 1.0, 0.0)
            values = ((jnp.exp(logits[where, :] - log_rows) - hit) * valid).astype(LOW)
            low_logits[where, :] = values
            return grad + mm(values, table[where, :], TN)

        grad = lax.fori_loop(0, tiles, backward, jnp.zeros((group, D), WIDE))
        grad_picked[...] = grad.astype(LOW).reshape(mp, count, D)
        keep["picked"], keep["low_logits"] = group_picked, low_logits
        yield from reducing(grad_picked, got_picked, base + 3)
        grad_two = grad_picked[here].astype(WIDE)
        keep[8] = column_sum(grad_two * plain_two)
        keep[9] = column_sum(grad_two)
        grad_sum_two = norm_back(grad_two, plain_two, scale_two, row(8))
        low_two = grad_sum_two.astype(LOW)
        keep[7] = column_sum(low_two.astype(WIDE))
        down[here] = low_two
        yield from gathering(down, base + 4)
        group_down = down[...].reshape(group, D)
        grad_active = mm(group_down, ffn[1], NN)
        grad_before = (grad_active * slope).astype(LOW)
        grad_one[...] = mm(grad_before, ffn[0], NT).astype(LOW).reshape(mp, count, D)
        keep["up"] = (group_one, grad_before)
        keep["down"] = (group_down, active)
        yield from reducing(grad_one, got_one, base + 5)
        grad = grad_sum_two + grad_one[here].astype(WIDE)
        keep[5] = column_sum(grad * plain_one)
        keep[6] = column_sum(grad)
        grad = norm_back(grad, plain_one, scale_one, row(5))
        low = grad.astype(LOW)
        keep[4] = column_sum(low.astype(WIDE))
        grad_zero_ref[rows, :] = grad
        grad_mixed_ref[rows, :] = mm(low, out_weight[...], NT).astype(LOW)
        keep["out"] = low

    def both(name):
        return [jnp.concatenate([kept[0][name][side], kept[1][name][side]], 0) for side in range(2)]

    def table_part(first, last):
        def work():
            def body(index, carry):
                where = pl.ds(pl.multiple_of(index * vocab_tile, 16), vocab_tile)
                total = mm(kept[0]["low_logits"][where, :], kept[0]["picked"], NN)
                total = total + mm(kept[1]["low_logits"][where, :], kept[1]["picked"], NN)
                grad_table_ref[where, :] = total.astype(LOW)
                return carry

            lax.fori_loop(first, last, body, 0)

        return work

    def up_part():
        left, right = both("up")
        grad_ffn_ref[0] = mm(left, right, TN).astype(LOW)
        bias_out[...] = column_sum(right.astype(WIDE))

    def down_part():
        left, right = both("down")
        grad_ffn_ref[1] = mm(left, right, TN).astype(LOW)

    tiles = vocab // vocab_tile
    quarter = max(1, tiles // 4)
    fillers = [
        table_part(first, min(first + quarter, tiles)) for first in range(0, tiles, quarter)
    ]
    late = [up_part, down_part]
    runs = [run(0), run(1)]
    live = [True, True]
    while any(live):
        for part in range(2):
            if live[part]:
                live[part] = next(runs[part], "done") != "done"
        if "down" in kept[1] and late:
            late.pop(0)()
        elif "low_logits" in kept[1] and fillers:
            fillers.pop(0)()
    for work in fillers + late:
        work()
    grad_out_ref[...] = mm(
        mixed_ref[...], jnp.concatenate([kept[0]["out"], kept[1]["out"]], 0), TN
    ).astype(LOW)
    first_lane = lax.broadcasted_iota(jnp.int32, (8, LANES), 1) == 0
    first_row = lax.broadcasted_iota(jnp.int32, (8, LANES), 0)
    loss, count = (kept[0][name] + kept[1][name] for name in ("loss", "count"))
    sums_ref[...] = jnp.where(
        first_lane & (first_row == 0), loss, jnp.where(first_lane & (first_row == 1), count, 0.0)
    )
    for index in range(16):
        value = kept[0][index] + kept[1][index] if 4 <= index < 10 else jnp.zeros((1, D), WIDE)
        rows_ref[index : index + 1, :] = value
    ring.finish()
    for made in waiting:
        made.wait_send()


def head_step(mp, mixed, zero, weights, small, ffn, table, marks_zero, marks_one):
    slots, hidden, vocab = mixed.shape[0], ffn.shape[2], table.shape[0]
    vmem = pl.BlockSpec(memory_space=pltpu.VMEM)
    anywhere = pl.BlockSpec(memory_space=pl.ANY)
    dma = pltpu.SemaphoreType.DMA
    tile = next(t for t in (480, 512, 256, 128) if vocab % t == 0)
    scratch = []
    for first, count in halves_of(slots):
        group = mp * count
        scratch += [pltpu.VMEM((mp, count, D), LOW)] * 6
        scratch += [pltpu.VMEM((mp - 1, count, D), LOW)] * 3
        scratch += [
            pltpu.VMEM((vocab, group), WIDE),
            pltpu.VMEM((vocab, group), LOW),
            pltpu.VMEM((mp, 8, pad_up(group, LANES)), WIDE),
        ]

    def body(*refs):
        head_kernel(mp, tile, refs)

    return pl.pallas_call(
        body,
        out_shape=(
            jax.ShapeDtypeStruct((slots, D), WIDE),
            jax.ShapeDtypeStruct((slots, D), LOW),
            jax.ShapeDtypeStruct((D, D), LOW),
            jax.ShapeDtypeStruct((2, D, hidden), LOW),
            jax.ShapeDtypeStruct((vocab, D), LOW),
            jax.ShapeDtypeStruct((16, D), WIDE),
            jax.ShapeDtypeStruct((1, hidden), WIDE),
            jax.ShapeDtypeStruct((8, LANES), WIDE),
        ),
        in_specs=[vmem, vmem, anywhere, vmem, anywhere, anywhere, vmem, vmem],
        out_specs=(vmem,) * 8,
        scratch_shapes=[
            pltpu.VMEM((2, D, hidden), LOW),
            pltpu.VMEM((vocab, D), LOW),
            pltpu.VMEM((D, D), LOW),
            *scratch,
            dma((3,)),
            dma((12, 2, mp - 1)),
            dma((12, 2, mp - 1)),
            dma((2, mp)),
            dma((2, mp)),
        ],
        compiler_params=pltpu.CompilerParams(
            collective_id=3, has_side_effects=True, vmem_limit_bytes=58 * 2**20
        ),
        name="head_step",
    )(mixed, zero, weights, small, ffn, table, marks_zero, marks_one)


ROWS = 576
KINDS = ((6, 3), (0, 4), (3, 4))


def token_base():
    base = np.zeros((16, ROWS), np.int32)
    visual = GRID * GRID
    cells = np.arange(visual)
    place, column = cells // GRID, cells % GRID
    left, top = column * 1000 // GRID, place * 1000 // GRID
    right, bottom = (column + 1) * 1000 // GRID, (place + 1) * 1000 // GRID
    rows = (left, top, right, bottom, bottom - top, right - left, cells, -1, 1)
    for index, values in enumerate(rows):
        base[index, TEXT : TEXT + visual] = values
    base[6, :TEXT] = np.arange(TEXT)
    return jnp.asarray(base)


def edge_hot():
    entry = lax.broadcasted_iota(jnp.int32, (D, LANES), 0)
    place = lax.broadcasted_iota(jnp.int32, (D, LANES), 1)
    first = jnp.clip(place - NB // 2, 0, NB - 1) * H
    return jnp.where((entry >= first) & (entry < first + H), 1.0, 0.0).astype(LOW)


def head_mask():
    entry = lax.broadcasted_iota(jnp.int32, (16, D), 1)
    return lax.rem(entry, H) == lax.broadcasted_iota(jnp.int32, (16, D), 0)


def edge_rows(small_ref, kind):
    first = 10 + FF // D
    row = small_ref[first + kind : first + kind + 1, :]
    return mm(jnp.where(head_mask(), row, 0.0).astype(LOW), edge_hot(), NN)


def edge_rows_back(grad):
    high = grad.astype(LOW)
    low = (grad - high.astype(WIDE)).astype(LOW)
    hot = edge_hot()
    return column_sum(jnp.where(head_mask(), mm(high, hot, NT) + mm(low, hot, NT), 0.0))


def key_hot(rows_ref, kind):
    column, shift = KINDS[kind]
    coarse_row = jnp.right_shift(rows_ref[column : column + 1, :], shift)
    place = lax.broadcasted_iota(jnp.int32, (2 * NB, ROWS), 0)
    first = jnp.where(place == coarse_row, 1.0, 0.0).astype(LOW)
    second = jnp.where(place == coarse_row + NB, 1.0, 0.0).astype(LOW)
    return first, second


def below_of(rows_ref, slot_ref, kind):
    column, shift = KINDS[kind]
    mask = 2**shift - 1
    rest_key = jnp.bitwise_and(rows_ref[column : column + 1, :], mask)
    rest_slot = jnp.bitwise_and(slot_ref[:, column : column + 1], mask)
    return rest_key < rest_slot


def take_slots(slots, pos_ref, pairs):
    def body(index, carry):
        at = pos_ref[index]
        for source, target in pairs:
            target[pl.ds(index, 1), :] = source[pl.ds(at, 1), :]
        return carry

    lax.fori_loop(0, slots, body, 0)


def half_mask(rows):
    slots = rows // 2
    row = lax.broadcasted_iota(jnp.int32, (rows, LANES), 0)
    lane = lax.broadcasted_iota(jnp.int32, (rows, LANES), 1)
    return (row < slots) == (lane < HD)


def pair_rows(value):
    both = jnp.concatenate([value, value], 0)
    return jnp.where(half_mask(both.shape[0]), both, jnp.zeros((), both.dtype))


def pair_lanes(value):
    slots = value.shape[0] // 2
    lane = lax.broadcasted_iota(jnp.int32, (slots, LANES), 1)
    return jnp.where(lane < HD, value[:slots], value[slots:])


def front_early(pos_ref, places, visual_proj, features_ref, boxes_ref, small_ref, columns_ref,
                rows_ref, scratch):
    normed_ref, slot_ref, bias_ref, spread_ref, stacked_ref = scratch
    slots = slot_ref.shape[0]
    tile = 96
    lookups = (0, 1, 0, 1, 2, 3)
    visual = features_ref.shape[0]
    normed_ref[0:TEXT, :] = places.astype(WIDE)
    visual_rows = mm(features_ref[...], visual_proj, NN)
    normed_ref[TEXT : TEXT + visual, :] = visual_rows + places[0:visual].astype(WIDE)
    normed_ref[TEXT + visual : ROWS, :] = jnp.zeros((ROWS - TEXT - visual, D), WIDE)

    def embed(index, carry):
        where = pl.ds(pl.multiple_of(index * tile, 16), tile)
        place = lax.broadcasted_iota(jnp.int32, (tile, NBOX), 1)
        found = []
        for column, table in enumerate(lookups):
            hot = jnp.where(place == columns_ref[where, column : column + 1], 1.0, 0.0).astype(LOW)
            found.append(mm(hot, boxes_ref[table], NN))
        normed_ref[where, :] = normed_ref[where, :] + jnp.concatenate(found, -1)
        return carry

    lax.fori_loop(0, ROWS // tile, embed, 0)
    take_slots(slots, pos_ref, ((columns_ref, slot_ref),))
    lane = lax.broadcasted_iota(jnp.int32, (NB, LANES), 1)
    for kind in range(3):
        column, shift = KINDS[kind]
        edges = edge_rows(small_ref, kind)
        for head in range(H):
            edge = jnp.broadcast_to(edges[head : head + 1, :], (NB, LANES))
            near = pltpu.roll(edge, NB, 1, stride=1, stride_axis=0)
            far = pltpu.roll(edge, 1, 1, stride=1, stride_axis=0)
            spread_ref[:, head * LANES : (head + 1) * LANES] = jnp.where(
                lane < NB, near, far
            ).astype(LOW)
        coarse_slot = jnp.right_shift(slot_ref[:, column : column + 1], shift)
        place = lax.broadcasted_iota(jnp.int32, (slots, NB), 1)
        hot = jnp.where(place == coarse_slot, 1.0, 0.0).astype(LOW)
        wide = mm(hot, spread_ref[...], NN).astype(LOW)
        for head in range(H):
            stacked_ref[head * slots : (head + 1) * slots, :] = wide[
                :, head * LANES : (head + 1) * LANES
            ]
        first, second = key_hot(rows_ref, kind)
        below = below_of(rows_ref, slot_ref, kind)

        def add(head, carry):
            where = pl.ds(pl.multiple_of(head * 2 * slots, 16), 2 * slots)
            rows = stacked_ref[where, :]
            both = jnp.concatenate([below, below], 0)
            found = jnp.where(both, mm(rows, second, NN), mm(rows, first, NN))
            bias_ref[where, :] = found if kind == 0 else bias_ref[where, :] + found
            return carry

        lax.fori_loop(0, H // 2, add, 0)


def front_late(pos_ref, word, small_ref, rows_ref, weight, hook, outs, scratch):
    (
        mixed_ref, zero_ref, zero_low_ref, low_ref, plain_ref, scale_ref, query_ref, key_ref,
        value_ref, shares_ref,
    ) = outs
    normed_ref, slot_ref, bias_ref = scratch[:3]
    slots = mixed_ref.shape[0]
    row = lambda index: small_ref[index : index + 1, :]
    tile = 96
    normed_ref[0:TEXT, :] = normed_ref[0:TEXT, :] + word

    def normalize(index, carry):
        where = pl.ds(pl.multiple_of(index * tile, 16), tile)
        plain, scale = norm_rows(normed_ref[where, :])
        normed = plain * row(0) + row(1)
        plain_ref[where, :] = plain
        scale_ref[where, :] = scale
        normed_ref[where, :] = normed
        low_ref[where, :] = normed.astype(LOW)
        return carry

    lax.fori_loop(0, ROWS // tile, normalize, 0)
    take_slots(slots, pos_ref, ((normed_ref, zero_ref),))
    low = low_ref[...]
    zero_low = zero_ref[...].astype(LOW)
    zero_low_ref[...] = zero_low
    hook()
    query_ref[...] = (mm(zero_low, weight(0), NN) + row(2)).astype(LOW)
    key_ref[...] = mm(low, weight(1), NN).astype(LOW)
    value_ref[...] = (mm(low, weight(2), NN) + row(3)).astype(LOW)
    hook()
    owner = rows_ref[7:8, :]
    allowed = ((slot_ref[:, 7:8] == owner) | (owner < 0)) & (rows_ref[8:9, :] > 0)
    allowed = jnp.concatenate([allowed, allowed], 0)
    for pair in range(H // 2):
        if pair == H // 4:
            hook()
        lanes = slice(pair * LANES, (pair + 1) * LANES)
        rows = slice(pair * 2 * slots, (pair + 1) * 2 * slots)
        scores = mm(pair_rows(query_ref[:, lanes]), key_ref[:, lanes], NT) * 0.125
        scores = jnp.where(allowed, scores + bias_ref[rows, :], MASKED)
        powers = jnp.exp(scores - jnp.max(scores, -1, keepdims=True))
        shares = powers / jnp.sum(powers, -1, keepdims=True)
        shares_ref[rows, :] = shares
        mixed_ref[:, lanes] = pair_lanes(mm(shares.astype(LOW), value_ref[:, lanes], NN)).astype(LOW)


def front_shapes(slots):
    shape = jax.ShapeDtypeStruct
    outs = (
        shape((slots, D), LOW), shape((slots, D), WIDE), shape((slots, D), LOW),
        shape((ROWS, D), LOW), shape((ROWS, D), WIDE), shape((ROWS, 1), WIDE),
        shape((slots, D), LOW), shape((ROWS, D), LOW), shape((ROWS, D), LOW),
        shape((H * slots, ROWS), WIDE),
    )
    scratch = [
        pltpu.VMEM((ROWS, D), WIDE),
        pltpu.VMEM((slots, 16), jnp.int32),
        pltpu.VMEM((H * slots, ROWS), WIDE),
        pltpu.VMEM((NB, H * LANES), LOW),
        pltpu.VMEM((H * slots, LANES), LOW),
    ]
    return outs, scratch


def front_again(pos, word, features, places, boxes, visual, small, columns, rows, weights):
    outs, scratch = front_shapes(pos.shape[0])
    vmem = pl.BlockSpec(memory_space=pltpu.VMEM)

    def body(
        pos_ref, word_ref, features_ref, places_ref, boxes_ref, visual_ref, small_ref, columns_ref,
        rows_ref, weights_ref, *rest,
    ):
        front_early(
            pos_ref, places_ref[...], visual_ref[...], features_ref, boxes_ref, small_ref,
            columns_ref, rows_ref, rest[10:],
        )
        front_late(
            pos_ref, word_ref[...].astype(WIDE), small_ref, rows_ref,
            lambda part: weights_ref[part], lambda: None, rest[:10], rest[10:],
        )

    return pl.pallas_call(
        body,
        out_shape=outs,
        in_specs=[pl.BlockSpec(memory_space=pltpu.SMEM)] + [vmem] * 9,
        out_specs=(vmem,) * 10,
        scratch_shapes=scratch,
        compiler_params=pltpu.CompilerParams(vmem_limit_bytes=56 * 2**20),
        name="front_again",
    )(pos, word, features, places, boxes, visual, small, columns, rows, weights)


def gather_kernel(plan, table_rows, refs):
    (
        pos_ref, label_in, valid_in, word_in, proj_in, boxes_in, places_in, visual_in, small_in,
        ffn_in, tokens_ref, box_in, segment_in, alive_in, features_ref, base_in,
        table_out, proj_out, boxes_out, places_out, visual_out, ffn_out, small_out, place_out,
        ids_out, most_out, rows_ref, columns_ref, marks_zero, marks_one, *rest,
    ) = refs
    outs_ref, rest = rest[:10], rest[10:]
    scratch, outs_buf, rest = rest[:5], rest[5:15], rest[15:]
    (
        table_buf, shared_buf, ffn_buf, boxes_ref, packed, got, key_ref, ids_ref, most_ref, out_sem,
        send_sem, recv_sem, word_send, word_recv, most_send, most_recv,
    ) = rest
    dp, mp = plan.dp, plan.mp
    me = lax.axis_index("dp")
    here = lax.axis_index("mp")
    depth = bits_of(dp)
    rows = word_in.shape[0]
    table_buf[me, 0:rows, :] = word_in[...].astype(LOW)
    barrier = pltpu.get_barrier_semaphore()
    for other in range(1, dp):
        pl.semaphore_signal(
            barrier, 1, device_id={"dp": lax.rem(me + other, dp)}, device_id_type=MESH
        )
    for other in range(1, mp):
        pl.semaphore_signal(
            barrier, 1, device_id={"mp": lax.rem(here + other, mp)}, device_id_type=MESH
        )
    pl.semaphore_wait(barrier, dp + mp - 2)

    half = table_rows // 2
    pieces = (
        (table_buf, 0, half),
        (table_buf, half, half),
        (shared_buf, plan.places_at, plan.shared - plan.places_at),
        (shared_buf, 0, plan.places_at),
        (ffn_buf, 0, ffn_buf.shape[1]),
    )
    orders = (list(range(1, depth)) + [0], list(range(depth - 1, -1, -1)))
    started = []

    def part_of(piece, stream, slot):
        buffer, first, count = pieces[piece]
        return buffer.at[slot, pl.ds(first, count), lanes_of(stream)]

    def copy(piece, stream, step, place, slot):
        part = part_of(piece, stream, slot)
        index = 2**step - 1 + place
        return pltpu.make_async_remote_copy(
            src_ref=part, dst_ref=part,
            send_sem=send_sem.at[piece, stream, index],
            recv_sem=recv_sem.at[piece, stream, index],
            device_id={"dp": flip(me, orders[stream][step])},
            device_id_type=MESH,
        )

    def start(piece, step):
        for stream in range(2):
            for place, slot in enumerate(combos(me, orders[stream][:step])):
                made = copy(piece, stream, step, place, slot)
                made.start()
                started.append(made)

    def wait(piece, step):
        for stream in range(2):
            peer = flip(me, orders[stream][step])
            for place, slot in enumerate(combos(peer, orders[stream][:step])):
                copy(piece, stream, step, place, slot).wait_recv()

    outs = []

    def put(source, target):
        made = pltpu.make_async_copy(source, target, out_sem.at[len(outs)])
        made.start()
        outs.append(made)

    start(0, 0)
    start(1, 0)

    def cast(target, first, source):
        count = source.shape[0]
        target[me, first : first + count, : source.shape[1]] = source.astype(LOW)

    for part in range(4):
        cast(shared_buf, part * plan.proj, proj_in[part])
    cast(shared_buf, plan.places_at, places_in[...])
    cast(shared_buf, plan.visual_at, visual_in[...])
    pieces_box = plan.box // 32
    for part in range(plan.box_parts):
        row, lane = plan.box_slot(part)
        first = 32 * (part % pieces_box)
        shared_buf[me, row : row + 32, lane : lane + LANES] = boxes_in[
            part // pieces_box, first : first + 32, :
        ].astype(LOW)
    row, lane = plan.box_slot(plan.box_parts)
    cut = small_in.shape[1]
    shared_buf[me, row : row + 32, lane : lane + LANES] = jnp.zeros((32, LANES), LOW)
    shared_buf[me, row : row + VROWS, lane : lane + cut] = small_in[...].astype(LOW)
    for part in range(plan.box_parts + 1, 6 * (plan.shared - plan.box_at) // 32):
        spare_row, spare_lane = plan.box_slot(part)
        shared_buf[me, spare_row : spare_row + 32, spare_lane : spare_lane + LANES] = jnp.zeros(
            (32, LANES), LOW
        )
    ffn_rows = ffn_out.shape[2]
    wide = ffn_in.shape[2]
    for part in range(2):
        at, shift = ffn_slot(part, 0, ffn_rows, wide)
        ffn_buf[me, at : at + ffn_in.shape[1], shift : shift + wide] = ffn_in[part].astype(LOW)

    start(2, 0)

    vocab, room = rows * dp, got.shape[1]
    tokens = tokens_ref[...]
    first = lax.broadcasted_iota(jnp.int32, (TEXT, TEXT), 0)
    second = lax.broadcasted_iota(jnp.int32, (TEXT, TEXT), 1)
    before = jnp.where(first < second, 1.0, 0.0).astype(LOW)

    def ranked(ids, shard):
        inside = (ids >= shard * vocab) & (ids < (shard + 1) * vocab)
        rank = mm(jnp.where(inside, 1.0, 0.0).astype(LOW), before, NN).astype(jnp.int32)
        return inside, rank

    inside, rank = ranked(tokens, here)
    key_ref[...] = jnp.where(inside & (rank < room), rank, -1)
    own = tokens_ref[pl.ds(here, 1), :]
    place = jnp.full((1, TEXT), -1, jnp.int32)
    for shard in range(mp):
        inside, rank = ranked(own, shard)
        place = jnp.where(inside & (rank < room), rank + shard * room, place)
    place_out[...] = place
    most = jnp.zeros((mp, 1), WIDE)
    for shard in range(mp):
        inside = (tokens >= shard * vocab) & (tokens < (shard + 1) * vocab)
        most = jnp.maximum(most, jnp.sum(jnp.where(inside, 1.0, 0.0), -1, keepdims=True))
    most = jnp.max(most, 0, keepdims=True)
    most_ref[me] = jnp.broadcast_to(most, (8, LANES))
    most_copies = []
    for other in range(1, dp):
        made = pltpu.make_async_remote_copy(
            src_ref=most_ref.at[me], dst_ref=most_ref.at[me],
            send_sem=most_send.at[other], recv_sem=most_recv.at[other],
            device_id={"dp": lax.rem(me + other, dp)}, device_id_type=MESH,
        )
        made.start()
        most_copies.append(made)
    ids = tokens - here * vocab
    if table_rows != rows:
        ids = jnp.where(ids >= 0, ids // rows * table_rows + ids % rows, 0)
    ids_ref[...] = ids
    entry = lax.broadcasted_iota(jnp.int32, (room, TEXT), 0)

    def listed(slot):
        chosen = entry == key_ref[pl.ds(slot, 1), :]
        return jnp.sum(jnp.where(chosen, ids_ref[pl.ds(slot, 1), :] + 1, 0), -1, keepdims=True) - 1

    turns = [lax.rem(here + other, mp) for other in range(1, mp)] + [here]
    lists = [listed(slot) for slot in turns]
    columns = jnp.concatenate([listed(slot) for slot in range(mp)], 0)
    all_room = room * mp
    corner = lax.broadcasted_iota(jnp.int32, (all_room, all_room), 0) == lax.broadcasted_iota(
        jnp.int32, (all_room, all_room), 1
    )
    ids_out[...] = column_sum(jnp.where(corner, columns, 0))

    rows_ref[...] = base_in[...]
    rows_ref[0:4, 0:TEXT] = box_in[...]
    rows_ref[4:5, 0:TEXT] = box_in[3:4, :] - box_in[1:2, :]
    rows_ref[5:6, 0:TEXT] = box_in[2:3, :] - box_in[0:1, :]
    rows_ref[7:8, 0:TEXT] = segment_in[...]
    rows_ref[8:9, 0:TEXT] = alive_in[...]

    def row_of(width, count, source):
        place = lax.broadcasted_iota(jnp.int32, (1, width), 1)
        return lax.fori_loop(
            0, count, lambda index, row: jnp.where(place == index, source(index), row),
            jnp.zeros((1, width), jnp.int32),
        )

    slots = pos_ref.shape[0]
    rows_ref[9:10, :] = row_of(ROWS, slots, lambda index: pos_ref[index])
    for marks_ref, (begin, size) in zip((marks_zero, marks_one), halves_of(slots)):
        for kind, source in enumerate((label_in, valid_in)):
            marks_ref[kind : kind + 1, :] = row_of(
                size * mp, size * mp,
                lambda index: source[index // size * slots + begin + index % size],
            )
    corner = lax.broadcasted_iota(jnp.int32, (ROWS, ROWS), 0) == lax.broadcasted_iota(
        jnp.int32, (ROWS, ROWS), 1
    )
    columns_ref[...] = jnp.zeros((ROWS, 16), jnp.int32)
    for index in range(9):
        columns_ref[:, index : index + 1] = jnp.sum(
            jnp.where(corner, rows_ref[index : index + 1, :], 0), -1, keepdims=True
        )

    for step in range(depth):
        for piece in range(2):
            wait(piece, step)
            if step < depth - 1:
                start(piece, step + 1)
        if step == depth - 2:
            wait(2, 0)
            start(2, 1)
            start(3, 0)
    put(table_buf, table_out)

    word_copies = []
    for turn in range(0, mp, 2):
        wanted = jnp.concatenate(lists[turn : turn + 2], 0)
        column = lax.broadcasted_iota(jnp.int32, (2 * room, dp * table_rows), 1)
        hot = jnp.where(column == wanted, 1.0, 0.0).astype(LOW)
        found = mm(hot, table_buf[...].reshape(dp * table_rows, D), NN).astype(LOW)
        for part in range(2):
            slot = turns[turn + part]
            rows_of = found[part * room : (part + 1) * room]
            if turn + part == mp - 1:
                got[here] = rows_of
                continue
            packed[turn + part] = rows_of
            made = pltpu.make_async_remote_copy(
                src_ref=packed.at[turn + part], dst_ref=got.at[here],
                send_sem=word_send.at[turn + part], recv_sem=word_recv.at[turn + part],
                device_id={"mp": slot}, device_id_type=MESH,
            )
            made.start()
            word_copies.append(made)

    wait(3, 0)
    start(3, 1)
    start(4, 0)

    def finish(piece):
        for step in range(1, depth):
            wait(piece, step)
            if step < depth - 1:
                start(piece, step + 1)

    finish(2)
    put(shared_buf.at[:, pl.ds(plan.places_at, plan.places)], places_out)
    put(shared_buf.at[:, pl.ds(plan.visual_at, plan.visual)], visual_out)
    for part in range(plan.box_parts):
        at, shift = plan.box_slot(part)
        put(
            shared_buf.at[:, pl.ds(at, 32), pl.ds(shift, LANES)],
            boxes_out.at[part // pieces_box, :, pl.ds(32 * (part % pieces_box), 32)],
        )
    for part in range(plan.box_parts):
        at, shift = plan.box_slot(part)
        for owner in range(dp):
            line = owner * plan.box + 32 * (part % pieces_box)
            boxes_ref[part // pieces_box, line : line + 32, :] = shared_buf[
                owner, at : at + 32, shift : shift + LANES
            ]
    row, lane = plan.box_slot(plan.box_parts)
    for part in range(dp):
        small_out[:, part * cut : (part + 1) * cut] = shared_buf[
            part, row : row + 24, lane : lane + cut
        ].astype(WIDE)

    def whole_rows(first, count):
        part = shared_buf[:, first : first + count // dp, :]
        return part.reshape(count, D)

    front_early(
        pos_ref, whole_rows(plan.places_at, TEXT), whole_rows(plan.visual_at, VCH), features_ref,
        boxes_ref, small_out, columns_ref, rows_ref, scratch,
    )
    for other in range(1, mp):
        source = lax.rem(here + mp - other, mp)
        pltpu.make_async_copy(got.at[source], got.at[source], word_recv.at[other - 1]).wait()
    across = jnp.sum(jnp.where(first == second, place, 0), -1, keepdims=True)
    column = lax.broadcasted_iota(jnp.int32, (TEXT, all_room), 1)
    hot = jnp.where(column == across, 1.0, 0.0).astype(LOW)
    word = mm(hot, got[...].reshape(all_room, D), NN)

    stages = [0]

    def hook():
        stage = stages[0]
        stages[0] = stage + 1
        if stage == 0:
            finish(3)
            for part in range(4):
                put(shared_buf.at[:, pl.ds(part * plan.proj, plan.proj)], proj_out.at[part])
        if stage < depth:
            wait(4, stage)
            if stage < depth - 1:
                start(4, stage + 1)
        for number in {0: (1, 2, 3, 4, 5), 1: (6, 7, 8)}.get(stage, ()):
            put(outs_buf[number], outs_ref[number])

    front_late(
        pos_ref, word, small_out, rows_ref, lambda part: whole_rows(part * plan.proj, D), hook,
        outs_buf, scratch,
    )
    put(outs_buf[0], outs_ref[0])
    put(outs_buf[9], outs_ref[9])
    while stages[0] < depth:
        hook()
    for other in range(1, dp):
        source = lax.rem(me + dp - other, dp)
        pltpu.make_async_copy(
            most_ref.at[source], most_ref.at[source], most_recv.at[other]
        ).wait()
    most = most_ref[0]
    for part in range(1, dp):
        most = jnp.maximum(most, most_ref[part])
    most_out[...] = most[0:1, 0:1]
    for part in range(2):
        at, shift = ffn_slot(part, 0, ffn_rows, wide)
        put(ffn_buf.at[:, pl.ds(at, ffn_rows), pl.ds(shift, wide)], ffn_out.at[part])
    for made in started:
        made.wait_send()
    for made in word_copies + most_copies:
        made.wait_send()
    for made in outs:
        made.wait()


def word_room(mp):
    return pad_up(TEXT // mp * 11 // 8, 16)


def front_step(
    plan, pos, label, valid, word, proj, boxes, places, visual, small, ffn, tokens, box, segment,
    alive, features,
):
    dp, mp = plan.dp, plan.mp
    slots = pos.shape[0]
    table_rows, ffn_rows, wide = pad_up(word.shape[0], 32), pad_up(ffn.shape[1], 16), ffn.shape[2]
    ffn_all = 2 * ffn_rows * wide // D
    room = word_room(mp)
    anywhere = pl.BlockSpec(memory_space=pl.ANY)
    vmem = pl.BlockSpec(memory_space=pltpu.VMEM)
    smem = pl.BlockSpec(memory_space=pltpu.SMEM)
    dma = pltpu.SemaphoreType.DMA
    shape = jax.ShapeDtypeStruct
    outs, scratch = front_shapes(slots)

    def body(*refs):
        gather_kernel(plan, table_rows, refs)

    return pl.pallas_call(
        body,
        out_shape=(
            shape((dp, table_rows, D), LOW), shape((4, dp, plan.proj, D), LOW),
            shape((4, dp, plan.box, LANES), LOW), shape((dp, plan.places, D), LOW),
            shape((dp, plan.visual, D), LOW), shape((2, dp, ffn_rows, wide), LOW),
            shape((24, D), WIDE), shape((1, TEXT), jnp.int32), shape((1, mp * room), jnp.int32),
            shape((1, 1), WIDE), shape((16, ROWS), jnp.int32), shape((ROWS, 16), jnp.int32),
            *(shape((2, mp * size), jnp.int32) for _, size in halves_of(slots)),
            *outs,
        ),
        in_specs=[smem] * 3 + [vmem] * 13,
        out_specs=(anywhere,) * 6 + (vmem,) * 8 + (anywhere,) * 10,
        scratch_shapes=[
            *scratch,
            *(pltpu.VMEM(part.shape, part.dtype) for part in outs),
            pltpu.VMEM((dp, table_rows, D), LOW),
            pltpu.VMEM((dp, plan.shared, D), LOW),
            pltpu.VMEM((dp, ffn_all, D), LOW),
            pltpu.VMEM((4, NBOX, LANES), LOW),
            pltpu.VMEM((mp - 1, room, D), LOW),
            pltpu.VMEM((mp, room, D), LOW),
            pltpu.VMEM((mp, TEXT), jnp.int32),
            pltpu.VMEM((mp, TEXT), jnp.int32),
            pltpu.VMEM((dp, 8, LANES), WIDE),
            dma((plan.box_parts + 20,)),
            dma((5, 2, dp - 1)),
            dma((5, 2, dp - 1)),
            dma((mp - 1,)),
            dma((mp - 1,)),
            dma((dp,)),
            dma((dp,)),
        ],
        compiler_params=pltpu.CompilerParams(
            collective_id=1, has_side_effects=True, vmem_limit_bytes=60 * 2**20
        ),
        name="front_step",
    )(
        pos, label, valid, word, proj, boxes, places, visual, small, ffn, tokens, box, segment,
        alive, features, token_base(),
    )


def back_kernel(plan, table_rows, ffn_rows, refs):
    (
        pos_ref, grad_zero_ref, grad_mixed_ref, shares_ref, query_ref, key_ref, value_ref,
        zero_low_ref, low_ref, plain_ref, scale_ref, features_ref, small_ref, columns_ref,
        rows_ref, weights_in, table_in, out_in, ffn_in, head_in, bias_in, tile_in, place_in, ids_in,
        shared_out, split_out, tile_out, word_out,
        slot_ref, score_ref, grad_query, grad_key, grad_value, grad_rows, grad_low, turned_ref,
        grad_slot, edges_ref, weights_ref,
        shared_acc, split_acc, shared_got, split_got, ring_got, ring_own, half_got, half_own, packed, words, small_all,
        tile_mp, tile_dp,
        load_sem, send_sem, recv_sem, ring_send, ring_recv, word_send, word_recv, tile_send,
        tile_recv,
    ) = refs
    dp, mp = plan.dp, plan.mp
    me, here = lax.axis_index("dp"), lax.axis_index("mp")
    depth, ring_depth = bits_of(dp), bits_of(mp)
    slots = grad_zero_ref.shape[0]
    loads = []
    if plan.proj * dp != D:
        shared_acc[...] = jnp.zeros(shared_acc.shape, LOW)

    def load(source, target):
        loads.append(pltpu.make_async_copy(source, target, load_sem.at[len(loads)]))
        loads[-1].start()

    load(out_in, shared_acc.at[:, pl.ds(3 * plan.proj, plan.proj)])
    for part in range(2):
        wide = ffn_in.shape[3]
        row, lane = ffn_slot(part, table_rows, ffn_rows, wide)
        load(ffn_in.at[part], split_acc.at[:, pl.ds(row, ffn_rows), pl.ds(lane, wide)])
    load(weights_in.at[0:3], weights_ref)
    load(table_in, split_acc.at[:, pl.ds(0, table_rows)])

    barrier = pltpu.get_barrier_semaphore()
    for other in range(1, dp):
        pl.semaphore_signal(
            barrier, 1, device_id={"dp": lax.rem(me + other, dp)}, device_id_type=MESH
        )
    for other in range(1, mp):
        pl.semaphore_signal(
            barrier, 1, device_id={"mp": lax.rem(here + other, mp)}, device_id_type=MESH
        )
    pl.semaphore_wait(barrier, dp + mp - 2)

    orders = ([0] + list(range(depth - 1, 0, -1)), list(range(depth)))
    out_at, rest = 3 * plan.proj, split_acc.shape[1] - table_rows
    pieces = (
        (shared_acc, shared_got, out_at, plan.proj),
        (shared_acc, shared_got, 0, out_at),
        (shared_acc, shared_got, plan.places_at, plan.shared - plan.places_at),
        (split_acc, split_got, table_rows, rest),
        (split_acc, split_got, 0, table_rows // 2),
        (split_acc, split_got, table_rows // 2, table_rows // 2),
    )

    def chunk(order, step, free, away):
        index = 0
        for place, bit in enumerate(order):
            mine = (me // 2**bit) % 2
            if place < step or (place == step and not away):
                index = index + mine * 2**bit
            elif place == step:
                index = index + (1 - mine) * 2**bit
            else:
                index = index + ((free >> (place - step - 1)) & 1) * 2**bit
        return index

    def slot_base(step):
        return sum(2 ** (depth - 1 - s) for s in range(step))

    def send_one(piece, stream, step, free):
        acc, got, first, rows = pieces[piece]
        order = orders[stream]
        pltpu.make_async_remote_copy(
            src_ref=acc.at[chunk(order, step, free, True), pl.ds(first, rows), lanes_of(stream)],
            dst_ref=got.at[slot_base(step) + free, pl.ds(first, rows), lanes_of(stream)],
            send_sem=send_sem.at[piece, stream, step],
            recv_sem=recv_sem.at[piece, stream, step],
            device_id={"dp": flip(me, order[step])},
            device_id_type=MESH,
        ).start()

    def send(piece, step):
        for stream in range(2):
            for free in range(2 ** (depth - 1 - step)):
                send_one(piece, stream, step, free)

    def wait_bytes(piece, stream, step, sem):
        acc, got, first, rows = pieces[piece]
        count = 2 ** (depth - 1 - step)
        where = got.at[pl.ds(slot_base(step), count), pl.ds(first, rows), lanes_of(stream)]
        pltpu.make_async_copy(where, where, sem.at[piece, stream, step]).wait()

    def add(piece, stream, step):
        acc, got, first, rows = pieces[piece]
        order = orders[stream]
        wait_bytes(piece, stream, step, recv_sem)
        tile = row_tile(rows)
        last = step == depth - 1
        for free in range(2 ** (depth - 1 - step)):
            kept = chunk(order, step, free, False)

            def body(index, carry):
                at = pl.multiple_of(first + index * tile, 16)
                where = pl.ds(at, tile)
                total = acc[kept, where, lanes_of(stream)].astype(WIDE) + got[
                    slot_base(step) + free, where, lanes_of(stream)
                ].astype(WIDE)
                if last and acc is split_acc:
                    split_out[where, lanes_of(stream)] = total
                elif last:
                    ring_own[where, lanes_of(stream)] = total.astype(LOW)
                else:
                    acc[kept, where, lanes_of(stream)] = total.astype(LOW)
                return carry

            lax.fori_loop(0, rows // tile, body, 0)

    parity = lax.rem(here, 2)
    mine = pl.ds(pl.multiple_of(parity * HALF, LANES), HALF)
    other_half = pl.ds(pl.multiple_of((1 - parity) * HALF, LANES), HALF)

    def ring_copy(piece, step):
        where = pl.ds(pieces[piece][2], pieces[piece][3])
        if step == 0:
            source, target = ring_own.at[where, other_half], ring_got.at[where]
        else:
            source, target = half_own.at[step - 1, where], half_got.at[step - 1, where]
        return pltpu.make_async_remote_copy(
            src_ref=source,
            dst_ref=target,
            send_sem=ring_send.at[piece, step],
            recv_sem=ring_recv.at[piece, step],
            device_id={"mp": flip(here, step % ring_depth)},
            device_id_type=MESH,
        )

    def ring_step(piece, step):
        first, rows = pieces[piece][2:]
        ring_copy(piece, step).wait_recv()
        tile = row_tile(rows)

        def body(index, carry):
            where = pl.ds(pl.multiple_of(first + index * tile, 16), tile)
            if step == 0:
                total = ring_own[where, mine].astype(WIDE) + ring_got[where, :].astype(WIDE)
            elif step < ring_depth:
                total = half_own[step - 1, where, :].astype(WIDE) + half_got[
                    step - 1, where, :
                ].astype(WIDE)
            if step < ring_depth:
                half_own[step, where, :] = total.astype(LOW)
            else:
                shared_out[where, mine] = half_own[step - 1, where, :].astype(WIDE)
                shared_out[where, other_half] = half_got[step - 1, where, :].astype(WIDE)
            return carry

        lax.fori_loop(0, rows // tile, body, 0)
        if step < ring_depth:
            ring_copy(piece, step + 1).start()

    def advance(piece, step):
        for stream in range(2):
            add(piece, stream, step)
            if step < depth - 1:
                for free in range(2 ** (depth - 2 - step)):
                    send_one(piece, stream, step + 1, free)
        if step == depth - 1 and piece < 3:
            ring_copy(piece, 0).start()

    room = words.shape[1]

    def scatter(index):
        local = ids_in[...] - index * table_rows
        entry = lax.broadcasted_iota(jnp.int32, (table_rows, mp * room), 0)
        hot = jnp.where(entry == local, 1.0, 0.0).astype(LOW)
        where = (index, pl.ds(0, table_rows))
        total = split_acc[where].astype(WIDE) + mm(hot, words[...].reshape(mp * room, D), NN)
        split_acc[where] = total.astype(LOW)

    count = 2 ** (depth - 1)
    other_core, own_core = 1 - me % 2, me % 2

    def scatter_other(index, carry):
        scatter(other_core + 2 * index)
        return carry

    def scatter_own(index, carry):
        scatter(own_core + 2 * index)
        return carry

    for copy in loads[:3]:
        copy.wait()
    send(0, 0)
    send(3, 0)

    take_slots(slots, pos_ref, ((columns_ref, slot_ref),))
    for pair in range(H // 2):
        lanes = slice(pair * LANES, (pair + 1) * LANES)
        rows = slice(pair * 2 * slots, (pair + 1) * 2 * slots)
        grad_mixed = pair_rows(grad_mixed_ref[:, lanes])
        shares = shares_ref[rows, :]
        grad_value[:, lanes] = mm(shares.astype(LOW), grad_mixed, TN).astype(LOW)
        grad_shares = mm(grad_mixed, value_ref[:, lanes], NT)
        scores = shares * (grad_shares - jnp.sum(shares * grad_shares, -1, keepdims=True))
        scores = scores.astype(LOW)
        score_ref[rows, :] = scores
        grad_query[:, lanes] = pair_lanes(mm(scores, key_ref[:, lanes], NN) * 0.125).astype(LOW)
        grad_key[:, lanes] = (mm(scores, pair_rows(query_ref[:, lanes]), TN) * 0.125).astype(LOW)
    advance(0, 0)
    advance(3, 0)

    loads[3].wait()
    grad_slot[...] = grad_zero_ref[...] + mm(grad_query[...], weights_ref[0], NT)
    entry = lax.broadcasted_iota(jnp.int32, (ROWS, slots), 0)
    put = jnp.where(entry == rows_ref[9:10, 0:slots], 1.0, 0.0).astype(LOW)
    high = grad_slot[...].astype(LOW)
    small_part = (grad_slot[...] - high.astype(WIDE)).astype(LOW)
    grad_rows[...] = (
        mm(grad_key[...], weights_ref[1], NT)
        + mm(grad_value[...], weights_ref[2], NT)
        + (mm(put, high, NN) + mm(put, small_part, NN))
    )
    gain = small_ref[0:1, :]
    tile = 96

    def normed_back(index, carry):
        where = pl.ds(pl.multiple_of(index * tile, 16), tile)
        grad, plain = grad_rows[where, :], plain_ref[where, :]
        value = norm_back(grad, plain, scale_ref[where, :], gain)
        grad_rows[where, :] = value
        grad_low[where, :] = value.astype(LOW)
        return carry[0] + column_sum(grad * plain), carry[1] + column_sum(grad)

    blank = jnp.zeros((1, D), WIDE)
    gains, shifts = lax.fori_loop(0, ROWS // tile, normed_back, (blank, blank))
    small_all[0:1, :] = gains
    small_all[1:2, :] = shifts

    keep_words = pltpu.make_async_copy(grad_low.at[0:TEXT], word_out, load_sem.at[5])
    keep_words.start()
    entry = lax.broadcasted_iota(jnp.int32, (mp * room, TEXT), 0)
    hot = jnp.where(entry == place_in[...], 1.0, 0.0).astype(LOW)
    packed[...] = mm(hot, grad_low[0:TEXT, :], NN).astype(LOW).reshape(mp, room, D)
    word_copies = []
    for other in range(1, mp):
        target = lax.rem(here + other, mp)
        word_copies.append(
            pltpu.make_async_remote_copy(
                src_ref=packed.at[target], dst_ref=words.at[here],
                send_sem=word_send.at[other - 1], recv_sem=word_recv.at[other - 1],
                device_id={"mp": target}, device_id_type=MESH,
            )
        )
        word_copies[-1].start()
    words[here] = packed[here]

    rows = D // dp
    for part, (left, right) in enumerate(
        ((zero_low_ref, grad_query), (low_ref, grad_key), (low_ref, grad_value))
    ):
        grad = mm(left[...], right[...], TN).reshape(dp, rows, D)
        first = part * plan.proj
        shared_acc[:, first : first + rows, :] = grad.astype(LOW)
    send(1, 0)
    advance(0, 1)
    advance(3, 1)

    extra, rows = ROWS - TEXT, TEXT // dp
    grad_rows[0:extra, :] = grad_rows[0:extra, :] + grad_rows[TEXT:ROWS, :]
    first = plan.places_at
    shared_acc[:, first : first + rows, :] = grad_rows[0:TEXT, :].reshape(dp, rows, D).astype(LOW)
    visual, rows, first = features_ref.shape[0], VCH // dp, plan.visual_at
    grad = mm(features_ref[...], grad_low[TEXT : TEXT + visual, :], TN)
    shared_acc[:, first : first + rows, :] = grad.reshape(dp, rows, D).astype(LOW)
    block = max(plan.box, 256)
    chunks, pieces_box = block // plan.box, plan.box // 32

    def table(index, carry):
        entry = lax.broadcasted_iota(jnp.int32, (block, ROWS), 0) + index * block
        found = []
        for column in range(6):
            hot = jnp.where(entry == rows_ref[column : column + 1, :], 1.0, 0.0).astype(LOW)
            found.append(mm(hot, grad_low[:, column * LANES : (column + 1) * LANES], NN))
        for number, grad in enumerate((found[0] + found[2], found[1] + found[3], *found[4:])):
            for part in range(block // 32):
                at, lane = plan.box_slot(number * pieces_box + part % pieces_box)
                shared_acc[index * chunks + part // pieces_box, at : at + 32, lane : lane + LANES] = (
                    grad[part * 32 : part * 32 + 32].astype(LOW)
                )
        return carry

    lax.fori_loop(0, NBOX // block, table, 0)
    advance(1, 0)

    lane = lax.broadcasted_iota(jnp.int32, (NB, LANES), 1)
    for kind in range(3):
        column, shift = KINDS[kind]
        first, second = key_hot(rows_ref, kind)
        below = below_of(rows_ref, slot_ref, kind)
        coarse_slot = jnp.right_shift(slot_ref[:, column : column + 1], shift)
        place = lax.broadcasted_iota(jnp.int32, (slots, NB), 1)
        hot = jnp.where(place == NB - 1 - coarse_slot, 1.0, 0.0).astype(LOW)

        def collect(pair, carry):
            where = pl.ds(pl.multiple_of(pair * 2 * slots, 16), 2 * slots)
            both = jnp.concatenate([below, below], 0)
            scores = score_ref[where, :]
            none = jnp.zeros((), LOW)
            found = mm(jnp.where(both, none, scores), first, NT) + mm(
                jnp.where(both, scores, none), second, NT
            )
            turned_ref[where, :] = found.astype(LOW)
            return carry

        lax.fori_loop(0, H // 2, collect, 0)
        for head in range(H):
            part = mm(hot, turned_ref[head * slots : (head + 1) * slots, :], TN)
            near = pltpu.roll(jnp.where(lane < NB, part, 0.0), 1, 1, stride=1, stride_axis=0)
            far = pltpu.roll(jnp.where(lane < NB, 0.0, part), NB, 1, stride=1, stride_axis=0)
            edges_ref[head : head + 1, :] = column_sum(near + far)
        edges_ref[H:16, :] = jnp.zeros((16 - H, LANES), WIDE)
        small_all[14 + kind : 15 + kind, :] = edge_rows_back(edges_ref[...])

    hidden = bias_in.shape[1]
    start = here * hidden
    small_all[2:3, :] = column_sum(grad_query[...].astype(WIDE))
    small_all[3:4, :] = column_sum(grad_value[...].astype(WIDE))
    small_all[4:10, :] = head_in[4:10, :]
    small_all[10:14, :] = jnp.zeros((4, D), WIDE)
    small_all[
        pl.ds(10 + start // D, 1), pl.ds(pl.multiple_of(lax.rem(start, D), LANES), hidden)
    ] = bias_in[...]
    cut = D // dp
    row, lane = plan.box_slot(plan.box_parts)
    shared_acc[:, pl.ds(row, 32), pl.ds(lane, LANES)] = jnp.zeros((dp, 32, LANES), LOW)
    for part in range(dp):
        shared_acc[part, row : row + VROWS, lane : lane + cut] = small_all[
            0:VROWS, part * cut : (part + 1) * cut
        ].astype(LOW)
    for part in range(plan.box_parts + 1, 6 * (plan.shared - plan.box_at) // 32):
        row, lane = plan.box_slot(part)
        shared_acc[:, pl.ds(row, 32), pl.ds(lane, LANES)] = jnp.zeros((dp, 32, LANES), LOW)
    send(2, 0)
    for step in range(2, depth):
        advance(0, step)
        advance(3, step)
    advance(2, 0)
    loads[4].wait()
    for other in range(1, mp):
        source = lax.rem(here + mp - other, mp)
        pltpu.make_async_copy(words.at[source], words.at[source], word_recv.at[other - 1]).wait()
    lax.fori_loop(0, count, scatter_other, 0)
    send(4, 0)
    send(5, 0)
    advance(1, 1)
    ring_step(0, 0)
    lax.fori_loop(0, count, scatter_own, 0)
    ring_step(0, 1)
    for step in range(2, depth - 1):
        advance(1, step)
    advance(2, 1)
    advance(1, depth - 1)
    for step in range(2, depth - 1):
        advance(2, step)
    advance(4, 0)
    advance(5, 0)
    advance(2, depth - 1)
    ring_queue = [(0, step) for step in range(2, ring_depth + 1)]
    ring_queue += [(piece, step) for step in range(ring_depth + 1) for piece in (1, 2)]
    for step in range(1, depth):
        for piece in (4, 5):
            share = -(-len(ring_queue) // (2 * (depth - step) - (piece - 4)))
            for turn in ring_queue[: share - 1 if step == depth - 1 and piece == 5 else share]:
                ring_step(*turn)
                ring_queue.remove(turn)
            advance(piece, step)
    for turn in ring_queue:
        ring_step(*turn)

    def squares(ref, rows):
        tile = row_tile(rows)

        def body(index, total):
            values = ref[pl.ds(pl.multiple_of(index * tile, 16), tile), :]
            return total + jnp.sum((values * values).reshape(tile // 8, 8, D), 0)

        total = lax.fori_loop(0, rows // tile, body, jnp.zeros((8, D), WIDE))
        folded = total[:, 0:LANES]
        for part in range(1, D // LANES):
            folded = folded + total[:, part * LANES : (part + 1) * LANES]
        return folded

    folded = squares(shared_out, plan.shared) * (1.0 / mp) + squares(split_out, split_out.shape[0])
    tile_mp[here, 0] = folded
    tile_mp[here, 1] = tile_in[...]

    def exchange(buffer, axis, index, count, base):
        copies = []
        for other in range(1, count):
            copies.append(
                pltpu.make_async_remote_copy(
                    src_ref=buffer.at[index],
                    dst_ref=buffer.at[index],
                    send_sem=tile_send.at[base + other],
                    recv_sem=tile_recv.at[base + other],
                    device_id={axis: lax.rem(index + other, count)},
                    device_id_type=MESH,
                )
            )
        for copy in copies:
            copy.start()
        for other in range(1, count):
            source = lax.rem(index + count - other, count)
            pltpu.make_async_copy(
                buffer.at[source], buffer.at[source], tile_recv.at[base + other]
            ).wait()
        return copies

    pending = exchange(tile_mp, "mp", here, mp, 0)
    total = tile_mp[0]
    for index in range(1, mp):
        total = total + tile_mp[index]
    tile_dp[me] = total
    pending = pending + exchange(tile_dp, "dp", me, dp, mp)
    total = tile_dp[0]
    for index in range(1, dp):
        total = total + tile_dp[index]
    tile_out[...] = total
    for copy in pending:
        copy.wait_send()
    keep_words.wait()
    for copy in word_copies:
        copy.wait_send()
    for piece in range(len(pieces)):
        for stream in range(2):
            for step in range(depth):
                wait_bytes(piece, stream, step, send_sem)
    for piece in range(3):
        for step in range(ring_depth + 1):
            ring_copy(piece, step).wait_send()


def back_step(
    plan, pos, grad_zero, grad_mixed, shares, query, key, value, zero_low, low, plain, scale,
    features, small, columns, rows, weights, table, out, ffn, head, bias, tile, place, ids,
):
    dp, mp = plan.dp, plan.mp
    slots = pos.shape[0]
    table_rows, ffn_rows = table.shape[1], ffn.shape[2]
    split = table_rows + 2 * ffn_rows * ffn.shape[3] // D
    depth, ring_depth = bits_of(dp), bits_of(mp)
    anywhere = pl.BlockSpec(memory_space=pl.ANY)
    vmem = pl.BlockSpec(memory_space=pltpu.VMEM)
    dma = pltpu.SemaphoreType.DMA
    low_scratch = lambda *shape: pltpu.VMEM(shape, LOW)
    wide_scratch = lambda *shape: pltpu.VMEM(shape, WIDE)

    def body(*refs):
        back_kernel(plan, table_rows, ffn_rows, refs)

    return pl.pallas_call(
        body,
        out_shape=(
            jax.ShapeDtypeStruct((plan.shared, D), WIDE),
            jax.ShapeDtypeStruct((split, D), WIDE),
            jax.ShapeDtypeStruct((2, 8, LANES), WIDE),
            jax.ShapeDtypeStruct((TEXT, D), LOW),
        ),
        in_specs=[pl.BlockSpec(memory_space=pltpu.SMEM)]
        + [vmem] * 14
        + [anywhere] * 4
        + [vmem] * 5,
        out_specs=(vmem, vmem, vmem, anywhere),
        scratch_shapes=[
            pltpu.VMEM((slots, 16), jnp.int32),
            low_scratch(H * slots, ROWS),
            low_scratch(slots, D),
            low_scratch(ROWS, D),
            low_scratch(ROWS, D),
            wide_scratch(ROWS, D),
            low_scratch(ROWS, D),
            low_scratch(H * slots, LANES),
            wide_scratch(slots, D),
            wide_scratch(16, LANES),
            low_scratch(3, D, D),
            low_scratch(dp, plan.shared, D),
            low_scratch(dp, split, D),
            low_scratch(dp - 1, plan.shared, D),
            low_scratch(dp - 1, split, D),
            low_scratch(plan.shared, HALF),
            low_scratch(plan.shared, D),
            low_scratch(ring_depth, plan.shared, HALF),
            low_scratch(ring_depth, plan.shared, HALF),
            low_scratch(mp, word_room(mp), D),
            low_scratch(mp, word_room(mp), D),
            wide_scratch(24, D),
            wide_scratch(mp, 2, 8, LANES),
            wide_scratch(dp, 2, 8, LANES),
            dma((6,)),
            dma((6, 2, depth)),
            dma((6, 2, depth)),
            dma((3, ring_depth + 1)),
            dma((3, ring_depth + 1)),
            dma((mp - 1,)),
            dma((mp - 1,)),
            dma((mp + dp,)),
            dma((mp + dp,)),
        ],
        compiler_params=pltpu.CompilerParams(
            collective_id=5, has_side_effects=True, vmem_limit_bytes=62 * 2**20
        ),
        name="back_step",
    )(
        pos, grad_zero, grad_mixed, shares, query, key, value, zero_low, low, plain, scale,
        features, small, columns, rows, weights, table, out, ffn, head, bias, tile, place, ids,
    )


def on_device(
    tokens, text_box, segments, alive_text, features, mask_pos, mask_label, mask_valid, *states
):
    (projections, box_tables, position_table, visual_proj, small_params, word_table, feedforward) = (
        states[::3]
    )
    dp, mp = lax.axis_size("dp"), lax.axis_size("mp")
    plan = Plan(dp, mp)
    (
        table_parts, proj_parts, box_parts, place_parts, visual_parts, ffn_parts, small, places,
        ids, most, info, columns, marks_zero, marks_one, *front,
    ) = front_step(
        plan, mask_pos, mask_label, mask_valid, word_table, projections, box_tables,
        position_table, visual_proj, small_params, feedforward, tokens, text_box[0].T, segments,
        alive_text, features,
    )

    def joined(parts, rows):
        parts = parts[..., :rows, :]
        return parts.reshape(parts.shape[:-3] + (dp * rows, parts.shape[-1]))

    work_table = joined(table_parts, word_table.shape[0])
    work_proj = joined(proj_parts, D // dp)
    work_boxes = joined(box_parts, NBOX // dp)
    work_places = joined(place_parts, TEXT // dp)
    work_visual = joined(visual_parts, VCH // dp)
    work_ffn = joined(ffn_parts, D // dp)
    vocab_shard = work_table.shape[0]
    room = word_room(mp)
    crowded = most[0, 0] > room

    def local_words():
        local_ids = tokens - lax.axis_index("mp") * vocab_shard
        inside = (local_ids >= 0) & (local_ids < vocab_shard)
        return inside, jnp.clip(local_ids, 0, vocab_shard - 1)

    def exchange_words(state):
        inside, index = local_words()
        found = jnp.where(inside[..., None], jnp.take(work_table, index, axis=0), jnp.zeros((), LOW))
        word = lax.psum_scatter(found, "mp", scatter_dimension=0, tiled=True)[0]
        again = front_again(
            mask_pos, word, features, work_places, work_boxes, work_visual, small, columns, info,
            work_proj,
        )
        return (False, *again)

    _, *front = lax.while_loop(lambda state: state[0], exchange_words, (crowded, *front))
    (
        mixed, slot_zero, slot_low, normed_low, plain, scale, queries, keys, values, shares,
    ) = front
    (
        grad_slot, grad_mixed, grad_out_weight, grad_ffn, grad_table, head_rows, grad_ffn_bias,
        own_tile,
    ) = head_step(
        mp, mixed, slot_zero, work_proj, small, work_ffn, work_table,
        marks_zero, marks_one,
    )
    def split_rows(part):
        rows = part.shape[-2] // dp
        part = part.astype(LOW).reshape(part.shape[:-2] + (dp, rows, part.shape[-1]))
        extra = [(0, 0)] * (part.ndim - 2) + [(0, pad_up(rows, 16) - rows), (0, 0)]
        return jnp.pad(part, extra) if extra[-2][1] else part

    table_split, ffn_split = split_rows(grad_table), split_rows(grad_ffn)
    shared_sum, split_sum, totals, grad_word = back_step(
        plan, mask_pos, grad_slot, grad_mixed, shares, queries, keys, values, slot_low, normed_low,
        plain, scale, features, small, columns, info, work_proj, table_split,
        split_rows(grad_out_weight), ffn_split, head_rows, grad_ffn_bias, own_tile, places, ids,
    )
    def exchange_word_gradients(state):
        inside, index = local_words()
        shard = tokens // vocab_shard
        same = (shard[..., None] == jnp.arange(mp)).astype(jnp.int32)
        rank = jnp.sum((jnp.cumsum(same, 1) - same) * same, -1)
        late = rank >= room
        own = lax.dynamic_index_in_dim(late, lax.axis_index("mp"), 0, False)
        sent = jnp.where(own[:, None], grad_word, jnp.zeros((), LOW))
        group = lax.all_gather(sent, "mp", axis=0).astype(WIDE)
        group = jnp.where((inside & late)[..., None], group, 0.0)
        extra = jnp.zeros((vocab_shard, D), WIDE).at[index].add(group)
        part = lax.psum_scatter(extra, "dp", scatter_dimension=0, tiled=True)
        split = state[1].at[: part.shape[0]].add(part)
        squares = jnp.sum(shared_sum * shared_sum) / mp + jnp.sum(split * split)
        squares = lax.psum(squares, ("dp", "mp"))
        return False, split, jnp.zeros_like(totals).at[0, 0, 0].set(squares).at[1].set(totals[1])

    _, split_sum, totals = lax.while_loop(
        lambda state: state[0], exchange_word_gradients, (crowded, split_sum, totals)
    )
    outputs = adam_update(
        plan, table_split.shape[1], ffn_split.shape[2], shared_sum, split_sum, totals, states
    )
    return tuple(outputs[:21]) + tuple(part.reshape(()) for part in outputs[21:])


def solution(mesh):
    in_specs = (
        P("dp", None),
        P(("dp", "mp"), None, None),
        P(("dp", "mp"), None),
        P(("dp", "mp"), None),
        P(("dp", "mp"), None),
        P(("dp", "mp")),
        P("dp"),
        P("dp"),
        P(None, "dp", None),
        P(None, "dp", None),
        P(None, "dp", None),
        P(None, "dp", None),
        P(None, "dp", None),
        P(None, "dp", None),
        P("dp", None),
        P("dp", None),
        P("dp", None),
        P("dp", None),
        P("dp", None),
        P("dp", None),
        P(None, "dp"),
        P(None, "dp"),
        P(None, "dp"),
        P(("mp", "dp"), None),
        P(("mp", "dp"), None),
        P(("mp", "dp"), None),
        P(None, "dp", "mp"),
        P(None, "dp", "mp"),
        P(None, "dp", "mp"),
    )
    out_specs = (
        P(None, "dp", None),
        P(None, "dp", None),
        P(None, "dp", None),
        P(None, "dp", None),
        P(None, "dp", None),
        P(None, "dp", None),
        P("dp", None),
        P("dp", None),
        P("dp", None),
        P("dp", None),
        P("dp", None),
        P("dp", None),
        P(None, "dp"),
        P(None, "dp"),
        P(None, "dp"),
        P(("mp", "dp"), None),
        P(("mp", "dp"), None),
        P(("mp", "dp"), None),
        P(None, "dp", "mp"),
        P(None, "dp", "mp"),
        P(None, "dp", "mp"),
        P(),
        P(),
        P(),
    )
    return jax.shard_map(
        on_device, mesh=mesh, in_specs=in_specs, out_specs=out_specs, check_vma=False
    )
```

```python
import jax
import jax.numpy as jnp
import numpy as np
from jax import lax
from jax.experimental import pallas as pl
from jax.experimental.pallas import tpu as pltpu
from jax.sharding import PartitionSpec as P

D = 768
H = 12
HD = 64
FF = 3072
NB = 64
GRID = 7
TEXT = 512
STEP = 10
VCH = 256
NBOX = 1024
VROWS = 17


MASKED = -1e30
CLIP = 0.005
BETA_ONE = 0.9
BETA_TWO = 0.999
EPSILON = 1e-08
DECAY = 0.01
RATES = (0.02, 0.03, 0.03, 0.04, 0.3, 0.05, 0.02)


def adam_step(weight, grad, first, second, rate):
    first = BETA_ONE * first + (1.0 - BETA_ONE) * grad
    second = BETA_TWO * second + (1.0 - BETA_TWO) * grad * grad
    fixed_first = first * (1.0 / (1.0 - BETA_ONE**STEP))
    fixed_second = second * (1.0 / (1.0 - BETA_TWO**STEP))
    weight = weight - rate * (fixed_first / (jnp.sqrt(fixed_second) + EPSILON) + DECAY * weight)
    return (weight, first, second)


MESH = pl.DeviceIdType.MESH
LOW = jnp.bfloat16
WIDE = jnp.float32
LANES = 128
HALF = D // 2


def pad_up(count, unit):
    return (count + unit - 1) // unit * unit


def bits_of(count):
    return count.bit_length() - 1


def flip(index, bit):
    return index + (1 - 2 * ((index // 2**bit) % 2)) * 2**bit


class Plan:
    def __init__(self, dp, mp):
        self.dp, self.mp = dp, mp
        self.proj = pad_up(D // dp, 16)
        self.places = pad_up(TEXT // dp, 16)
        self.visual = pad_up(VCH // dp, 16)
        self.box = NBOX // dp
        self.box_parts = 4 * (self.box // 32)
        self.places_at = 4 * self.proj
        self.visual_at = self.places_at + self.places
        self.box_at = self.visual_at + self.visual
        self.box_rows = 32 * ((self.box_parts + 6) // 6)
        self.shared = pad_up(self.box_at + self.box_rows, 32 * mp)

    def box_slot(self, part):
        return self.box_at + 32 * (part // 6), LANES * (part % 6)


def group_of(axis, index):
    return {axis: index}


def lanes_of(stream):
    return pl.ds(stream * HALF, HALF)


def ffn_slot(part, table_rows, ffn_rows, wide):
    return table_rows + part * wide // D * ffn_rows, part * wide % D


def row_tile(rows):
    return next(t for t in (48, 32, 16) if rows % t == 0)


def adam_kernel(plan, table_rows, ffn_rows, refs):
    shared_ref, split_ref, tile_ref = refs[:3]
    states, outs, scalars = refs[3:24], refs[24:45], refs[45:48]
    held, load_sem, store_sem = refs[48:69], refs[69], refs[70]
    order = (5, 6, 0, 1, 2, 3, 4)
    loads, stores = {}, []
    for index in order:
        for part in range(3 * index, 3 * index + 3):
            loads[part] = pltpu.make_async_copy(states[part], held[part], load_sem.at[part])
            loads[part].start()
    totals = tile_ref[...]
    count = totals[1, 1:2, 0:1]
    norm = jnp.sqrt(jnp.sum(totals[0], keepdims=True)) / count
    scale = jnp.minimum(1.0, CLIP / norm) / count
    scalars[0][...] = totals[1, 0:1, 0:1]
    scalars[1][...] = count
    scalars[2][...] = norm

    def update(index, where, grad):
        mine = held[3 * index : 3 * index + 3]
        weight, first, second = (ref[where] for ref in mine)
        for ref, value in zip(mine, adam_step(weight, grad * scale, first, second, RATES[index])):
            ref[where] = value

    def blocks(index, lead, source, at, lane=0, wide=D):
        rows = held[3 * index].shape[-2]
        tile = next(t for t in (32, 24, 16, 8) if rows % t == 0)

        def body(step, carry):
            here = pl.multiple_of(step * tile, 8)
            where = (pl.ds(here, tile), slice(None))
            grad = source[pl.ds(pl.multiple_of(at + here, 8), tile), pl.ds(lane, wide)]
            update(index, where if lead is None else (lead,) + where, grad)
            return carry

        lax.fori_loop(0, rows // tile, body, 0)

    pieces_box = plan.box // 32
    for index in order:
        for part in range(3 * index, 3 * index + 3):
            loads[part].wait()
        if index == 0:
            for part in range(4):
                blocks(0, part, shared_ref, part * plan.proj)
        elif index == 1:
            for part in range(plan.box_parts):
                row, lane = plan.box_slot(part)
                grad = shared_ref[pl.ds(row, 32), pl.ds(lane, LANES)]
                update(1, (part // pieces_box, pl.ds(32 * (part % pieces_box), 32)), grad)
        elif index == 2:
            blocks(2, None, shared_ref, plan.places_at)
        elif index == 3:
            blocks(3, None, shared_ref, plan.visual_at)
        elif index == 4:
            row, lane = plan.box_slot(plan.box_parts)
            grad = shared_ref[pl.ds(row, 32), pl.ds(lane, LANES)]
            update(4, (slice(None), slice(None)), grad[:VROWS, : held[12].shape[1]])
        elif index == 5:
            blocks(5, None, split_ref, 0)
        else:
            for part in range(2):
                wide = held[18].shape[2]
                row, lane = ffn_slot(part, table_rows, ffn_rows, wide)
                blocks(6, part, split_ref, row, lane, wide)
        for part in range(3 * index, 3 * index + 3):
            stores.append(pltpu.make_async_copy(held[part], outs[part], store_sem.at[part]))
            stores[-1].start()
    for store in stores:
        store.wait()


def adam_update(plan, table_rows, ffn_rows, shared, split, tile, states):
    vmem = pl.BlockSpec(memory_space=pltpu.VMEM)
    anywhere = pl.BlockSpec(memory_space=pl.ANY)
    scalar = jax.ShapeDtypeStruct((1, 1), WIDE)

    def body(*refs):
        adam_kernel(plan, table_rows, ffn_rows, refs)

    return pl.pallas_call(
        body,
        out_shape=tuple(jax.ShapeDtypeStruct(part.shape, WIDE) for part in states) + (scalar,) * 3,
        in_specs=[vmem] * 3 + [anywhere] * 21,
        out_specs=(anywhere,) * 21 + (vmem,) * 3,
        scratch_shapes=[pltpu.VMEM(part.shape, WIDE) for part in states]
        + [pltpu.SemaphoreType.DMA((21,)), pltpu.SemaphoreType.DMA((21,))],
        compiler_params=pltpu.CompilerParams(vmem_limit_bytes=58 * 2**20),
        name="adam_update",
    )(shared, split, tile, *states)


def combos(index, bits):
    found = [index]
    for bit in bits:
        found = found + [flip(one, bit) for one in found]
    return found


class Ring:
    def __init__(self, mp, sems):
        self.mp, self.here = mp, lax.axis_index("mp")
        self.send, self.recv = sems
        depth = bits_of(mp)
        self.depth = depth
        self.orders = (list(range(depth)), list(range(depth - 1, -1, -1)))
        self.started = []

    def barrier(self):
        barrier = pltpu.get_barrier_semaphore()
        for other in range(1, self.mp):
            pl.semaphore_signal(
                barrier, 1, device_id={"mp": lax.rem(self.here + other, self.mp)},
                device_id_type=MESH,
            )
        pl.semaphore_wait(barrier, self.mp - 1)

    def copy(self, source, target, number, stream, index, peer):
        made = pltpu.make_async_remote_copy(
            src_ref=source, dst_ref=target,
            send_sem=self.send.at[number, stream, index],
            recv_sem=self.recv.at[number, stream, index],
            device_id={"mp": peer}, device_id_type=MESH,
        )
        return made

    def gather_send(self, buffer, number, stream, step, place):
        order = self.orders[stream]
        peer = flip(self.here, order[step])
        part = buffer.at[combos(self.here, order[:step])[place], :, lanes_of(stream)]
        made = self.copy(part, part, number, stream, 2**step - 1 + place, peer)
        made.start()
        self.started.append(made)

    def gather_start(self, buffer, number, stream):
        for step in range(self.depth):
            self.gather_send(buffer, number, stream, step, 0)

    def gather_wait(self, buffer, number, stream, step):
        order = self.orders[stream]
        peer = flip(self.here, order[step])
        for place, slot in enumerate(combos(peer, order[:step])):
            part = buffer.at[slot, :, lanes_of(stream)]
            self.copy(part, part, number, stream, 2**step - 1 + place, peer).wait_recv()
        for later in range(step + 1, self.depth):
            for place in range(2**step, 2 ** (step + 1)):
                self.gather_send(buffer, number, stream, later, place)

    def base(self, step):
        return sum(2 ** (self.depth - 1 - s) for s in range(step))

    def reduce_one(self, buffer, got, number, stream, step, place):
        order = self.orders[stream]
        peer = flip(self.here, order[step])
        slot = combos(peer, order[step + 1 :])[place]
        index = self.base(step) + place
        made = self.copy(
            buffer.at[slot, :, lanes_of(stream)],
            got.at[index, :, lanes_of(stream)],
            number, stream, index, peer,
        )
        made.start()
        self.started.append(made)

    def reduce_start(self, buffer, got, number, stream, step):
        for place in range(2 ** (self.depth - 1 - step)):
            self.reduce_one(buffer, got, number, stream, step, place)

    def reduce_wait(self, buffer, got, number, stream, step):
        order = self.orders[stream]
        peer = flip(self.here, order[step])
        for place, slot in enumerate(combos(self.here, order[step + 1 :])):
            index = self.base(step) + place
            part = got.at[index, :, lanes_of(stream)]
            self.copy(part, part, number, stream, index, peer).wait_recv()
            where = (slot, slice(None), lanes_of(stream))
            total = buffer[where].astype(WIDE) + got[index, :, lanes_of(stream)].astype(WIDE)
            buffer[where] = total.astype(buffer.dtype)

    def reduce_begin(self, buffer, got, number):
        for stream in range(2):
            self.reduce_start(buffer, got, number, stream, 0)

    def finish(self):
        for made in self.started:
            made.wait_send()


def mm(left, right, dims):
    return lax.dot_general(left, right, (dims, ((), ())), preferred_element_type=WIDE)


NN, NT, TN = ((1,), (0,)), ((1,), (1,)), ((0,), (0,))


def norm_rows(value):
    centred = value - jnp.mean(value, -1, keepdims=True)
    scale = lax.rsqrt(jnp.mean(centred * centred, -1, keepdims=True) + 1e-05)
    return centred * scale, scale


def norm_back(grad, plain, scale, gain):
    inner = grad * gain
    return scale * (
        inner
        - jnp.mean(inner, -1, keepdims=True)
        - plain * jnp.mean(inner * plain, -1, keepdims=True)
    )


def column_sum(value):
    return jnp.sum(value, 0, keepdims=True)


def halves_of(slots):
    first = pad_up(slots // 2, 16)
    return ((0, first), (first, slots - first))


def head_kernel(mp, vocab_tile, refs):
    (
        mixed_ref, zero_ref, weights_in, small_ref, ffn_ref, table_ref, marks_zero, marks_one,
        grad_zero_ref, grad_mixed_ref, grad_out_ref, ffn_out, table_out, rows_ref, bias_out,
        sums_ref,
        ffn, table, out_weight, grad_ffn_ref, grad_table_ref, *scratch,
    ) = refs
    load_sem, send_sem, recv_sem, stat_send, stat_recv = scratch[-5:]
    ring = Ring(mp, (send_sem, recv_sem))
    here = ring.here
    slots, vocab, hidden = mixed_ref.shape[0], table.shape[0], ffn.shape[2]
    load_ffn = pltpu.make_async_copy(ffn_ref, ffn, load_sem.at[0])
    load_table = pltpu.make_async_copy(table_ref, table, load_sem.at[1])
    load_out = pltpu.make_async_copy(weights_in.at[3], out_weight, load_sem.at[2])
    load_out.start()
    load_ffn.start()
    load_table.start()
    ring.barrier()
    row = lambda index: small_ref[index : index + 1, :]
    start = here * hidden
    bias = small_ref[
        pl.ds(10 + start // D, 1), pl.ds(pl.multiple_of(lax.rem(start, D), LANES), hidden)
    ]
    load_out.wait()
    kept = [{}, {}]
    waiting = []

    def gathering(buffer, number):
        for stream in range(2):
            ring.gather_start(buffer, number, stream)
        for step in range(ring.depth):
            yield
            for stream in range(2):
                ring.gather_wait(buffer, number, stream, step)

    def reducing(buffer, got, number):
        ring.reduce_begin(buffer, got, number)
        for step in range(ring.depth):
            yield
            for stream in range(2):
                ring.reduce_wait(buffer, got, number, stream, step)
                if step < ring.depth - 1:
                    ring.reduce_start(buffer, got, number, stream, step + 1)

    def run(part):
        first, count = halves_of(slots)[part]
        group = count * mp
        rows = slice(first, first + count)
        keep = kept[part]
        one, picked, down, sums_two, grad_picked, grad_one, *rest = scratch[12 * part : 12 * part + 12]
        got_two, got_picked, got_one, logits, low_logits, stats = rest
        marks_ref = marks_one if part else marks_zero
        base = 6 * part

        out = mm(mixed_ref[rows, :], out_weight[...], NN) + row(4)
        plain_one, scale_one = norm_rows(zero_ref[rows, :] + out)
        normed_one = plain_one * row(5) + row(6)
        one[here] = normed_one.astype(LOW)
        yield from gathering(one, base)
        if part == 0:
            load_ffn.wait()
        group_one = one[...].reshape(group, D)
        before = mm(group_one, ffn[0], NN) + bias
        erf_part = 0.5 * (1.0 + lax.erf(before * (0.5**0.5)))
        active = (before * erf_part).astype(LOW)
        sums_two[...] = mm(active, ffn[1], NT).astype(LOW).reshape(mp, count, D)
        slope = erf_part + before * jnp.exp(-0.5 * before * before) * 0.3989422804014327
        yield from reducing(sums_two, got_two, base + 1)
        plain_two, scale_two = norm_rows(normed_one + (sums_two[here].astype(WIDE) + row(7)))
        picked[here] = (plain_two * row(8) + row(9)).astype(LOW)
        yield from gathering(picked, base + 2)
        if part == 0:
            load_table.wait()
        group_picked = picked[...].reshape(group, D)
        label = marks_ref[0:1, :] - here * vocab
        valid = marks_ref[1:2, :].astype(WIDE)
        tiles = vocab // vocab_tile

        def forward(index, carry):
            highest, total, target = carry
            where = pl.ds(pl.multiple_of(index * vocab_tile, 16), vocab_tile)
            values = mm(table[where, :], group_picked, NT)
            logits[where, :] = values
            higher = jnp.maximum(highest, jnp.max(values, 0, keepdims=True))
            total = total * jnp.exp(highest - higher) + column_sum(jnp.exp(values - higher))
            word = lax.broadcasted_iota(jnp.int32, (vocab_tile, group), 0) + index * vocab_tile
            target = target + column_sum(jnp.where(word == label, values, 0.0))
            return higher, total, target

        blank = jnp.zeros((1, group), WIDE)
        highest, total, target = lax.fori_loop(0, tiles, forward, (blank - 1e30, blank, blank))
        stats[here, 0:1, 0:group] = highest
        stats[here, 1:2, 0:group] = total
        stats[here, 2:3, 0:group] = target
        for other in range(1, mp):
            made = pltpu.make_async_remote_copy(
                src_ref=stats.at[here], dst_ref=stats.at[here],
                send_sem=stat_send.at[part, other], recv_sem=stat_recv.at[part, other],
                device_id={"mp": lax.rem(here + other, mp)}, device_id_type=MESH,
            )
            made.start()
            waiting.append(made)
        yield
        for other in range(1, mp):
            source = lax.rem(here + mp - other, mp)
            pltpu.make_async_copy(
                stats.at[source], stats.at[source], stat_recv.at[part, other]
            ).wait()
        highest = stats[0, 0:1, 0:group]
        for index in range(1, mp):
            highest = jnp.maximum(highest, stats[index, 0:1, 0:group])
        total, target = blank, blank
        for index in range(mp):
            scaled = jnp.exp(stats[index, 0:1, 0:group] - highest)
            total = total + stats[index, 1:2, 0:group] * scaled
            target = target + stats[index, 2:3, 0:group]
        log_rows = highest + jnp.log(total)
        place = lax.broadcasted_iota(jnp.int32, (1, group), 1)
        own = (place >= here * count) & (place < (here + 1) * count)
        keep["loss"] = jnp.sum(
            jnp.where(own, valid * (log_rows - target), 0.0), -1, keepdims=True
        )
        keep["count"] = jnp.sum(jnp.where(own, valid, 0.0), -1, keepdims=True)

        def backward(index, grad):
            where = pl.ds(pl.multiple_of(index * vocab_tile, 16), vocab_tile)
            word = lax.broadcasted_iota(jnp.int32, (vocab_tile, group), 0) + index * vocab_tile
            hit = jnp.where(word == label, 1.0, 0.0)
            values = ((jnp.exp(logits[where, :] - log_rows) - hit) * valid).astype(LOW)
            low_logits[where, :] = values
            return grad + mm(values, table[where, :], TN)

        grad = lax.fori_loop(0, tiles, backward, jnp.zeros((group, D), WIDE))
        grad_picked[...] = grad.astype(LOW).reshape(mp, count, D)
        keep["picked"], keep["low_logits"] = group_picked, low_logits
        yield from reducing(grad_picked, got_picked, base + 3)
        grad_two = grad_picked[here].astype(WIDE)
        keep[8] = column_sum(grad_two * plain_two)
        keep[9] = column_sum(grad_two)
        grad_sum_two = norm_back(grad_two, plain_two, scale_two, row(8))
        low_two = grad_sum_two.astype(LOW)
        keep[7] = column_sum(low_two.astype(WIDE))
        down[here] = low_two
        yield from gathering(down, base + 4)
        group_down = down[...].reshape(group, D)
        grad_active = mm(group_down, ffn[1], NN)
        grad_before = (grad_active * slope).astype(LOW)
        grad_one[...] = mm(grad_before, ffn[0], NT).astype(LOW).reshape(mp, count, D)
        keep["up"] = (group_one, grad_before)
        keep["down"] = (group_down, active)
        yield from reducing(grad_one, got_one, base + 5)
        grad = grad_sum_two + grad_one[here].astype(WIDE)
        keep[5] = column_sum(grad * plain_one)
        keep[6] = column_sum(grad)
        grad = norm_back(grad, plain_one, scale_one, row(5))
        low = grad.astype(LOW)
        keep[4] = column_sum(low.astype(WIDE))
        grad_zero_ref[rows, :] = grad
        grad_mixed_ref[rows, :] = mm(low, out_weight[...], NT).astype(LOW)
        keep["out"] = low

    def both(name):
        return [jnp.concatenate([kept[0][name][side], kept[1][name][side]], 0) for side in range(2)]

    stores = []

    def keep_result(source, target):
        stores.append(pltpu.make_async_copy(source, target, load_sem.at[3 + len(stores)]))
        stores[-1].start()

    def table_part(first, last):
        def work():
            def body(index, carry):
                where = pl.ds(pl.multiple_of(index * vocab_tile, 16), vocab_tile)
                total = mm(kept[0]["low_logits"][where, :], kept[0]["picked"], NN)
                total = total + mm(kept[1]["low_logits"][where, :], kept[1]["picked"], NN)
                grad_table_ref[where, :] = total.astype(LOW)
                return carry

            lax.fori_loop(first, last, body, 0)
            where = pl.ds(first * vocab_tile, (last - first) * vocab_tile)
            keep_result(grad_table_ref.at[where], table_out.at[where])

        return work

    def up_part():
        left, right = both("up")
        grad_ffn_ref[0] = mm(left, right, TN).astype(LOW)
        bias_out[...] = column_sum(right.astype(WIDE))
        keep_result(grad_ffn_ref.at[0], ffn_out.at[0])

    def down_part():
        left, right = both("down")
        grad_ffn_ref[1] = mm(left, right, TN).astype(LOW)
        keep_result(grad_ffn_ref.at[1], ffn_out.at[1])

    tiles = vocab // vocab_tile
    quarter = max(1, tiles // 4)
    fillers = [
        table_part(first, min(first + quarter, tiles)) for first in range(0, tiles, quarter)
    ]
    late = [up_part, down_part]
    runs = [run(0), run(1)]
    live = [True, True]
    while any(live):
        for part in range(2):
            if live[part]:
                live[part] = next(runs[part], "done") != "done"
        if "down" in kept[1] and late:
            late.pop(0)()
        elif "low_logits" in kept[1] and fillers:
            fillers.pop(0)()
    for work in fillers + late:
        work()
    grad_out_ref[...] = mm(
        mixed_ref[...], jnp.concatenate([kept[0]["out"], kept[1]["out"]], 0), TN
    ).astype(LOW)
    first_lane = lax.broadcasted_iota(jnp.int32, (8, LANES), 1) == 0
    first_row = lax.broadcasted_iota(jnp.int32, (8, LANES), 0)
    loss, count = (kept[0][name] + kept[1][name] for name in ("loss", "count"))
    sums_ref[...] = jnp.where(
        first_lane & (first_row == 0), loss, jnp.where(first_lane & (first_row == 1), count, 0.0)
    )
    for index in range(16):
        value = kept[0][index] + kept[1][index] if 4 <= index < 10 else jnp.zeros((1, D), WIDE)
        rows_ref[index : index + 1, :] = value
    for made in stores:
        made.wait()
    ring.finish()
    for made in waiting:
        made.wait_send()


def head_step(mp, mixed, zero, weights, small, ffn, table, marks_zero, marks_one):
    slots, hidden, vocab = mixed.shape[0], ffn.shape[2], table.shape[0]
    vmem = pl.BlockSpec(memory_space=pltpu.VMEM)
    anywhere = pl.BlockSpec(memory_space=pl.ANY)
    dma = pltpu.SemaphoreType.DMA
    tile = next(t for t in (480, 512, 256, 128) if vocab % t == 0)
    scratch = []
    for first, count in halves_of(slots):
        group = mp * count
        scratch += [pltpu.VMEM((mp, count, D), LOW)] * 6
        scratch += [pltpu.VMEM((mp - 1, count, D), LOW)] * 3
        scratch += [
            pltpu.VMEM((vocab, group), WIDE),
            pltpu.VMEM((vocab, group), LOW),
            pltpu.VMEM((mp, 8, pad_up(group, LANES)), WIDE),
        ]

    def body(*refs):
        head_kernel(mp, tile, refs)

    return pl.pallas_call(
        body,
        out_shape=(
            jax.ShapeDtypeStruct((slots, D), WIDE),
            jax.ShapeDtypeStruct((slots, D), LOW),
            jax.ShapeDtypeStruct((D, D), LOW),
            jax.ShapeDtypeStruct((2, D, hidden), LOW),
            jax.ShapeDtypeStruct((vocab, D), LOW),
            jax.ShapeDtypeStruct((16, D), WIDE),
            jax.ShapeDtypeStruct((1, hidden), WIDE),
            jax.ShapeDtypeStruct((8, LANES), WIDE),
        ),
        in_specs=[vmem, vmem, anywhere, vmem, anywhere, anywhere, vmem, vmem],
        out_specs=(vmem,) * 3 + (anywhere,) * 2 + (vmem,) * 3,
        scratch_shapes=[
            pltpu.VMEM((2, D, hidden), LOW),
            pltpu.VMEM((vocab, D), LOW),
            pltpu.VMEM((D, D), LOW),
            pltpu.VMEM((2, D, hidden), LOW),
            pltpu.VMEM((vocab, D), LOW),
            *scratch,
            dma((16,)),
            dma((12, 2, mp - 1)),
            dma((12, 2, mp - 1)),
            dma((2, mp)),
            dma((2, mp)),
        ],
        compiler_params=pltpu.CompilerParams(
            collective_id=3, has_side_effects=True, vmem_limit_bytes=58 * 2**20
        ),
        name="head_step",
    )(mixed, zero, weights, small, ffn, table, marks_zero, marks_one)


ROWS = 576
KINDS = ((6, 3), (0, 4), (3, 4))


def token_base():
    base = np.zeros((16, ROWS), np.int32)
    visual = GRID * GRID
    cells = np.arange(visual)
    place, column = cells // GRID, cells % GRID
    left, top = column * 1000 // GRID, place * 1000 // GRID
    right, bottom = (column + 1) * 1000 // GRID, (place + 1) * 1000 // GRID
    rows = (left, top, right, bottom, bottom - top, right - left, cells, -1, 1)
    for index, values in enumerate(rows):
        base[index, TEXT : TEXT + visual] = values
    base[6, :TEXT] = np.arange(TEXT)
    return jnp.asarray(base)


def edge_hot():
    entry = lax.broadcasted_iota(jnp.int32, (D, LANES), 0)
    place = lax.broadcasted_iota(jnp.int32, (D, LANES), 1)
    first = jnp.clip(place - NB // 2, 0, NB - 1) * H
    return jnp.where((entry >= first) & (entry < first + H), 1.0, 0.0).astype(LOW)


def head_mask():
    entry = lax.broadcasted_iota(jnp.int32, (16, D), 1)
    return lax.rem(entry, H) == lax.broadcasted_iota(jnp.int32, (16, D), 0)


def edge_rows(small_ref, kind):
    first = 10 + FF // D
    row = small_ref[first + kind : first + kind + 1, :]
    return mm(jnp.where(head_mask(), row, 0.0).astype(LOW), edge_hot(), NN)


def edge_rows_back(grad):
    high = grad.astype(LOW)
    low = (grad - high.astype(WIDE)).astype(LOW)
    hot = edge_hot()
    return column_sum(jnp.where(head_mask(), mm(high, hot, NT) + mm(low, hot, NT), 0.0))


def key_hot(rows_ref, kind):
    column, shift = KINDS[kind]
    coarse_row = jnp.right_shift(rows_ref[column : column + 1, :], shift)
    place = lax.broadcasted_iota(jnp.int32, (2 * NB, ROWS), 0)
    first = jnp.where(place == coarse_row, 1.0, 0.0).astype(LOW)
    second = jnp.where(place == coarse_row + NB, 1.0, 0.0).astype(LOW)
    return first, second


def below_of(rows_ref, slot_ref, kind):
    column, shift = KINDS[kind]
    mask = 2**shift - 1
    rest_key = jnp.bitwise_and(rows_ref[column : column + 1, :], mask)
    rest_slot = jnp.bitwise_and(slot_ref[:, column : column + 1], mask)
    return rest_key < rest_slot


def take_slots(slots, pos_ref, pairs):
    def body(index, carry):
        at = pos_ref[index]
        for source, target in pairs:
            target[pl.ds(index, 1), :] = source[pl.ds(at, 1), :]
        return carry

    lax.fori_loop(0, slots, body, 0)


def half_mask(rows):
    slots = rows // 2
    row = lax.broadcasted_iota(jnp.int32, (rows, LANES), 0)
    lane = lax.broadcasted_iota(jnp.int32, (rows, LANES), 1)
    return (row < slots) == (lane < HD)


def pair_rows(value):
    both = jnp.concatenate([value, value], 0)
    return jnp.where(half_mask(both.shape[0]), both, jnp.zeros((), both.dtype))


def pair_lanes(value):
    slots = value.shape[0] // 2
    lane = lax.broadcasted_iota(jnp.int32, (slots, LANES), 1)
    return jnp.where(lane < HD, value[:slots], value[slots:])


def front_early(pos_ref, places, visual_proj, features_ref, boxes_ref, small_ref, columns_ref,
                rows_ref, scratch):
    normed_ref, slot_ref, bias_ref, spread_ref, stacked_ref = scratch
    slots = slot_ref.shape[0]
    tile = 96
    lookups = (0, 1, 0, 1, 2, 3)
    visual = features_ref.shape[0]
    normed_ref[0:TEXT, :] = places.astype(WIDE)
    visual_rows = mm(features_ref[...], visual_proj, NN)
    normed_ref[TEXT : TEXT + visual, :] = visual_rows + places[0:visual].astype(WIDE)
    normed_ref[TEXT + visual : ROWS, :] = jnp.zeros((ROWS - TEXT - visual, D), WIDE)

    def embed(index, carry):
        where = pl.ds(pl.multiple_of(index * tile, 16), tile)
        place = lax.broadcasted_iota(jnp.int32, (tile, NBOX), 1)
        found = []
        for column, table in enumerate(lookups):
            hot = jnp.where(place == columns_ref[where, column : column + 1], 1.0, 0.0).astype(LOW)
            found.append(mm(hot, boxes_ref[table], NN))
        normed_ref[where, :] = normed_ref[where, :] + jnp.concatenate(found, -1)
        return carry

    lax.fori_loop(0, ROWS // tile, embed, 0)
    take_slots(slots, pos_ref, ((columns_ref, slot_ref),))
    lane = lax.broadcasted_iota(jnp.int32, (NB, LANES), 1)
    for kind in range(3):
        column, shift = KINDS[kind]
        edges = edge_rows(small_ref, kind)
        for head in range(H):
            edge = jnp.broadcast_to(edges[head : head + 1, :], (NB, LANES))
            near = pltpu.roll(edge, NB, 1, stride=1, stride_axis=0)
            far = pltpu.roll(edge, 1, 1, stride=1, stride_axis=0)
            spread_ref[:, head * LANES : (head + 1) * LANES] = jnp.where(
                lane < NB, near, far
            ).astype(LOW)
        coarse_slot = jnp.right_shift(slot_ref[:, column : column + 1], shift)
        place = lax.broadcasted_iota(jnp.int32, (slots, NB), 1)
        hot = jnp.where(place == coarse_slot, 1.0, 0.0).astype(LOW)
        wide = mm(hot, spread_ref[...], NN).astype(LOW)
        for head in range(H):
            stacked_ref[head * slots : (head + 1) * slots, :] = wide[
                :, head * LANES : (head + 1) * LANES
            ]
        first, second = key_hot(rows_ref, kind)
        below = below_of(rows_ref, slot_ref, kind)

        def add(head, carry):
            where = pl.ds(pl.multiple_of(head * 2 * slots, 16), 2 * slots)
            rows = stacked_ref[where, :]
            both = jnp.concatenate([below, below], 0)
            found = jnp.where(both, mm(rows, second, NN), mm(rows, first, NN))
            bias_ref[where, :] = found if kind == 0 else bias_ref[where, :] + found
            return carry

        lax.fori_loop(0, H // 2, add, 0)


def front_late(pos_ref, word, small_ref, rows_ref, weight, hook, outs, scratch):
    (
        mixed_ref, zero_ref, zero_low_ref, low_ref, plain_ref, scale_ref, query_ref, key_ref,
        value_ref, shares_ref,
    ) = outs
    normed_ref, slot_ref, bias_ref = scratch[:3]
    slots = mixed_ref.shape[0]
    row = lambda index: small_ref[index : index + 1, :]
    tile = 96
    normed_ref[0:TEXT, :] = normed_ref[0:TEXT, :] + word

    def normalize(index, carry):
        where = pl.ds(pl.multiple_of(index * tile, 16), tile)
        plain, scale = norm_rows(normed_ref[where, :])
        normed = plain * row(0) + row(1)
        plain_ref[where, :] = plain
        scale_ref[where, :] = scale
        normed_ref[where, :] = normed
        low_ref[where, :] = normed.astype(LOW)
        return carry

    lax.fori_loop(0, ROWS // tile, normalize, 0)
    take_slots(slots, pos_ref, ((normed_ref, zero_ref),))
    low = low_ref[...]
    zero_low = zero_ref[...].astype(LOW)
    zero_low_ref[...] = zero_low
    hook()
    query_ref[...] = (mm(zero_low, weight(0), NN) + row(2)).astype(LOW)
    key_ref[...] = mm(low, weight(1), NN).astype(LOW)
    value_ref[...] = (mm(low, weight(2), NN) + row(3)).astype(LOW)
    hook()
    owner = rows_ref[7:8, :]
    allowed = ((slot_ref[:, 7:8] == owner) | (owner < 0)) & (rows_ref[8:9, :] > 0)
    allowed = jnp.concatenate([allowed, allowed], 0)
    for pair in range(H // 2):
        if pair == H // 4:
            hook()
        lanes = slice(pair * LANES, (pair + 1) * LANES)
        rows = slice(pair * 2 * slots, (pair + 1) * 2 * slots)
        scores = mm(pair_rows(query_ref[:, lanes]), key_ref[:, lanes], NT) * 0.125
        scores = jnp.where(allowed, scores + bias_ref[rows, :], MASKED)
        powers = jnp.exp(scores - jnp.max(scores, -1, keepdims=True))
        shares = powers / jnp.sum(powers, -1, keepdims=True)
        shares_ref[rows, :] = shares
        mixed_ref[:, lanes] = pair_lanes(mm(shares.astype(LOW), value_ref[:, lanes], NN)).astype(LOW)


def front_shapes(slots):
    shape = jax.ShapeDtypeStruct
    outs = (
        shape((slots, D), LOW), shape((slots, D), WIDE), shape((slots, D), LOW),
        shape((ROWS, D), LOW), shape((ROWS, D), WIDE), shape((ROWS, 1), WIDE),
        shape((slots, D), LOW), shape((ROWS, D), LOW), shape((ROWS, D), LOW),
        shape((H * slots, ROWS), WIDE),
    )
    scratch = [
        pltpu.VMEM((ROWS, D), WIDE),
        pltpu.VMEM((slots, 16), jnp.int32),
        pltpu.VMEM((H * slots, ROWS), WIDE),
        pltpu.VMEM((NB, H * LANES), LOW),
        pltpu.VMEM((H * slots, LANES), LOW),
    ]
    return outs, scratch


def front_again(pos, word, features, places, boxes, visual, small, columns, rows, weights):
    outs, scratch = front_shapes(pos.shape[0])
    vmem = pl.BlockSpec(memory_space=pltpu.VMEM)

    def body(
        pos_ref, word_ref, features_ref, places_ref, boxes_ref, visual_ref, small_ref, columns_ref,
        rows_ref, weights_ref, *rest,
    ):
        front_early(
            pos_ref, places_ref[...], visual_ref[...], features_ref, boxes_ref, small_ref,
            columns_ref, rows_ref, rest[10:],
        )
        front_late(
            pos_ref, word_ref[...].astype(WIDE), small_ref, rows_ref,
            lambda part: weights_ref[part], lambda: None, rest[:10], rest[10:],
        )

    return pl.pallas_call(
        body,
        out_shape=outs,
        in_specs=[pl.BlockSpec(memory_space=pltpu.SMEM)] + [vmem] * 9,
        out_specs=(vmem,) * 10,
        scratch_shapes=scratch,
        compiler_params=pltpu.CompilerParams(vmem_limit_bytes=56 * 2**20),
        name="front_again",
    )(pos, word, features, places, boxes, visual, small, columns, rows, weights)


def gather_kernel(plan, table_rows, refs):
    (
        pos_ref, label_in, valid_in, word_in, proj_in, boxes_in, places_in, visual_in, small_in,
        ffn_in, tokens_ref, box_in, segment_in, alive_in, features_ref, base_in,
        table_out, proj_out, boxes_out, places_out, visual_out, ffn_out, small_out, place_out,
        ids_out, most_out, rows_ref, columns_ref, marks_zero, marks_one, *rest,
    ) = refs
    outs_ref, rest = rest[:10], rest[10:]
    scratch, outs_buf, rest = rest[:5], rest[5:15], rest[15:]
    (
        table_buf, shared_buf, ffn_buf, boxes_ref, packed, got, key_ref, ids_ref, most_ref, out_sem,
        send_sem, recv_sem, word_send, word_recv, most_send, most_recv,
    ) = rest
    dp, mp = plan.dp, plan.mp
    me = lax.axis_index("dp")
    here = lax.axis_index("mp")
    depth = bits_of(dp)
    rows = word_in.shape[0]
    table_buf[me, 0:rows, :] = word_in[...].astype(LOW)
    barrier = pltpu.get_barrier_semaphore()
    for other in range(1, dp):
        pl.semaphore_signal(
            barrier, 1, device_id={"dp": lax.rem(me + other, dp)}, device_id_type=MESH
        )
    for other in range(1, mp):
        pl.semaphore_signal(
            barrier, 1, device_id={"mp": lax.rem(here + other, mp)}, device_id_type=MESH
        )
    pl.semaphore_wait(barrier, dp + mp - 2)

    half = table_rows // 2
    pieces = (
        (table_buf, 0, half),
        (table_buf, half, half),
        (shared_buf, plan.places_at, plan.shared - plan.places_at),
        (shared_buf, 0, plan.places_at),
        (ffn_buf, 0, ffn_buf.shape[1]),
    )
    orders = (list(range(1, depth)) + [0], list(range(depth - 1, -1, -1)))
    started = []

    def part_of(piece, stream, slot):
        buffer, first, count = pieces[piece]
        return buffer.at[slot, pl.ds(first, count), lanes_of(stream)]

    def copy(piece, stream, step, place, slot):
        part = part_of(piece, stream, slot)
        index = 2**step - 1 + place
        return pltpu.make_async_remote_copy(
            src_ref=part, dst_ref=part,
            send_sem=send_sem.at[piece, stream, index],
            recv_sem=recv_sem.at[piece, stream, index],
            device_id={"dp": flip(me, orders[stream][step])},
            device_id_type=MESH,
        )

    def start(piece, step):
        for stream in range(2):
            for place, slot in enumerate(combos(me, orders[stream][:step])):
                made = copy(piece, stream, step, place, slot)
                made.start()
                started.append(made)

    def wait(piece, step):
        for stream in range(2):
            peer = flip(me, orders[stream][step])
            for place, slot in enumerate(combos(peer, orders[stream][:step])):
                copy(piece, stream, step, place, slot).wait_recv()

    outs = []

    def put(source, target):
        made = pltpu.make_async_copy(source, target, out_sem.at[len(outs)])
        made.start()
        outs.append(made)

    start(0, 0)
    start(1, 0)

    def cast(target, first, source):
        count = source.shape[0]
        target[me, first : first + count, : source.shape[1]] = source.astype(LOW)

    for part in range(4):
        cast(shared_buf, part * plan.proj, proj_in[part])
    cast(shared_buf, plan.places_at, places_in[...])
    cast(shared_buf, plan.visual_at, visual_in[...])
    pieces_box = plan.box // 32
    for part in range(plan.box_parts):
        row, lane = plan.box_slot(part)
        first = 32 * (part % pieces_box)
        shared_buf[me, row : row + 32, lane : lane + LANES] = boxes_in[
            part // pieces_box, first : first + 32, :
        ].astype(LOW)
    row, lane = plan.box_slot(plan.box_parts)
    cut = small_in.shape[1]
    shared_buf[me, row : row + 32, lane : lane + LANES] = jnp.zeros((32, LANES), LOW)
    shared_buf[me, row : row + VROWS, lane : lane + cut] = small_in[...].astype(LOW)
    for part in range(plan.box_parts + 1, 6 * (plan.shared - plan.box_at) // 32):
        spare_row, spare_lane = plan.box_slot(part)
        shared_buf[me, spare_row : spare_row + 32, spare_lane : spare_lane + LANES] = jnp.zeros(
            (32, LANES), LOW
        )
    ffn_rows = ffn_out.shape[2]
    wide = ffn_in.shape[2]
    for part in range(2):
        at, shift = ffn_slot(part, 0, ffn_rows, wide)
        ffn_buf[me, at : at + ffn_in.shape[1], shift : shift + wide] = ffn_in[part].astype(LOW)

    start(2, 0)

    vocab, room = rows * dp, got.shape[1]
    tokens = tokens_ref[...]
    first = lax.broadcasted_iota(jnp.int32, (TEXT, TEXT), 0)
    second = lax.broadcasted_iota(jnp.int32, (TEXT, TEXT), 1)
    before = jnp.where(first < second, 1.0, 0.0).astype(LOW)

    def ranked(ids, shard):
        inside = (ids >= shard * vocab) & (ids < (shard + 1) * vocab)
        rank = mm(jnp.where(inside, 1.0, 0.0).astype(LOW), before, NN).astype(jnp.int32)
        return inside, rank

    inside, rank = ranked(tokens, here)
    key_ref[...] = jnp.where(inside & (rank < room), rank, -1)
    own = tokens_ref[pl.ds(here, 1), :]
    place = jnp.full((1, TEXT), -1, jnp.int32)
    for shard in range(mp):
        inside, rank = ranked(own, shard)
        place = jnp.where(inside & (rank < room), rank + shard * room, place)
    place_out[...] = place
    most = jnp.zeros((mp, 1), WIDE)
    for shard in range(mp):
        inside = (tokens >= shard * vocab) & (tokens < (shard + 1) * vocab)
        most = jnp.maximum(most, jnp.sum(jnp.where(inside, 1.0, 0.0), -1, keepdims=True))
    most = jnp.max(most, 0, keepdims=True)
    most_ref[me] = jnp.broadcast_to(most, (8, LANES))
    most_copies = []
    for other in range(1, dp):
        made = pltpu.make_async_remote_copy(
            src_ref=most_ref.at[me], dst_ref=most_ref.at[me],
            send_sem=most_send.at[other], recv_sem=most_recv.at[other],
            device_id={"dp": lax.rem(me + other, dp)}, device_id_type=MESH,
        )
        made.start()
        most_copies.append(made)
    ids = tokens - here * vocab
    if table_rows != rows:
        ids = jnp.where(ids >= 0, ids // rows * table_rows + ids % rows, 0)
    ids_ref[...] = ids
    entry = lax.broadcasted_iota(jnp.int32, (room, TEXT), 0)

    def listed(slot):
        chosen = entry == key_ref[pl.ds(slot, 1), :]
        return jnp.sum(jnp.where(chosen, ids_ref[pl.ds(slot, 1), :] + 1, 0), -1, keepdims=True) - 1

    turns = [lax.rem(here + other, mp) for other in range(1, mp)] + [here]
    lists = [listed(slot) for slot in turns]
    columns = jnp.concatenate([listed(slot) for slot in range(mp)], 0)
    all_room = room * mp
    corner = lax.broadcasted_iota(jnp.int32, (all_room, all_room), 0) == lax.broadcasted_iota(
        jnp.int32, (all_room, all_room), 1
    )
    ids_out[...] = column_sum(jnp.where(corner, columns, 0))

    rows_ref[...] = base_in[...]
    rows_ref[0:4, 0:TEXT] = box_in[...]
    rows_ref[4:5, 0:TEXT] = box_in[3:4, :] - box_in[1:2, :]
    rows_ref[5:6, 0:TEXT] = box_in[2:3, :] - box_in[0:1, :]
    rows_ref[7:8, 0:TEXT] = segment_in[...]
    rows_ref[8:9, 0:TEXT] = alive_in[...]

    def row_of(width, count, source):
        place = lax.broadcasted_iota(jnp.int32, (1, width), 1)
        return lax.fori_loop(
            0, count, lambda index, row: jnp.where(place == index, source(index), row),
            jnp.zeros((1, width), jnp.int32),
        )

    slots = pos_ref.shape[0]
    rows_ref[9:10, :] = row_of(ROWS, slots, lambda index: pos_ref[index])
    for marks_ref, (begin, size) in zip((marks_zero, marks_one), halves_of(slots)):
        for kind, source in enumerate((label_in, valid_in)):
            marks_ref[kind : kind + 1, :] = row_of(
                size * mp, size * mp,
                lambda index: source[index // size * slots + begin + index % size],
            )
    corner = lax.broadcasted_iota(jnp.int32, (ROWS, ROWS), 0) == lax.broadcasted_iota(
        jnp.int32, (ROWS, ROWS), 1
    )
    columns_ref[...] = jnp.zeros((ROWS, 16), jnp.int32)
    for index in range(9):
        columns_ref[:, index : index + 1] = jnp.sum(
            jnp.where(corner, rows_ref[index : index + 1, :], 0), -1, keepdims=True
        )

    for step in range(depth):
        for piece in range(2):
            wait(piece, step)
            if step < depth - 1:
                start(piece, step + 1)
        if step == depth - 2:
            wait(2, 0)
            start(2, 1)
            start(3, 0)
    put(table_buf, table_out)

    word_copies = []
    for turn in range(0, mp, 2):
        wanted = jnp.concatenate(lists[turn : turn + 2], 0)
        column = lax.broadcasted_iota(jnp.int32, (2 * room, dp * table_rows), 1)
        hot = jnp.where(column == wanted, 1.0, 0.0).astype(LOW)
        found = mm(hot, table_buf[...].reshape(dp * table_rows, D), NN).astype(LOW)
        for part in range(2):
            slot = turns[turn + part]
            rows_of = found[part * room : (part + 1) * room]
            if turn + part == mp - 1:
                got[here] = rows_of
                continue
            packed[turn + part] = rows_of
            made = pltpu.make_async_remote_copy(
                src_ref=packed.at[turn + part], dst_ref=got.at[here],
                send_sem=word_send.at[turn + part], recv_sem=word_recv.at[turn + part],
                device_id={"mp": slot}, device_id_type=MESH,
            )
            made.start()
            word_copies.append(made)

    wait(3, 0)
    start(3, 1)
    start(4, 0)

    def finish(piece):
        for step in range(1, depth):
            wait(piece, step)
            if step < depth - 1:
                start(piece, step + 1)

    finish(2)
    put(shared_buf.at[:, pl.ds(plan.places_at, plan.places)], places_out)
    put(shared_buf.at[:, pl.ds(plan.visual_at, plan.visual)], visual_out)
    for part in range(plan.box_parts):
        at, shift = plan.box_slot(part)
        put(
            shared_buf.at[:, pl.ds(at, 32), pl.ds(shift, LANES)],
            boxes_out.at[part // pieces_box, :, pl.ds(32 * (part % pieces_box), 32)],
        )
    for part in range(plan.box_parts):
        at, shift = plan.box_slot(part)
        for owner in range(dp):
            line = owner * plan.box + 32 * (part % pieces_box)
            boxes_ref[part // pieces_box, line : line + 32, :] = shared_buf[
                owner, at : at + 32, shift : shift + LANES
            ]
    row, lane = plan.box_slot(plan.box_parts)
    for part in range(dp):
        small_out[:, part * cut : (part + 1) * cut] = shared_buf[
            part, row : row + 24, lane : lane + cut
        ].astype(WIDE)

    def whole_rows(first, count):
        part = shared_buf[:, first : first + count // dp, :]
        return part.reshape(count, D)

    front_early(
        pos_ref, whole_rows(plan.places_at, TEXT), whole_rows(plan.visual_at, VCH), features_ref,
        boxes_ref, small_out, columns_ref, rows_ref, scratch,
    )
    for other in range(1, mp):
        source = lax.rem(here + mp - other, mp)
        pltpu.make_async_copy(got.at[source], got.at[source], word_recv.at[other - 1]).wait()
    across = jnp.sum(jnp.where(first == second, place, 0), -1, keepdims=True)
    column = lax.broadcasted_iota(jnp.int32, (TEXT, all_room), 1)
    hot = jnp.where(column == across, 1.0, 0.0).astype(LOW)
    word = mm(hot, got[...].reshape(all_room, D), NN)

    stages = [0]

    def hook():
        stage = stages[0]
        stages[0] = stage + 1
        if stage == 0:
            finish(3)
            for part in range(4):
                put(shared_buf.at[:, pl.ds(part * plan.proj, plan.proj)], proj_out.at[part])
        if stage < depth:
            wait(4, stage)
            if stage < depth - 1:
                start(4, stage + 1)
        for number in {0: (1, 2, 3, 4, 5), 1: (6, 7, 8)}.get(stage, ()):
            put(outs_buf[number], outs_ref[number])

    front_late(
        pos_ref, word, small_out, rows_ref, lambda part: whole_rows(part * plan.proj, D), hook,
        outs_buf, scratch,
    )
    put(outs_buf[0], outs_ref[0])
    put(outs_buf[9], outs_ref[9])
    while stages[0] < depth:
        hook()
    for other in range(1, dp):
        source = lax.rem(me + dp - other, dp)
        pltpu.make_async_copy(
            most_ref.at[source], most_ref.at[source], most_recv.at[other]
        ).wait()
    most = most_ref[0]
    for part in range(1, dp):
        most = jnp.maximum(most, most_ref[part])
    most_out[...] = most[0:1, 0:1]
    for part in range(2):
        at, shift = ffn_slot(part, 0, ffn_rows, wide)
        put(ffn_buf.at[:, pl.ds(at, ffn_rows), pl.ds(shift, wide)], ffn_out.at[part])
    for made in started:
        made.wait_send()
    for made in word_copies + most_copies:
        made.wait_send()
    for made in outs:
        made.wait()


def word_room(mp):
    return pad_up(TEXT // mp * 11 // 8, 16)


def front_step(
    plan, pos, label, valid, word, proj, boxes, places, visual, small, ffn, tokens, box, segment,
    alive, features,
):
    dp, mp = plan.dp, plan.mp
    slots = pos.shape[0]
    table_rows, ffn_rows, wide = pad_up(word.shape[0], 32), pad_up(ffn.shape[1], 16), ffn.shape[2]
    ffn_all = 2 * ffn_rows * wide // D
    room = word_room(mp)
    anywhere = pl.BlockSpec(memory_space=pl.ANY)
    vmem = pl.BlockSpec(memory_space=pltpu.VMEM)
    smem = pl.BlockSpec(memory_space=pltpu.SMEM)
    dma = pltpu.SemaphoreType.DMA
    shape = jax.ShapeDtypeStruct
    outs, scratch = front_shapes(slots)

    def body(*refs):
        gather_kernel(plan, table_rows, refs)

    return pl.pallas_call(
        body,
        out_shape=(
            shape((dp, table_rows, D), LOW), shape((4, dp, plan.proj, D), LOW),
            shape((4, dp, plan.box, LANES), LOW), shape((dp, plan.places, D), LOW),
            shape((dp, plan.visual, D), LOW), shape((2, dp, ffn_rows, wide), LOW),
            shape((24, D), WIDE), shape((1, TEXT), jnp.int32), shape((1, mp * room), jnp.int32),
            shape((1, 1), WIDE), shape((16, ROWS), jnp.int32), shape((ROWS, 16), jnp.int32),
            *(shape((2, mp * size), jnp.int32) for _, size in halves_of(slots)),
            *outs,
        ),
        in_specs=[smem] * 3 + [vmem] * 13,
        out_specs=(anywhere,) * 6 + (vmem,) * 8 + (anywhere,) * 10,
        scratch_shapes=[
            *scratch,
            *(pltpu.VMEM(part.shape, part.dtype) for part in outs),
            pltpu.VMEM((dp, table_rows, D), LOW),
            pltpu.VMEM((dp, plan.shared, D), LOW),
            pltpu.VMEM((dp, ffn_all, D), LOW),
            pltpu.VMEM((4, NBOX, LANES), LOW),
            pltpu.VMEM((mp - 1, room, D), LOW),
            pltpu.VMEM((mp, room, D), LOW),
            pltpu.VMEM((mp, TEXT), jnp.int32),
            pltpu.VMEM((mp, TEXT), jnp.int32),
            pltpu.VMEM((dp, 8, LANES), WIDE),
            dma((plan.box_parts + 20,)),
            dma((5, 2, dp - 1)),
            dma((5, 2, dp - 1)),
            dma((mp - 1,)),
            dma((mp - 1,)),
            dma((dp,)),
            dma((dp,)),
        ],
        compiler_params=pltpu.CompilerParams(
            collective_id=1, has_side_effects=True, vmem_limit_bytes=60 * 2**20
        ),
        name="front_step",
    )(
        pos, label, valid, word, proj, boxes, places, visual, small, ffn, tokens, box, segment,
        alive, features, token_base(),
    )


def back_kernel(plan, table_rows, ffn_rows, refs):
    (
        pos_ref, grad_zero_ref, grad_mixed_ref, shares_ref, query_ref, key_ref, value_ref,
        zero_low_ref, low_ref, plain_ref, scale_ref, features_ref, small_ref, columns_ref,
        rows_ref, weights_in, table_in, out_in, ffn_in, head_in, bias_in, tile_in, place_in, ids_in,
        shared_out, split_out, tile_out, word_out,
        slot_ref, score_ref, grad_query, grad_key, grad_value, grad_rows, grad_low, turned_ref,
        grad_slot, edges_ref, weights_ref,
        shared_acc, split_acc, shared_got, split_got, ring_got, ring_own, half_got, half_own, packed, words, small_all,
        tile_mp, tile_dp,
        load_sem, send_sem, recv_sem, ring_send, ring_recv, word_send, word_recv, tile_send,
        tile_recv,
    ) = refs
    dp, mp = plan.dp, plan.mp
    me, here = lax.axis_index("dp"), lax.axis_index("mp")
    depth, ring_depth = bits_of(dp), bits_of(mp)
    slots = grad_zero_ref.shape[0]
    loads = []
    if plan.proj * dp != D:
        shared_acc[...] = jnp.zeros(shared_acc.shape, LOW)

    def load(source, target):
        loads.append(pltpu.make_async_copy(source, target, load_sem.at[len(loads)]))
        loads[-1].start()

    load(out_in, shared_acc.at[:, pl.ds(3 * plan.proj, plan.proj)])
    for part in range(2):
        wide = ffn_in.shape[3]
        row, lane = ffn_slot(part, table_rows, ffn_rows, wide)
        load(ffn_in.at[part], split_acc.at[:, pl.ds(row, ffn_rows), pl.ds(lane, wide)])
    load(weights_in.at[0:3], weights_ref)
    load(table_in, split_acc.at[:, pl.ds(0, table_rows)])

    barrier = pltpu.get_barrier_semaphore()
    for other in range(1, dp):
        pl.semaphore_signal(
            barrier, 1, device_id={"dp": lax.rem(me + other, dp)}, device_id_type=MESH
        )
    for other in range(1, mp):
        pl.semaphore_signal(
            barrier, 1, device_id={"mp": lax.rem(here + other, mp)}, device_id_type=MESH
        )
    pl.semaphore_wait(barrier, dp + mp - 2)

    orders = ([0] + list(range(depth - 1, 0, -1)), list(range(depth)))
    out_at, rest = 3 * plan.proj, split_acc.shape[1] - table_rows
    pieces = (
        (shared_acc, shared_got, out_at, plan.proj),
        (shared_acc, shared_got, 0, out_at),
        (shared_acc, shared_got, plan.places_at, plan.shared - plan.places_at),
        (split_acc, split_got, table_rows, rest),
        (split_acc, split_got, 0, table_rows // 2),
        (split_acc, split_got, table_rows // 2, table_rows // 2),
    )

    def chunk(order, step, free, away):
        index = 0
        for place, bit in enumerate(order):
            mine = (me // 2**bit) % 2
            if place < step or (place == step and not away):
                index = index + mine * 2**bit
            elif place == step:
                index = index + (1 - mine) * 2**bit
            else:
                index = index + ((free >> (place - step - 1)) & 1) * 2**bit
        return index

    def slot_base(step):
        return sum(2 ** (depth - 1 - s) for s in range(step))

    def send_one(piece, stream, step, free):
        acc, got, first, rows = pieces[piece]
        order = orders[stream]
        pltpu.make_async_remote_copy(
            src_ref=acc.at[chunk(order, step, free, True), pl.ds(first, rows), lanes_of(stream)],
            dst_ref=got.at[slot_base(step) + free, pl.ds(first, rows), lanes_of(stream)],
            send_sem=send_sem.at[piece, stream, step],
            recv_sem=recv_sem.at[piece, stream, step],
            device_id={"dp": flip(me, order[step])},
            device_id_type=MESH,
        ).start()

    def send(piece, step):
        for stream in range(2):
            for free in range(2 ** (depth - 1 - step)):
                send_one(piece, stream, step, free)

    def wait_bytes(piece, stream, step, sem):
        acc, got, first, rows = pieces[piece]
        count = 2 ** (depth - 1 - step)
        where = got.at[pl.ds(slot_base(step), count), pl.ds(first, rows), lanes_of(stream)]
        pltpu.make_async_copy(where, where, sem.at[piece, stream, step]).wait()

    def add(piece, stream, step):
        acc, got, first, rows = pieces[piece]
        order = orders[stream]
        wait_bytes(piece, stream, step, recv_sem)
        tile = row_tile(rows)
        last = step == depth - 1
        for free in range(2 ** (depth - 1 - step)):
            kept = chunk(order, step, free, False)

            def body(index, carry):
                at = pl.multiple_of(first + index * tile, 16)
                where = pl.ds(at, tile)
                total = acc[kept, where, lanes_of(stream)].astype(WIDE) + got[
                    slot_base(step) + free, where, lanes_of(stream)
                ].astype(WIDE)
                if last and acc is split_acc:
                    split_out[where, lanes_of(stream)] = total
                elif last:
                    ring_own[where, lanes_of(stream)] = total.astype(LOW)
                else:
                    acc[kept, where, lanes_of(stream)] = total.astype(LOW)
                return carry

            lax.fori_loop(0, rows // tile, body, 0)

    parity = lax.rem(here, 2)
    mine = pl.ds(pl.multiple_of(parity * HALF, LANES), HALF)
    other_half = pl.ds(pl.multiple_of((1 - parity) * HALF, LANES), HALF)

    def ring_copy(piece, step):
        where = pl.ds(pieces[piece][2], pieces[piece][3])
        if step == 0:
            source, target = ring_own.at[where, other_half], ring_got.at[where]
        else:
            source, target = half_own.at[step - 1, where], half_got.at[step - 1, where]
        return pltpu.make_async_remote_copy(
            src_ref=source,
            dst_ref=target,
            send_sem=ring_send.at[piece, step],
            recv_sem=ring_recv.at[piece, step],
            device_id={"mp": flip(here, step % ring_depth)},
            device_id_type=MESH,
        )

    def ring_step(piece, step):
        first, rows = pieces[piece][2:]
        ring_copy(piece, step).wait_recv()
        tile = row_tile(rows)

        def body(index, carry):
            where = pl.ds(pl.multiple_of(first + index * tile, 16), tile)
            if step == 0:
                total = ring_own[where, mine].astype(WIDE) + ring_got[where, :].astype(WIDE)
            elif step < ring_depth:
                total = half_own[step - 1, where, :].astype(WIDE) + half_got[
                    step - 1, where, :
                ].astype(WIDE)
            if step < ring_depth:
                half_own[step, where, :] = total.astype(LOW)
            else:
                shared_out[where, mine] = half_own[step - 1, where, :].astype(WIDE)
                shared_out[where, other_half] = half_got[step - 1, where, :].astype(WIDE)
            return carry

        lax.fori_loop(0, rows // tile, body, 0)
        if step < ring_depth:
            ring_copy(piece, step + 1).start()

    def advance(piece, step):
        for stream in range(2):
            add(piece, stream, step)
            if step < depth - 1:
                for free in range(2 ** (depth - 2 - step)):
                    send_one(piece, stream, step + 1, free)
        if step == depth - 1 and piece < 3:
            ring_copy(piece, 0).start()

    room = words.shape[1]

    def scatter(index):
        local = ids_in[...] - index * table_rows
        entry = lax.broadcasted_iota(jnp.int32, (table_rows, mp * room), 0)
        hot = jnp.where(entry == local, 1.0, 0.0).astype(LOW)
        where = (index, pl.ds(0, table_rows))
        total = split_acc[where].astype(WIDE) + mm(hot, words[...].reshape(mp * room, D), NN)
        split_acc[where] = total.astype(LOW)

    count = 2 ** (depth - 1)
    other_core, own_core = 1 - me % 2, me % 2

    def scatter_other(index, carry):
        scatter(other_core + 2 * index)
        return carry

    def scatter_own(index, carry):
        scatter(own_core + 2 * index)
        return carry

    for copy in loads[:3]:
        copy.wait()
    send(0, 0)
    send(3, 0)

    take_slots(slots, pos_ref, ((columns_ref, slot_ref),))
    for pair in range(H // 2):
        lanes = slice(pair * LANES, (pair + 1) * LANES)
        rows = slice(pair * 2 * slots, (pair + 1) * 2 * slots)
        grad_mixed = pair_rows(grad_mixed_ref[:, lanes])
        shares = shares_ref[rows, :]
        grad_value[:, lanes] = mm(shares.astype(LOW), grad_mixed, TN).astype(LOW)
        grad_shares = mm(grad_mixed, value_ref[:, lanes], NT)
        scores = shares * (grad_shares - jnp.sum(shares * grad_shares, -1, keepdims=True))
        scores = scores.astype(LOW)
        score_ref[rows, :] = scores
        grad_query[:, lanes] = pair_lanes(mm(scores, key_ref[:, lanes], NN) * 0.125).astype(LOW)
        grad_key[:, lanes] = (mm(scores, pair_rows(query_ref[:, lanes]), TN) * 0.125).astype(LOW)
    advance(0, 0)
    advance(3, 0)

    loads[3].wait()
    grad_slot[...] = grad_zero_ref[...] + mm(grad_query[...], weights_ref[0], NT)
    entry = lax.broadcasted_iota(jnp.int32, (ROWS, slots), 0)
    put = jnp.where(entry == rows_ref[9:10, 0:slots], 1.0, 0.0).astype(LOW)
    high = grad_slot[...].astype(LOW)
    small_part = (grad_slot[...] - high.astype(WIDE)).astype(LOW)
    grad_rows[...] = (
        mm(grad_key[...], weights_ref[1], NT)
        + mm(grad_value[...], weights_ref[2], NT)
        + (mm(put, high, NN) + mm(put, small_part, NN))
    )
    gain = small_ref[0:1, :]
    tile = 96

    def normed_back(index, carry):
        where = pl.ds(pl.multiple_of(index * tile, 16), tile)
        grad, plain = grad_rows[where, :], plain_ref[where, :]
        value = norm_back(grad, plain, scale_ref[where, :], gain)
        grad_rows[where, :] = value
        grad_low[where, :] = value.astype(LOW)
        return carry[0] + column_sum(grad * plain), carry[1] + column_sum(grad)

    blank = jnp.zeros((1, D), WIDE)
    gains, shifts = lax.fori_loop(0, ROWS // tile, normed_back, (blank, blank))
    small_all[0:1, :] = gains
    small_all[1:2, :] = shifts

    keep_words = pltpu.make_async_copy(grad_low.at[0:TEXT], word_out, load_sem.at[5])
    keep_words.start()
    entry = lax.broadcasted_iota(jnp.int32, (mp * room, TEXT), 0)
    hot = jnp.where(entry == place_in[...], 1.0, 0.0).astype(LOW)
    packed[...] = mm(hot, grad_low[0:TEXT, :], NN).astype(LOW).reshape(mp, room, D)
    word_copies = []
    for other in range(1, mp):
        target = lax.rem(here + other, mp)
        word_copies.append(
            pltpu.make_async_remote_copy(
                src_ref=packed.at[target], dst_ref=words.at[here],
                send_sem=word_send.at[other - 1], recv_sem=word_recv.at[other - 1],
                device_id={"mp": target}, device_id_type=MESH,
            )
        )
        word_copies[-1].start()
    words[here] = packed[here]

    rows = D // dp
    for part, (left, right) in enumerate(
        ((zero_low_ref, grad_query), (low_ref, grad_key), (low_ref, grad_value))
    ):
        grad = mm(left[...], right[...], TN).reshape(dp, rows, D)
        first = part * plan.proj
        shared_acc[:, first : first + rows, :] = grad.astype(LOW)
    send(1, 0)
    advance(0, 1)
    advance(3, 1)

    extra, rows = ROWS - TEXT, TEXT // dp
    grad_rows[0:extra, :] = grad_rows[0:extra, :] + grad_rows[TEXT:ROWS, :]
    first = plan.places_at
    shared_acc[:, first : first + rows, :] = grad_rows[0:TEXT, :].reshape(dp, rows, D).astype(LOW)
    visual, rows, first = features_ref.shape[0], VCH // dp, plan.visual_at
    grad = mm(features_ref[...], grad_low[TEXT : TEXT + visual, :], TN)
    shared_acc[:, first : first + rows, :] = grad.reshape(dp, rows, D).astype(LOW)
    block = max(plan.box, 256)
    chunks, pieces_box = block // plan.box, plan.box // 32

    def table(index, carry):
        entry = lax.broadcasted_iota(jnp.int32, (block, ROWS), 0) + index * block
        found = []
        for column in range(6):
            hot = jnp.where(entry == rows_ref[column : column + 1, :], 1.0, 0.0).astype(LOW)
            found.append(mm(hot, grad_low[:, column * LANES : (column + 1) * LANES], NN))
        for number, grad in enumerate((found[0] + found[2], found[1] + found[3], *found[4:])):
            for part in range(block // 32):
                at, lane = plan.box_slot(number * pieces_box + part % pieces_box)
                shared_acc[index * chunks + part // pieces_box, at : at + 32, lane : lane + LANES] = (
                    grad[part * 32 : part * 32 + 32].astype(LOW)
                )
        return carry

    lax.fori_loop(0, NBOX // block, table, 0)
    advance(1, 0)

    lane = lax.broadcasted_iota(jnp.int32, (NB, LANES), 1)
    for kind in range(3):
        column, shift = KINDS[kind]
        first, second = key_hot(rows_ref, kind)
        below = below_of(rows_ref, slot_ref, kind)
        coarse_slot = jnp.right_shift(slot_ref[:, column : column + 1], shift)
        place = lax.broadcasted_iota(jnp.int32, (slots, NB), 1)
        hot = jnp.where(place == NB - 1 - coarse_slot, 1.0, 0.0).astype(LOW)

        def collect(pair, carry):
            where = pl.ds(pl.multiple_of(pair * 2 * slots, 16), 2 * slots)
            both = jnp.concatenate([below, below], 0)
            scores = score_ref[where, :]
            none = jnp.zeros((), LOW)
            found = mm(jnp.where(both, none, scores), first, NT) + mm(
                jnp.where(both, scores, none), second, NT
            )
            turned_ref[where, :] = found.astype(LOW)
            return carry

        lax.fori_loop(0, H // 2, collect, 0)
        for head in range(H):
            part = mm(hot, turned_ref[head * slots : (head + 1) * slots, :], TN)
            near = pltpu.roll(jnp.where(lane < NB, part, 0.0), 1, 1, stride=1, stride_axis=0)
            far = pltpu.roll(jnp.where(lane < NB, 0.0, part), NB, 1, stride=1, stride_axis=0)
            edges_ref[head : head + 1, :] = column_sum(near + far)
        edges_ref[H:16, :] = jnp.zeros((16 - H, LANES), WIDE)
        small_all[14 + kind : 15 + kind, :] = edge_rows_back(edges_ref[...])

    hidden = bias_in.shape[1]
    start = here * hidden
    small_all[2:3, :] = column_sum(grad_query[...].astype(WIDE))
    small_all[3:4, :] = column_sum(grad_value[...].astype(WIDE))
    small_all[4:10, :] = head_in[4:10, :]
    small_all[10:14, :] = jnp.zeros((4, D), WIDE)
    small_all[
        pl.ds(10 + start // D, 1), pl.ds(pl.multiple_of(lax.rem(start, D), LANES), hidden)
    ] = bias_in[...]
    cut = D // dp
    row, lane = plan.box_slot(plan.box_parts)
    shared_acc[:, pl.ds(row, 32), pl.ds(lane, LANES)] = jnp.zeros((dp, 32, LANES), LOW)
    for part in range(dp):
        shared_acc[part, row : row + VROWS, lane : lane + cut] = small_all[
            0:VROWS, part * cut : (part + 1) * cut
        ].astype(LOW)
    for part in range(plan.box_parts + 1, 6 * (plan.shared - plan.box_at) // 32):
        row, lane = plan.box_slot(part)
        shared_acc[:, pl.ds(row, 32), pl.ds(lane, LANES)] = jnp.zeros((dp, 32, LANES), LOW)
    send(2, 0)
    for step in range(2, depth):
        advance(0, step)
        advance(3, step)
    advance(2, 0)
    loads[4].wait()
    for other in range(1, mp):
        source = lax.rem(here + mp - other, mp)
        pltpu.make_async_copy(words.at[source], words.at[source], word_recv.at[other - 1]).wait()
    lax.fori_loop(0, count, scatter_other, 0)
    send(4, 0)
    send(5, 0)
    advance(1, 1)
    ring_step(0, 0)
    lax.fori_loop(0, count, scatter_own, 0)
    ring_step(0, 1)
    for step in range(2, depth - 1):
        advance(1, step)
    advance(2, 1)
    advance(1, depth - 1)
    for step in range(2, depth - 1):
        advance(2, step)
    advance(4, 0)
    advance(5, 0)
    advance(2, depth - 1)
    ring_queue = [(0, step) for step in range(2, ring_depth + 1)]
    ring_queue += [(piece, step) for step in range(ring_depth + 1) for piece in (1, 2)]
    for step in range(1, depth):
        for piece in (4, 5):
            share = -(-len(ring_queue) // (2 * (depth - step) - (piece - 4)))
            for turn in ring_queue[: share - 1 if step == depth - 1 and piece == 5 else share]:
                ring_step(*turn)
                ring_queue.remove(turn)
            advance(piece, step)
    for turn in ring_queue:
        ring_step(*turn)

    def squares(ref, rows):
        tile = row_tile(rows)

        def body(index, total):
            values = ref[pl.ds(pl.multiple_of(index * tile, 16), tile), :]
            return total + jnp.sum((values * values).reshape(tile // 8, 8, D), 0)

        total = lax.fori_loop(0, rows // tile, body, jnp.zeros((8, D), WIDE))
        folded = total[:, 0:LANES]
        for part in range(1, D // LANES):
            folded = folded + total[:, part * LANES : (part + 1) * LANES]
        return folded

    folded = squares(shared_out, plan.shared) * (1.0 / mp) + squares(split_out, split_out.shape[0])
    tile_mp[here, 0] = folded
    tile_mp[here, 1] = tile_in[...]

    def exchange(buffer, axis, index, count, base):
        copies = []
        for other in range(1, count):
            copies.append(
                pltpu.make_async_remote_copy(
                    src_ref=buffer.at[index],
                    dst_ref=buffer.at[index],
                    send_sem=tile_send.at[base + other],
                    recv_sem=tile_recv.at[base + other],
                    device_id={axis: lax.rem(index + other, count)},
                    device_id_type=MESH,
                )
            )
        for copy in copies:
            copy.start()
        for other in range(1, count):
            source = lax.rem(index + count - other, count)
            pltpu.make_async_copy(
                buffer.at[source], buffer.at[source], tile_recv.at[base + other]
            ).wait()
        return copies

    pending = exchange(tile_mp, "mp", here, mp, 0)
    total = tile_mp[0]
    for index in range(1, mp):
        total = total + tile_mp[index]
    tile_dp[me] = total
    pending = pending + exchange(tile_dp, "dp", me, dp, mp)
    total = tile_dp[0]
    for index in range(1, dp):
        total = total + tile_dp[index]
    tile_out[...] = total
    for copy in pending:
        copy.wait_send()
    keep_words.wait()
    for copy in word_copies:
        copy.wait_send()
    for piece in range(len(pieces)):
        for stream in range(2):
            for step in range(depth):
                wait_bytes(piece, stream, step, send_sem)
    for piece in range(3):
        for step in range(ring_depth + 1):
            ring_copy(piece, step).wait_send()


def back_step(
    plan, pos, grad_zero, grad_mixed, shares, query, key, value, zero_low, low, plain, scale,
    features, small, columns, rows, weights, table, out, ffn, head, bias, tile, place, ids,
):
    dp, mp = plan.dp, plan.mp
    slots = pos.shape[0]
    table_rows, ffn_rows = table.shape[1], ffn.shape[2]
    split = table_rows + 2 * ffn_rows * ffn.shape[3] // D
    depth, ring_depth = bits_of(dp), bits_of(mp)
    anywhere = pl.BlockSpec(memory_space=pl.ANY)
    vmem = pl.BlockSpec(memory_space=pltpu.VMEM)
    dma = pltpu.SemaphoreType.DMA
    low_scratch = lambda *shape: pltpu.VMEM(shape, LOW)
    wide_scratch = lambda *shape: pltpu.VMEM(shape, WIDE)

    def body(*refs):
        back_kernel(plan, table_rows, ffn_rows, refs)

    return pl.pallas_call(
        body,
        out_shape=(
            jax.ShapeDtypeStruct((plan.shared, D), WIDE),
            jax.ShapeDtypeStruct((split, D), WIDE),
            jax.ShapeDtypeStruct((2, 8, LANES), WIDE),
            jax.ShapeDtypeStruct((TEXT, D), LOW),
        ),
        in_specs=[pl.BlockSpec(memory_space=pltpu.SMEM)]
        + [vmem] * 14
        + [anywhere] * 4
        + [vmem] * 5,
        out_specs=(vmem, vmem, vmem, anywhere),
        scratch_shapes=[
            pltpu.VMEM((slots, 16), jnp.int32),
            low_scratch(H * slots, ROWS),
            low_scratch(slots, D),
            low_scratch(ROWS, D),
            low_scratch(ROWS, D),
            wide_scratch(ROWS, D),
            low_scratch(ROWS, D),
            low_scratch(H * slots, LANES),
            wide_scratch(slots, D),
            wide_scratch(16, LANES),
            low_scratch(3, D, D),
            low_scratch(dp, plan.shared, D),
            low_scratch(dp, split, D),
            low_scratch(dp - 1, plan.shared, D),
            low_scratch(dp - 1, split, D),
            low_scratch(plan.shared, HALF),
            low_scratch(plan.shared, D),
            low_scratch(ring_depth, plan.shared, HALF),
            low_scratch(ring_depth, plan.shared, HALF),
            low_scratch(mp, word_room(mp), D),
            low_scratch(mp, word_room(mp), D),
            wide_scratch(24, D),
            wide_scratch(mp, 2, 8, LANES),
            wide_scratch(dp, 2, 8, LANES),
            dma((6,)),
            dma((6, 2, depth)),
            dma((6, 2, depth)),
            dma((3, ring_depth + 1)),
            dma((3, ring_depth + 1)),
            dma((mp - 1,)),
            dma((mp - 1,)),
            dma((mp + dp,)),
            dma((mp + dp,)),
        ],
        compiler_params=pltpu.CompilerParams(
            collective_id=5, has_side_effects=True, vmem_limit_bytes=62 * 2**20
        ),
        name="back_step",
    )(
        pos, grad_zero, grad_mixed, shares, query, key, value, zero_low, low, plain, scale,
        features, small, columns, rows, weights, table, out, ffn, head, bias, tile, place, ids,
    )


def on_device(
    tokens, text_box, segments, alive_text, features, mask_pos, mask_label, mask_valid, *states
):
    (projections, box_tables, position_table, visual_proj, small_params, word_table, feedforward) = (
        states[::3]
    )
    dp, mp = lax.axis_size("dp"), lax.axis_size("mp")
    plan = Plan(dp, mp)
    (
        table_parts, proj_parts, box_parts, place_parts, visual_parts, ffn_parts, small, places,
        ids, most, info, columns, marks_zero, marks_one, *front,
    ) = front_step(
        plan, mask_pos, mask_label, mask_valid, word_table, projections, box_tables,
        position_table, visual_proj, small_params, feedforward, tokens, text_box[0].T, segments,
        alive_text, features,
    )

    def joined(parts, rows):
        parts = parts[..., :rows, :]
        return parts.reshape(parts.shape[:-3] + (dp * rows, parts.shape[-1]))

    work_table = joined(table_parts, word_table.shape[0])
    work_proj = joined(proj_parts, D // dp)
    work_boxes = joined(box_parts, NBOX // dp)
    work_places = joined(place_parts, TEXT // dp)
    work_visual = joined(visual_parts, VCH // dp)
    work_ffn = joined(ffn_parts, D // dp)
    vocab_shard = work_table.shape[0]
    room = word_room(mp)
    crowded = most[0, 0] > room

    def local_words():
        local_ids = tokens - lax.axis_index("mp") * vocab_shard
        inside = (local_ids >= 0) & (local_ids < vocab_shard)
        return inside, jnp.clip(local_ids, 0, vocab_shard - 1)

    def exchange_words(state):
        inside, index = local_words()
        found = jnp.where(inside[..., None], jnp.take(work_table, index, axis=0), jnp.zeros((), LOW))
        word = lax.psum_scatter(found, "mp", scatter_dimension=0, tiled=True)[0]
        again = front_again(
            mask_pos, word, features, work_places, work_boxes, work_visual, small, columns, info,
            work_proj,
        )
        return (False, *again)

    _, *front = lax.while_loop(lambda state: state[0], exchange_words, (crowded, *front))
    (
        mixed, slot_zero, slot_low, normed_low, plain, scale, queries, keys, values, shares,
    ) = front
    (
        grad_slot, grad_mixed, grad_out_weight, grad_ffn, grad_table, head_rows, grad_ffn_bias,
        own_tile,
    ) = head_step(
        mp, mixed, slot_zero, work_proj, small, work_ffn, work_table,
        marks_zero, marks_one,
    )
    def split_rows(part):
        rows = part.shape[-2] // dp
        part = part.astype(LOW).reshape(part.shape[:-2] + (dp, rows, part.shape[-1]))
        extra = [(0, 0)] * (part.ndim - 2) + [(0, pad_up(rows, 16) - rows), (0, 0)]
        return jnp.pad(part, extra) if extra[-2][1] else part

    table_split, ffn_split = split_rows(grad_table), split_rows(grad_ffn)
    shared_sum, split_sum, totals, grad_word = back_step(
        plan, mask_pos, grad_slot, grad_mixed, shares, queries, keys, values, slot_low, normed_low,
        plain, scale, features, small, columns, info, work_proj, table_split,
        split_rows(grad_out_weight), ffn_split, head_rows, grad_ffn_bias, own_tile, places, ids,
    )
    def exchange_word_gradients(state):
        inside, index = local_words()
        shard = tokens // vocab_shard
        same = (shard[..., None] == jnp.arange(mp)).astype(jnp.int32)
        rank = jnp.sum((jnp.cumsum(same, 1) - same) * same, -1)
        late = rank >= room
        own = lax.dynamic_index_in_dim(late, lax.axis_index("mp"), 0, False)
        sent = jnp.where(own[:, None], grad_word, jnp.zeros((), LOW))
        group = lax.all_gather(sent, "mp", axis=0).astype(WIDE)
        group = jnp.where((inside & late)[..., None], group, 0.0)
        extra = jnp.zeros((vocab_shard, D), WIDE).at[index].add(group)
        part = lax.psum_scatter(extra, "dp", scatter_dimension=0, tiled=True)
        split = state[1].at[: part.shape[0]].add(part)
        squares = jnp.sum(shared_sum * shared_sum) / mp + jnp.sum(split * split)
        squares = lax.psum(squares, ("dp", "mp"))
        return False, split, jnp.zeros_like(totals).at[0, 0, 0].set(squares).at[1].set(totals[1])

    _, split_sum, totals = lax.while_loop(
        lambda state: state[0], exchange_word_gradients, (crowded, split_sum, totals)
    )
    outputs = adam_update(
        plan, table_split.shape[1], ffn_split.shape[2], shared_sum, split_sum, totals, states
    )
    return tuple(outputs[:21]) + tuple(part.reshape(()) for part in outputs[21:])


def solution(mesh):
    in_specs = (
        P("dp", None),
        P(("dp", "mp"), None, None),
        P(("dp", "mp"), None),
        P(("dp", "mp"), None),
        P(("dp", "mp"), None),
        P(("dp", "mp")),
        P("dp"),
        P("dp"),
        P(None, "dp", None),
        P(None, "dp", None),
        P(None, "dp", None),
        P(None, "dp", None),
        P(None, "dp", None),
        P(None, "dp", None),
        P("dp", None),
        P("dp", None),
        P("dp", None),
        P("dp", None),
        P("dp", None),
        P("dp", None),
        P(None, "dp"),
        P(None, "dp"),
        P(None, "dp"),
        P(("mp", "dp"), None),
        P(("mp", "dp"), None),
        P(("mp", "dp"), None),
        P(None, "dp", "mp"),
        P(None, "dp", "mp"),
        P(None, "dp", "mp"),
    )
    out_specs = (
        P(None, "dp", None),
        P(None, "dp", None),
        P(None, "dp", None),
        P(None, "dp", None),
        P(None, "dp", None),
        P(None, "dp", None),
        P("dp", None),
        P("dp", None),
        P("dp", None),
        P("dp", None),
        P("dp", None),
        P("dp", None),
        P(None, "dp"),
        P(None, "dp"),
        P(None, "dp"),
        P(("mp", "dp"), None),
        P(("mp", "dp"), None),
        P(("mp", "dp"), None),
        P(None, "dp", "mp"),
        P(None, "dp", "mp"),
        P(None, "dp", "mp"),
        P(),
        P(),
        P(),
    )
    return jax.shard_map(
        on_device, mesh=mesh, in_specs=in_specs, out_specs=out_specs, check_vma=False
    )
```

```python
import jax
import jax.numpy as jnp
import numpy as np
from jax import lax
from jax.experimental import pallas as pl
from jax.experimental.pallas import tpu as pltpu
from jax.sharding import PartitionSpec as P

D = 768
H = 12
HD = 64
FF = 3072
NB = 64
GRID = 7
TEXT = 512
STEP = 10
VCH = 256
NBOX = 1024
VROWS = 17


MASKED = -1e30
CLIP = 0.005
BETA_ONE = 0.9
BETA_TWO = 0.999
EPSILON = 1e-08
DECAY = 0.01
RATES = (0.02, 0.03, 0.03, 0.04, 0.3, 0.05, 0.02)


def adam_step(weight, grad, first, second, rate):
    first = BETA_ONE * first + (1.0 - BETA_ONE) * grad
    second = BETA_TWO * second + (1.0 - BETA_TWO) * grad * grad
    fixed_first = first * (1.0 / (1.0 - BETA_ONE**STEP))
    fixed_second = second * (1.0 / (1.0 - BETA_TWO**STEP))
    weight = weight - rate * (fixed_first / (jnp.sqrt(fixed_second) + EPSILON) + DECAY * weight)
    return (weight, first, second)


MESH = pl.DeviceIdType.MESH
LOW = jnp.bfloat16
WIDE = jnp.float32
LANES = 128
HALF = D // 2


def pad_up(count, unit):
    return (count + unit - 1) // unit * unit


def bits_of(count):
    return count.bit_length() - 1


def flip(index, bit):
    return index + (1 - 2 * ((index // 2**bit) % 2)) * 2**bit


class Plan:
    def __init__(self, dp, mp):
        self.dp, self.mp = dp, mp
        self.proj = pad_up(D // dp, 16)
        self.places = pad_up(TEXT // dp, 16)
        self.visual = pad_up(VCH // dp, 16)
        self.box = NBOX // dp
        self.box_parts = 4 * (self.box // 32)
        self.places_at = 4 * self.proj
        self.visual_at = self.places_at + self.places
        self.box_at = self.visual_at + self.visual
        self.box_rows = 32 * ((self.box_parts + 6) // 6)
        self.shared = pad_up(self.box_at + self.box_rows, 32 * mp)

    def box_slot(self, part):
        return self.box_at + 32 * (part // 6), LANES * (part % 6)


def group_of(axis, index):
    return {axis: index}


def lanes_of(stream):
    return pl.ds(stream * HALF, HALF)


def ffn_slot(part, table_rows, ffn_rows, wide):
    return table_rows + part * wide // D * ffn_rows, part * wide % D


def row_tile(rows):
    return next(t for t in (48, 32, 16) if rows % t == 0)


def adam_kernel(plan, table_rows, ffn_rows, refs):
    shared_ref, split_ref, tile_ref = refs[:3]
    states, outs, scalars = refs[3:24], refs[24:45], refs[45:48]
    held, load_sem, store_sem = refs[48:69], refs[69], refs[70]
    order = (5, 6, 0, 1, 2, 3, 4)
    loads, stores = {}, []
    for index in order:
        for part in range(3 * index, 3 * index + 3):
            loads[part] = pltpu.make_async_copy(states[part], held[part], load_sem.at[part])
            loads[part].start()
    totals = tile_ref[...]
    count = totals[1, 1:2, 0:1]
    norm = jnp.sqrt(jnp.sum(totals[0], keepdims=True)) / count
    scale = jnp.minimum(1.0, CLIP / norm) / count
    scalars[0][...] = totals[1, 0:1, 0:1]
    scalars[1][...] = count
    scalars[2][...] = norm

    def update(index, where, grad):
        mine = held[3 * index : 3 * index + 3]
        weight, first, second = (ref[where] for ref in mine)
        for ref, value in zip(mine, adam_step(weight, grad * scale, first, second, RATES[index])):
            ref[where] = value

    def blocks(index, lead, source, at, lane=0, wide=D):
        rows = held[3 * index].shape[-2]
        tile = next(t for t in (32, 24, 16, 8) if rows % t == 0)

        def body(step, carry):
            here = pl.multiple_of(step * tile, 8)
            where = (pl.ds(here, tile), slice(None))
            grad = source[pl.ds(pl.multiple_of(at + here, 8), tile), pl.ds(lane, wide)]
            update(index, where if lead is None else (lead,) + where, grad)
            return carry

        lax.fori_loop(0, rows // tile, body, 0)

    pieces_box = plan.box // 32
    for index in order:
        for part in range(3 * index, 3 * index + 3):
            loads[part].wait()
        if index == 0:
            for part in range(4):
                blocks(0, part, shared_ref, part * plan.proj)
        elif index == 1:
            for part in range(plan.box_parts):
                row, lane = plan.box_slot(part)
                grad = shared_ref[pl.ds(row, 32), pl.ds(lane, LANES)]
                update(1, (part // pieces_box, pl.ds(32 * (part % pieces_box), 32)), grad)
        elif index == 2:
            blocks(2, None, shared_ref, plan.places_at)
        elif index == 3:
            blocks(3, None, shared_ref, plan.visual_at)
        elif index == 4:
            row, lane = plan.box_slot(plan.box_parts)
            grad = shared_ref[pl.ds(row, 32), pl.ds(lane, LANES)]
            update(4, (slice(None), slice(None)), grad[:VROWS, : held[12].shape[1]])
        elif index == 5:
            blocks(5, None, split_ref, 0)
        else:
            for part in range(2):
                wide = held[18].shape[2]
                row, lane = ffn_slot(part, table_rows, ffn_rows, wide)
                blocks(6, part, split_ref, row, lane, wide)
        for part in range(3 * index, 3 * index + 3):
            stores.append(pltpu.make_async_copy(held[part], outs[part], store_sem.at[part]))
            stores[-1].start()
    for store in stores:
        store.wait()


def adam_update(plan, table_rows, ffn_rows, shared, split, tile, states):
    vmem = pl.BlockSpec(memory_space=pltpu.VMEM)
    anywhere = pl.BlockSpec(memory_space=pl.ANY)
    scalar = jax.ShapeDtypeStruct((1, 1), WIDE)

    def body(*refs):
        adam_kernel(plan, table_rows, ffn_rows, refs)

    return pl.pallas_call(
        body,
        out_shape=tuple(jax.ShapeDtypeStruct(part.shape, WIDE) for part in states) + (scalar,) * 3,
        in_specs=[vmem] * 3 + [anywhere] * 21,
        out_specs=(anywhere,) * 21 + (vmem,) * 3,
        scratch_shapes=[pltpu.VMEM(part.shape, WIDE) for part in states]
        + [pltpu.SemaphoreType.DMA((21,)), pltpu.SemaphoreType.DMA((21,))],
        compiler_params=pltpu.CompilerParams(vmem_limit_bytes=58 * 2**20),
        name="adam_update",
    )(shared, split, tile, *states)


def combos(index, bits):
    found = [index]
    for bit in bits:
        found = found + [flip(one, bit) for one in found]
    return found


class Ring:
    def __init__(self, mp, sems):
        self.mp, self.here = mp, lax.axis_index("mp")
        self.send, self.recv = sems
        depth = bits_of(mp)
        self.depth = depth
        self.orders = (list(range(depth)), list(range(depth - 1, -1, -1)))
        self.started = []

    def barrier(self):
        barrier = pltpu.get_barrier_semaphore()
        for other in range(1, self.mp):
            pl.semaphore_signal(
                barrier, 1, device_id={"mp": lax.rem(self.here + other, self.mp)},
                device_id_type=MESH,
            )
        pl.semaphore_wait(barrier, self.mp - 1)

    def copy(self, source, target, number, stream, index, peer):
        made = pltpu.make_async_remote_copy(
            src_ref=source, dst_ref=target,
            send_sem=self.send.at[number, stream, index],
            recv_sem=self.recv.at[number, stream, index],
            device_id={"mp": peer}, device_id_type=MESH,
        )
        return made

    def gather_send(self, buffer, number, stream, step, place):
        order = self.orders[stream]
        peer = flip(self.here, order[step])
        part = buffer.at[combos(self.here, order[:step])[place], :, lanes_of(stream)]
        made = self.copy(part, part, number, stream, 2**step - 1 + place, peer)
        made.start()
        self.started.append(made)

    def gather_start(self, buffer, number, stream):
        for step in range(self.depth):
            self.gather_send(buffer, number, stream, step, 0)

    def gather_wait(self, buffer, number, stream, step):
        order = self.orders[stream]
        peer = flip(self.here, order[step])
        for place, slot in enumerate(combos(peer, order[:step])):
            part = buffer.at[slot, :, lanes_of(stream)]
            self.copy(part, part, number, stream, 2**step - 1 + place, peer).wait_recv()
        for later in range(step + 1, self.depth):
            for place in range(2**step, 2 ** (step + 1)):
                self.gather_send(buffer, number, stream, later, place)

    def base(self, step):
        return sum(2 ** (self.depth - 1 - s) for s in range(step))

    def reduce_one(self, buffer, got, number, stream, step, place):
        order = self.orders[stream]
        peer = flip(self.here, order[step])
        slot = combos(peer, order[step + 1 :])[place]
        index = self.base(step) + place
        made = self.copy(
            buffer.at[slot, :, lanes_of(stream)],
            got.at[index, :, lanes_of(stream)],
            number, stream, index, peer,
        )
        made.start()
        self.started.append(made)

    def reduce_start(self, buffer, got, number, stream, step):
        for place in range(2 ** (self.depth - 1 - step)):
            self.reduce_one(buffer, got, number, stream, step, place)

    def reduce_wait(self, buffer, got, number, stream, step):
        order = self.orders[stream]
        peer = flip(self.here, order[step])
        for place, slot in enumerate(combos(self.here, order[step + 1 :])):
            index = self.base(step) + place
            part = got.at[index, :, lanes_of(stream)]
            self.copy(part, part, number, stream, index, peer).wait_recv()
            where = (slot, slice(None), lanes_of(stream))
            total = buffer[where].astype(WIDE) + got[index, :, lanes_of(stream)].astype(WIDE)
            buffer[where] = total.astype(buffer.dtype)

    def reduce_begin(self, buffer, got, number):
        for stream in range(2):
            self.reduce_start(buffer, got, number, stream, 0)

    def finish(self):
        for made in self.started:
            made.wait_send()


def mm(left, right, dims):
    return lax.dot_general(left, right, (dims, ((), ())), preferred_element_type=WIDE)


NN, NT, TN = ((1,), (0,)), ((1,), (1,)), ((0,), (0,))


def norm_rows(value):
    centred = value - jnp.mean(value, -1, keepdims=True)
    scale = lax.rsqrt(jnp.mean(centred * centred, -1, keepdims=True) + 1e-05)
    return centred * scale, scale


def norm_back(grad, plain, scale, gain):
    inner = grad * gain
    return scale * (
        inner
        - jnp.mean(inner, -1, keepdims=True)
        - plain * jnp.mean(inner * plain, -1, keepdims=True)
    )


def column_sum(value):
    return jnp.sum(value, 0, keepdims=True)


def halves_of(slots):
    first = pad_up(slots // 2, 16)
    return ((0, first), (first, slots - first))


def head_kernel(mp, vocab_tile, refs):
    (
        mixed_ref, zero_ref, weights_in, small_ref, ffn_ref, table_ref, marks_zero, marks_one,
        grad_zero_ref, grad_mixed_ref, grad_out_ref, ffn_out, table_out, rows_ref, bias_out,
        sums_ref,
        ffn, table, out_weight, grad_ffn_ref, grad_table_ref, *scratch,
    ) = refs
    load_sem, send_sem, recv_sem, stat_send, stat_recv = scratch[-5:]
    ring = Ring(mp, (send_sem, recv_sem))
    here = ring.here
    slots, vocab, hidden = mixed_ref.shape[0], table.shape[0], ffn.shape[2]
    load_ffn = pltpu.make_async_copy(ffn_ref, ffn, load_sem.at[0])
    load_table = pltpu.make_async_copy(table_ref, table, load_sem.at[1])
    load_out = pltpu.make_async_copy(weights_in.at[3], out_weight, load_sem.at[2])
    load_out.start()
    load_ffn.start()
    load_table.start()
    ring.barrier()
    row = lambda index: small_ref[index : index + 1, :]
    start = here * hidden
    bias = small_ref[
        pl.ds(10 + start // D, 1), pl.ds(pl.multiple_of(lax.rem(start, D), LANES), hidden)
    ]
    load_out.wait()
    kept = [{}, {}]
    waiting = []

    def gathering(buffer, number):
        for stream in range(2):
            ring.gather_start(buffer, number, stream)
        for step in range(ring.depth):
            yield
            for stream in range(2):
                ring.gather_wait(buffer, number, stream, step)

    def reducing(buffer, got, number):
        ring.reduce_begin(buffer, got, number)
        for step in range(ring.depth):
            yield
            for stream in range(2):
                ring.reduce_wait(buffer, got, number, stream, step)
                if step < ring.depth - 1:
                    ring.reduce_start(buffer, got, number, stream, step + 1)

    def run(part):
        first, count = halves_of(slots)[part]
        group = count * mp
        rows = slice(first, first + count)
        keep = kept[part]
        one, picked, down, sums_two, grad_picked, grad_one, *rest = scratch[12 * part : 12 * part + 12]
        got_two, got_picked, got_one, logits, low_logits, stats = rest
        marks_ref = marks_one if part else marks_zero
        base = 6 * part

        out = mm(mixed_ref[rows, :], out_weight[...], NN) + row(4)
        plain_one, scale_one = norm_rows(zero_ref[rows, :] + out)
        normed_one = plain_one * row(5) + row(6)
        one[here] = normed_one.astype(LOW)
        yield from gathering(one, base)
        if part == 0:
            load_ffn.wait()
        group_one = one[...].reshape(group, D)
        before = mm(group_one, ffn[0], NN) + bias
        erf_part = 0.5 * (1.0 + lax.erf(before * (0.5**0.5)))
        active = (before * erf_part).astype(LOW)
        sums_two[...] = mm(active, ffn[1], NT).astype(LOW).reshape(mp, count, D)
        slope = erf_part + before * jnp.exp(-0.5 * before * before) * 0.3989422804014327
        yield from reducing(sums_two, got_two, base + 1)
        plain_two, scale_two = norm_rows(normed_one + (sums_two[here].astype(WIDE) + row(7)))
        picked[here] = (plain_two * row(8) + row(9)).astype(LOW)
        yield from gathering(picked, base + 2)
        if part == 0:
            load_table.wait()
        group_picked = picked[...].reshape(group, D)
        label = marks_ref[0:1, :] - here * vocab
        valid = marks_ref[1:2, :].astype(WIDE)
        tiles = vocab // vocab_tile

        def forward(index, carry):
            highest, total, target = carry
            where = pl.ds(pl.multiple_of(index * vocab_tile, 16), vocab_tile)
            values = mm(table[where, :], group_picked, NT)
            logits[where, :] = values
            higher = jnp.maximum(highest, jnp.max(values, 0, keepdims=True))
            total = total * jnp.exp(highest - higher) + column_sum(jnp.exp(values - higher))
            word = lax.broadcasted_iota(jnp.int32, (vocab_tile, group), 0) + index * vocab_tile
            target = target + column_sum(jnp.where(word == label, values, 0.0))
            return higher, total, target

        blank = jnp.zeros((1, group), WIDE)
        highest, total, target = lax.fori_loop(0, tiles, forward, (blank - 1e30, blank, blank))
        stats[here, 0:1, 0:group] = highest
        stats[here, 1:2, 0:group] = total
        stats[here, 2:3, 0:group] = target
        for other in range(1, mp):
            made = pltpu.make_async_remote_copy(
                src_ref=stats.at[here], dst_ref=stats.at[here],
                send_sem=stat_send.at[part, other], recv_sem=stat_recv.at[part, other],
                device_id={"mp": lax.rem(here + other, mp)}, device_id_type=MESH,
            )
            made.start()
            waiting.append(made)
        yield
        for other in range(1, mp):
            source = lax.rem(here + mp - other, mp)
            pltpu.make_async_copy(
                stats.at[source], stats.at[source], stat_recv.at[part, other]
            ).wait()
        highest = stats[0, 0:1, 0:group]
        for index in range(1, mp):
            highest = jnp.maximum(highest, stats[index, 0:1, 0:group])
        total, target = blank, blank
        for index in range(mp):
            scaled = jnp.exp(stats[index, 0:1, 0:group] - highest)
            total = total + stats[index, 1:2, 0:group] * scaled
            target = target + stats[index, 2:3, 0:group]
        log_rows = highest + jnp.log(total)
        place = lax.broadcasted_iota(jnp.int32, (1, group), 1)
        own = (place >= here * count) & (place < (here + 1) * count)
        keep["loss"] = jnp.sum(
            jnp.where(own, valid * (log_rows - target), 0.0), -1, keepdims=True
        )
        keep["count"] = jnp.sum(jnp.where(own, valid, 0.0), -1, keepdims=True)

        def backward(index, grad):
            where = pl.ds(pl.multiple_of(index * vocab_tile, 16), vocab_tile)
            word = lax.broadcasted_iota(jnp.int32, (vocab_tile, group), 0) + index * vocab_tile
            hit = jnp.where(word == label, 1.0, 0.0)
            values = ((jnp.exp(logits[where, :] - log_rows) - hit) * valid).astype(LOW)
            low_logits[where, :] = values
            return grad + mm(values, table[where, :], TN)

        grad = lax.fori_loop(0, tiles, backward, jnp.zeros((group, D), WIDE))
        grad_picked[...] = grad.astype(LOW).reshape(mp, count, D)
        keep["picked"], keep["low_logits"] = group_picked, low_logits
        yield from reducing(grad_picked, got_picked, base + 3)
        grad_two = grad_picked[here].astype(WIDE)
        keep[8] = column_sum(grad_two * plain_two)
        keep[9] = column_sum(grad_two)
        grad_sum_two = norm_back(grad_two, plain_two, scale_two, row(8))
        low_two = grad_sum_two.astype(LOW)
        keep[7] = column_sum(low_two.astype(WIDE))
        down[here] = low_two
        yield from gathering(down, base + 4)
        group_down = down[...].reshape(group, D)
        grad_active = mm(group_down, ffn[1], NN)
        grad_before = (grad_active * slope).astype(LOW)
        grad_one[...] = mm(grad_before, ffn[0], NT).astype(LOW).reshape(mp, count, D)
        keep["up"] = (group_one, grad_before)
        keep["down"] = (group_down, active)
        yield from reducing(grad_one, got_one, base + 5)
        grad = grad_sum_two + grad_one[here].astype(WIDE)
        keep[5] = column_sum(grad * plain_one)
        keep[6] = column_sum(grad)
        grad = norm_back(grad, plain_one, scale_one, row(5))
        low = grad.astype(LOW)
        keep[4] = column_sum(low.astype(WIDE))
        grad_zero_ref[rows, :] = grad
        grad_mixed_ref[rows, :] = mm(low, out_weight[...], NT).astype(LOW)
        keep["out"] = low

    def both(name):
        return [jnp.concatenate([kept[0][name][side], kept[1][name][side]], 0) for side in range(2)]

    stores = []

    def keep_result(source, target):
        stores.append(pltpu.make_async_copy(source, target, load_sem.at[3 + len(stores)]))
        stores[-1].start()

    def table_part(first, last):
        def work():
            def body(index, carry):
                where = pl.ds(pl.multiple_of(index * vocab_tile, 16), vocab_tile)
                total = mm(kept[0]["low_logits"][where, :], kept[0]["picked"], NN)
                total = total + mm(kept[1]["low_logits"][where, :], kept[1]["picked"], NN)
                grad_table_ref[where, :] = total.astype(LOW)
                return carry

            lax.fori_loop(first, last, body, 0)
            where = pl.ds(first * vocab_tile, (last - first) * vocab_tile)
            keep_result(grad_table_ref.at[where], table_out.at[where])

        return work

    def up_part():
        left, right = both("up")
        grad_ffn_ref[0] = mm(left, right, TN).astype(LOW)
        bias_out[...] = column_sum(right.astype(WIDE))
        keep_result(grad_ffn_ref.at[0], ffn_out.at[0])

    def down_part():
        left, right = both("down")
        grad_ffn_ref[1] = mm(left, right, TN).astype(LOW)
        keep_result(grad_ffn_ref.at[1], ffn_out.at[1])

    tiles = vocab // vocab_tile
    quarter = max(1, tiles // 4)
    fillers = [
        table_part(first, min(first + quarter, tiles)) for first in range(0, tiles, quarter)
    ]
    late = [up_part, down_part]
    runs = [run(0), run(1)]
    live = [True, True]
    while any(live):
        for part in range(2):
            if live[part]:
                live[part] = next(runs[part], "done") != "done"
        if "down" in kept[1] and late:
            late.pop(0)()
        elif "low_logits" in kept[1] and fillers:
            fillers.pop(0)()
    for work in fillers + late:
        work()
    grad_out_ref[...] = mm(
        mixed_ref[...], jnp.concatenate([kept[0]["out"], kept[1]["out"]], 0), TN
    ).astype(LOW)
    first_lane = lax.broadcasted_iota(jnp.int32, (8, LANES), 1) == 0
    first_row = lax.broadcasted_iota(jnp.int32, (8, LANES), 0)
    loss, count = (kept[0][name] + kept[1][name] for name in ("loss", "count"))
    sums_ref[...] = jnp.where(
        first_lane & (first_row == 0), loss, jnp.where(first_lane & (first_row == 1), count, 0.0)
    )
    for index in range(16):
        value = kept[0][index] + kept[1][index] if 4 <= index < 10 else jnp.zeros((1, D), WIDE)
        rows_ref[index : index + 1, :] = value
    for made in stores:
        made.wait()
    ring.finish()
    for made in waiting:
        made.wait_send()


def head_step(mp, mixed, zero, weights, small, ffn, table, marks_zero, marks_one):
    slots, hidden, vocab = mixed.shape[0], ffn.shape[2], table.shape[0]
    vmem = pl.BlockSpec(memory_space=pltpu.VMEM)
    anywhere = pl.BlockSpec(memory_space=pl.ANY)
    dma = pltpu.SemaphoreType.DMA
    tile = next(t for t in (480, 512, 256, 128) if vocab % t == 0)
    scratch = []
    for first, count in halves_of(slots):
        group = mp * count
        scratch += [pltpu.VMEM((mp, count, D), LOW)] * 6
        scratch += [pltpu.VMEM((mp - 1, count, D), LOW)] * 3
        scratch += [
            pltpu.VMEM((vocab, group), WIDE),
            pltpu.VMEM((vocab, group), LOW),
            pltpu.VMEM((mp, 8, pad_up(group, LANES)), WIDE),
        ]

    def body(*refs):
        head_kernel(mp, tile, refs)

    return pl.pallas_call(
        body,
        out_shape=(
            jax.ShapeDtypeStruct((slots, D), WIDE),
            jax.ShapeDtypeStruct((slots, D), LOW),
            jax.ShapeDtypeStruct((D, D), LOW),
            jax.ShapeDtypeStruct((2, D, hidden), LOW),
            jax.ShapeDtypeStruct((vocab, D), LOW),
            jax.ShapeDtypeStruct((16, D), WIDE),
            jax.ShapeDtypeStruct((1, hidden), WIDE),
            jax.ShapeDtypeStruct((8, LANES), WIDE),
        ),
        in_specs=[vmem, vmem, anywhere, vmem, anywhere, anywhere, vmem, vmem],
        out_specs=(vmem,) * 3 + (anywhere,) * 2 + (vmem,) * 3,
        scratch_shapes=[
            pltpu.VMEM((2, D, hidden), LOW),
            pltpu.VMEM((vocab, D), LOW),
            pltpu.VMEM((D, D), LOW),
            pltpu.VMEM((2, D, hidden), LOW),
            pltpu.VMEM((vocab, D), LOW),
            *scratch,
            dma((16,)),
            dma((12, 2, mp - 1)),
            dma((12, 2, mp - 1)),
            dma((2, mp)),
            dma((2, mp)),
        ],
        compiler_params=pltpu.CompilerParams(
            collective_id=3, has_side_effects=True, vmem_limit_bytes=58 * 2**20
        ),
        name="head_step",
    )(mixed, zero, weights, small, ffn, table, marks_zero, marks_one)


ROWS = 576
KINDS = ((6, 3), (0, 4), (3, 4))


def token_base():
    base = np.zeros((16, ROWS), np.int32)
    visual = GRID * GRID
    cells = np.arange(visual)
    place, column = cells // GRID, cells % GRID
    left, top = column * 1000 // GRID, place * 1000 // GRID
    right, bottom = (column + 1) * 1000 // GRID, (place + 1) * 1000 // GRID
    rows = (left, top, right, bottom, bottom - top, right - left, cells, -1, 1)
    for index, values in enumerate(rows):
        base[index, TEXT : TEXT + visual] = values
    base[6, :TEXT] = np.arange(TEXT)
    return jnp.asarray(base)


def edge_hot():
    entry = lax.broadcasted_iota(jnp.int32, (D, LANES), 0)
    place = lax.broadcasted_iota(jnp.int32, (D, LANES), 1)
    first = jnp.clip(place - NB // 2, 0, NB - 1) * H
    return jnp.where((entry >= first) & (entry < first + H), 1.0, 0.0).astype(LOW)


def head_mask():
    entry = lax.broadcasted_iota(jnp.int32, (16, D), 1)
    return lax.rem(entry, H) == lax.broadcasted_iota(jnp.int32, (16, D), 0)


def edge_rows(small_ref, kind):
    first = 10 + FF // D
    row = small_ref[first + kind : first + kind + 1, :]
    return mm(jnp.where(head_mask(), row, 0.0).astype(LOW), edge_hot(), NN)


def edge_rows_back(grad):
    high = grad.astype(LOW)
    low = (grad - high.astype(WIDE)).astype(LOW)
    hot = edge_hot()
    return column_sum(jnp.where(head_mask(), mm(high, hot, NT) + mm(low, hot, NT), 0.0))


def key_hot(rows_ref, kind):
    column, shift = KINDS[kind]
    coarse_row = jnp.right_shift(rows_ref[column : column + 1, :], shift)
    place = lax.broadcasted_iota(jnp.int32, (2 * NB, ROWS), 0)
    first = jnp.where(place == coarse_row, 1.0, 0.0).astype(LOW)
    second = jnp.where(place == coarse_row + NB, 1.0, 0.0).astype(LOW)
    return first, second


def below_of(rows_ref, slot_ref, kind):
    column, shift = KINDS[kind]
    mask = 2**shift - 1
    rest_key = jnp.bitwise_and(rows_ref[column : column + 1, :], mask)
    rest_slot = jnp.bitwise_and(slot_ref[:, column : column + 1], mask)
    return rest_key < rest_slot


def take_slots(slots, pos_ref, pairs):
    def body(index, carry):
        at = pos_ref[index]
        for source, target in pairs:
            target[pl.ds(index, 1), :] = source[pl.ds(at, 1), :]
        return carry

    lax.fori_loop(0, slots, body, 0)


def half_mask(rows):
    slots = rows // 2
    row = lax.broadcasted_iota(jnp.int32, (rows, LANES), 0)
    lane = lax.broadcasted_iota(jnp.int32, (rows, LANES), 1)
    return (row < slots) == (lane < HD)


def pair_rows(value):
    both = jnp.concatenate([value, value], 0)
    return jnp.where(half_mask(both.shape[0]), both, jnp.zeros((), both.dtype))


def pair_lanes(value):
    slots = value.shape[0] // 2
    lane = lax.broadcasted_iota(jnp.int32, (slots, LANES), 1)
    return jnp.where(lane < HD, value[:slots], value[slots:])


def front_early(pos_ref, places, visual_proj, features_ref, boxes_ref, small_ref, columns_ref,
                rows_ref, scratch):
    normed_ref, slot_ref, bias_ref, spread_ref, stacked_ref = scratch
    slots = slot_ref.shape[0]
    tile = 96
    lookups = (0, 1, 0, 1, 2, 3)
    visual = features_ref.shape[0]
    normed_ref[0:TEXT, :] = places.astype(WIDE)
    visual_rows = mm(features_ref[...], visual_proj, NN)
    normed_ref[TEXT : TEXT + visual, :] = visual_rows + places[0:visual].astype(WIDE)
    normed_ref[TEXT + visual : ROWS, :] = jnp.zeros((ROWS - TEXT - visual, D), WIDE)

    def embed(index, carry):
        where = pl.ds(pl.multiple_of(index * tile, 16), tile)
        place = lax.broadcasted_iota(jnp.int32, (tile, NBOX), 1)
        found = []
        for column, table in enumerate(lookups):
            hot = jnp.where(place == columns_ref[where, column : column + 1], 1.0, 0.0).astype(LOW)
            found.append(mm(hot, boxes_ref[table], NN))
        normed_ref[where, :] = normed_ref[where, :] + jnp.concatenate(found, -1)
        return carry

    lax.fori_loop(0, ROWS // tile, embed, 0)
    take_slots(slots, pos_ref, ((columns_ref, slot_ref),))
    lane = lax.broadcasted_iota(jnp.int32, (NB, LANES), 1)
    for kind in range(3):
        column, shift = KINDS[kind]
        edges = edge_rows(small_ref, kind)
        for head in range(H):
            edge = jnp.broadcast_to(edges[head : head + 1, :], (NB, LANES))
            near = pltpu.roll(edge, NB, 1, stride=1, stride_axis=0)
            far = pltpu.roll(edge, 1, 1, stride=1, stride_axis=0)
            spread_ref[:, head * LANES : (head + 1) * LANES] = jnp.where(
                lane < NB, near, far
            ).astype(LOW)
        coarse_slot = jnp.right_shift(slot_ref[:, column : column + 1], shift)
        place = lax.broadcasted_iota(jnp.int32, (slots, NB), 1)
        hot = jnp.where(place == coarse_slot, 1.0, 0.0).astype(LOW)
        wide = mm(hot, spread_ref[...], NN).astype(LOW)
        for head in range(H):
            stacked_ref[head * slots : (head + 1) * slots, :] = wide[
                :, head * LANES : (head + 1) * LANES
            ]
        first, second = key_hot(rows_ref, kind)
        below = below_of(rows_ref, slot_ref, kind)

        def add(head, carry):
            where = pl.ds(pl.multiple_of(head * 2 * slots, 16), 2 * slots)
            rows = stacked_ref[where, :]
            both = jnp.concatenate([below, below], 0)
            found = jnp.where(both, mm(rows, second, NN), mm(rows, first, NN))
            bias_ref[where, :] = found if kind == 0 else bias_ref[where, :] + found
            return carry

        lax.fori_loop(0, H // 2, add, 0)


def front_late(pos_ref, word, small_ref, rows_ref, weight, hook, outs, scratch):
    (
        mixed_ref, zero_ref, zero_low_ref, low_ref, plain_ref, scale_ref, query_ref, key_ref,
        value_ref, shares_ref,
    ) = outs
    normed_ref, slot_ref, bias_ref = scratch[:3]
    slots = mixed_ref.shape[0]
    row = lambda index: small_ref[index : index + 1, :]
    tile = 96
    normed_ref[0:TEXT, :] = normed_ref[0:TEXT, :] + word

    def normalize(index, carry):
        where = pl.ds(pl.multiple_of(index * tile, 16), tile)
        plain, scale = norm_rows(normed_ref[where, :])
        normed = plain * row(0) + row(1)
        plain_ref[where, :] = plain
        scale_ref[where, :] = scale
        normed_ref[where, :] = normed
        low_ref[where, :] = normed.astype(LOW)
        return carry

    lax.fori_loop(0, ROWS // tile, normalize, 0)
    take_slots(slots, pos_ref, ((normed_ref, zero_ref),))
    low = low_ref[...]
    zero_low = zero_ref[...].astype(LOW)
    zero_low_ref[...] = zero_low
    hook()
    query_ref[...] = (mm(zero_low, weight(0), NN) + row(2)).astype(LOW)
    key_ref[...] = mm(low, weight(1), NN).astype(LOW)
    value_ref[...] = (mm(low, weight(2), NN) + row(3)).astype(LOW)
    hook()
    owner = rows_ref[7:8, :]
    allowed = ((slot_ref[:, 7:8] == owner) | (owner < 0)) & (rows_ref[8:9, :] > 0)
    allowed = jnp.concatenate([allowed, allowed], 0)
    for pair in range(H // 2):
        if pair == H // 4:
            hook()
        lanes = slice(pair * LANES, (pair + 1) * LANES)
        rows = slice(pair * 2 * slots, (pair + 1) * 2 * slots)
        scores = mm(pair_rows(query_ref[:, lanes]), key_ref[:, lanes], NT) * 0.125
        scores = jnp.where(allowed, scores + bias_ref[rows, :], MASKED)
        powers = jnp.exp(scores - jnp.max(scores, -1, keepdims=True))
        shares = powers / jnp.sum(powers, -1, keepdims=True)
        shares_ref[rows, :] = shares
        mixed_ref[:, lanes] = pair_lanes(mm(shares.astype(LOW), value_ref[:, lanes], NN)).astype(LOW)


def front_shapes(slots):
    shape = jax.ShapeDtypeStruct
    outs = (
        shape((slots, D), LOW), shape((slots, D), WIDE), shape((slots, D), LOW),
        shape((ROWS, D), LOW), shape((ROWS, D), WIDE), shape((ROWS, 1), WIDE),
        shape((slots, D), LOW), shape((ROWS, D), LOW), shape((ROWS, D), LOW),
        shape((H * slots, ROWS), WIDE),
    )
    scratch = [
        pltpu.VMEM((ROWS, D), WIDE),
        pltpu.VMEM((slots, 16), jnp.int32),
        pltpu.VMEM((H * slots, ROWS), WIDE),
        pltpu.VMEM((NB, H * LANES), LOW),
        pltpu.VMEM((H * slots, LANES), LOW),
    ]
    return outs, scratch


def front_again(pos, word, features, places, boxes, visual, small, columns, rows, weights):
    outs, scratch = front_shapes(pos.shape[0])
    vmem = pl.BlockSpec(memory_space=pltpu.VMEM)

    def body(
        pos_ref, word_ref, features_ref, places_ref, boxes_ref, visual_ref, small_ref, columns_ref,
        rows_ref, weights_ref, *rest,
    ):
        front_early(
            pos_ref, places_ref[...], visual_ref[...], features_ref, boxes_ref, small_ref,
            columns_ref, rows_ref, rest[10:],
        )
        front_late(
            pos_ref, word_ref[...].astype(WIDE), small_ref, rows_ref,
            lambda part: weights_ref[part], lambda: None, rest[:10], rest[10:],
        )

    return pl.pallas_call(
        body,
        out_shape=outs,
        in_specs=[pl.BlockSpec(memory_space=pltpu.SMEM)] + [vmem] * 9,
        out_specs=(vmem,) * 10,
        scratch_shapes=scratch,
        compiler_params=pltpu.CompilerParams(vmem_limit_bytes=56 * 2**20),
        name="front_again",
    )(pos, word, features, places, boxes, visual, small, columns, rows, weights)


def gather_kernel(plan, table_rows, refs):
    (
        pos_ref, label_in, valid_in, word_in, proj_in, boxes_in, places_in, visual_in, small_in,
        ffn_in, tokens_ref, box_in, segment_in, alive_in, features_ref, base_in,
        table_out, proj_out, boxes_out, places_out, visual_out, ffn_out, small_out, place_out,
        ids_out, most_out, rows_ref, columns_ref, marks_zero, marks_one, *rest,
    ) = refs
    outs_ref, rest = rest[:10], rest[10:]
    scratch, outs_buf, rest = rest[:5], rest[5:15], rest[15:]
    (
        table_buf, shared_buf, ffn_buf, boxes_ref, packed, got, key_ref, ids_ref, most_ref, out_sem,
        send_sem, recv_sem, word_send, word_recv, most_send, most_recv,
    ) = rest
    dp, mp = plan.dp, plan.mp
    me = lax.axis_index("dp")
    here = lax.axis_index("mp")
    depth = bits_of(dp)
    rows = word_in.shape[0]
    table_buf[me, 0:rows, :] = word_in[...].astype(LOW)
    barrier = pltpu.get_barrier_semaphore()
    for other in range(1, dp):
        pl.semaphore_signal(
            barrier, 1, device_id={"dp": lax.rem(me + other, dp)}, device_id_type=MESH
        )
    for other in range(1, mp):
        pl.semaphore_signal(
            barrier, 1, device_id={"mp": lax.rem(here + other, mp)}, device_id_type=MESH
        )
    pl.semaphore_wait(barrier, dp + mp - 2)

    half = table_rows // 2
    pieces = (
        (table_buf, 0, half),
        (table_buf, half, half),
        (shared_buf, plan.places_at, plan.shared - plan.places_at),
        (shared_buf, 0, 3 * plan.proj),
        (ffn_buf, 0, ffn_buf.shape[1]),
        (shared_buf, 3 * plan.proj, plan.proj),
    )
    orders = (list(range(1, depth)) + [0], list(range(depth - 1, -1, -1)))
    started = []

    def part_of(piece, stream, slot):
        buffer, first, count = pieces[piece]
        return buffer.at[slot, pl.ds(first, count), lanes_of(stream)]

    def copy(piece, stream, step, place, slot):
        part = part_of(piece, stream, slot)
        index = 2**step - 1 + place
        return pltpu.make_async_remote_copy(
            src_ref=part, dst_ref=part,
            send_sem=send_sem.at[piece, stream, index],
            recv_sem=recv_sem.at[piece, stream, index],
            device_id={"dp": flip(me, orders[stream][step])},
            device_id_type=MESH,
        )

    def start(piece, step):
        for stream in range(2):
            for place, slot in enumerate(combos(me, orders[stream][:step])):
                made = copy(piece, stream, step, place, slot)
                made.start()
                started.append(made)

    def wait(piece, step):
        for stream in range(2):
            peer = flip(me, orders[stream][step])
            for place, slot in enumerate(combos(peer, orders[stream][:step])):
                copy(piece, stream, step, place, slot).wait_recv()

    outs = []

    def put(source, target):
        made = pltpu.make_async_copy(source, target, out_sem.at[len(outs)])
        made.start()
        outs.append(made)

    start(0, 0)
    start(1, 0)

    def cast(target, first, source):
        count = source.shape[0]
        target[me, first : first + count, : source.shape[1]] = source.astype(LOW)

    for part in range(4):
        cast(shared_buf, part * plan.proj, proj_in[part])
    cast(shared_buf, plan.places_at, places_in[...])
    cast(shared_buf, plan.visual_at, visual_in[...])
    pieces_box = plan.box // 32
    for part in range(plan.box_parts):
        row, lane = plan.box_slot(part)
        first = 32 * (part % pieces_box)
        shared_buf[me, row : row + 32, lane : lane + LANES] = boxes_in[
            part // pieces_box, first : first + 32, :
        ].astype(LOW)
    row, lane = plan.box_slot(plan.box_parts)
    cut = small_in.shape[1]
    shared_buf[me, row : row + 32, lane : lane + LANES] = jnp.zeros((32, LANES), LOW)
    shared_buf[me, row : row + VROWS, lane : lane + cut] = small_in[...].astype(LOW)
    for part in range(plan.box_parts + 1, 6 * (plan.shared - plan.box_at) // 32):
        spare_row, spare_lane = plan.box_slot(part)
        shared_buf[me, spare_row : spare_row + 32, spare_lane : spare_lane + LANES] = jnp.zeros(
            (32, LANES), LOW
        )
    ffn_rows = ffn_out.shape[2]
    wide = ffn_in.shape[2]
    for part in range(2):
        at, shift = ffn_slot(part, 0, ffn_rows, wide)
        ffn_buf[me, at : at + ffn_in.shape[1], shift : shift + wide] = ffn_in[part].astype(LOW)

    start(2, 0)

    vocab, room = rows * dp, got.shape[1]
    tokens = tokens_ref[...]
    first = lax.broadcasted_iota(jnp.int32, (TEXT, TEXT), 0)
    second = lax.broadcasted_iota(jnp.int32, (TEXT, TEXT), 1)
    before = jnp.where(first < second, 1.0, 0.0).astype(LOW)

    def ranked(ids, shard):
        inside = (ids >= shard * vocab) & (ids < (shard + 1) * vocab)
        rank = mm(jnp.where(inside, 1.0, 0.0).astype(LOW), before, NN).astype(jnp.int32)
        return inside, rank

    inside, rank = ranked(tokens, here)
    key_ref[...] = jnp.where(inside & (rank < room), rank, -1)
    own = tokens_ref[pl.ds(here, 1), :]
    place = jnp.full((1, TEXT), -1, jnp.int32)
    for shard in range(mp):
        inside, rank = ranked(own, shard)
        place = jnp.where(inside & (rank < room), rank + shard * room, place)
    place_out[...] = place
    most = jnp.zeros((mp, 1), WIDE)
    for shard in range(mp):
        inside = (tokens >= shard * vocab) & (tokens < (shard + 1) * vocab)
        most = jnp.maximum(most, jnp.sum(jnp.where(inside, 1.0, 0.0), -1, keepdims=True))
    most = jnp.max(most, 0, keepdims=True)
    most_ref[me] = jnp.broadcast_to(most, (8, LANES))
    most_copies = []
    for other in range(1, dp):
        made = pltpu.make_async_remote_copy(
            src_ref=most_ref.at[me], dst_ref=most_ref.at[me],
            send_sem=most_send.at[other], recv_sem=most_recv.at[other],
            device_id={"dp": lax.rem(me + other, dp)}, device_id_type=MESH,
        )
        made.start()
        most_copies.append(made)
    ids = tokens - here * vocab
    if table_rows != rows:
        ids = jnp.where(ids >= 0, ids // rows * table_rows + ids % rows, 0)
    ids_ref[...] = ids
    entry = lax.broadcasted_iota(jnp.int32, (room, TEXT), 0)

    def listed(slot):
        chosen = entry == key_ref[pl.ds(slot, 1), :]
        return jnp.sum(jnp.where(chosen, ids_ref[pl.ds(slot, 1), :] + 1, 0), -1, keepdims=True) - 1

    turns = [lax.rem(here + other, mp) for other in range(1, mp)] + [here]
    lists = [listed(slot) for slot in turns]
    columns = jnp.concatenate([listed(slot) for slot in range(mp)], 0)
    all_room = room * mp
    corner = lax.broadcasted_iota(jnp.int32, (all_room, all_room), 0) == lax.broadcasted_iota(
        jnp.int32, (all_room, all_room), 1
    )
    ids_out[...] = column_sum(jnp.where(corner, columns, 0))

    rows_ref[...] = base_in[...]
    rows_ref[0:4, 0:TEXT] = box_in[...]
    rows_ref[4:5, 0:TEXT] = box_in[3:4, :] - box_in[1:2, :]
    rows_ref[5:6, 0:TEXT] = box_in[2:3, :] - box_in[0:1, :]
    rows_ref[7:8, 0:TEXT] = segment_in[...]
    rows_ref[8:9, 0:TEXT] = alive_in[...]

    def row_of(width, count, source):
        place = lax.broadcasted_iota(jnp.int32, (1, width), 1)
        return lax.fori_loop(
            0, count, lambda index, row: jnp.where(place == index, source(index), row),
            jnp.zeros((1, width), jnp.int32),
        )

    slots = pos_ref.shape[0]
    rows_ref[9:10, :] = row_of(ROWS, slots, lambda index: pos_ref[index])
    for marks_ref, (begin, size) in zip((marks_zero, marks_one), halves_of(slots)):
        for kind, source in enumerate((label_in, valid_in)):
            marks_ref[kind : kind + 1, :] = row_of(
                size * mp, size * mp,
                lambda index: source[index // size * slots + begin + index % size],
            )
    corner = lax.broadcasted_iota(jnp.int32, (ROWS, ROWS), 0) == lax.broadcasted_iota(
        jnp.int32, (ROWS, ROWS), 1
    )
    columns_ref[...] = jnp.zeros((ROWS, 16), jnp.int32)
    for index in range(9):
        columns_ref[:, index : index + 1] = jnp.sum(
            jnp.where(corner, rows_ref[index : index + 1, :], 0), -1, keepdims=True
        )

    for step in range(depth):
        for piece in range(2):
            wait(piece, step)
            if step < depth - 1:
                start(piece, step + 1)
        if step == depth - 2:
            wait(2, 0)
            start(2, 1)
            start(3, 0)
    put(table_buf, table_out)

    word_copies = []
    for turn in range(0, mp, 2):
        wanted = jnp.concatenate(lists[turn : turn + 2], 0)
        column = lax.broadcasted_iota(jnp.int32, (2 * room, dp * table_rows), 1)
        hot = jnp.where(column == wanted, 1.0, 0.0).astype(LOW)
        found = mm(hot, table_buf[...].reshape(dp * table_rows, D), NN).astype(LOW)
        for part in range(2):
            slot = turns[turn + part]
            rows_of = found[part * room : (part + 1) * room]
            if turn + part == mp - 1:
                got[here] = rows_of
                continue
            packed[turn + part] = rows_of
            made = pltpu.make_async_remote_copy(
                src_ref=packed.at[turn + part], dst_ref=got.at[here],
                send_sem=word_send.at[turn + part], recv_sem=word_recv.at[turn + part],
                device_id={"mp": slot}, device_id_type=MESH,
            )
            made.start()
            word_copies.append(made)

    wait(3, 0)
    start(3, 1)
    start(4, 0)
    start(5, 0)

    def finish(piece):
        for step in range(1, depth):
            wait(piece, step)
            if step < depth - 1:
                start(piece, step + 1)

    finish(2)
    put(shared_buf.at[:, pl.ds(plan.places_at, plan.places)], places_out)
    put(shared_buf.at[:, pl.ds(plan.visual_at, plan.visual)], visual_out)
    for part in range(plan.box_parts):
        at, shift = plan.box_slot(part)
        put(
            shared_buf.at[:, pl.ds(at, 32), pl.ds(shift, LANES)],
            boxes_out.at[part // pieces_box, :, pl.ds(32 * (part % pieces_box), 32)],
        )
    for part in range(plan.box_parts):
        at, shift = plan.box_slot(part)
        for owner in range(dp):
            line = owner * plan.box + 32 * (part % pieces_box)
            boxes_ref[part // pieces_box, line : line + 32, :] = shared_buf[
                owner, at : at + 32, shift : shift + LANES
            ]
    row, lane = plan.box_slot(plan.box_parts)
    for part in range(dp):
        small_out[:, part * cut : (part + 1) * cut] = shared_buf[
            part, row : row + 24, lane : lane + cut
        ].astype(WIDE)

    def whole_rows(first, count):
        part = shared_buf[:, first : first + count // dp, :]
        return part.reshape(count, D)

    front_early(
        pos_ref, whole_rows(plan.places_at, TEXT), whole_rows(plan.visual_at, VCH), features_ref,
        boxes_ref, small_out, columns_ref, rows_ref, scratch,
    )
    for other in range(1, mp):
        source = lax.rem(here + mp - other, mp)
        pltpu.make_async_copy(got.at[source], got.at[source], word_recv.at[other - 1]).wait()
    across = jnp.sum(jnp.where(first == second, place, 0), -1, keepdims=True)
    column = lax.broadcasted_iota(jnp.int32, (TEXT, all_room), 1)
    hot = jnp.where(column == across, 1.0, 0.0).astype(LOW)
    word = mm(hot, got[...].reshape(all_room, D), NN)

    stages = [0]

    def late_step(step):
        for piece in (4, 5):
            wait(piece, step)
            if step < depth - 1:
                start(piece, step + 1)

    def hook():
        stage = stages[0]
        stages[0] = stage + 1
        if stage == 0:
            finish(3)
            for part in range(3):
                put(shared_buf.at[:, pl.ds(part * plan.proj, plan.proj)], proj_out.at[part])
        if stage == 0:
            late_step(0)
        for number in {0: (1, 2, 3, 4, 5), 1: (6, 7, 8)}.get(stage, ()):
            put(outs_buf[number], outs_ref[number])

    front_late(
        pos_ref, word, small_out, rows_ref, lambda part: whole_rows(part * plan.proj, D), hook,
        outs_buf, scratch,
    )
    put(outs_buf[0], outs_ref[0])
    put(outs_buf[9], outs_ref[9])
    for step in range(1, depth):
        late_step(step)
    for other in range(1, dp):
        source = lax.rem(me + dp - other, dp)
        pltpu.make_async_copy(
            most_ref.at[source], most_ref.at[source], most_recv.at[other]
        ).wait()
    most = most_ref[0]
    for part in range(1, dp):
        most = jnp.maximum(most, most_ref[part])
    most_out[...] = most[0:1, 0:1]
    put(shared_buf.at[:, pl.ds(3 * plan.proj, plan.proj)], proj_out.at[3])
    for part in range(2):
        at, shift = ffn_slot(part, 0, ffn_rows, wide)
        put(ffn_buf.at[:, pl.ds(at, ffn_rows), pl.ds(shift, wide)], ffn_out.at[part])
    for made in started:
        made.wait_send()
    for made in word_copies + most_copies:
        made.wait_send()
    for made in outs:
        made.wait()


def word_room(mp):
    return pad_up(TEXT // mp * 11 // 8, 16)


def front_step(
    plan, pos, label, valid, word, proj, boxes, places, visual, small, ffn, tokens, box, segment,
    alive, features,
):
    dp, mp = plan.dp, plan.mp
    slots = pos.shape[0]
    table_rows, ffn_rows, wide = pad_up(word.shape[0], 32), pad_up(ffn.shape[1], 16), ffn.shape[2]
    ffn_all = 2 * ffn_rows * wide // D
    room = word_room(mp)
    anywhere = pl.BlockSpec(memory_space=pl.ANY)
    vmem = pl.BlockSpec(memory_space=pltpu.VMEM)
    smem = pl.BlockSpec(memory_space=pltpu.SMEM)
    dma = pltpu.SemaphoreType.DMA
    shape = jax.ShapeDtypeStruct
    outs, scratch = front_shapes(slots)

    def body(*refs):
        gather_kernel(plan, table_rows, refs)

    return pl.pallas_call(
        body,
        out_shape=(
            shape((dp, table_rows, D), LOW), shape((4, dp, plan.proj, D), LOW),
            shape((4, dp, plan.box, LANES), LOW), shape((dp, plan.places, D), LOW),
            shape((dp, plan.visual, D), LOW), shape((2, dp, ffn_rows, wide), LOW),
            shape((24, D), WIDE), shape((1, TEXT), jnp.int32), shape((1, mp * room), jnp.int32),
            shape((1, 1), WIDE), shape((16, ROWS), jnp.int32), shape((ROWS, 16), jnp.int32),
            *(shape((2, mp * size), jnp.int32) for _, size in halves_of(slots)),
            *outs,
        ),
        in_specs=[smem] * 3 + [vmem] * 13,
        out_specs=(anywhere,) * 6 + (vmem,) * 8 + (anywhere,) * 10,
        scratch_shapes=[
            *scratch,
            *(pltpu.VMEM(part.shape, part.dtype) for part in outs),
            pltpu.VMEM((dp, table_rows, D), LOW),
            pltpu.VMEM((dp, plan.shared, D), LOW),
            pltpu.VMEM((dp, ffn_all, D), LOW),
            pltpu.VMEM((4, NBOX, LANES), LOW),
            pltpu.VMEM((mp - 1, room, D), LOW),
            pltpu.VMEM((mp, room, D), LOW),
            pltpu.VMEM((mp, TEXT), jnp.int32),
            pltpu.VMEM((mp, TEXT), jnp.int32),
            pltpu.VMEM((dp, 8, LANES), WIDE),
            dma((plan.box_parts + 20,)),
            dma((6, 2, dp - 1)),
            dma((6, 2, dp - 1)),
            dma((mp - 1,)),
            dma((mp - 1,)),
            dma((dp,)),
            dma((dp,)),
        ],
        compiler_params=pltpu.CompilerParams(
            collective_id=1, has_side_effects=True, vmem_limit_bytes=60 * 2**20
        ),
        name="front_step",
    )(
        pos, label, valid, word, proj, boxes, places, visual, small, ffn, tokens, box, segment,
        alive, features, token_base(),
    )


def back_kernel(plan, table_rows, ffn_rows, refs):
    (
        pos_ref, grad_zero_ref, grad_mixed_ref, shares_ref, query_ref, key_ref, value_ref,
        zero_low_ref, low_ref, plain_ref, scale_ref, features_ref, small_ref, columns_ref,
        rows_ref, weights_in, table_in, out_in, ffn_in, head_in, bias_in, tile_in, place_in, ids_in,
        shared_out, split_out, tile_out, word_out,
        slot_ref, score_ref, grad_query, grad_key, grad_value, grad_rows, grad_low, turned_ref,
        grad_slot, edges_ref, weights_ref,
        shared_acc, split_acc, shared_got, split_got, ring_got, ring_own, half_got, half_own, packed, words, small_all,
        tile_mp, tile_dp,
        load_sem, send_sem, recv_sem, ring_send, ring_recv, word_send, word_recv, tile_send,
        tile_recv,
    ) = refs
    dp, mp = plan.dp, plan.mp
    me, here = lax.axis_index("dp"), lax.axis_index("mp")
    depth, ring_depth = bits_of(dp), bits_of(mp)
    slots = grad_zero_ref.shape[0]
    loads = []
    if plan.proj * dp != D:
        shared_acc[...] = jnp.zeros(shared_acc.shape, LOW)

    def load(source, target):
        loads.append(pltpu.make_async_copy(source, target, load_sem.at[len(loads)]))
        loads[-1].start()

    load(out_in, shared_acc.at[:, pl.ds(3 * plan.proj, plan.proj)])
    for part in range(2):
        wide = ffn_in.shape[3]
        row, lane = ffn_slot(part, table_rows, ffn_rows, wide)
        load(ffn_in.at[part], split_acc.at[:, pl.ds(row, ffn_rows), pl.ds(lane, wide)])
    load(weights_in.at[0:3], weights_ref)
    load(table_in, split_acc.at[:, pl.ds(0, table_rows)])

    barrier = pltpu.get_barrier_semaphore()
    for other in range(1, dp):
        pl.semaphore_signal(
            barrier, 1, device_id={"dp": lax.rem(me + other, dp)}, device_id_type=MESH
        )
    for other in range(1, mp):
        pl.semaphore_signal(
            barrier, 1, device_id={"mp": lax.rem(here + other, mp)}, device_id_type=MESH
        )
    pl.semaphore_wait(barrier, dp + mp - 2)

    orders = ([0] + list(range(depth - 1, 0, -1)), list(range(depth)))
    out_at, rest = 3 * plan.proj, split_acc.shape[1] - table_rows
    pieces = (
        (shared_acc, shared_got, out_at, plan.proj),
        (shared_acc, shared_got, 0, out_at),
        (shared_acc, shared_got, plan.places_at, plan.shared - plan.places_at),
        (split_acc, split_got, table_rows, rest),
        (split_acc, split_got, 0, table_rows // 2),
        (split_acc, split_got, table_rows // 2, table_rows // 2),
    )

    def chunk(order, step, free, away):
        index = 0
        for place, bit in enumerate(order):
            mine = (me // 2**bit) % 2
            if place < step or (place == step and not away):
                index = index + mine * 2**bit
            elif place == step:
                index = index + (1 - mine) * 2**bit
            else:
                index = index + ((free >> (place - step - 1)) & 1) * 2**bit
        return index

    def slot_base(step):
        return sum(2 ** (depth - 1 - s) for s in range(step))

    def send_one(piece, stream, step, free):
        acc, got, first, rows = pieces[piece]
        order = orders[stream]
        pltpu.make_async_remote_copy(
            src_ref=acc.at[chunk(order, step, free, True), pl.ds(first, rows), lanes_of(stream)],
            dst_ref=got.at[slot_base(step) + free, pl.ds(first, rows), lanes_of(stream)],
            send_sem=send_sem.at[piece, stream, step],
            recv_sem=recv_sem.at[piece, stream, step],
            device_id={"dp": flip(me, order[step])},
            device_id_type=MESH,
        ).start()

    def send(piece, step):
        for stream in range(2):
            for free in range(2 ** (depth - 1 - step)):
                send_one(piece, stream, step, free)

    def wait_bytes(piece, stream, step, sem):
        acc, got, first, rows = pieces[piece]
        count = 2 ** (depth - 1 - step)
        where = got.at[pl.ds(slot_base(step), count), pl.ds(first, rows), lanes_of(stream)]
        pltpu.make_async_copy(where, where, sem.at[piece, stream, step]).wait()

    def add(piece, stream, step):
        acc, got, first, rows = pieces[piece]
        order = orders[stream]
        wait_bytes(piece, stream, step, recv_sem)
        tile = row_tile(rows)
        last = step == depth - 1
        for free in range(2 ** (depth - 1 - step)):
            kept = chunk(order, step, free, False)

            def body(index, carry):
                at = pl.multiple_of(first + index * tile, 16)
                where = pl.ds(at, tile)
                total = acc[kept, where, lanes_of(stream)].astype(WIDE) + got[
                    slot_base(step) + free, where, lanes_of(stream)
                ].astype(WIDE)
                if last and acc is split_acc:
                    split_out[where, lanes_of(stream)] = total
                elif last:
                    ring_own[where, lanes_of(stream)] = total.astype(LOW)
                else:
                    acc[kept, where, lanes_of(stream)] = total.astype(LOW)
                return carry

            lax.fori_loop(0, rows // tile, body, 0)

    parity = lax.rem(here, 2)
    mine = pl.ds(pl.multiple_of(parity * HALF, LANES), HALF)
    other_half = pl.ds(pl.multiple_of((1 - parity) * HALF, LANES), HALF)

    def ring_copy(piece, step):
        where = pl.ds(pieces[piece][2], pieces[piece][3])
        if step == 0:
            source, target = ring_own.at[where, other_half], ring_got.at[where]
        else:
            source, target = half_own.at[step - 1, where], half_got.at[step - 1, where]
        return pltpu.make_async_remote_copy(
            src_ref=source,
            dst_ref=target,
            send_sem=ring_send.at[piece, step],
            recv_sem=ring_recv.at[piece, step],
            device_id={"mp": flip(here, step % ring_depth)},
            device_id_type=MESH,
        )

    def ring_step(piece, step):
        first, rows = pieces[piece][2:]
        ring_copy(piece, step).wait_recv()
        tile = row_tile(rows)

        def body(index, carry):
            where = pl.ds(pl.multiple_of(first + index * tile, 16), tile)
            if step == 0:
                total = ring_own[where, mine].astype(WIDE) + ring_got[where, :].astype(WIDE)
            elif step < ring_depth:
                total = half_own[step - 1, where, :].astype(WIDE) + half_got[
                    step - 1, where, :
                ].astype(WIDE)
            if step < ring_depth:
                half_own[step, where, :] = total.astype(LOW)
            else:
                shared_out[where, mine] = half_own[step - 1, where, :].astype(WIDE)
                shared_out[where, other_half] = half_got[step - 1, where, :].astype(WIDE)
            return carry

        lax.fori_loop(0, rows // tile, body, 0)
        if step < ring_depth:
            ring_copy(piece, step + 1).start()

    def advance(piece, step):
        for stream in range(2):
            add(piece, stream, step)
            if step < depth - 1:
                for free in range(2 ** (depth - 2 - step)):
                    send_one(piece, stream, step + 1, free)
        if step == depth - 1 and piece < 3:
            ring_copy(piece, 0).start()

    room = words.shape[1]

    def scatter(index):
        local = ids_in[...] - index * table_rows
        entry = lax.broadcasted_iota(jnp.int32, (table_rows, mp * room), 0)
        hot = jnp.where(entry == local, 1.0, 0.0).astype(LOW)
        where = (index, pl.ds(0, table_rows))
        total = split_acc[where].astype(WIDE) + mm(hot, words[...].reshape(mp * room, D), NN)
        split_acc[where] = total.astype(LOW)

    count = 2 ** (depth - 1)
    other_core, own_core = 1 - me % 2, me % 2

    def scatter_other(index, carry):
        scatter(other_core + 2 * index)
        return carry

    def scatter_own(index, carry):
        scatter(own_core + 2 * index)
        return carry

    for copy in loads[:3]:
        copy.wait()
    send(0, 0)
    send(3, 0)

    take_slots(slots, pos_ref, ((columns_ref, slot_ref),))
    for pair in range(H // 2):
        lanes = slice(pair * LANES, (pair + 1) * LANES)
        rows = slice(pair * 2 * slots, (pair + 1) * 2 * slots)
        grad_mixed = pair_rows(grad_mixed_ref[:, lanes])
        shares = shares_ref[rows, :]
        grad_value[:, lanes] = mm(shares.astype(LOW), grad_mixed, TN).astype(LOW)
        grad_shares = mm(grad_mixed, value_ref[:, lanes], NT)
        scores = shares * (grad_shares - jnp.sum(shares * grad_shares, -1, keepdims=True))
        scores = scores.astype(LOW)
        score_ref[rows, :] = scores
        grad_query[:, lanes] = pair_lanes(mm(scores, key_ref[:, lanes], NN) * 0.125).astype(LOW)
        grad_key[:, lanes] = (mm(scores, pair_rows(query_ref[:, lanes]), TN) * 0.125).astype(LOW)
    advance(0, 0)
    advance(3, 0)

    loads[3].wait()
    grad_slot[...] = grad_zero_ref[...] + mm(grad_query[...], weights_ref[0], NT)
    entry = lax.broadcasted_iota(jnp.int32, (ROWS, slots), 0)
    put = jnp.where(entry == rows_ref[9:10, 0:slots], 1.0, 0.0).astype(LOW)
    high = grad_slot[...].astype(LOW)
    small_part = (grad_slot[...] - high.astype(WIDE)).astype(LOW)
    grad_rows[...] = (
        mm(grad_key[...], weights_ref[1], NT)
        + mm(grad_value[...], weights_ref[2], NT)
        + (mm(put, high, NN) + mm(put, small_part, NN))
    )
    gain = small_ref[0:1, :]
    tile = 96

    def normed_back(index, carry):
        where = pl.ds(pl.multiple_of(index * tile, 16), tile)
        grad, plain = grad_rows[where, :], plain_ref[where, :]
        value = norm_back(grad, plain, scale_ref[where, :], gain)
        grad_rows[where, :] = value
        grad_low[where, :] = value.astype(LOW)
        return carry[0] + column_sum(grad * plain), carry[1] + column_sum(grad)

    blank = jnp.zeros((1, D), WIDE)
    gains, shifts = lax.fori_loop(0, ROWS // tile, normed_back, (blank, blank))
    small_all[0:1, :] = gains
    small_all[1:2, :] = shifts

    keep_words = pltpu.make_async_copy(grad_low.at[0:TEXT], word_out, load_sem.at[5])
    keep_words.start()
    entry = lax.broadcasted_iota(jnp.int32, (mp * room, TEXT), 0)
    hot = jnp.where(entry == place_in[...], 1.0, 0.0).astype(LOW)
    packed[...] = mm(hot, grad_low[0:TEXT, :], NN).astype(LOW).reshape(mp, room, D)
    word_copies = []
    for other in range(1, mp):
        target = lax.rem(here + other, mp)
        word_copies.append(
            pltpu.make_async_remote_copy(
                src_ref=packed.at[target], dst_ref=words.at[here],
                send_sem=word_send.at[other - 1], recv_sem=word_recv.at[other - 1],
                device_id={"mp": target}, device_id_type=MESH,
            )
        )
        word_copies[-1].start()
    words[here] = packed[here]

    rows = D // dp
    for part, (left, right) in enumerate(
        ((zero_low_ref, grad_query), (low_ref, grad_key), (low_ref, grad_value))
    ):
        grad = mm(left[...], right[...], TN).reshape(dp, rows, D)
        first = part * plan.proj
        shared_acc[:, first : first + rows, :] = grad.astype(LOW)
    send(1, 0)
    advance(0, 1)
    advance(3, 1)

    extra, rows = ROWS - TEXT, TEXT // dp
    grad_rows[0:extra, :] = grad_rows[0:extra, :] + grad_rows[TEXT:ROWS, :]
    first = plan.places_at
    shared_acc[:, first : first + rows, :] = grad_rows[0:TEXT, :].reshape(dp, rows, D).astype(LOW)
    visual, rows, first = features_ref.shape[0], VCH // dp, plan.visual_at
    grad = mm(features_ref[...], grad_low[TEXT : TEXT + visual, :], TN)
    shared_acc[:, first : first + rows, :] = grad.reshape(dp, rows, D).astype(LOW)
    block = max(plan.box, 256)
    chunks, pieces_box = block // plan.box, plan.box // 32

    def table(index, carry):
        entry = lax.broadcasted_iota(jnp.int32, (block, ROWS), 0) + index * block
        found = []
        for column in range(6):
            hot = jnp.where(entry == rows_ref[column : column + 1, :], 1.0, 0.0).astype(LOW)
            found.append(mm(hot, grad_low[:, column * LANES : (column + 1) * LANES], NN))
        for number, grad in enumerate((found[0] + found[2], found[1] + found[3], *found[4:])):
            for part in range(block // 32):
                at, lane = plan.box_slot(number * pieces_box + part % pieces_box)
                shared_acc[index * chunks + part // pieces_box, at : at + 32, lane : lane + LANES] = (
                    grad[part * 32 : part * 32 + 32].astype(LOW)
                )
        return carry

    lax.fori_loop(0, NBOX // block, table, 0)
    advance(1, 0)

    lane = lax.broadcasted_iota(jnp.int32, (NB, LANES), 1)
    for kind in range(3):
        column, shift = KINDS[kind]
        first, second = key_hot(rows_ref, kind)
        below = below_of(rows_ref, slot_ref, kind)
        coarse_slot = jnp.right_shift(slot_ref[:, column : column + 1], shift)
        place = lax.broadcasted_iota(jnp.int32, (slots, NB), 1)
        hot = jnp.where(place == NB - 1 - coarse_slot, 1.0, 0.0).astype(LOW)

        def collect(pair, carry):
            where = pl.ds(pl.multiple_of(pair * 2 * slots, 16), 2 * slots)
            both = jnp.concatenate([below, below], 0)
            scores = score_ref[where, :]
            none = jnp.zeros((), LOW)
            found = mm(jnp.where(both, none, scores), first, NT) + mm(
                jnp.where(both, scores, none), second, NT
            )
            turned_ref[where, :] = found.astype(LOW)
            return carry

        lax.fori_loop(0, H // 2, collect, 0)
        for head in range(H):
            part = mm(hot, turned_ref[head * slots : (head + 1) * slots, :], TN)
            near = pltpu.roll(jnp.where(lane < NB, part, 0.0), 1, 1, stride=1, stride_axis=0)
            far = pltpu.roll(jnp.where(lane < NB, 0.0, part), NB, 1, stride=1, stride_axis=0)
            edges_ref[head : head + 1, :] = column_sum(near + far)
        edges_ref[H:16, :] = jnp.zeros((16 - H, LANES), WIDE)
        small_all[14 + kind : 15 + kind, :] = edge_rows_back(edges_ref[...])

    hidden = bias_in.shape[1]
    start = here * hidden
    small_all[2:3, :] = column_sum(grad_query[...].astype(WIDE))
    small_all[3:4, :] = column_sum(grad_value[...].astype(WIDE))
    small_all[4:10, :] = head_in[4:10, :]
    small_all[10:14, :] = jnp.zeros((4, D), WIDE)
    small_all[
        pl.ds(10 + start // D, 1), pl.ds(pl.multiple_of(lax.rem(start, D), LANES), hidden)
    ] = bias_in[...]
    cut = D // dp
    row, lane = plan.box_slot(plan.box_parts)
    shared_acc[:, pl.ds(row, 32), pl.ds(lane, LANES)] = jnp.zeros((dp, 32, LANES), LOW)
    for part in range(dp):
        shared_acc[part, row : row + VROWS, lane : lane + cut] = small_all[
            0:VROWS, part * cut : (part + 1) * cut
        ].astype(LOW)
    for part in range(plan.box_parts + 1, 6 * (plan.shared - plan.box_at) // 32):
        row, lane = plan.box_slot(part)
        shared_acc[:, pl.ds(row, 32), pl.ds(lane, LANES)] = jnp.zeros((dp, 32, LANES), LOW)
    send(2, 0)
    for step in range(2, depth):
        advance(0, step)
        advance(3, step)
    advance(2, 0)
    loads[4].wait()
    for other in range(1, mp):
        source = lax.rem(here + mp - other, mp)
        pltpu.make_async_copy(words.at[source], words.at[source], word_recv.at[other - 1]).wait()
    lax.fori_loop(0, count, scatter_other, 0)
    send(4, 0)
    send(5, 0)
    advance(1, 1)
    ring_step(0, 0)
    lax.fori_loop(0, count, scatter_own, 0)
    ring_step(0, 1)
    for step in range(2, depth - 1):
        advance(1, step)
    advance(2, 1)
    advance(1, depth - 1)
    for step in range(2, depth - 1):
        advance(2, step)
    advance(4, 0)
    advance(5, 0)
    advance(2, depth - 1)
    ring_queue = [(0, step) for step in range(2, ring_depth + 1)]
    ring_queue += [(piece, step) for step in range(ring_depth + 1) for piece in (1, 2)]
    for step in range(1, depth):
        for piece in (4, 5):
            share = -(-len(ring_queue) // (2 * (depth - step) - (piece - 4)))
            for turn in ring_queue[: share - 1 if step == depth - 1 and piece == 5 else share]:
                ring_step(*turn)
                ring_queue.remove(turn)
            advance(piece, step)
    for turn in ring_queue:
        ring_step(*turn)

    def squares(ref, rows):
        tile = row_tile(rows)

        def body(index, total):
            values = ref[pl.ds(pl.multiple_of(index * tile, 16), tile), :]
            return total + jnp.sum((values * values).reshape(tile // 8, 8, D), 0)

        total = lax.fori_loop(0, rows // tile, body, jnp.zeros((8, D), WIDE))
        folded = total[:, 0:LANES]
        for part in range(1, D // LANES):
            folded = folded + total[:, part * LANES : (part + 1) * LANES]
        return folded

    folded = squares(shared_out, plan.shared) * (1.0 / mp) + squares(split_out, split_out.shape[0])
    tile_mp[here, 0] = folded
    tile_mp[here, 1] = tile_in[...]

    def exchange(buffer, axis, index, count, base):
        copies = []
        for other in range(1, count):
            copies.append(
                pltpu.make_async_remote_copy(
                    src_ref=buffer.at[index],
                    dst_ref=buffer.at[index],
                    send_sem=tile_send.at[base + other],
                    recv_sem=tile_recv.at[base + other],
                    device_id={axis: lax.rem(index + other, count)},
                    device_id_type=MESH,
                )
            )
        for copy in copies:
            copy.start()
        for other in range(1, count):
            source = lax.rem(index + count - other, count)
            pltpu.make_async_copy(
                buffer.at[source], buffer.at[source], tile_recv.at[base + other]
            ).wait()
        return copies

    pending = exchange(tile_mp, "mp", here, mp, 0)
    total = tile_mp[0]
    for index in range(1, mp):
        total = total + tile_mp[index]
    tile_dp[me] = total
    pending = pending + exchange(tile_dp, "dp", me, dp, mp)
    total = tile_dp[0]
    for index in range(1, dp):
        total = total + tile_dp[index]
    tile_out[...] = total
    for copy in pending:
        copy.wait_send()
    keep_words.wait()
    for copy in word_copies:
        copy.wait_send()
    for piece in range(len(pieces)):
        for stream in range(2):
            for step in range(depth):
                wait_bytes(piece, stream, step, send_sem)
    for piece in range(3):
        for step in range(ring_depth + 1):
            ring_copy(piece, step).wait_send()


def back_step(
    plan, pos, grad_zero, grad_mixed, shares, query, key, value, zero_low, low, plain, scale,
    features, small, columns, rows, weights, table, out, ffn, head, bias, tile, place, ids,
):
    dp, mp = plan.dp, plan.mp
    slots = pos.shape[0]
    table_rows, ffn_rows = table.shape[1], ffn.shape[2]
    split = table_rows + 2 * ffn_rows * ffn.shape[3] // D
    depth, ring_depth = bits_of(dp), bits_of(mp)
    anywhere = pl.BlockSpec(memory_space=pl.ANY)
    vmem = pl.BlockSpec(memory_space=pltpu.VMEM)
    dma = pltpu.SemaphoreType.DMA
    low_scratch = lambda *shape: pltpu.VMEM(shape, LOW)
    wide_scratch = lambda *shape: pltpu.VMEM(shape, WIDE)

    def body(*refs):
        back_kernel(plan, table_rows, ffn_rows, refs)

    return pl.pallas_call(
        body,
        out_shape=(
            jax.ShapeDtypeStruct((plan.shared, D), WIDE),
            jax.ShapeDtypeStruct((split, D), WIDE),
            jax.ShapeDtypeStruct((2, 8, LANES), WIDE),
            jax.ShapeDtypeStruct((TEXT, D), LOW),
        ),
        in_specs=[pl.BlockSpec(memory_space=pltpu.SMEM)]
        + [vmem] * 14
        + [anywhere] * 4
        + [vmem] * 5,
        out_specs=(vmem, vmem, vmem, anywhere),
        scratch_shapes=[
            pltpu.VMEM((slots, 16), jnp.int32),
            low_scratch(H * slots, ROWS),
            low_scratch(slots, D),
            low_scratch(ROWS, D),
            low_scratch(ROWS, D),
            wide_scratch(ROWS, D),
            low_scratch(ROWS, D),
            low_scratch(H * slots, LANES),
            wide_scratch(slots, D),
            wide_scratch(16, LANES),
            low_scratch(3, D, D),
            low_scratch(dp, plan.shared, D),
            low_scratch(dp, split, D),
            low_scratch(dp - 1, plan.shared, D),
            low_scratch(dp - 1, split, D),
            low_scratch(plan.shared, HALF),
            low_scratch(plan.shared, D),
            low_scratch(ring_depth, plan.shared, HALF),
            low_scratch(ring_depth, plan.shared, HALF),
            low_scratch(mp, word_room(mp), D),
            low_scratch(mp, word_room(mp), D),
            wide_scratch(24, D),
            wide_scratch(mp, 2, 8, LANES),
            wide_scratch(dp, 2, 8, LANES),
            dma((6,)),
            dma((6, 2, depth)),
            dma((6, 2, depth)),
            dma((3, ring_depth + 1)),
            dma((3, ring_depth + 1)),
            dma((mp - 1,)),
            dma((mp - 1,)),
            dma((mp + dp,)),
            dma((mp + dp,)),
        ],
        compiler_params=pltpu.CompilerParams(
            collective_id=5, has_side_effects=True, vmem_limit_bytes=62 * 2**20
        ),
        name="back_step",
    )(
        pos, grad_zero, grad_mixed, shares, query, key, value, zero_low, low, plain, scale,
        features, small, columns, rows, weights, table, out, ffn, head, bias, tile, place, ids,
    )


def on_device(
    tokens, text_box, segments, alive_text, features, mask_pos, mask_label, mask_valid, *states
):
    (projections, box_tables, position_table, visual_proj, small_params, word_table, feedforward) = (
        states[::3]
    )
    dp, mp = lax.axis_size("dp"), lax.axis_size("mp")
    plan = Plan(dp, mp)
    (
        table_parts, proj_parts, box_parts, place_parts, visual_parts, ffn_parts, small, places,
        ids, most, info, columns, marks_zero, marks_one, *front,
    ) = front_step(
        plan, mask_pos, mask_label, mask_valid, word_table, projections, box_tables,
        position_table, visual_proj, small_params, feedforward, tokens, text_box[0].T, segments,
        alive_text, features,
    )

    def joined(parts, rows):
        parts = parts[..., :rows, :]
        return parts.reshape(parts.shape[:-3] + (dp * rows, parts.shape[-1]))

    work_table = joined(table_parts, word_table.shape[0])
    work_proj = joined(proj_parts, D // dp)
    work_boxes = joined(box_parts, NBOX // dp)
    work_places = joined(place_parts, TEXT // dp)
    work_visual = joined(visual_parts, VCH // dp)
    work_ffn = joined(ffn_parts, D // dp)
    vocab_shard = work_table.shape[0]
    room = word_room(mp)
    crowded = most[0, 0] > room

    def local_words():
        local_ids = tokens - lax.axis_index("mp") * vocab_shard
        inside = (local_ids >= 0) & (local_ids < vocab_shard)
        return inside, jnp.clip(local_ids, 0, vocab_shard - 1)

    def exchange_words(state):
        inside, index = local_words()
        found = jnp.where(inside[..., None], jnp.take(work_table, index, axis=0), jnp.zeros((), LOW))
        word = lax.psum_scatter(found, "mp", scatter_dimension=0, tiled=True)[0]
        again = front_again(
            mask_pos, word, features, work_places, work_boxes, work_visual, small, columns, info,
            work_proj,
        )
        return (False, *again)

    _, *front = lax.while_loop(lambda state: state[0], exchange_words, (crowded, *front))
    (
        mixed, slot_zero, slot_low, normed_low, plain, scale, queries, keys, values, shares,
    ) = front
    (
        grad_slot, grad_mixed, grad_out_weight, grad_ffn, grad_table, head_rows, grad_ffn_bias,
        own_tile,
    ) = head_step(
        mp, mixed, slot_zero, work_proj, small, work_ffn, work_table,
        marks_zero, marks_one,
    )
    def split_rows(part):
        rows = part.shape[-2] // dp
        part = part.astype(LOW).reshape(part.shape[:-2] + (dp, rows, part.shape[-1]))
        extra = [(0, 0)] * (part.ndim - 2) + [(0, pad_up(rows, 16) - rows), (0, 0)]
        return jnp.pad(part, extra) if extra[-2][1] else part

    table_split, ffn_split = split_rows(grad_table), split_rows(grad_ffn)
    shared_sum, split_sum, totals, grad_word = back_step(
        plan, mask_pos, grad_slot, grad_mixed, shares, queries, keys, values, slot_low, normed_low,
        plain, scale, features, small, columns, info, work_proj, table_split,
        split_rows(grad_out_weight), ffn_split, head_rows, grad_ffn_bias, own_tile, places, ids,
    )
    def exchange_word_gradients(state):
        inside, index = local_words()
        shard = tokens // vocab_shard
        same = (shard[..., None] == jnp.arange(mp)).astype(jnp.int32)
        rank = jnp.sum((jnp.cumsum(same, 1) - same) * same, -1)
        late = rank >= room
        own = lax.dynamic_index_in_dim(late, lax.axis_index("mp"), 0, False)
        sent = jnp.where(own[:, None], grad_word, jnp.zeros((), LOW))
        group = lax.all_gather(sent, "mp", axis=0).astype(WIDE)
        group = jnp.where((inside & late)[..., None], group, 0.0)
        extra = jnp.zeros((vocab_shard, D), WIDE).at[index].add(group)
        part = lax.psum_scatter(extra, "dp", scatter_dimension=0, tiled=True)
        split = state[1].at[: part.shape[0]].add(part)
        squares = jnp.sum(shared_sum * shared_sum) / mp + jnp.sum(split * split)
        squares = lax.psum(squares, ("dp", "mp"))
        return False, split, jnp.zeros_like(totals).at[0, 0, 0].set(squares).at[1].set(totals[1])

    _, split_sum, totals = lax.while_loop(
        lambda state: state[0], exchange_word_gradients, (crowded, split_sum, totals)
    )
    outputs = adam_update(
        plan, table_split.shape[1], ffn_split.shape[2], shared_sum, split_sum, totals, states
    )
    return tuple(outputs[:21]) + tuple(part.reshape(()) for part in outputs[21:])


def solution(mesh):
    in_specs = (
        P("dp", None),
        P(("dp", "mp"), None, None),
        P(("dp", "mp"), None),
        P(("dp", "mp"), None),
        P(("dp", "mp"), None),
        P(("dp", "mp")),
        P("dp"),
        P("dp"),
        P(None, "dp", None),
        P(None, "dp", None),
        P(None, "dp", None),
        P(None, "dp", None),
        P(None, "dp", None),
        P(None, "dp", None),
        P("dp", None),
        P("dp", None),
        P("dp", None),
        P("dp", None),
        P("dp", None),
        P("dp", None),
        P(None, "dp"),
        P(None, "dp"),
        P(None, "dp"),
        P(("mp", "dp"), None),
        P(("mp", "dp"), None),
        P(("mp", "dp"), None),
        P(None, "dp", "mp"),
        P(None, "dp", "mp"),
        P(None, "dp", "mp"),
    )
    out_specs = (
        P(None, "dp", None),
        P(None, "dp", None),
        P(None, "dp", None),
        P(None, "dp", None),
        P(None, "dp", None),
        P(None, "dp", None),
        P("dp", None),
        P("dp", None),
        P("dp", None),
        P("dp", None),
        P("dp", None),
        P("dp", None),
        P(None, "dp"),
        P(None, "dp"),
        P(None, "dp"),
        P(("mp", "dp"), None),
        P(("mp", "dp"), None),
        P(("mp", "dp"), None),
        P(None, "dp", "mp"),
        P(None, "dp", "mp"),
        P(None, "dp", "mp"),
        P(),
        P(),
        P(),
    )
    return jax.shard_map(
        on_device, mesh=mesh, in_specs=in_specs, out_specs=out_specs, check_vma=False
    )
```
